32 devices in a mesh: groups: 2 (over x), lon: 8 (over z, y), lat: 2 (over core).
Axes of the slice: x: 2, y: 2, z: 4, core: 2. Of those that a mesh axis runs over, the one named last changes fastest.
Arguments:
- lam_in: float32 [2048, 1024], P(('groups', 'lat'), 'lon'), parts along dimension 0, may hold values from -6 to 6
- flux_east: float32 [2048, 1024], P(('groups', 'lat'), 'lon'), parts along dimension 0, may hold values from -6 to 6
- flux_north: float32 [2048, 1024], P(('groups', 'lat'), 'lon'), parts along dimension 0, may hold values from -6 to 6
- depth: float32 [2048, 1024], P(('groups', 'lat'), 'lon'), parts along dimension 0, may hold values from 0.2 to 2
- drag: float32 [2048, 1024], P(('groups', 'lat'), 'lon'), parts along dimension 0, may hold values from 0.05 to 1
- ocean: int32 [2048, 1024], P(('groups', 'lat'), 'lon'), parts along dimension 0, may hold values 0 or 1
- coarse_of: int32 [1024, 1024], P('lat', 'lon'), may hold values from 0 to 8191, as said below
- green: float32 [8192, 8192], P(('lon', 'lat')), may hold values from -3 to 3
Outputs:
- lam_out: float32 [2048, 1024], P(('groups', 'lat'), 'lon'), parts along dimension 0
- east_out: float32 [2048, 1024], P(('groups', 'lat'), 'lon'), parts along dimension 0
- north_out: float32 [2048, 1024], P(('groups', 'lat'), 'lon'), parts along dimension 0
- bands: float32 [3, 4, 512, 1024], P(None, ('groups', 'lat'), 'lon'), parts along dimension 1
The draws below stay inside these ranges and needn't reach their ends.
There are 2 independent parts, one for each index of `groups`. The reference program is written for one: setup_inputs(seed, part) draws one part's arguments, and reference() takes and returns one part's arrays. A program takes and returns all parts, laid end to end along the dimension named above; an argument that names none is the same for every part. Nothing has to cross between parts.
Inputs may be any that keep to these rules, and one draw needn't show every extreme that they name: `coarse_of`: block (latitude band b, longitude band a) of 512 x 128 cells holds only the coarse points (a * 2 + b) * 512 to that plus 512 - 1; the first 512 cells of each block in row-major order hold these points in order, so that every point has a cell.
All inputs are finite; a program needn't handle non-finite values. No bound on the sum of `ocean` on one device may be relied on, other than what follows from the above.
Results may differ from the reference program's by a relative error of at most 0.0001.
Values sent between devices are 32-bit elements; how exact they have to be, the bound alone decides.
No kernel may reach another device: no remote copies, remote signals or barrier semaphores. Data moves between devices by JAX's collectives and lax.ppermute only.
A program may use at most 64 MiB of HBM per device.

```python
import math
import jax
import jax.numpy as jnp
from jax import lax

CLAT = 512
CLON = 128
NCOARSE = 8192
ITERS = 2
NLAT = 1024
NLON = 1024
COARSE_DEV = 512
N_LAT = 2


def draw_coarse_of(key, part):
    key = jax.random.fold_in(key, 7)
    row = lax.broadcasted_iota(jnp.int32, (NLAT, NLON), 0)
    col = lax.broadcasted_iota(jnp.int32, (NLAT, NLON), 1)
    band_lat = row // CLAT
    band_lon = col // CLON
    inner = row % CLAT * CLON + col % CLON
    picked = jax.random.randint(key, (NLAT, NLON), 0, COARSE_DEV, dtype=jnp.int32)
    local = jnp.where(inner < COARSE_DEV, inner, picked)
    return ((band_lon * (NLAT // CLAT) + band_lat) * COARSE_DEV + local).astype(jnp.int32)


def plant(array, stream_key, low, high):
    extent = array.shape
    spot = [jax.random.randint(jax.random.fold_in(stream_key, axis), (), 0, extent[axis]) for axis in range(len(extent))]
    array = array.at[tuple(spot)].set(low)
    longest = extent.index(max(extent))
    spot[longest] = (spot[longest] + 1) % extent[longest]
    return array.at[tuple(spot)].set(high)


def shard_levels(stream_key, dims, cuts, low, top_value):
    level = 1.0
    for axis_at, blocks in cuts:
        draws = jax.random.uniform(jax.random.fold_in(jax.random.fold_in(stream_key, 6), axis_at), (blocks,), jnp.float32, low / len(cuts), top_value / len(cuts))
        level = level * jnp.repeat(jnp.exp(draws), dims[axis_at] // blocks).reshape((-1,) + (1,) * (len(dims) - 1 - axis_at))
    return level


def gaussian(rng, shape, spread, reach, split=(), kind=jnp.bfloat16):
    values = jax.random.normal(rng, shape, jnp.float32) * spread
    if len(split) > 0:
        values = shard_levels(rng, shape, split, -0.22, 0.18) * values
    return jnp.clip(values, min=-reach, max=reach).astype(kind)


def setup_inputs(seed: int = 0, part: int = 0) -> dict:
    keys = jax.random.split(jax.random.key(seed), 9)
    part_keys = jax.random.split(jax.random.fold_in(keys[8], part), 9)
    return {
        "lam_in": gaussian(part_keys[0], (NLAT, NLON), 1.0, 6.0, ((0, 2), (1, 8)), jnp.float32),
        "flux_east": gaussian(part_keys[1], (NLAT, NLON), 1.0, 6.0, ((0, 2), (1, 8)), jnp.float32),
        "flux_north": gaussian(part_keys[2], (NLAT, NLON), 1.0, 6.0, ((0, 2), (1, 8)), jnp.float32),
        "depth": jnp.clip(jnp.exp(math.log(2.0) - 2.3025851 * jax.random.uniform(part_keys[3], (NLAT, NLON), jnp.float32) ** shard_levels(part_keys[3], (NLAT, NLON), ((0, 2), (1, 8)), -0.2, 0.2)), 0.2, 2.0),
        "drag": jnp.clip(jnp.exp(math.log(1.0) - 2.9957323 * jax.random.uniform(part_keys[4], (NLAT, NLON), jnp.float32) ** shard_levels(part_keys[4], (NLAT, NLON), ((0, 2), (1, 8)), -0.2, 0.2)), 0.05, 1.0),
        "ocean": plant((jax.random.randint(part_keys[5], (NLAT, NLON), 0, 4) < 3).astype(jnp.int32), jax.random.fold_in(part_keys[5], 1), 0, 1),
        "coarse_of": draw_coarse_of(jax.random.fold_in(keys[8], 71), part),
        "green": gaussian(keys[7], (NCOARSE, NCOARSE), 0.5, 3.0, ((0, 16),), jnp.float32),
    }


flux_ratio = 0.25
slope_ratio = 0.25
drag_step = 1.0
attract_coef = 0.5


def north_of(field):
    return jnp.concatenate([field[1:], jnp.zeros_like(field[:1])], axis=0)


def south_of(field):
    return jnp.concatenate([jnp.zeros_like(field[:1]), field[:-1]], axis=0)


def reference(lam_in, flux_east, flux_north, depth, drag, ocean, coarse_of, green):
    ocean_f = ocean.astype(jnp.float32)
    depth_u = 0.5 * (depth + jnp.roll(depth, -1, 1))
    damp_u = ocean_f * jnp.roll(ocean_f, -1, 1) / (1.0 + drag_step * 0.5 * (drag + jnp.roll(drag, -1, 1)))
    depth_v = 0.5 * (depth + north_of(depth))
    damp_v = ocean_f * north_of(ocean_f) / (1.0 + drag_step * 0.5 * (drag + north_of(drag)))
    flat_ids = coarse_of.reshape(-1).astype(jnp.int32)
    counts = jax.ops.segment_sum(jnp.ones(flat_ids.shape, jnp.float32), flat_ids, NCOARSE)
    lam, east, north = lam_in, flux_east, flux_north
    for step in range(ITERS):
        adj_u = damp_u * (east + flux_ratio * depth_u * (jnp.roll(lam, -1, 1) - lam))
        adj_v = damp_v * (north + flux_ratio * depth_v * (north_of(lam) - lam))
        source = slope_ratio * (jnp.roll(adj_u, 1, 1) - adj_u + south_of(adj_v) - adj_v)
        loads = jax.ops.segment_sum(source.reshape(-1), flat_ids, NCOARSE) / counts
        potential = jnp.dot(green, loads, precision=lax.Precision.HIGHEST)
        lam = ocean_f * (lam + source - attract_coef * potential[flat_ids].reshape(lam.shape))
        east, north = adj_u, adj_v
    slope_x = jnp.roll(lam, -1, 1) - lam
    slope_y = north_of(lam) - lam
    bands = jnp.stack([lam, slope_x, slope_y]).reshape(3, N_LAT, CLAT, NLON)
    return lam, east, north, bands
```

```python
import functools

import jax
import jax.numpy as jnp
from jax import lax
from jax.experimental import pallas as pl
from jax.experimental.pallas import tpu as pltpu
from jax.sharding import PartitionSpec as P

f32 = jnp.float32
bf16 = jnp.bfloat16
i32 = jnp.int32

LANES = 128
LOW = 32
HIGH = 16
PIECES = 2
SEG_ROWS = 128
STEP_ROWS = 64
HIGHEST = lax.Precision.HIGHEST

flux_ratio = 0.25
slope_ratio = 0.25
drag_step = 1.0
attract_coef = 0.5

LAM, DEPTH, DRAG, OCEAN, POINT, FLUX = range(6)
ADJ_W, ADJ_E, C_W, C_E, G_W, G_E, ID_W, ID_E = range(8)
ADJ_L, C_L, G_L, ID_L = range(4)


def iota(shape, dim):
    return lax.broadcasted_iota(i32, shape, dim)


def roll_east(x):
    return pltpu.roll(x, LANES - 1, 1)


def roll_west(x):
    return pltpu.roll(x, 1, 1)


def local_ids(ids, points):
    return lax.bitwise_and(ids, points - 1)


def bf16_pieces(values):
    out = []
    for piece in range(PIECES):
        top = values.astype(bf16).astype(f32)
        out.append(top)
        if piece < PIECES - 1:
            values = values - top
    return out


def segment_part(values, ids, points, with_counts=False):
    blocks = points // LANES
    high = lax.shift_right_logical(ids, 5)
    high = lax.bitwise_and(high, 3) * blocks + lax.shift_right_logical(high, 2)
    low = lax.bitwise_and(ids, LOW - 1)
    high_iota = iota((HIGH, LANES), 0)
    low_iota = iota((LOW, LANES), 0)
    pieces = bf16_pieces(values)
    left, right = [], []
    for row in range(values.shape[0]):
        mask = jnp.broadcast_to(high[row : row + 1], (HIGH, LANES)) == high_iota
        parts = [
            jnp.where(mask, jnp.broadcast_to(piece[row : row + 1], (HIGH, LANES)), 0.0)
            for piece in pieces
        ]
        if with_counts:
            parts.append(jnp.where(mask, 1.0, 0.0))
        left.append(jnp.concatenate(parts, 0).astype(bf16))
        mask = jnp.broadcast_to(low[row : row + 1], (LOW, LANES)) == low_iota
        right.append(jnp.where(mask, 1.0, 0.0).astype(bf16))
    return lax.dot_general(
        jnp.concatenate(left, 1),
        jnp.concatenate(right, 1),
        (((1,), (1,)), ((), ())),
        preferred_element_type=f32,
    )


def segment_all(value_ref, id_ref, points, with_counts=False):
    rows = value_ref.shape[0]
    parts = PIECES + int(with_counts)

    def step(index, total):
        at = pl.ds(pl.multiple_of(index * SEG_ROWS, SEG_ROWS), SEG_ROWS)
        return total + segment_part(
            value_ref[at, :], local_ids(id_ref[at, :], points), points, with_counts
        )

    return lax.fori_loop(0, rows // SEG_ROWS, step, jnp.zeros((parts * HIGH, LOW), f32))


def sum_pieces(parts):
    total = parts[:HIGH]
    for piece in range(1, PIECES):
        total = total + parts[piece * HIGH : (piece + 1) * HIGH]
    return total


def as_points(table, points):
    blocks = points // LANES
    return jnp.concatenate([table[q * blocks : (q + 1) * blocks] for q in range(4)], 1)


def fold(line):
    return jnp.concatenate(
        [line[:, k * LANES : (k + 1) * LANES] for k in range(line.shape[1] // LANES)], 0
    )


def unfold(block):
    return jnp.concatenate([block[k : k + 1] for k in range(block.shape[0])], 1)


def take_sides(block):
    sub, lane = iota((8, LANES), 0), iota((8, LANES), 1)
    pick = ((sub == 0) & (lane == 0)) | ((sub == 1) & (lane == LANES - 1))
    return lax.dot_general(
        pick.astype(f32), block, (((1,), (1,)), ((), ())), precision=HIGHEST,
        preferred_element_type=f32,
    )


def put_sides(lines, entries):
    sub, lane = iota((8, LANES), 0), iota((8, LANES), 1)
    parts = []
    for first, last in entries:
        part = jnp.zeros((8, LANES), f32)
        if first is not None:
            part = jnp.where((sub == first[0]) & (lane == 0), first[1], part)
        if last is not None:
            part = jnp.where((sub == last[0]) & (lane == LANES - 1), last[1], part)
        parts.append(part)
    return lax.dot_general(
        lines, jnp.concatenate(parts, 1), (((0,), (0,)), ((), ())), precision=HIGHEST,
        preferred_element_type=f32,
    )


def green_product(green_ref, load_row, acc_ref):
    points, total = green_ref.shape
    tall = 32

    def step(index, carry):
        at = pl.ds(pl.multiple_of(index * tall, tall), tall)
        acc = jnp.zeros((tall, LANES), f32)
        for k in range(total // LANES):
            acc = acc + green_ref[at, k * LANES : (k + 1) * LANES] * jnp.broadcast_to(
                load_row(k), (tall, LANES)
            )
        acc_ref[at, :] = acc
        return carry

    lax.fori_loop(0, points // tall, step, 0)
    return lax.dot_general(
        jnp.ones((8, LANES), f32), acc_ref[...], (((1,), (1,)), ((), ())), precision=HIGHEST,
        preferred_element_type=f32,
    )


def spread(potential, ids):
    points = potential.shape[1]
    rows = ids.shape[0]
    low = lax.bitwise_and(ids, LANES - 1)
    block = lax.shift_right_logical(ids, 7)
    out = None
    for k in range(points // LANES):
        table = potential[:, k * LANES : (k + 1) * LANES]
        table = jnp.broadcast_to(table[None], (rows // 8, 8, LANES)).reshape(rows, LANES)
        value = jnp.take_along_axis(table, low, axis=1, mode="promise_in_bounds")
        out = value if out is None else jnp.where(block == k, value, out)
    return out


def next_rows(ref, start, count, last=None):
    if start + count < ref.shape[0]:
        return ref[start + 1 : start + count + 1, :]
    return jnp.concatenate([ref[start + 1 :, :], jnp.zeros((1, LANES), ref.dtype)], 0)


def south_rows(first, block):
    return jnp.concatenate([first, block[:-1]], 0)


def pack_kernel(lam, east, north, depth, drag, ocean, coarse, to_east, to_west, to_lat, *, points):
    rows = lam.shape[0]
    lat = lax.axis_index("lat")
    sides = take_sides(
        jnp.concatenate(
            [
                lam[...],
                depth[...],
                drag[...],
                ocean[...].astype(f32),
                local_ids(coarse[...], points).astype(f32),
                east[...],
            ],
            0,
        )
    )
    zero = jnp.zeros((2, rows), f32)
    to_west[...] = jnp.concatenate(
        [sides[0:1, k * rows : (k + 1) * rows] for k in range(6)] + [zero], 0
    )
    to_east[...] = jnp.concatenate(
        [sides[1:2, k * rows : (k + 1) * rows] for k in range(6)] + [zero], 0
    )

    def border(row):
        return jnp.concatenate(
            [
                lam[row : row + 1, :],
                depth[row : row + 1, :],
                drag[row : row + 1, :],
                ocean[row : row + 1, :].astype(f32),
                local_ids(coarse[row : row + 1, :], points).astype(f32),
                north[row : row + 1, :],
                jnp.zeros((2, LANES), f32),
            ],
            0,
        )

    to_lat[...] = jnp.where(lat == 0, border(rows - 1), border(0))


def inner_kernel(
    lam, east, north, depth, drag, ocean, coarse,
    held, gu, cu, gv, cv, sums, source, *, points,
):
    rows = lam.shape[0]
    inner = iota((STEP_ROWS, LANES), 1) < LANES - 1
    carry = jnp.zeros((1, LANES), f32)
    for start in range(0, rows, STEP_ROWS):
        at = slice(start, start + STEP_ROWS)
        lam_c, depth_c, drag_c = lam[at, :], depth[at, :], drag[at, :]
        ocean_c = ocean[at, :].astype(f32)
        damp = jnp.where(
            inner,
            ocean_c * roll_east(ocean_c) / (1.0 + drag_step * 0.5 * (drag_c + roll_east(drag_c))),
            0.0,
        )
        ratio = damp * (flux_ratio * 0.5) * (depth_c + roll_east(depth_c))
        adj_u = damp * east[at, :] + ratio * (roll_east(lam_c) - lam_c)
        cu[at, :] = ratio
        gu[at, :] = damp * adj_u
        ocean_n = next_rows(ocean, start, STEP_ROWS).astype(f32)
        damp = (
            ocean_c
            * ocean_n
            / (1.0 + drag_step * 0.5 * (drag_c + next_rows(drag, start, STEP_ROWS)))
        )
        ratio = damp * (flux_ratio * 0.5) * (depth_c + next_rows(depth, start, STEP_ROWS))
        adj_v = damp * north[at, :] + ratio * (next_rows(lam, start, STEP_ROWS) - lam_c)
        cv[at, :] = ratio
        gv[at, :] = damp * adj_v
        src = slope_ratio * (roll_west(adj_u) - adj_u + south_rows(carry, adj_v) - adj_v)
        carry = adj_v[STEP_ROWS - 1 :]
        source[at, :] = src
        held[at, :] = lam_c + src
    sums[...] = segment_all(source, coarse, points, True)


def face(low, high, flux):
    damp = (
        low[OCEAN : OCEAN + 1]
        * high[OCEAN : OCEAN + 1]
        / (1.0 + drag_step * 0.5 * (low[DRAG : DRAG + 1] + high[DRAG : DRAG + 1]))
    )
    ratio = damp * (flux_ratio * 0.5) * (low[DEPTH : DEPTH + 1] + high[DEPTH : DEPTH + 1])
    adj = damp * flux + ratio * (high[LAM : LAM + 1] - low[LAM : LAM + 1])
    return adj, ratio, damp * adj


def rim_kernel(
    own_east, own_west, own_lat, from_west, from_east, from_lat, sums,
    payload, lines, lat_lines, *, points,
):
    lat = lax.axis_index("lat")
    blocks = points // LANES
    west, east = own_west[...], own_east[...]
    far_west, far_east = from_west[...], from_east[...]
    mine, other = own_lat[...], from_lat[...]
    adj_w, c_w, g_w = face(far_west, west, far_west[FLUX : FLUX + 1])
    adj_e, c_e, g_e = face(east, far_east, east[FLUX : FLUX + 1])
    lower = jnp.where(lat == 0, mine, other)
    upper = jnp.where(lat == 0, other, mine)
    adj_l, c_l, g_l = face(lower, upper, lower[FLUX : FLUX + 1])
    lines[...] = jnp.concatenate(
        [adj_w, adj_e, c_w, c_e, g_w, g_e, far_west[POINT : POINT + 1], far_east[POINT : POINT + 1]],
        0,
    )
    lat_lines[...] = jnp.concatenate(
        [adj_l, c_l, g_l, other[POINT : POINT + 1], jnp.zeros((4, LANES), f32)], 0
    )
    sign = jnp.where(lat == 0, -slope_ratio, slope_ratio)
    pad = jnp.zeros((1, LANES), f32)
    values = jnp.concatenate(
        [fold(slope_ratio * adj_w), fold(-slope_ratio * adj_e), sign * adj_l, pad], 0
    )
    ids = jnp.concatenate(
        [
            fold(west[POINT : POINT + 1]),
            fold(east[POINT : POINT + 1]),
            mine[POINT : POINT + 1],
            pad,
        ],
        0,
    ).astype(i32)
    total = sum_pieces(sums[...]) + sum_pieces(segment_part(values, ids, points))
    counts = as_points(sums[PIECES * HIGH : (PIECES + 1) * HIGH, :], points)
    inverse = 1.0 / counts
    loads = as_points(total, points) * inverse
    part = jnp.concatenate([loads, inverse], 0)
    if part.shape[0] < 8:
        part = jnp.concatenate([part, jnp.zeros((8 - part.shape[0], LANES), f32)], 0)
    for target in range(payload.shape[0]):
        payload[target] = part


def neighbours(n_lon, n_lat):
    lon, lat = lax.axis_index("lon"), lax.axis_index("lat")
    west = lax.rem(lon + n_lon - 1, n_lon) * n_lat + lat
    east = lax.rem(lon + 1, n_lon) * n_lat + lat
    other = lon * n_lat + (1 - lat)
    return west, east, other


def second_kernel(
    first, green, coarse, ocean, held_in, gu, cu, gv, cv, lines, lat_lines,
    payload, held, adj_u_out, adj_v_out, acc, lam, source, sides, *, points, n_lon, n_lat,
):
    rows = coarse.shape[0]
    blocks = points // LANES
    lat = lax.axis_index("lat")
    south_end = jnp.where(lat == 1, 1.0, 0.0)
    north_end = jnp.where(lat == 0, 1.0, 0.0)
    potential = green_product(
        green, lambda k: first[k // blocks, k % blocks : k % blocks + 1, :], acc
    )
    put = put_sides(
        lines[...],
        [
            ((ADJ_W, slope_ratio), (ADJ_E, -slope_ratio)),
            ((C_W, 1.0), (C_E, 1.0)),
            (None, (G_E, 1.0)),
        ],
    )
    adj_l = lat_lines[ADJ_L : ADJ_L + 1, :]
    c_l = lat_lines[C_L : C_L + 1, :]
    g_l = lat_lines[G_L : G_L + 1, :]
    row = iota((STEP_ROWS, LANES), 0)
    lane = iota((STEP_ROWS, LANES), 1)
    lam[rows : rows + 8, :] = jnp.zeros((8, LANES), f32)
    for start in range(0, rows, STEP_ROWS):
        at = slice(start, start + STEP_ROWS)
        pot = spread(potential, local_ids(coarse[at, :], points))
        value = held_in[at, :] + put[at, :LANES] - attract_coef * pot
        if start == 0:
            value = value + jnp.where(row == 0, south_end * slope_ratio * adj_l, 0.0)
        if start == rows - STEP_ROWS:
            value = value - jnp.where(row == STEP_ROWS - 1, north_end * slope_ratio * adj_l, 0.0)
        value = ocean[at, :].astype(f32) * value
        lam[at, :] = value
        sides[rows + start : rows + start + STEP_ROWS, :] = value
    carry = south_end * c_l * lam[0:1, :]
    to_lat_south = -slope_ratio * carry
    for start in range(0, rows, STEP_ROWS):
        at = slice(start, start + STEP_ROWS)
        lam_c = lam[at, :]
        c_side = put[at, LANES : 2 * LANES]
        east_c = jnp.where(lane == LANES - 1, c_side, cu[at, :])
        adj_u = (
            gu[at, :]
            + put[at, 2 * LANES :]
            + east_c * (jnp.where(lane == LANES - 1, 0.0, roll_east(lam_c)) - lam_c)
        )
        west_part = c_side * lam_c
        g_c, c_c = gv[at, :], cv[at, :]
        if start == rows - STEP_ROWS:
            last = row == STEP_ROWS - 1
            g_c = g_c + jnp.where(last, north_end * g_l, 0.0)
            c_c = c_c + jnp.where(last, north_end * c_l, 0.0)
        adj_v = g_c + c_c * (lam[start + 1 : start + STEP_ROWS + 1, :] - lam_c)
        src = slope_ratio * (
            jnp.where(lane == 0, west_part, roll_west(adj_u))
            - adj_u
            + south_rows(carry, adj_v)
            - adj_v
        )
        carry = adj_v[STEP_ROWS - 1 :]
        adj_u_out[at, :] = adj_u
        adj_v_out[at, :] = adj_v
        source[at, :] = src
        held[at, :] = lam_c + src
        sides[at, :] = jnp.where(lane == 0, -slope_ratio * west_part, slope_ratio * adj_u)
    to_lat = jnp.where(lat == 0, slope_ratio * carry, to_lat_south)
    edge = jnp.where(lat == 0, lam[rows - 1 : rows, :], lam[0:1, :])
    taken = take_sides(sides[...])
    own = as_points(sum_pieces(segment_all(source, coarse, points)), points)

    def away(line, ids):
        return as_points(sum_pieces(segment_part(line, ids.astype(i32), points)), points)

    east_part = away(fold(taken[1:2, :rows]), fold(lines[ID_E : ID_E + 1, :]))
    west_part = away(fold(taken[0:1, :rows]), fold(lines[ID_W : ID_W + 1, :]))
    pad = jnp.zeros((1, LANES), f32)
    lat_part = away(
        jnp.concatenate([to_lat, pad], 0),
        jnp.concatenate([lat_lines[ID_L : ID_L + 1, :], pad], 0),
    )
    part = jnp.concatenate([own, east_part, west_part, lat_part], 0)
    spare = payload.shape[1] - part.shape[0]
    part = jnp.concatenate([part, jnp.zeros((spare, LANES), f32)], 0)
    for target in range(payload.shape[0]):
        payload[target] = part
    west, east, other = neighbours(n_lon, n_lat)
    begin = 4 * blocks
    tall = rows // LANES
    payload[west, begin : begin + tall, :] = fold(taken[0:1, rows:])
    payload[east, begin : begin + tall, :] = fold(taken[1:2, rows:])
    payload[other, begin + tall : begin + tall + 1, :] = edge


def last_kernel(
    first, second, green, coarse, ocean, held, adj_u_in, adj_v_in, lines, lat_lines,
    lam_out, east_out, north_out, payload, edge, acc, loads, *, points, n_lon, n_lat,
):
    rows = coarse.shape[0]
    blocks = points // LANES
    tall = rows // LANES
    lat = lax.axis_index("lat")
    for lon in range(n_lon):
        for band in range(n_lat):
            here = lon * n_lat + band
            west = (lon - 1) % n_lon * n_lat + band
            east = (lon + 1) % n_lon * n_lat + band
            other = lon * n_lat + 1 - band
            total = (
                second[here, :blocks, :]
                + second[west, blocks : 2 * blocks, :]
                + second[east, 2 * blocks : 3 * blocks, :]
                + second[other, 3 * blocks : 4 * blocks, :]
            )
            loads[here * blocks : (here + 1) * blocks, :] = (
                total * first[here, blocks : 2 * blocks, :]
            )
    potential = green_product(green, lambda k: loads[k : k + 1, :], acc)
    west, east, other = neighbours(n_lon, n_lat)
    begin = 4 * blocks
    lam_w = unfold(second[west, begin : begin + tall, :])
    lam_e = unfold(second[east, begin : begin + tall, :])
    lam_l = second[other, begin + tall : begin + tall + 1, :]
    add_e = lines[C_E : C_E + 1, :] * lam_e
    add_w = lines[G_W : G_W + 1, :] - lines[C_W : C_W + 1, :] * lam_w
    put = put_sides(
        jnp.concatenate([add_w, add_e, jnp.zeros((6, rows), f32)], 0),
        [((0, slope_ratio), (1, -slope_ratio)), (None, (1, 1.0))],
    )
    c_l = lat_lines[C_L : C_L + 1, :]
    g_l = lat_lines[G_L : G_L + 1, :]
    from_north = jnp.where(lat == 0, c_l * lam_l, 0.0)
    from_south = jnp.where(lat == 1, g_l - c_l * lam_l, 0.0)
    row = iota((STEP_ROWS, LANES), 0)
    for start in range(0, rows, STEP_ROWS):
        at = slice(start, start + STEP_ROWS)
        pot = spread(potential, local_ids(coarse[at, :], points))
        value = held[at, :] + put[at, :LANES] - attract_coef * pot
        north = adj_v_in[at, :]
        if start == 0:
            value = value + jnp.where(row == 0, slope_ratio * from_south, 0.0)
        if start == rows - STEP_ROWS:
            last = row == STEP_ROWS - 1
            value = value - jnp.where(last, slope_ratio * from_north, 0.0)
            north = north + jnp.where(last, from_north, 0.0)
        lam_out[at, :] = ocean[at, :].astype(f32) * value
        east_out[at, :] = adj_u_in[at, :] + put[at, LANES:]
        north_out[at, :] = north
    edge[...] = lam_out[0:1, :]
    span = rows // n_lon
    for target in range(n_lon):
        stop = (target + 1) * span
        payload[target, :span, :] = lam_out[target * span : stop, :]
        if target < n_lon - 1:
            payload[target, span : span + 8, :] = lam_out[stop : stop + 8, :]
        else:
            payload[target, span : span + 8, :] = jnp.zeros((8, LANES), f32)


def bands_kernel(parts, bands):
    count, tall, _ = parts.shape
    span = tall - 8
    lane = iota((span, LANES), 1)
    for k in range(count):
        here = parts[k, :span, :]
        east = parts[(k + 1) % count, :span, :]
        at = slice(k * LANES, (k + 1) * LANES)
        bands[0, 0, :, at] = here
        bands[1, 0, :, at] = jnp.where(lane == LANES - 1, roll_east(east), roll_east(here)) - here
        bands[2, 0, :, at] = parts[k, 1 : span + 1, :] - here


def call(kernel, shapes, scratch, args, name):
    vmem = pl.BlockSpec(memory_space=pltpu.VMEM)
    return pl.pallas_call(
        kernel,
        out_shape=[jax.ShapeDtypeStruct(shape, f32) for shape in shapes],
        in_specs=[vmem] * len(args),
        out_specs=[vmem] * len(shapes),
        scratch_shapes=scratch,
        compiler_params=pltpu.CompilerParams(vmem_limit_bytes=16 << 20),
        name=name,
    )(*args)


def body(n_lon, n_lat, lam_in, flux_east, flux_north, depth, drag, ocean, coarse_of, green):
    rows, cols = lam_in.shape
    points = green.shape[0]
    blocks = points // LANES
    owners = n_lon * n_lat
    grid = (rows, cols)
    fields = (lam_in, flux_east, flux_north, depth, drag, ocean, coarse_of)
    to_east, to_west, to_lat = call(
        functools.partial(pack_kernel, points=points),
        [(8, rows), (8, rows), (8, cols)], [], fields, "pack",
    )
    forward = [(k, (k + 1) % n_lon) for k in range(n_lon)]
    backward = [(target, source) for source, target in forward]
    from_west = lax.ppermute(to_east, "lon", forward)
    from_east = lax.ppermute(to_west, "lon", backward)
    from_lat = lax.ppermute(to_lat, "lat", [(0, 1), (1, 0)])
    held, gu, cu, gv, cv, sums = call(
        functools.partial(inner_kernel, points=points),
        [grid] * 5 + [((PIECES + 1) * HIGH, LOW)],
        [pltpu.VMEM(grid, f32)], fields, "inner",
    )
    payload, lines, lat_lines = call(
        functools.partial(rim_kernel, points=points),
        [(owners, 8, LANES), (8, rows), (8, LANES)], [],
        (to_east, to_west, to_lat, from_west, from_east, from_lat, sums), "rim",
    )
    first = lax.all_to_all(payload, ("lon", "lat"), 0, 0, tiled=True)
    tall = -(-(4 * blocks + rows // LANES + 1) // 8) * 8
    payload, held, adj_u, adj_v = call(
        functools.partial(second_kernel, points=points, n_lon=n_lon, n_lat=n_lat),
        [(owners, tall, LANES), grid, grid, grid],
        [
            pltpu.VMEM((points, LANES), f32),
            pltpu.VMEM((rows + 8, cols), f32),
            pltpu.VMEM(grid, f32),
            pltpu.VMEM((2 * rows, cols), f32),
        ],
        (first, green, coarse_of, ocean, held, gu, cu, gv, cv, lines, lat_lines), "second",
    )
    second = lax.all_to_all(payload, ("lon", "lat"), 0, 0, tiled=True)
    span = rows // n_lon
    lam, east, north, payload, edge = call(
        functools.partial(last_kernel, points=points, n_lon=n_lon, n_lat=n_lat),
        [grid, grid, grid, (n_lon, span + 8, cols), (1, cols)],
        [pltpu.VMEM((points, LANES), f32), pltpu.VMEM((owners * blocks, LANES), f32)],
        (first, second, green, coarse_of, ocean, held, adj_u, adj_v, lines, lat_lines), "last",
    )
    edge = lax.ppermute(edge, "lat", [(1, 0)])
    payload = lax.dynamic_update_slice(payload, edge[None], (n_lon - 1, span, 0))
    parts = lax.all_to_all(payload, "lon", 0, 0, tiled=True)
    (bands,) = call(bands_kernel, [(3, 1, span, n_lon * cols)], [], (parts,), "bands")
    return lam, east, north, bands


def solution(mesh):
    cells = P(("groups", "lat"), "lon")
    n_lon, n_lat = mesh.shape["lon"], mesh.shape["lat"]
    return jax.shard_map(
        functools.partial(body, n_lon, n_lat),
        mesh=mesh,
        in_specs=(cells,) * 6 + (P("lat", "lon"), P(("lon", "lat"), None)),
        out_specs=(cells,) * 3 + (P(None, ("groups", "lat"), "lon", None),),
        check_vma=False,
    )
```

```python
import functools

import jax
import jax.numpy as jnp
from jax import lax
from jax.experimental import pallas as pl
from jax.experimental.pallas import tpu as pltpu
from jax.sharding import PartitionSpec as P

f32 = jnp.float32
bf16 = jnp.bfloat16
i32 = jnp.int32

LANES = 128
LOW = 32
HIGH = 16
PIECES = 2
SEG_ROWS = 128
STEP_ROWS = 64
HIGHEST = lax.Precision.HIGHEST

flux_ratio = 0.25
slope_ratio = 0.25
drag_step = 1.0
attract_coef = 0.5

LAM, DEPTH, DRAG, OCEAN, POINT, FLUX = range(6)
ADJ_W, ADJ_E, C_W, C_E, G_W, G_E, ID_W, ID_E = range(8)
ADJ_L, C_L, G_L, ID_L = range(4)


def iota(shape, dim):
    return lax.broadcasted_iota(i32, shape, dim)


def roll_east(x):
    return pltpu.roll(x, LANES - 1, 1)


def roll_west(x):
    return pltpu.roll(x, 1, 1)


def local_ids(ids, points):
    return lax.bitwise_and(ids, points - 1)


def bf16_pieces(values):
    out = []
    for piece in range(PIECES):
        top = values.astype(bf16).astype(f32)
        out.append(top)
        if piece < PIECES - 1:
            values = values - top
    return out


def segment_part(values, ids, points, with_counts=False):
    blocks = points // LANES
    high = lax.shift_right_logical(ids, 5)
    high = lax.bitwise_and(high, 3) * blocks + lax.shift_right_logical(high, 2)
    low = lax.bitwise_and(ids, LOW - 1)
    high_iota = iota((HIGH, LANES), 0)
    low_iota = iota((LOW, LANES), 0)
    pieces = bf16_pieces(values)
    left, right = [], []
    for row in range(values.shape[0]):
        mask = jnp.broadcast_to(high[row : row + 1], (HIGH, LANES)) == high_iota
        parts = [
            jnp.where(mask, jnp.broadcast_to(piece[row : row + 1], (HIGH, LANES)), 0.0)
            for piece in pieces
        ]
        if with_counts:
            parts.append(jnp.where(mask, 1.0, 0.0))
        left.append(jnp.concatenate(parts, 0).astype(bf16))
        mask = jnp.broadcast_to(low[row : row + 1], (LOW, LANES)) == low_iota
        right.append(jnp.where(mask, 1.0, 0.0).astype(bf16))
    return lax.dot_general(
        jnp.concatenate(left, 1),
        jnp.concatenate(right, 1),
        (((1,), (1,)), ((), ())),
        preferred_element_type=f32,
    )


def segment_all(value_ref, id_ref, points, with_counts=False):
    rows = value_ref.shape[0]
    parts = PIECES + int(with_counts)

    def step(index, total):
        at = pl.ds(pl.multiple_of(index * SEG_ROWS, SEG_ROWS), SEG_ROWS)
        return total + segment_part(
            value_ref[at, :], local_ids(id_ref[at, :], points), points, with_counts
        )

    return lax.fori_loop(0, rows // SEG_ROWS, step, jnp.zeros((parts * HIGH, LOW), f32))


def sum_pieces(parts):
    total = parts[:HIGH]
    for piece in range(1, PIECES):
        total = total + parts[piece * HIGH : (piece + 1) * HIGH]
    return total


def as_points(table, points):
    blocks = points // LANES
    return jnp.concatenate([table[q * blocks : (q + 1) * blocks] for q in range(4)], 1)


def fold(line):
    return jnp.concatenate(
        [line[:, k * LANES : (k + 1) * LANES] for k in range(line.shape[1] // LANES)], 0
    )


def unfold(block):
    return jnp.concatenate([block[k : k + 1] for k in range(block.shape[0])], 1)


def take_sides(block):
    sub, lane = iota((8, LANES), 0), iota((8, LANES), 1)
    pick = ((sub == 0) & (lane == 0)) | ((sub == 1) & (lane == LANES - 1))
    return lax.dot_general(
        pick.astype(f32), block, (((1,), (1,)), ((), ())), precision=HIGHEST,
        preferred_element_type=f32,
    )


def put_sides(lines, entries):
    sub, lane = iota((8, LANES), 0), iota((8, LANES), 1)
    parts = []
    for first, last in entries:
        part = jnp.zeros((8, LANES), f32)
        if first is not None:
            part = jnp.where((sub == first[0]) & (lane == 0), first[1], part)
        if last is not None:
            part = jnp.where((sub == last[0]) & (lane == LANES - 1), last[1], part)
        parts.append(part)
    return lax.dot_general(
        lines, jnp.concatenate(parts, 1), (((0,), (0,)), ((), ())), precision=HIGHEST,
        preferred_element_type=f32,
    )


def green_product(green_ref, load_row, acc_ref, first=0, points=None):
    total = green_ref.shape[1]
    points = green_ref.shape[0] - first if points is None else points
    tall = 32

    def step(index, carry):
        start = pl.multiple_of(index * tall, tall)
        acc = jnp.zeros((tall, LANES), f32)
        for k in range(total // LANES):
            acc = acc + green_ref[
                pl.ds(first + start, tall), k * LANES : (k + 1) * LANES
            ] * jnp.broadcast_to(load_row(k), (tall, LANES))
        acc_ref[pl.ds(start, tall), :] = acc
        return carry

    lax.fori_loop(0, points // tall, step, 0)
    return lax.dot_general(
        jnp.ones((8, LANES), f32), acc_ref[0:points, :], (((1,), (1,)), ((), ())),
        precision=HIGHEST, preferred_element_type=f32,
    )


def spread(potential, ids):
    points = potential.shape[1]
    rows = ids.shape[0]
    low = lax.bitwise_and(ids, LANES - 1)
    block = lax.shift_right_logical(ids, 7)
    out = None
    for k in range(points // LANES):
        table = potential[:, k * LANES : (k + 1) * LANES]
        table = jnp.broadcast_to(table[None], (rows // 8, 8, LANES)).reshape(rows, LANES)
        value = jnp.take_along_axis(table, low, axis=1, mode="promise_in_bounds")
        out = value if out is None else jnp.where(block == k, value, out)
    return out


def next_rows(ref, start, count, last=None):
    if start + count < ref.shape[0]:
        return ref[start + 1 : start + count + 1, :]
    return jnp.concatenate([ref[start + 1 :, :], jnp.zeros((1, LANES), ref.dtype)], 0)


def south_rows(first, block):
    return jnp.concatenate([first, block[:-1]], 0)


def pack_kernel(*refs, points):
    far, (to_east, to_west, to_lat), near, done = refs[:7], refs[7:10], refs[10:17], refs[17]
    copies = [pltpu.make_async_copy(far[k], near[k], done.at[k]) for k in range(7)]
    for copy in copies:
        copy.start()
    for copy in copies:
        copy.wait()
    lam, east, north, depth, drag, ocean, coarse = near
    rows = lam.shape[0]
    lat = lax.axis_index("lat")
    sides = take_sides(
        jnp.concatenate(
            [
                lam[...],
                depth[...],
                drag[...],
                ocean[...].astype(f32),
                local_ids(coarse[...], points).astype(f32),
                east[...],
            ],
            0,
        )
    )
    zero = jnp.zeros((2, rows), f32)
    to_west[...] = jnp.concatenate(
        [sides[0:1, k * rows : (k + 1) * rows] for k in range(6)] + [zero], 0
    )
    to_east[...] = jnp.concatenate(
        [sides[1:2, k * rows : (k + 1) * rows] for k in range(6)] + [zero], 0
    )

    def border(row):
        return jnp.concatenate(
            [
                lam[row : row + 1, :],
                depth[row : row + 1, :],
                drag[row : row + 1, :],
                ocean[row : row + 1, :].astype(f32),
                local_ids(coarse[row : row + 1, :], points).astype(f32),
                north[row : row + 1, :],
                jnp.zeros((2, LANES), f32),
            ],
            0,
        )

    to_lat[...] = jnp.where(lat == 0, border(rows - 1), border(0))


def inner_kernel(
    lam, east, north, depth, drag, ocean, coarse,
    held, gu, cu, gv, cv, sums, source, *, points,
):
    rows = lam.shape[0]
    inner = iota((STEP_ROWS, LANES), 1) < LANES - 1
    carry = jnp.zeros((1, LANES), f32)
    for start in range(0, rows, STEP_ROWS):
        at = slice(start, start + STEP_ROWS)
        lam_c, depth_c, drag_c = lam[at, :], depth[at, :], drag[at, :]
        ocean_c = ocean[at, :].astype(f32)
        damp = jnp.where(
            inner,
            ocean_c * roll_east(ocean_c) / (1.0 + drag_step * 0.5 * (drag_c + roll_east(drag_c))),
            0.0,
        )
        ratio = damp * (flux_ratio * 0.5) * (depth_c + roll_east(depth_c))
        adj_u = damp * east[at, :] + ratio * (roll_east(lam_c) - lam_c)
        cu[at, :] = ratio
        gu[at, :] = damp * adj_u
        ocean_n = next_rows(ocean, start, STEP_ROWS).astype(f32)
        damp = (
            ocean_c
            * ocean_n
            / (1.0 + drag_step * 0.5 * (drag_c + next_rows(drag, start, STEP_ROWS)))
        )
        ratio = damp * (flux_ratio * 0.5) * (depth_c + next_rows(depth, start, STEP_ROWS))
        adj_v = damp * north[at, :] + ratio * (next_rows(lam, start, STEP_ROWS) - lam_c)
        cv[at, :] = ratio
        gv[at, :] = damp * adj_v
        src = slope_ratio * (roll_west(adj_u) - adj_u + south_rows(carry, adj_v) - adj_v)
        carry = adj_v[STEP_ROWS - 1 :]
        source[at, :] = src
        held[at, :] = lam_c + src
    sums[...] = segment_all(source, coarse, points, True)


def face(low, high, flux):
    damp = (
        low[OCEAN : OCEAN + 1]
        * high[OCEAN : OCEAN + 1]
        / (1.0 + drag_step * 0.5 * (low[DRAG : DRAG + 1] + high[DRAG : DRAG + 1]))
    )
    ratio = damp * (flux_ratio * 0.5) * (low[DEPTH : DEPTH + 1] + high[DEPTH : DEPTH + 1])
    adj = damp * flux + ratio * (high[LAM : LAM + 1] - low[LAM : LAM + 1])
    return adj, ratio, damp * adj


def rim_kernel(
    own_east, own_west, own_lat, from_west, from_east, from_lat, sums,
    payload, lines, lat_lines, *, points,
):
    lat = lax.axis_index("lat")
    blocks = points // LANES
    west, east = own_west[...], own_east[...]
    far_west, far_east = from_west[...], from_east[...]
    mine, other = own_lat[...], from_lat[...]
    adj_w, c_w, g_w = face(far_west, west, far_west[FLUX : FLUX + 1])
    adj_e, c_e, g_e = face(east, far_east, east[FLUX : FLUX + 1])
    lower = jnp.where(lat == 0, mine, other)
    upper = jnp.where(lat == 0, other, mine)
    adj_l, c_l, g_l = face(lower, upper, lower[FLUX : FLUX + 1])
    lines[...] = jnp.concatenate(
        [adj_w, adj_e, c_w, c_e, g_w, g_e, far_west[POINT : POINT + 1], far_east[POINT : POINT + 1]],
        0,
    )
    lat_lines[...] = jnp.concatenate(
        [adj_l, c_l, g_l, other[POINT : POINT + 1], jnp.zeros((4, LANES), f32)], 0
    )
    sign = jnp.where(lat == 0, -slope_ratio, slope_ratio)
    pad = jnp.zeros((1, LANES), f32)
    values = jnp.concatenate(
        [fold(slope_ratio * adj_w), fold(-slope_ratio * adj_e), sign * adj_l, pad], 0
    )
    ids = jnp.concatenate(
        [
            fold(west[POINT : POINT + 1]),
            fold(east[POINT : POINT + 1]),
            mine[POINT : POINT + 1],
            pad,
        ],
        0,
    ).astype(i32)
    total = sum_pieces(sums[...]) + sum_pieces(segment_part(values, ids, points))
    counts = as_points(sums[PIECES * HIGH : (PIECES + 1) * HIGH, :], points)
    inverse = 1.0 / counts
    loads = as_points(total, points) * inverse
    part = jnp.concatenate([loads, inverse], 0)
    if part.shape[0] < 8:
        part = jnp.concatenate([part, jnp.zeros((8 - part.shape[0], LANES), f32)], 0)
    for target in range(payload.shape[0]):
        payload[target] = part


def neighbours(n_lon, n_lat):
    lon, lat = lax.axis_index("lon"), lax.axis_index("lat")
    west = lax.rem(lon + n_lon - 1, n_lon) * n_lat + lat
    east = lax.rem(lon + 1, n_lon) * n_lat + lat
    other = lon * n_lat + (1 - lat)
    return west, east, other


def second_kernel(
    first, green, coarse, ocean, held_in, gu, cu, gv, cv, lines, lat_lines,
    payload, held, adj_u_out, adj_v_out, acc, lam, source, sides, *, points, n_lon, n_lat,
):
    rows = coarse.shape[0]
    blocks = points // LANES
    lat = lax.axis_index("lat")
    south_end = jnp.where(lat == 1, 1.0, 0.0)
    north_end = jnp.where(lat == 0, 1.0, 0.0)
    potential = green_product(
        green, lambda k: first[k // blocks, k % blocks : k % blocks + 1, :], acc
    )
    put = put_sides(
        lines[...],
        [
            ((ADJ_W, slope_ratio), (ADJ_E, -slope_ratio)),
            ((C_W, 1.0), (C_E, 1.0)),
            (None, (G_E, 1.0)),
        ],
    )
    adj_l = lat_lines[ADJ_L : ADJ_L + 1, :]
    c_l = lat_lines[C_L : C_L + 1, :]
    g_l = lat_lines[G_L : G_L + 1, :]
    row = iota((STEP_ROWS, LANES), 0)
    lane = iota((STEP_ROWS, LANES), 1)
    lam[rows : rows + 8, :] = jnp.zeros((8, LANES), f32)
    for start in range(0, rows, STEP_ROWS):
        at = slice(start, start + STEP_ROWS)
        pot = spread(potential, local_ids(coarse[at, :], points))
        value = held_in[at, :] + put[at, :LANES] - attract_coef * pot
        if start == 0:
            value = value + jnp.where(row == 0, south_end * slope_ratio * adj_l, 0.0)
        if start == rows - STEP_ROWS:
            value = value - jnp.where(row == STEP_ROWS - 1, north_end * slope_ratio * adj_l, 0.0)
        value = ocean[at, :].astype(f32) * value
        lam[at, :] = value
        sides[rows + start : rows + start + STEP_ROWS, :] = value
    carry = south_end * c_l * lam[0:1, :]
    to_lat_south = -slope_ratio * carry
    for start in range(0, rows, STEP_ROWS):
        at = slice(start, start + STEP_ROWS)
        lam_c = lam[at, :]
        c_side = put[at, LANES : 2 * LANES]
        east_c = jnp.where(lane == LANES - 1, c_side, cu[at, :])
        adj_u = (
            gu[at, :]
            + put[at, 2 * LANES :]
            + east_c * (jnp.where(lane == LANES - 1, 0.0, roll_east(lam_c)) - lam_c)
        )
        west_part = c_side * lam_c
        g_c, c_c = gv[at, :], cv[at, :]
        if start == rows - STEP_ROWS:
            last = row == STEP_ROWS - 1
            g_c = g_c + jnp.where(last, north_end * g_l, 0.0)
            c_c = c_c + jnp.where(last, north_end * c_l, 0.0)
        adj_v = g_c + c_c * (lam[start + 1 : start + STEP_ROWS + 1, :] - lam_c)
        src = slope_ratio * (
            jnp.where(lane == 0, west_part, roll_west(adj_u))
            - adj_u
            + south_rows(carry, adj_v)
            - adj_v
        )
        carry = adj_v[STEP_ROWS - 1 :]
        adj_u_out[at, :] = adj_u
        adj_v_out[at, :] = adj_v
        source[at, :] = src
        held[at, :] = lam_c + src
        sides[at, :] = jnp.where(lane == 0, -slope_ratio * west_part, slope_ratio * adj_u)
    to_lat = jnp.where(lat == 0, slope_ratio * carry, to_lat_south)
    edge = jnp.where(lat == 0, lam[rows - 1 : rows, :], lam[0:1, :])
    taken = take_sides(sides[...])
    own = as_points(sum_pieces(segment_all(source, coarse, points)), points)

    def away(line, ids):
        return as_points(sum_pieces(segment_part(line, ids.astype(i32), points)), points)

    east_part = away(fold(taken[1:2, :rows]), fold(lines[ID_E : ID_E + 1, :]))
    west_part = away(fold(taken[0:1, :rows]), fold(lines[ID_W : ID_W + 1, :]))
    pad = jnp.zeros((1, LANES), f32)
    lat_part = away(
        jnp.concatenate([to_lat, pad], 0),
        jnp.concatenate([lat_lines[ID_L : ID_L + 1, :], pad], 0),
    )
    part = jnp.concatenate([own, east_part, west_part, lat_part], 0)
    spare = payload.shape[1] - part.shape[0]
    part = jnp.concatenate([part, jnp.zeros((spare, LANES), f32)], 0)
    for target in range(payload.shape[0]):
        payload[target] = part
    west, east, other = neighbours(n_lon, n_lat)
    begin = 4 * blocks
    tall = rows // LANES
    payload[west, begin : begin + tall, :] = fold(taken[0:1, rows:])
    payload[east, begin : begin + tall, :] = fold(taken[1:2, rows:])
    payload[other, begin + tall : begin + tall + 1, :] = edge


def edge_kernel(
    first, second, green, ocean, held, lines, lat_lines,
    edge, loads, start_pot, put, north_line, acc, *, points, n_lon, n_lat,
):
    rows = held.shape[0]
    blocks = points // LANES
    tall = rows // LANES
    lat = lax.axis_index("lat")
    for lon in range(n_lon):
        for band in range(n_lat):
            here = lon * n_lat + band
            west = (lon - 1) % n_lon * n_lat + band
            east = (lon + 1) % n_lon * n_lat + band
            other = lon * n_lat + 1 - band
            total = (
                second[here, :blocks, :]
                + second[west, blocks : 2 * blocks, :]
                + second[east, 2 * blocks : 3 * blocks, :]
                + second[other, 3 * blocks : 4 * blocks, :]
            )
            loads[here * blocks : (here + 1) * blocks, :] = (
                total * first[here, blocks : 2 * blocks, :]
            )
    potential = green_product(green, lambda k: loads[k : k + 1, :], acc, 0, LANES)
    start_pot[...] = potential
    west, east, other = neighbours(n_lon, n_lat)
    begin = 4 * blocks
    lam_w = unfold(second[west, begin : begin + tall, :])
    lam_e = unfold(second[east, begin : begin + tall, :])
    lam_l = second[other, begin + tall : begin + tall + 1, :]
    add_e = lines[C_E : C_E + 1, :] * lam_e
    add_w = lines[G_W : G_W + 1, :] - lines[C_W : C_W + 1, :] * lam_w
    c_l = lat_lines[C_L : C_L + 1, :]
    g_l = lat_lines[G_L : G_L + 1, :]
    from_north = jnp.where(lat == 0, c_l * lam_l, 0.0)
    from_south = jnp.where(lat == 1, g_l - c_l * lam_l, 0.0)
    put[...] = put_sides(
        jnp.concatenate([add_w, add_e, jnp.zeros((6, rows), f32)], 0),
        [((0, slope_ratio), (1, -slope_ratio)), (None, (1, 1.0))],
    )
    put[0:1, :LANES] = put[0:1, :LANES] + slope_ratio * from_south
    put[rows - 1 : rows, :LANES] = put[rows - 1 : rows, :LANES] - slope_ratio * from_north
    north_line[...] = from_north
    edge[...] = ocean[0:1, :].astype(f32) * (
        held[0:1, :] + put[0:1, :LANES] - attract_coef * potential[0:1, :]
    )


def last_kernel(
    loads, start_pot, put, north_line, green, coarse, ocean, held, adj_u_in, adj_v_in,
    lam_out, east_out, north_out, payload, acc, *, points, n_lon,
):
    rows = coarse.shape[0]
    potential = start_pot[...]
    if points > LANES:
        rest = green_product(green, lambda k: loads[k : k + 1, :], acc, LANES, points - LANES)
        potential = jnp.concatenate([potential, rest], 1)
    row = iota((STEP_ROWS, LANES), 0)
    for start in range(0, rows, STEP_ROWS):
        at = slice(start, start + STEP_ROWS)
        pot = spread(potential, local_ids(coarse[at, :], points))
        north = adj_v_in[at, :]
        if start == rows - STEP_ROWS:
            north = north + jnp.where(row == STEP_ROWS - 1, north_line[...], 0.0)
        lam_out[at, :] = ocean[at, :].astype(f32) * (
            held[at, :] + put[at, :LANES] - attract_coef * pot
        )
        east_out[at, :] = adj_u_in[at, :] + put[at, LANES:]
        north_out[at, :] = north
    span = rows // n_lon
    for target in range(n_lon):
        stop = (target + 1) * span
        payload[target, :span, :] = lam_out[target * span : stop, :]
        if target < n_lon - 1:
            payload[target, span : span + 8, :] = lam_out[stop : stop + 8, :]
        else:
            payload[target, span : span + 8, :] = jnp.zeros((8, LANES), f32)


def bands_kernel(parts, bands):
    count, tall, _ = parts.shape
    span = tall - 8
    lane = iota((span, LANES), 1)
    for k in range(count):
        here = parts[k, :span, :]
        east = parts[(k + 1) % count, :span, :]
        at = slice(k * LANES, (k + 1) * LANES)
        bands[0, 0, :, at] = here
        bands[1, 0, :, at] = jnp.where(lane == LANES - 1, roll_east(east), roll_east(here)) - here
        bands[2, 0, :, at] = parts[k, 1 : span + 1, :] - here


def call(kernel, shapes, scratch, args, name, far=False):
    vmem = pl.BlockSpec(memory_space=pltpu.VMEM)
    shapes = [(shape, f32) if isinstance(shape[0], int) else shape for shape in shapes]
    return pl.pallas_call(
        kernel,
        out_shape=[jax.ShapeDtypeStruct(shape, kind) for shape, kind in shapes],
        in_specs=[pl.BlockSpec(memory_space=pltpu.HBM) if far else vmem] * len(args),
        out_specs=[vmem] * len(shapes),
        scratch_shapes=scratch,
        compiler_params=pltpu.CompilerParams(vmem_limit_bytes=(52 << 20) if far else 16 << 20),
        cost_estimate=pl.CostEstimate(flops=4 << 30, bytes_accessed=16 << 20, transcendentals=0),
        name=name,
    )(*args)


def body(n_lon, n_lat, lam_in, flux_east, flux_north, depth, drag, ocean, coarse_of, green):
    rows, cols = lam_in.shape
    points = green.shape[0]
    blocks = points // LANES
    owners = n_lon * n_lat
    grid = (rows, cols)
    fields = (lam_in, flux_east, flux_north, depth, drag, ocean, coarse_of)
    to_east, to_west, to_lat, *fields = call(
        functools.partial(pack_kernel, points=points),
        [(8, rows), (8, rows), (8, cols)] + [(grid, field.dtype) for field in fields],
        [pltpu.SemaphoreType.DMA((7,))], fields, "pack", far=True,
    )
    ocean, coarse_of = fields[5:]
    forward = [(k, (k + 1) % n_lon) for k in range(n_lon)]
    backward = [(target, source) for source, target in forward]
    from_west = lax.ppermute(to_east, "lon", forward)
    from_east = lax.ppermute(to_west, "lon", backward)
    from_lat = lax.ppermute(to_lat, "lat", [(0, 1), (1, 0)])
    held, gu, cu, gv, cv, sums = call(
        functools.partial(inner_kernel, points=points),
        [grid] * 5 + [((PIECES + 1) * HIGH, LOW)],
        [pltpu.VMEM(grid, f32)], fields, "inner",
    )
    payload, lines, lat_lines = call(
        functools.partial(rim_kernel, points=points),
        [(owners, 8, LANES), (8, rows), (8, LANES)], [],
        (to_east, to_west, to_lat, from_west, from_east, from_lat, sums), "rim",
    )
    first = lax.all_to_all(payload, ("lon", "lat"), 0, 0, tiled=True)
    tall = -(-(4 * blocks + rows // LANES + 1) // 8) * 8
    payload, held, adj_u, adj_v = call(
        functools.partial(second_kernel, points=points, n_lon=n_lon, n_lat=n_lat),
        [(owners, tall, LANES), grid, grid, grid],
        [
            pltpu.VMEM((points, LANES), f32),
            pltpu.VMEM((rows + 8, cols), f32),
            pltpu.VMEM(grid, f32),
            pltpu.VMEM((2 * rows, cols), f32),
        ],
        (first, green, coarse_of, ocean, held, gu, cu, gv, cv, lines, lat_lines), "second",
    )
    second = lax.all_to_all(payload, ("lon", "lat"), 0, 0, tiled=True)
    span = rows // n_lon
    edge, loads, start_pot, put, north_line = call(
        functools.partial(edge_kernel, points=points, n_lon=n_lon, n_lat=n_lat),
        [(1, cols), (owners * blocks, LANES), (8, LANES), (rows, 2 * cols), (1, cols)],
        [pltpu.VMEM((LANES, LANES), f32)],
        (first, second, green, ocean, held, lines, lat_lines), "edge",
    )
    lam, east, north, payload = call(
        functools.partial(last_kernel, points=points, n_lon=n_lon),
        [grid, grid, grid, (n_lon, span + 8, cols)],
        [pltpu.VMEM((points, LANES), f32)],
        (loads, start_pot, put, north_line, green, coarse_of, ocean, held, adj_u, adj_v), "last",
    )
    edge = lax.ppermute(edge, "lat", [(1, 0)])
    payload = lax.dynamic_update_slice(payload, edge[None], (n_lon - 1, span, 0))
    parts = lax.all_to_all(payload, "lon", 0, 0, tiled=True)
    (bands,) = call(bands_kernel, [(3, 1, span, n_lon * cols)], [], (parts,), "bands")
    return lam, east, north, bands


def solution(mesh):
    cells = P(("groups", "lat"), "lon")
    n_lon, n_lat = mesh.shape["lon"], mesh.shape["lat"]
    return jax.shard_map(
        functools.partial(body, n_lon, n_lat),
        mesh=mesh,
        in_specs=(cells,) * 6 + (P("lat", "lon"), P(("lon", "lat"), None)),
        out_specs=(cells,) * 3 + (P(None, ("groups", "lat"), "lon", None),),
        check_vma=False,
    )
```

```python
import functools

import jax
import jax.numpy as jnp
from jax import lax
from jax.experimental import pallas as pl
from jax.experimental.pallas import tpu as pltpu
from jax.sharding import PartitionSpec as P

f32 = jnp.float32
bf16 = jnp.bfloat16
i32 = jnp.int32

LANES = 128
LOW = 32
HIGH = 16
PIECES = 2
SEG_ROWS = 128
STEP_ROWS = 64

flux_ratio = 0.25
slope_ratio = 0.25
drag_step = 1.0
attract_coef = 0.5

LAM, DEPTH, DRAG, OCEAN, POINT, FLUX = range(6)
ADJ, RATIO, GAIN, BASE, MASK, OWN_ID, FAR_ID = range(7)
ADJ_L, C_L, G_L, ID_L, OWN_L = range(5)


def iota(shape, dim):
    return lax.broadcasted_iota(i32, shape, dim)


def roll_east(x):
    return pltpu.roll(x, LANES - 1, 1)


def roll_west(x):
    return pltpu.roll(x, 1, 1)


def local_ids(ids, points):
    return lax.bitwise_and(ids, points - 1)


def bf16_pieces(values, count=PIECES):
    out = []
    for piece in range(count):
        top = values.astype(bf16).astype(f32)
        out.append(top)
        if piece < count - 1:
            values = values - top
    return out


def one_hots(ids, points):
    blocks = points // LANES
    high = lax.shift_right_logical(ids, 5)
    high = lax.bitwise_and(high, 3) * blocks + lax.shift_right_logical(high, 2)
    low = lax.bitwise_and(ids, LOW - 1)
    high_iota = iota((HIGH, LANES), 0)
    low_iota = iota((LOW, LANES), 0)
    left, right = [], []
    for row in range(ids.shape[0]):
        mask = jnp.broadcast_to(high[row : row + 1], (HIGH, LANES)) == high_iota
        left.append(jnp.where(mask, 1.0, 0.0).astype(bf16))
        mask = jnp.broadcast_to(low[row : row + 1], (LOW, LANES)) == low_iota
        right.append(jnp.where(mask, 1.0, 0.0).astype(bf16))
    return jnp.concatenate(left, 1), jnp.concatenate(right, 1)


def segment_part(values, left, right, with_counts=False):
    parts = []
    for piece in bf16_pieces(values):
        line = jnp.concatenate(
            [
                jnp.broadcast_to(piece[row : row + 1], (HIGH, LANES)).astype(bf16)
                for row in range(values.shape[0])
            ],
            1,
        )
        parts.append(left * line)
    if with_counts:
        parts.append(left)
    return lax.dot_general(
        jnp.concatenate(parts, 0), right, (((1,), (1,)), ((), ())), preferred_element_type=f32
    )


def segment_few(values, ids, points):
    return sum_pieces(segment_part(values, *one_hots(ids, points)))


def sum_pieces(parts):
    total = parts[:HIGH]
    for piece in range(1, PIECES):
        total = total + parts[piece * HIGH : (piece + 1) * HIGH]
    return total


def as_points(table, points):
    blocks = points // LANES
    return jnp.concatenate([table[q * blocks : (q + 1) * blocks] for q in range(4)], 1)


def fold(line):
    return jnp.concatenate(
        [line[:, k * LANES : (k + 1) * LANES] for k in range(line.shape[1] // LANES)], 0
    )


def unfold(block):
    return jnp.concatenate([block[k : k + 1] for k in range(block.shape[0])], 1)


def take_sides(block, count=3):
    sub, lane = iota((8, LANES), 0), iota((8, LANES), 1)
    pick = ((sub == 0) & (lane == 0)) | ((sub == 1) & (lane == LANES - 1))
    pick = pick.astype(f32).astype(bf16)
    out = None
    for piece in reversed(bf16_pieces(block, count)):
        part = lax.dot_general(
            pick, piece.astype(bf16), (((1,), (1,)), ((), ())), preferred_element_type=f32
        )
        out = part if out is None else out + part
    return out


def put_sides(pair, entries):
    half = pair.shape[0] // 2
    lines = jnp.concatenate([unfold(pair[:half]), unfold(pair[half:])], 0)
    rows = lines.shape[1]
    pieces = bf16_pieces(lines, 3)
    stack = jnp.concatenate(pieces + [jnp.zeros((2, rows), f32)], 0)
    sub, lane = iota((8, LANES), 0), iota((8, LANES), 1)
    west = (sub < 6) & (lax.bitwise_and(sub, 1) == 0) & (lane == 0)
    east = (sub < 6) & (lax.bitwise_and(sub, 1) == 1) & (lane == LANES - 1)
    picks = [jnp.where(west, first, jnp.where(east, last, 0.0)) for first, last in entries]
    return lax.dot_general(
        stack, jnp.concatenate(picks, 1), (((0,), (0,)), ((), ())), preferred_element_type=f32
    )


def green_product(green_ref, load_row, acc_ref, first=0, points=None):
    total = green_ref.shape[1]
    points = green_ref.shape[0] - first if points is None else points
    tall = LANES

    def step(index, carry):
        start = pl.multiple_of(index * tall, tall)
        acc = jnp.zeros((tall, LANES), f32)
        for k in range(total // LANES):
            acc = acc + green_ref[
                pl.ds(first + start, tall), k * LANES : (k + 1) * LANES
            ] * jnp.broadcast_to(load_row(k), (tall, LANES))
        acc_ref[pl.ds(start, tall), :] = acc
        return carry

    lax.fori_loop(0, points // tall, step, 0)
    out = None
    for piece in reversed(bf16_pieces(acc_ref[0:points, :], 3)):
        part = lax.dot_general(
            jnp.ones((8, LANES), bf16), piece.astype(bf16), (((1,), (1,)), ((), ())),
            preferred_element_type=f32,
        )
        out = part if out is None else out + part
    return out


def spread(potential, ids):
    points = potential.shape[1]
    rows = ids.shape[0]
    low = lax.bitwise_and(ids, LANES - 1)
    block = lax.shift_right_logical(ids, 7)
    out = None
    for k in range(points // LANES):
        table = potential[:, k * LANES : (k + 1) * LANES]
        table = jnp.broadcast_to(table[None], (rows // 8, 8, LANES)).reshape(rows, LANES)
        value = jnp.take_along_axis(table, low, axis=1, mode="promise_in_bounds")
        out = value if out is None else jnp.where(block == k, value, out)
    return out


def next_rows(ref, start, count):
    if start + count < ref.shape[0]:
        return ref[start + 1 : start + count + 1, :]
    return jnp.concatenate([ref[start + 1 :, :], jnp.zeros((1, LANES), ref.dtype)], 0)


def south_rows(first, block):
    return jnp.concatenate([first, block[:-1]], 0)


def pack_kernel(*refs, points):
    far, (to_east, to_west, to_lat), near, done = refs[:7], refs[7:10], refs[10:17], refs[17]
    copies = [pltpu.make_async_copy(far[k], near[k], done.at[k]) for k in range(7)]
    for copy in copies:
        copy.start()
    lam, east, north, depth, drag, ocean, coarse = near
    rows = lam.shape[0]
    tall = rows // LANES
    lat = lax.axis_index("lat")
    order = (
        (LAM, 0, lam, 3), (FLUX, 1, east, 3), (None, 2, north, 0), (DEPTH, 3, depth, 3),
        (DRAG, 4, drag, 3), (OCEAN, 5, ocean, 1), (POINT, 6, coarse, 2),
    )
    for field, index, ref, pieces in order:
        copies[index].wait()
        if field is None:
            continue
        block = ref[...]
        if field == POINT:
            block = local_ids(block, points)
        sides = take_sides(block.astype(f32), pieces)
        at = slice(field * tall, (field + 1) * tall)
        to_west[at, :] = fold(sides[0:1])
        to_east[at, :] = fold(sides[1:2])

    def border(row):
        return jnp.concatenate(
            [
                lam[row : row + 1, :],
                depth[row : row + 1, :],
                drag[row : row + 1, :],
                ocean[row : row + 1, :].astype(f32),
                local_ids(coarse[row : row + 1, :], points).astype(f32),
                north[row : row + 1, :],
                jnp.zeros((2, LANES), f32),
            ],
            0,
        )

    to_lat[...] = jnp.where(lat == 0, border(rows - 1), border(0))


def inner_kernel(
    lam, east, north, depth, drag, ocean, coarse,
    held, gu, cu, gv, cv, sums, left, right, held_sides, source, *, points,
):
    rows = lam.shape[0]
    inner = iota((STEP_ROWS, LANES), 1) < LANES - 1
    carry = jnp.zeros((1, LANES), f32)
    for start in range(0, rows, STEP_ROWS):
        at = slice(start, start + STEP_ROWS)
        lam_c, depth_c, drag_c = lam[at, :], depth[at, :], drag[at, :]
        ocean_c = ocean[at, :].astype(f32)
        damp = jnp.where(
            inner,
            ocean_c * roll_east(ocean_c) / (1.0 + drag_step * 0.5 * (drag_c + roll_east(drag_c))),
            0.0,
        )
        ratio = damp * (flux_ratio * 0.5) * (depth_c + roll_east(depth_c))
        adj_u = damp * east[at, :] + ratio * (roll_east(lam_c) - lam_c)
        cu[at, :] = ratio
        gu[at, :] = damp * adj_u
        ocean_n = next_rows(ocean, start, STEP_ROWS).astype(f32)
        damp = (
            ocean_c
            * ocean_n
            / (1.0 + drag_step * 0.5 * (drag_c + next_rows(drag, start, STEP_ROWS)))
        )
        ratio = damp * (flux_ratio * 0.5) * (depth_c + next_rows(depth, start, STEP_ROWS))
        adj_v = damp * north[at, :] + ratio * (next_rows(lam, start, STEP_ROWS) - lam_c)
        cv[at, :] = ratio
        gv[at, :] = damp * adj_v
        src = slope_ratio * (roll_west(adj_u) - adj_u + south_rows(carry, adj_v) - adj_v)
        carry = adj_v[STEP_ROWS - 1 :]
        source[at, :] = src
        held[at, :] = lam_c + src
    total = jnp.zeros(sums.shape, f32)
    for start in range(0, rows, SEG_ROWS):
        at = slice(start, start + SEG_ROWS)
        cells = slice(start * LANES, (start + SEG_ROWS) * LANES)
        high, low = one_hots(local_ids(coarse[at, :], points), points)
        left[:, cells] = high
        right[:, cells] = low
        total = total + segment_part(source[at, :], high, low, True)
    sums[...] = total
    sides = take_sides(held[...])
    held_sides[...] = jnp.concatenate([fold(sides[0:1]), fold(sides[1:2])], 0)


def face(low, high, flux):
    damp = low[OCEAN] * high[OCEAN] / (1.0 + drag_step * 0.5 * (low[DRAG] + high[DRAG]))
    ratio = damp * (flux_ratio * 0.5) * (low[DEPTH] + high[DEPTH])
    adj = damp * flux + ratio * (high[LAM] - low[LAM])
    return adj, ratio, damp * adj


def west_rows():
    return iota((8, LANES), 0) < 4


def rim_kernel(
    own_east, own_west, own_lat, from_west, from_east, from_lat, sums, held_sides,
    payload, faces, lat_lines, *, points,
):
    lat = lax.axis_index("lat")
    half = held_sides.shape[0] // 2

    def pair(west, east):
        return [
            jnp.concatenate(
                [west[k * half : (k + 1) * half, :], east[k * half : (k + 1) * half, :]], 0
            )
            for k in range(6)
        ]

    own, far = pair(own_west, own_east), pair(from_west, from_east)
    is_west = west_rows()
    low = [jnp.where(is_west, there, here) for here, there in zip(own, far)]
    high = [jnp.where(is_west, here, there) for here, there in zip(own, far)]
    adj, ratio, gain = face(low, high, low[FLUX])
    mine, other = own_lat[...], from_lat[...]
    lower = jnp.where(lat == 0, mine, other)
    upper = jnp.where(lat == 0, other, mine)
    lower = [lower[k : k + 1] for k in range(6)]
    upper = [upper[k : k + 1] for k in range(6)]
    adj_l, c_l, g_l = face(lower, upper, lower[FLUX])
    lat_lines[...] = jnp.concatenate(
        [
            adj_l, c_l, g_l, other[POINT : POINT + 1], mine[POINT : POINT + 1],
            jnp.zeros((3, LANES), f32),
        ],
        0,
    )
    sign = jnp.where(is_west, slope_ratio, -slope_ratio)
    sign_l = jnp.where(lat == 0, -slope_ratio, slope_ratio)
    flow = sign * adj
    sub, lane = lax.bitwise_and(iota((8, LANES), 0), half - 1), iota((8, LANES), 1)
    corner = ((lat == 0) & (sub == half - 1) & (lane == LANES - 1)) | (
        (lat == 1) & (sub == 0) & (lane == 0)
    )
    at_corner = jnp.where(
        is_west,
        jnp.broadcast_to(adj_l[:, 0:1], (8, LANES)),
        jnp.broadcast_to(adj_l[:, LANES - 1 :], (8, LANES)),
    )
    faces[ADJ] = adj
    faces[RATIO] = ratio
    faces[GAIN] = gain
    faces[BASE] = held_sides[...] + flow + jnp.where(corner, sign_l * at_corner, 0.0)
    faces[MASK] = own[OCEAN]
    faces[OWN_ID] = own[POINT]
    faces[FAR_ID] = far[POINT]
    pad = jnp.zeros((1, LANES), f32)
    values = jnp.concatenate([flow, sign_l * adj_l, pad], 0)
    ids = jnp.concatenate([own[POINT], mine[POINT : POINT + 1], pad], 0).astype(i32)
    total = sum_pieces(sums[...]) + segment_few(values, ids, points)
    counts = as_points(sums[PIECES * HIGH : (PIECES + 1) * HIGH, :], points)
    inverse = 1.0 / counts
    loads = as_points(total, points) * inverse
    part = jnp.concatenate([loads, inverse], 0)
    if part.shape[0] < 8:
        part = jnp.concatenate([part, jnp.zeros((8 - part.shape[0], LANES), f32)], 0)
    for target in range(payload.shape[0]):
        payload[target] = part


def neighbours(n_lon, n_lat):
    lon, lat = lax.axis_index("lon"), lax.axis_index("lat")
    west = lax.rem(lon + n_lon - 1, n_lon) * n_lat + lat
    east = lax.rem(lon + 1, n_lon) * n_lat + lat
    other = lon * n_lat + (1 - lat)
    return west, east, other


def second_kernel(
    first, green, coarse, ocean, held_in, gu, cu, gv, cv, left, right, faces, lat_lines,
    payload, held, adj_u_out, adj_v_out, lam_sides, lam_edge, acc, lam, source,
    *, points, n_lon, n_lat,
):
    rows = coarse.shape[0]
    blocks = points // LANES
    lat = lax.axis_index("lat")
    south_end = jnp.where(lat == 1, 1.0, 0.0)
    north_end = jnp.where(lat == 0, 1.0, 0.0)
    potential = green_product(
        green, lambda k: first[k // blocks, k % blocks : k % blocks + 1, :], acc
    )
    put = put_sides(faces[ADJ], [(slope_ratio, -slope_ratio)])
    adj_l = lat_lines[ADJ_L : ADJ_L + 1, :]
    c_l = lat_lines[C_L : C_L + 1, :]
    g_l = lat_lines[G_L : G_L + 1, :]
    row = iota((STEP_ROWS, LANES), 0)
    lam[rows : rows + 8, :] = jnp.zeros((8, LANES), f32)
    for start in range(0, rows, STEP_ROWS):
        at = slice(start, start + STEP_ROWS)
        pot = spread(potential, local_ids(coarse[at, :], points))
        value = held_in[at, :] + put[at, :] - attract_coef * pot
        if start == 0:
            value = value + jnp.where(row == 0, south_end * slope_ratio * adj_l, 0.0)
        if start == rows - STEP_ROWS:
            value = value - jnp.where(row == STEP_ROWS - 1, north_end * slope_ratio * adj_l, 0.0)
        lam[at, :] = ocean[at, :].astype(f32) * value
    carry = jnp.zeros((1, LANES), f32)
    for start in range(0, rows, STEP_ROWS):
        at = slice(start, start + STEP_ROWS)
        lam_c = lam[at, :]
        adj_u = gu[at, :] + cu[at, :] * (roll_east(lam_c) - lam_c)
        adj_v = gv[at, :] + cv[at, :] * (lam[start + 1 : start + STEP_ROWS + 1, :] - lam_c)
        src = slope_ratio * (roll_west(adj_u) - adj_u + south_rows(carry, adj_v) - adj_v)
        carry = adj_v[STEP_ROWS - 1 :]
        adj_u_out[at, :] = adj_u
        adj_v_out[at, :] = adj_v
        source[at, :] = src
        held[at, :] = lam_c + src
    is_west = west_rows()
    sides = faces[MASK] * (
        faces[BASE] - attract_coef * spread(potential, faces[OWN_ID].astype(i32))
    )
    lam_sides[...] = sides
    pull = faces[RATIO] * sides
    flow = slope_ratio * jnp.where(is_west, pull, pull - faces[GAIN])
    edge = jnp.where(lat == 0, lam[rows - 1 : rows, :], lam[0:1, :])
    lam_edge[...] = edge
    pull = c_l * edge
    flow_l = slope_ratio * jnp.where(lat == 0, pull - g_l, pull)
    pad = jnp.zeros((1, LANES), f32)
    total = segment_part(
        jnp.concatenate([flow, flow_l, pad], 0),
        *one_hots(
            jnp.concatenate([faces[OWN_ID], lat_lines[OWN_L : OWN_L + 1, :], pad], 0).astype(i32),
            points,
        ),
    )
    for start in range(0, rows, SEG_ROWS):
        cells = slice(start * LANES, (start + SEG_ROWS) * LANES)
        total = total + segment_part(
            source[start : start + SEG_ROWS, :], left[:, cells], right[:, cells]
        )
    own = as_points(sum_pieces(total), points)
    far_id = faces[FAR_ID].astype(i32)
    half = far_id.shape[0] // 2

    def away(values, ids):
        return as_points(segment_few(-values, ids, points), points)

    west_part = away(flow[:half], far_id[:half])
    east_part = away(flow[half:], far_id[half:])
    lat_part = away(
        jnp.concatenate([flow_l, pad], 0),
        jnp.concatenate([lat_lines[ID_L : ID_L + 1, :], pad], 0).astype(i32),
    )
    part = jnp.concatenate([own, east_part, west_part, lat_part], 0)
    spare = payload.shape[1] - part.shape[0]
    part = jnp.concatenate([part, jnp.zeros((spare, LANES), f32)], 0)
    for target in range(payload.shape[0]):
        payload[target] = part
    west, east, other = neighbours(n_lon, n_lat)
    begin = 4 * blocks
    payload[west, begin : begin + half, :] = sides[:half]
    payload[east, begin : begin + half, :] = sides[half:]
    payload[other, begin + half : begin + half + 1, :] = edge


def edge_kernel(
    first, second, green, ocean, held, faces, lat_lines, lam_sides, lam_edge,
    edge, loads, start_pot, put, north_line, acc, *, points, n_lon, n_lat,
):
    rows = held.shape[0]
    blocks = points // LANES
    half = rows // LANES
    lat = lax.axis_index("lat")
    for lon in range(n_lon):
        for band in range(n_lat):
            here = lon * n_lat + band
            west = (lon - 1) % n_lon * n_lat + band
            east = (lon + 1) % n_lon * n_lat + band
            other = lon * n_lat + 1 - band
            total = (
                second[here, :blocks, :]
                + second[west, blocks : 2 * blocks, :]
                + second[east, 2 * blocks : 3 * blocks, :]
                + second[other, 3 * blocks : 4 * blocks, :]
            )
            loads[here * blocks : (here + 1) * blocks, :] = (
                total * first[here, blocks : 2 * blocks, :]
            )
    potential = green_product(green, lambda k: loads[k : k + 1, :], acc, 0, LANES)
    start_pot[...] = potential
    west, east, other = neighbours(n_lon, n_lat)
    begin = 4 * blocks
    far = jnp.concatenate(
        [second[west, begin : begin + half, :], second[east, begin : begin + half, :]], 0
    )
    rise = jnp.where(west_rows(), lam_sides[...] - far, far - lam_sides[...])
    adj = faces[GAIN] + faces[RATIO] * rise
    put[...] = put_sides(adj, [(slope_ratio, -slope_ratio), (0.0, 1.0)])
    rise = second[other, begin + half : begin + half + 1, :] - lam_edge[...]
    adj_l = lat_lines[G_L : G_L + 1, :] + lat_lines[C_L : C_L + 1, :] * jnp.where(
        lat == 0, rise, -rise
    )
    from_north = jnp.where(lat == 0, adj_l, 0.0)
    from_south = jnp.where(lat == 1, adj_l, 0.0)
    put[0:1, :LANES] = put[0:1, :LANES] + slope_ratio * from_south
    put[rows - 1 : rows, :LANES] = put[rows - 1 : rows, :LANES] - slope_ratio * from_north
    north_line[...] = from_north
    edge[...] = ocean[0:1, :].astype(f32) * (
        held[0:1, :] + put[0:1, :LANES] - attract_coef * potential[0:1, :]
    )


def last_kernel(
    loads, start_pot, put, north_line, green, coarse, ocean, held, adj_u_in, adj_v_in,
    lam_out, east_out, north_out, payload, acc, *, points, n_lon,
):
    rows = coarse.shape[0]
    potential = start_pot[...]
    if points > LANES:
        rest = green_product(green, lambda k: loads[k : k + 1, :], acc, LANES, points - LANES)
        potential = jnp.concatenate([potential, rest], 1)
    row = iota((STEP_ROWS, LANES), 0)
    for start in range(0, rows, STEP_ROWS):
        at = slice(start, start + STEP_ROWS)
        pot = spread(potential, local_ids(coarse[at, :], points))
        north = adj_v_in[at, :]
        if start == rows - STEP_ROWS:
            north = north + jnp.where(row == STEP_ROWS - 1, north_line[...], 0.0)
        lam_out[at, :] = ocean[at, :].astype(f32) * (
            held[at, :] + put[at, :LANES] - attract_coef * pot
        )
        east_out[at, :] = adj_u_in[at, :] + put[at, LANES:]
        north_out[at, :] = north
    span = rows // n_lon
    for target in range(n_lon):
        stop = (target + 1) * span
        payload[target, :span, :] = lam_out[target * span : stop, :]
        if target < n_lon - 1:
            payload[target, span : span + 8, :] = lam_out[stop : stop + 8, :]
        else:
            payload[target, span : span + 8, :] = jnp.zeros((8, LANES), f32)


def bands_kernel(parts, bands):
    count, tall, _ = parts.shape
    span = tall - 8
    lane = iota((span, LANES), 1)
    for k in range(count):
        here = parts[k, :span, :]
        east = parts[(k + 1) % count, :span, :]
        at = slice(k * LANES, (k + 1) * LANES)
        bands[0, 0, :, at] = here
        bands[1, 0, :, at] = jnp.where(lane == LANES - 1, roll_east(east), roll_east(here)) - here
        bands[2, 0, :, at] = parts[k, 1 : span + 1, :] - here


def call(kernel, shapes, scratch, args, name, far=False):
    vmem = pl.BlockSpec(memory_space=pltpu.VMEM)
    shapes = [(shape, f32) if isinstance(shape[0], int) else shape for shape in shapes]
    return pl.pallas_call(
        kernel,
        out_shape=[jax.ShapeDtypeStruct(shape, kind) for shape, kind in shapes],
        in_specs=[pl.BlockSpec(memory_space=pltpu.HBM) if far else vmem] * len(args),
        out_specs=[vmem] * len(shapes),
        scratch_shapes=scratch,
        compiler_params=pltpu.CompilerParams(vmem_limit_bytes=(52 << 20) if far else 16 << 20),
        cost_estimate=pl.CostEstimate(flops=4 << 30, bytes_accessed=16 << 20, transcendentals=0),
        name=name,
    )(*args)


def body(n_lon, n_lat, lam_in, flux_east, flux_north, depth, drag, ocean, coarse_of, green):
    rows, cols = lam_in.shape
    points = green.shape[0]
    blocks = points // LANES
    owners = n_lon * n_lat
    grid = (rows, cols)
    fields = (lam_in, flux_east, flux_north, depth, drag, ocean, coarse_of)
    tall = rows // LANES
    to_east, to_west, to_lat, *fields = call(
        functools.partial(pack_kernel, points=points),
        [(6 * tall, cols), (6 * tall, cols), (8, cols)]
        + [(grid, field.dtype) for field in fields],
        [pltpu.SemaphoreType.DMA((7,))], fields, "pack", far=True,
    )
    ocean, coarse_of = fields[5:]
    forward = [(k, (k + 1) % n_lon) for k in range(n_lon)]
    backward = [(target, source) for source, target in forward]
    from_west = lax.ppermute(to_east, "lon", forward)
    from_east = lax.ppermute(to_west, "lon", backward)
    from_lat = lax.ppermute(to_lat, "lat", [(0, 1), (1, 0)])
    held, gu, cu, gv, cv, sums, left, right, held_sides = call(
        functools.partial(inner_kernel, points=points),
        [grid] * 5
        + [((PIECES + 1) * HIGH, LOW), ((HIGH, rows * cols), bf16), ((LOW, rows * cols), bf16)]
        + [(2 * tall, cols)],
        [pltpu.VMEM(grid, f32)], fields, "inner",
    )
    payload, faces, lat_lines = call(
        functools.partial(rim_kernel, points=points),
        [(owners, 8, LANES), (7, 2 * tall, cols), (8, cols)], [],
        (to_east, to_west, to_lat, from_west, from_east, from_lat, sums, held_sides), "rim",
    )
    first = lax.all_to_all(payload, ("lon", "lat"), 0, 0, tiled=True)
    deep = -(-(4 * blocks + tall + 1) // 8) * 8
    payload, held, adj_u, adj_v, lam_sides, lam_edge = call(
        functools.partial(second_kernel, points=points, n_lon=n_lon, n_lat=n_lat),
        [(owners, deep, LANES), grid, grid, grid, (2 * tall, cols), (1, cols)],
        [
            pltpu.VMEM((points, LANES), f32),
            pltpu.VMEM((rows + 8, cols), f32),
            pltpu.VMEM(grid, f32),
        ],
        (first, green, coarse_of, ocean, held, gu, cu, gv, cv, left, right, faces, lat_lines),
        "second",
    )
    second = lax.all_to_all(payload, ("lon", "lat"), 0, 0, tiled=True)
    span = rows // n_lon
    edge, loads, start_pot, put, north_line = call(
        functools.partial(edge_kernel, points=points, n_lon=n_lon, n_lat=n_lat),
        [(1, cols), (owners * blocks, LANES), (8, LANES), (rows, 2 * cols), (1, cols)],
        [pltpu.VMEM((LANES, LANES), f32)],
        (first, second, green, ocean, held, faces, lat_lines, lam_sides, lam_edge), "edge",
    )
    lam, east, north, payload = call(
        functools.partial(last_kernel, points=points, n_lon=n_lon),
        [grid, grid, grid, (n_lon, span + 8, cols)],
        [pltpu.VMEM((points, LANES), f32)],
        (loads, start_pot, put, north_line, green, coarse_of, ocean, held, adj_u, adj_v), "last",
    )
    edge = lax.ppermute(edge, "lat", [(1, 0)])
    payload = lax.dynamic_update_slice(payload, edge[None], (n_lon - 1, span, 0))
    parts = lax.all_to_all(payload, "lon", 0, 0, tiled=True)
    (bands,) = call(bands_kernel, [(3, 1, span, n_lon * cols)], [], (parts,), "bands")
    return lam, east, north, bands


def solution(mesh):
    cells = P(("groups", "lat"), "lon")
    n_lon, n_lat = mesh.shape["lon"], mesh.shape["lat"]
    return jax.shard_map(
        functools.partial(body, n_lon, n_lat),
        mesh=mesh,
        in_specs=(cells,) * 6 + (P("lat", "lon"), P(("lon", "lat"), None)),
        out_specs=(cells,) * 3 + (P(None, ("groups", "lat"), "lon", None),),
        check_vma=False,
    )
```

```python
import functools

import jax
import jax.numpy as jnp
from jax import lax
from jax.experimental import pallas as pl
from jax.experimental.pallas import tpu as pltpu
from jax.sharding import PartitionSpec as P

f32 = jnp.float32
bf16 = jnp.bfloat16
i32 = jnp.int32

LANES = 128
LOW = 32
HIGH = 16
PIECES = 2
SEG_ROWS = 256
STEP_ROWS = 128

flux_ratio = 0.25
slope_ratio = 0.25
drag_step = 1.0
attract_coef = 0.5

LAM, DEPTH, DRAG, OCEAN, POINT, FLUX = range(6)
ADJ, RATIO, GAIN, BASE, MASK, OWN_ID, FAR_ID = range(7)
ADJ_L, C_L, G_L, ID_L, OWN_L = range(5)


def iota(shape, dim):
    return lax.broadcasted_iota(i32, shape, dim)


def roll_east(x):
    return pltpu.roll(x, LANES - 1, 1)


def roll_west(x):
    return pltpu.roll(x, 1, 1)


def local_ids(ids, points):
    return lax.bitwise_and(ids, points - 1)


def bf16_pieces(values, count=PIECES):
    out = []
    for piece in range(count):
        top = values.astype(bf16).astype(f32)
        out.append(top)
        if piece < count - 1:
            values = values - top
    return out


def one_hots(ids, points):
    blocks = points // LANES
    high = lax.shift_right_logical(ids, 5)
    high = lax.bitwise_and(high, 3) * blocks + lax.shift_right_logical(high, 2)
    low = lax.bitwise_and(ids, LOW - 1)
    high_iota = iota((HIGH, LANES), 0)
    low_iota = iota((LOW, LANES), 0)
    left, right = [], []
    for row in range(ids.shape[0]):
        mask = jnp.broadcast_to(high[row : row + 1], (HIGH, LANES)) == high_iota
        left.append(jnp.where(mask, 1.0, 0.0).astype(bf16))
        mask = jnp.broadcast_to(low[row : row + 1], (LOW, LANES)) == low_iota
        right.append(jnp.where(mask, 1.0, 0.0).astype(bf16))
    return jnp.concatenate(left, 1), jnp.concatenate(right, 1)


def segment_part(values, left, right, with_counts=False):
    parts = []
    for piece in bf16_pieces(values):
        line = jnp.concatenate(
            [
                jnp.broadcast_to(piece[row : row + 1], (HIGH, LANES)).astype(bf16)
                for row in range(values.shape[0])
            ],
            1,
        )
        parts.append(left * line)
    if with_counts:
        parts.append(left)
    return lax.dot_general(
        jnp.concatenate(parts, 0), right, (((1,), (1,)), ((), ())), preferred_element_type=f32
    )


def segment_few(values, ids, points):
    return sum_pieces(segment_part(values, *one_hots(ids, points)))


def sum_pieces(parts):
    total = parts[:HIGH]
    for piece in range(1, PIECES):
        total = total + parts[piece * HIGH : (piece + 1) * HIGH]
    return total


def as_points(table, points):
    blocks = points // LANES
    return jnp.concatenate([table[q * blocks : (q + 1) * blocks] for q in range(4)], 1)


def fold(line):
    return jnp.concatenate(
        [line[:, k * LANES : (k + 1) * LANES] for k in range(line.shape[1] // LANES)], 0
    )


def unfold(block):
    return jnp.concatenate([block[k : k + 1] for k in range(block.shape[0])], 1)


def take_sides(block, count=3):
    sub, lane = iota((8, LANES), 0), iota((8, LANES), 1)
    pick = ((sub == 0) & (lane == 0)) | ((sub == 1) & (lane == LANES - 1))
    pick = pick.astype(f32).astype(bf16)
    out = None
    for piece in reversed(bf16_pieces(block, count)):
        part = lax.dot_general(
            pick, piece.astype(bf16), (((1,), (1,)), ((), ())), preferred_element_type=f32
        )
        out = part if out is None else out + part
    return out


def put_sides(pair, entries):
    half = pair.shape[0] // 2
    lines = jnp.concatenate([unfold(pair[:half]), unfold(pair[half:])], 0)
    rows = lines.shape[1]
    pieces = bf16_pieces(lines, 3)
    stack = jnp.concatenate(pieces + [jnp.zeros((2, rows), f32)], 0)
    sub, lane = iota((8, LANES), 0), iota((8, LANES), 1)
    west = (sub < 6) & (lax.bitwise_and(sub, 1) == 0) & (lane == 0)
    east = (sub < 6) & (lax.bitwise_and(sub, 1) == 1) & (lane == LANES - 1)
    picks = [jnp.where(west, first, jnp.where(east, last, 0.0)) for first, last in entries]
    return lax.dot_general(
        stack, jnp.concatenate(picks, 1), (((0,), (0,)), ((), ())), preferred_element_type=f32
    )


def green_product(green_ref, load_row, acc_ref, first=0, points=None):
    total = green_ref.shape[1]
    points = green_ref.shape[0] - first if points is None else points
    tall = LANES

    def step(index, carry):
        start = pl.multiple_of(index * tall, tall)
        acc = jnp.zeros((tall, LANES), f32)
        for k in range(total // LANES):
            acc = acc + green_ref[
                pl.ds(first + start, tall), k * LANES : (k + 1) * LANES
            ] * jnp.broadcast_to(load_row(k), (tall, LANES))
        acc_ref[pl.ds(start, tall), :] = acc
        return carry

    lax.fori_loop(0, points // tall, step, 0)
    out = None
    for piece in reversed(bf16_pieces(acc_ref[0:points, :], 3)):
        part = lax.dot_general(
            jnp.ones((8, LANES), bf16), piece.astype(bf16), (((1,), (1,)), ((), ())),
            preferred_element_type=f32,
        )
        out = part if out is None else out + part
    return out


def spread(potential, ids):
    points = potential.shape[1]
    rows = ids.shape[0]
    low = lax.bitwise_and(ids, LANES - 1)
    block = lax.shift_right_logical(ids, 7)
    out = None
    for k in range(points // LANES):
        table = potential[:, k * LANES : (k + 1) * LANES]
        table = jnp.broadcast_to(table[None], (rows // 8, 8, LANES)).reshape(rows, LANES)
        value = jnp.take_along_axis(table, low, axis=1, mode="promise_in_bounds")
        out = value if out is None else jnp.where(block == k, value, out)
    return out


def next_rows(ref, start, count):
    if start + count < ref.shape[0]:
        return ref[start + 1 : start + count + 1, :]
    return jnp.concatenate([ref[start + 1 :, :], jnp.zeros((1, LANES), ref.dtype)], 0)


def south_rows(first, block):
    return jnp.concatenate([first, block[:-1]], 0)


def pack_kernel(*refs, points):
    far, (to_east, to_west, to_lat), near, done = refs[:7], refs[7:10], refs[10:17], refs[17]
    copies = [pltpu.make_async_copy(far[k], near[k], done.at[k]) for k in range(7)]
    for copy in copies:
        copy.start()
    lam, east, north, depth, drag, ocean, coarse = near
    rows = lam.shape[0]
    tall = rows // LANES
    lat = lax.axis_index("lat")
    order = (
        (LAM, 0, lam, 3), (FLUX, 1, east, 3), (None, 2, north, 0), (DEPTH, 3, depth, 3),
        (DRAG, 4, drag, 3), (OCEAN, 5, ocean, 1), (POINT, 6, coarse, 2),
    )
    for field, index, ref, pieces in order:
        copies[index].wait()
        if field is None:
            continue
        block = ref[...]
        if field == POINT:
            block = local_ids(block, points)
        sides = take_sides(block.astype(f32), pieces)
        at = slice(field * tall, (field + 1) * tall)
        to_west[at, :] = fold(sides[0:1])
        to_east[at, :] = fold(sides[1:2])

    def border(row):
        return jnp.concatenate(
            [
                lam[row : row + 1, :],
                depth[row : row + 1, :],
                drag[row : row + 1, :],
                ocean[row : row + 1, :].astype(f32),
                local_ids(coarse[row : row + 1, :], points).astype(f32),
                north[row : row + 1, :],
                jnp.zeros((2, LANES), f32),
            ],
            0,
        )

    to_lat[...] = jnp.where(lat == 0, border(rows - 1), border(0))


def inner_kernel(
    lam, east, north, depth, drag, ocean, coarse,
    held, gu, cu, gv, cv, sums, left, right, held_sides, source, *, points,
):
    rows = lam.shape[0]
    inner = iota((STEP_ROWS, LANES), 1) < LANES - 1
    carry = jnp.zeros((1, LANES), f32)
    for start in range(0, rows, STEP_ROWS):
        at = slice(start, start + STEP_ROWS)
        lam_c, depth_c, drag_c = lam[at, :], depth[at, :], drag[at, :]
        ocean_c = ocean[at, :].astype(f32)
        damp = jnp.where(
            inner,
            ocean_c * roll_east(ocean_c) / (1.0 + drag_step * 0.5 * (drag_c + roll_east(drag_c))),
            0.0,
        )
        ratio = damp * (flux_ratio * 0.5) * (depth_c + roll_east(depth_c))
        adj_u = damp * east[at, :] + ratio * (roll_east(lam_c) - lam_c)
        cu[at, :] = ratio
        gu[at, :] = damp * adj_u
        ocean_n = next_rows(ocean, start, STEP_ROWS).astype(f32)
        damp = (
            ocean_c
            * ocean_n
            / (1.0 + drag_step * 0.5 * (drag_c + next_rows(drag, start, STEP_ROWS)))
        )
        ratio = damp * (flux_ratio * 0.5) * (depth_c + next_rows(depth, start, STEP_ROWS))
        adj_v = damp * north[at, :] + ratio * (next_rows(lam, start, STEP_ROWS) - lam_c)
        cv[at, :] = ratio
        gv[at, :] = damp * adj_v
        src = slope_ratio * (roll_west(adj_u) - adj_u + south_rows(carry, adj_v) - adj_v)
        carry = adj_v[STEP_ROWS - 1 :]
        source[at, :] = src
        held[at, :] = lam_c + src
    total = jnp.zeros(sums.shape, f32)
    for start in range(0, rows, SEG_ROWS):
        at = slice(start, start + SEG_ROWS)
        cells = slice(start * LANES, (start + SEG_ROWS) * LANES)
        high, low = one_hots(local_ids(coarse[at, :], points), points)
        left[:, cells] = high
        right[:, cells] = low
        total = total + segment_part(source[at, :], high, low, True)
    sums[...] = total
    sides = take_sides(held[...])
    held_sides[...] = jnp.concatenate([fold(sides[0:1]), fold(sides[1:2])], 0)


def face(low, high, flux):
    damp = low[OCEAN] * high[OCEAN] / (1.0 + drag_step * 0.5 * (low[DRAG] + high[DRAG]))
    ratio = damp * (flux_ratio * 0.5) * (low[DEPTH] + high[DEPTH])
    adj = damp * flux + ratio * (high[LAM] - low[LAM])
    return adj, ratio, damp * adj


def west_rows():
    return iota((8, LANES), 0) < 4


def rim_kernel(
    own_east, own_west, own_lat, from_west, from_east, from_lat, sums, held_sides,
    payload, faces, lat_lines, *, points,
):
    lat = lax.axis_index("lat")
    half = held_sides.shape[0] // 2

    def pair(west, east):
        return [
            jnp.concatenate(
                [west[k * half : (k + 1) * half, :], east[k * half : (k + 1) * half, :]], 0
            )
            for k in range(6)
        ]

    own, far = pair(own_west, own_east), pair(from_west, from_east)
    is_west = west_rows()
    low = [jnp.where(is_west, there, here) for here, there in zip(own, far)]
    high = [jnp.where(is_west, here, there) for here, there in zip(own, far)]
    adj, ratio, gain = face(low, high, low[FLUX])
    mine, other = own_lat[...], from_lat[...]
    lower = jnp.where(lat == 0, mine, other)
    upper = jnp.where(lat == 0, other, mine)
    lower = [lower[k : k + 1] for k in range(6)]
    upper = [upper[k : k + 1] for k in range(6)]
    adj_l, c_l, g_l = face(lower, upper, lower[FLUX])
    lat_lines[...] = jnp.concatenate(
        [
            adj_l, c_l, g_l, other[POINT : POINT + 1], mine[POINT : POINT + 1],
            jnp.zeros((3, LANES), f32),
        ],
        0,
    )
    sign = jnp.where(is_west, slope_ratio, -slope_ratio)
    sign_l = jnp.where(lat == 0, -slope_ratio, slope_ratio)
    flow = sign * adj
    sub, lane = lax.bitwise_and(iota((8, LANES), 0), half - 1), iota((8, LANES), 1)
    corner = ((lat == 0) & (sub == half - 1) & (lane == LANES - 1)) | (
        (lat == 1) & (sub == 0) & (lane == 0)
    )
    at_corner = jnp.where(
        is_west,
        jnp.broadcast_to(adj_l[:, 0:1], (8, LANES)),
        jnp.broadcast_to(adj_l[:, LANES - 1 :], (8, LANES)),
    )
    faces[ADJ] = adj
    faces[RATIO] = ratio
    faces[GAIN] = gain
    faces[BASE] = held_sides[...] + flow + jnp.where(corner, sign_l * at_corner, 0.0)
    faces[MASK] = own[OCEAN]
    faces[OWN_ID] = own[POINT]
    faces[FAR_ID] = far[POINT]
    pad = jnp.zeros((1, LANES), f32)
    values = jnp.concatenate([flow, sign_l * adj_l, pad], 0)
    ids = jnp.concatenate([own[POINT], mine[POINT : POINT + 1], pad], 0).astype(i32)
    total = sum_pieces(sums[...]) + segment_few(values, ids, points)
    counts = as_points(sums[PIECES * HIGH : (PIECES + 1) * HIGH, :], points)
    inverse = 1.0 / counts
    loads = as_points(total, points) * inverse
    part = jnp.concatenate([loads, inverse], 0)
    if part.shape[0] < 8:
        part = jnp.concatenate([part, jnp.zeros((8 - part.shape[0], LANES), f32)], 0)
    for target in range(payload.shape[0]):
        payload[target] = part


def neighbours(n_lon, n_lat):
    lon, lat = lax.axis_index("lon"), lax.axis_index("lat")
    west = lax.rem(lon + n_lon - 1, n_lon) * n_lat + lat
    east = lax.rem(lon + 1, n_lon) * n_lat + lat
    other = lon * n_lat + (1 - lat)
    return west, east, other


def second_kernel(
    first, green, coarse, ocean, held_in, gu, cu, gv, cv, left, right, faces, lat_lines,
    payload, held, adj_u_out, adj_v_out, lam_sides, lam_edge, acc, lam, source,
    *, points, n_lon, n_lat,
):
    rows = coarse.shape[0]
    blocks = points // LANES
    lat = lax.axis_index("lat")
    south_end = jnp.where(lat == 1, 1.0, 0.0)
    north_end = jnp.where(lat == 0, 1.0, 0.0)
    potential = green_product(
        green, lambda k: first[k // blocks, k % blocks : k % blocks + 1, :], acc
    )
    put = put_sides(faces[ADJ], [(slope_ratio, -slope_ratio)])
    adj_l = lat_lines[ADJ_L : ADJ_L + 1, :]
    c_l = lat_lines[C_L : C_L + 1, :]
    g_l = lat_lines[G_L : G_L + 1, :]
    row = iota((STEP_ROWS, LANES), 0)
    lam[rows : rows + 8, :] = jnp.zeros((8, LANES), f32)
    for start in range(0, rows, STEP_ROWS):
        at = slice(start, start + STEP_ROWS)
        pot = spread(potential, local_ids(coarse[at, :], points))
        value = held_in[at, :] + put[at, :] - attract_coef * pot
        if start == 0:
            value = value + jnp.where(row == 0, south_end * slope_ratio * adj_l, 0.0)
        if start == rows - STEP_ROWS:
            value = value - jnp.where(row == STEP_ROWS - 1, north_end * slope_ratio * adj_l, 0.0)
        lam[at, :] = ocean[at, :].astype(f32) * value
    carry = jnp.zeros((1, LANES), f32)
    for start in range(0, rows, STEP_ROWS):
        at = slice(start, start + STEP_ROWS)
        lam_c = lam[at, :]
        adj_u = gu[at, :] + cu[at, :] * (roll_east(lam_c) - lam_c)
        adj_v = gv[at, :] + cv[at, :] * (lam[start + 1 : start + STEP_ROWS + 1, :] - lam_c)
        src = slope_ratio * (roll_west(adj_u) - adj_u + south_rows(carry, adj_v) - adj_v)
        carry = adj_v[STEP_ROWS - 1 :]
        adj_u_out[at, :] = adj_u
        adj_v_out[at, :] = adj_v
        source[at, :] = src
        held[at, :] = lam_c + src
    is_west = west_rows()
    sides = faces[MASK] * (
        faces[BASE] - attract_coef * spread(potential, faces[OWN_ID].astype(i32))
    )
    lam_sides[...] = sides
    pull = faces[RATIO] * sides
    flow = slope_ratio * jnp.where(is_west, pull, pull - faces[GAIN])
    edge = jnp.where(lat == 0, lam[rows - 1 : rows, :], lam[0:1, :])
    lam_edge[...] = edge
    pull = c_l * edge
    flow_l = slope_ratio * jnp.where(lat == 0, pull - g_l, pull)
    pad = jnp.zeros((1, LANES), f32)
    total = segment_part(
        jnp.concatenate([flow, flow_l, pad], 0),
        *one_hots(
            jnp.concatenate([faces[OWN_ID], lat_lines[OWN_L : OWN_L + 1, :], pad], 0).astype(i32),
            points,
        ),
    )
    def add(index, total):
        at = pl.ds(pl.multiple_of(index * SEG_ROWS, SEG_ROWS), SEG_ROWS)
        cells = pl.ds(pl.multiple_of(index * SEG_ROWS * LANES, SEG_ROWS * LANES), SEG_ROWS * LANES)
        return total + segment_part(source[at, :], left[:, cells], right[:, cells])

    total = lax.fori_loop(0, rows // SEG_ROWS, add, total)
    own = as_points(sum_pieces(total), points)
    far_id = faces[FAR_ID].astype(i32)
    half = far_id.shape[0] // 2

    def away(values, ids):
        return as_points(segment_few(-values, ids, points), points)

    west_part = away(flow[:half], far_id[:half])
    east_part = away(flow[half:], far_id[half:])
    lat_part = away(
        jnp.concatenate([flow_l, pad], 0),
        jnp.concatenate([lat_lines[ID_L : ID_L + 1, :], pad], 0).astype(i32),
    )
    west, east, other = neighbours(n_lon, n_lat)
    part = jnp.concatenate([own, east_part, west_part, lat_part], 0)
    begin = 4 * blocks
    deep = begin + half
    edge_rows = jnp.concatenate([edge, jnp.zeros((half - 1, LANES), f32)], 0)
    for target in range(n_lon * n_lat):
        shared = jnp.where(
            target == west, sides[:half], jnp.where(target == east, sides[half:], edge_rows)
        )
        payload[target * deep : (target + 1) * deep, :] = jnp.concatenate([part, shared], 0)


def edge_kernel(
    first, second, green, ocean, held, faces, lat_lines, lam_sides, lam_edge,
    edge, loads, start_pot, put, north_line, acc, *, points, n_lon, n_lat,
):
    rows = held.shape[0]
    blocks = points // LANES
    half = rows // LANES
    deep = 4 * blocks + half
    lat = lax.axis_index("lat")

    def received(owner, kind):
        start = owner * deep + kind * blocks
        return second[start : start + blocks, :]

    for lon in range(n_lon):
        for band in range(n_lat):
            here = lon * n_lat + band
            west = (lon - 1) % n_lon * n_lat + band
            east = (lon + 1) % n_lon * n_lat + band
            other = lon * n_lat + 1 - band
            total = received(here, 0) + received(west, 1) + received(east, 2) + received(other, 3)
            loads[here * blocks : (here + 1) * blocks, :] = (
                total * first[here, blocks : 2 * blocks, :]
            )
    potential = green_product(green, lambda k: loads[k : k + 1, :], acc, 0, LANES)
    start_pot[...] = potential
    west, east, other = neighbours(n_lon, n_lat)

    def shared(owner, count):
        return second[pl.ds(owner * deep + 4 * blocks, count), :]

    far = jnp.concatenate([shared(west, half), shared(east, half)], 0)
    rise = jnp.where(west_rows(), lam_sides[...] - far, far - lam_sides[...])
    adj = faces[GAIN] + faces[RATIO] * rise
    put[...] = put_sides(adj, [(slope_ratio, -slope_ratio), (0.0, 1.0)])
    rise = shared(other, 1) - lam_edge[...]
    adj_l = lat_lines[G_L : G_L + 1, :] + lat_lines[C_L : C_L + 1, :] * jnp.where(
        lat == 0, rise, -rise
    )
    from_north = jnp.where(lat == 0, adj_l, 0.0)
    from_south = jnp.where(lat == 1, adj_l, 0.0)
    put[0:1, :LANES] = put[0:1, :LANES] + slope_ratio * from_south
    put[rows - 1 : rows, :LANES] = put[rows - 1 : rows, :LANES] - slope_ratio * from_north
    north_line[...] = from_north
    edge[...] = ocean[0:1, :].astype(f32) * (
        held[0:1, :] + put[0:1, :LANES] - attract_coef * potential[0:1, :]
    )


def last_kernel(
    loads, start_pot, put, green, coarse, ocean, held, lam_out, payload, acc, *, points, n_lon,
):
    rows = coarse.shape[0]
    potential = start_pot[...]
    if points > LANES:
        rest = green_product(green, lambda k: loads[k : k + 1, :], acc, LANES, points - LANES)
        potential = jnp.concatenate([potential, rest], 1)
    for start in range(0, rows, STEP_ROWS):
        at = slice(start, start + STEP_ROWS)
        pot = spread(potential, local_ids(coarse[at, :], points))
        lam_out[at, :] = ocean[at, :].astype(f32) * (
            held[at, :] + put[at, :LANES] - attract_coef * pot
        )
    span = rows // n_lon
    for target in range(n_lon):
        start = target * (span + 1)
        payload[start : start + span, :] = lam_out[target * span : (target + 1) * span, :]
        if target < n_lon - 1:
            stop = (target + 1) * span
            payload[start + span : start + span + 1, :] = lam_out[stop : stop + 1, :]
        else:
            payload[start + span : start + span + 1, :] = jnp.zeros((1, LANES), f32)


def bands_kernel(
    parts, lam, adj_u, adj_v, put, north_line,
    lam_out, east_out, north_out, bands, east, north, planes, done, *, count,
):
    span = parts.shape[0] // count - 1
    rows = lam.shape[0]
    copies = [
        pltpu.make_async_copy(lam, lam_out, done.at[0]),
        pltpu.make_async_copy(east, east_out, done.at[1]),
        pltpu.make_async_copy(north, north_out, done.at[2]),
    ] + [
        pltpu.make_async_copy(planes.at[k], bands.at[k, 0], done.at[3 + k]) for k in range(3)
    ]
    copies[0].start()
    lane = iota((span, LANES), 1)
    for k in range(count):
        start = k * (span + 1)
        planes[0, :, k * LANES : (k + 1) * LANES] = parts[start : start + span, :]
    copies[3].start()
    for k in range(count):
        start = k * (span + 1)
        here = parts[start : start + span, :]
        planes[2, :, k * LANES : (k + 1) * LANES] = parts[start + 1 : start + 1 + span, :] - here
    copies[5].start()
    for k in range(count):
        at = slice(k * LANES, (k + 1) * LANES)
        here = planes[0, :, at]
        after = (k + 1) % count
        there = planes[0, :, after * LANES : (after + 1) * LANES]
        planes[1, :, at] = jnp.where(lane == LANES - 1, roll_east(there), roll_east(here)) - here
    copies[4].start()
    east[...] = adj_u[...] + put[:, LANES:]
    copies[1].start()
    north[...] = adj_v[...]
    north[rows - 1 : rows, :] = adj_v[rows - 1 : rows, :] + north_line[...]
    copies[2].start()
    for copy in copies:
        copy.wait()


def call(kernel, shapes, scratch, args, name, far=False, far_out=False):
    vmem = pl.BlockSpec(memory_space=pltpu.VMEM)
    shapes = [(shape, f32) if isinstance(shape[0], int) else shape for shape in shapes]
    return pl.pallas_call(
        kernel,
        out_shape=[jax.ShapeDtypeStruct(shape, kind) for shape, kind in shapes],
        in_specs=[pl.BlockSpec(memory_space=pltpu.HBM) if far else vmem] * len(args),
        out_specs=[pl.BlockSpec(memory_space=pl.ANY) if far_out else vmem] * len(shapes),
        scratch_shapes=scratch,
        compiler_params=pltpu.CompilerParams(vmem_limit_bytes=(52 << 20) if far else 16 << 20),
        cost_estimate=pl.CostEstimate(flops=4 << 30, bytes_accessed=16 << 20, transcendentals=0),
        name=name,
    )(*args)


def body(n_lon, n_lat, lam_in, flux_east, flux_north, depth, drag, ocean, coarse_of, green):
    rows, cols = lam_in.shape
    points = green.shape[0]
    blocks = points // LANES
    owners = n_lon * n_lat
    grid = (rows, cols)
    fields = (lam_in, flux_east, flux_north, depth, drag, ocean, coarse_of)
    tall = rows // LANES
    to_east, to_west, to_lat, *fields = call(
        functools.partial(pack_kernel, points=points),
        [(6 * tall, cols), (6 * tall, cols), (8, cols)]
        + [(grid, field.dtype) for field in fields],
        [pltpu.SemaphoreType.DMA((7,))], fields, "pack", far=True,
    )
    ocean, coarse_of = fields[5:]
    forward = [(k, (k + 1) % n_lon) for k in range(n_lon)]
    backward = [(target, source) for source, target in forward]
    from_west = lax.ppermute(to_east, "lon", forward)
    from_east = lax.ppermute(to_west, "lon", backward)
    from_lat = lax.ppermute(to_lat, "lat", [(0, 1), (1, 0)])
    held, gu, cu, gv, cv, sums, left, right, held_sides = call(
        functools.partial(inner_kernel, points=points),
        [grid] * 5
        + [((PIECES + 1) * HIGH, LOW), ((HIGH, rows * cols), bf16), ((LOW, rows * cols), bf16)]
        + [(2 * tall, cols)],
        [pltpu.VMEM(grid, f32)], fields, "inner",
    )
    payload, faces, lat_lines = call(
        functools.partial(rim_kernel, points=points),
        [(owners, 8, LANES), (7, 2 * tall, cols), (8, cols)], [],
        (to_east, to_west, to_lat, from_west, from_east, from_lat, sums, held_sides), "rim",
    )
    first = lax.all_to_all(payload, ("lon", "lat"), 0, 0, tiled=True)
    deep = 4 * blocks + tall
    payload, held, adj_u, adj_v, lam_sides, lam_edge = call(
        functools.partial(second_kernel, points=points, n_lon=n_lon, n_lat=n_lat),
        [(owners * deep, LANES), grid, grid, grid, (2 * tall, cols), (1, cols)],
        [
            pltpu.VMEM((points, LANES), f32),
            pltpu.VMEM((rows + 8, cols), f32),
            pltpu.VMEM(grid, f32),
        ],
        (first, green, coarse_of, ocean, held, gu, cu, gv, cv, left, right, faces, lat_lines),
        "second",
    )
    second = lax.all_to_all(
        payload.reshape(owners, deep, 1, LANES), ("lon", "lat"), 0, 0, tiled=True
    ).reshape(payload.shape)
    span = rows // n_lon
    edge, loads, start_pot, put, north_line = call(
        functools.partial(edge_kernel, points=points, n_lon=n_lon, n_lat=n_lat),
        [(1, cols), (owners * blocks, LANES), (8, LANES), (rows, 2 * cols), (1, cols)],
        [pltpu.VMEM((LANES, LANES), f32)],
        (first, second, green, ocean, held, faces, lat_lines, lam_sides, lam_edge), "edge",
    )
    lam, payload = call(
        functools.partial(last_kernel, points=points, n_lon=n_lon),
        [grid, (rows + n_lon, cols)],
        [pltpu.VMEM((points, LANES), f32)],
        (loads, start_pot, put, green, coarse_of, ocean, held), "last",
    )
    edge = lax.ppermute(edge, "lat", [(1, 0)])
    payload = lax.dynamic_update_slice(payload, edge, (rows + n_lon - 1, 0))
    parts = lax.all_to_all(
        payload.reshape(n_lon, span + 1, 1, LANES), "lon", 0, 0, tiled=True
    ).reshape(payload.shape)
    return tuple(
        call(
            functools.partial(bands_kernel, count=n_lon),
            [grid, grid, grid, (3, 1, span, n_lon * cols)],
            [
                pltpu.VMEM(grid, f32),
                pltpu.VMEM(grid, f32),
                pltpu.VMEM((3, span, n_lon * cols), f32),
                pltpu.SemaphoreType.DMA((6,)),
            ],
            (parts, lam, adj_u, adj_v, put, north_line), "bands", far_out=True,
        )
    )


def solution(mesh):
    cells = P(("groups", "lat"), "lon")
    n_lon, n_lat = mesh.shape["lon"], mesh.shape["lat"]
    return jax.shard_map(
        functools.partial(body, n_lon, n_lat),
        mesh=mesh,
        in_specs=(cells,) * 6 + (P("lat", "lon"), P(("lon", "lat"), None)),
        out_specs=(cells,) * 3 + (P(None, ("groups", "lat"), "lon", None),),
        check_vma=False,
    )
```

```python
import functools

import jax
import jax.numpy as jnp
from jax import lax
from jax.experimental import pallas as pl
from jax.experimental.pallas import tpu as pltpu
from jax.sharding import PartitionSpec as P

f32 = jnp.float32
bf16 = jnp.bfloat16
i32 = jnp.int32

LANES = 128
LOW = 32
HIGH = 16
PIECES = 2
SEG_ROWS = 256
STEP_ROWS = 128

flux_ratio = 0.25
slope_ratio = 0.25
drag_step = 1.0
attract_coef = 0.5

LAM, DEPTH, DRAG, OCEAN, POINT, FLUX = range(6)
ADJ, RATIO, GAIN, BASE, MASK, OWN_ID, FAR_ID = range(7)
ADJ_L, C_L, G_L, ID_L, OWN_L = range(5)


def iota(shape, dim):
    return lax.broadcasted_iota(i32, shape, dim)


def roll_east(x):
    return pltpu.roll(x, LANES - 1, 1)


def roll_west(x):
    return pltpu.roll(x, 1, 1)


def local_ids(ids, points):
    return lax.bitwise_and(ids, points - 1)


def bf16_pieces(values, count=PIECES):
    out = []
    for piece in range(count):
        top = values.astype(bf16).astype(f32)
        out.append(top)
        if piece < count - 1:
            values = values - top
    return out


def one_hots(ids, points):
    blocks = points // LANES
    high = lax.shift_right_logical(ids, 5)
    high = lax.bitwise_and(high, 3) * blocks + lax.shift_right_logical(high, 2)
    low = lax.bitwise_and(ids, LOW - 1)
    high_iota = iota((HIGH, LANES), 0)
    low_iota = iota((LOW, LANES), 0)
    left, right = [], []
    for row in range(ids.shape[0]):
        mask = jnp.broadcast_to(high[row : row + 1], (HIGH, LANES)) == high_iota
        left.append(jnp.where(mask, 1.0, 0.0).astype(bf16))
        mask = jnp.broadcast_to(low[row : row + 1], (LOW, LANES)) == low_iota
        right.append(jnp.where(mask, 1.0, 0.0).astype(bf16))
    return jnp.concatenate(left, 1), jnp.concatenate(right, 1)


def segment_part(values, left, right, with_counts=False):
    parts = []
    for piece in bf16_pieces(values):
        line = jnp.concatenate(
            [
                jnp.broadcast_to(piece[row : row + 1], (HIGH, LANES)).astype(bf16)
                for row in range(values.shape[0])
            ],
            1,
        )
        parts.append(left * line)
    if with_counts:
        parts.append(left)
    return lax.dot_general(
        jnp.concatenate(parts, 0), right, (((1,), (1,)), ((), ())), preferred_element_type=f32
    )


def segment_few(values, ids, points):
    return sum_pieces(segment_part(values, *one_hots(ids, points)))


def sum_pieces(parts):
    total = parts[:HIGH]
    for piece in range(1, PIECES):
        total = total + parts[piece * HIGH : (piece + 1) * HIGH]
    return total


def as_points(table, points):
    blocks = points // LANES
    return jnp.concatenate([table[q * blocks : (q + 1) * blocks] for q in range(4)], 1)


def fold(line):
    return jnp.concatenate(
        [line[:, k * LANES : (k + 1) * LANES] for k in range(line.shape[1] // LANES)], 0
    )


def unfold(block):
    return jnp.concatenate([block[k : k + 1] for k in range(block.shape[0])], 1)


def take_sides(block, count=3):
    sub, lane = iota((8, LANES), 0), iota((8, LANES), 1)
    pick = ((sub == 0) & (lane == 0)) | ((sub == 1) & (lane == LANES - 1))
    pick = pick.astype(f32).astype(bf16)
    out = None
    for piece in reversed(bf16_pieces(block, count)):
        part = lax.dot_general(
            pick, piece.astype(bf16), (((1,), (1,)), ((), ())), preferred_element_type=f32
        )
        out = part if out is None else out + part
    return out


def put_sides(pair, entries):
    half = pair.shape[0] // 2
    lines = jnp.concatenate([unfold(pair[:half]), unfold(pair[half:])], 0)
    rows = lines.shape[1]
    pieces = bf16_pieces(lines, 3)
    stack = jnp.concatenate(pieces + [jnp.zeros((2, rows), f32)], 0)
    sub, lane = iota((8, LANES), 0), iota((8, LANES), 1)
    west = (sub < 6) & (lax.bitwise_and(sub, 1) == 0) & (lane == 0)
    east = (sub < 6) & (lax.bitwise_and(sub, 1) == 1) & (lane == LANES - 1)
    picks = [jnp.where(west, first, jnp.where(east, last, 0.0)) for first, last in entries]
    return lax.dot_general(
        stack, jnp.concatenate(picks, 1), (((0,), (0,)), ((), ())), preferred_element_type=f32
    )


def sum_lanes(block):
    out = None
    for piece in reversed(bf16_pieces(block, 3)):
        part = lax.dot_general(
            jnp.ones((8, LANES), bf16), piece.astype(bf16), (((1,), (1,)), ((), ())),
            preferred_element_type=f32,
        )
        out = part if out is None else out + part
    return out


def green_rows(green_ref, start, load_row):
    acc = jnp.zeros((LANES, LANES), f32)
    for k in range(green_ref.shape[1] // LANES):
        acc = acc + green_ref[
            pl.ds(start, LANES), k * LANES : (k + 1) * LANES
        ] * jnp.broadcast_to(load_row(k), (LANES, LANES))
    return acc


def look_up(table, ids):
    rows = ids.shape[0]
    table = jnp.broadcast_to(table[None], (rows // 8, 8, LANES)).reshape(rows, LANES)
    return jnp.take_along_axis(table, ids, axis=1, mode="promise_in_bounds")


def spread(tables, ids):
    low = lax.bitwise_and(ids, LANES - 1)
    block = lax.shift_right_logical(ids, 7)
    out = None
    for k, table in enumerate(tables):
        value = look_up(table, low)
        out = value if out is None else jnp.where(block == k, value, out)
    return out


def green_spread(green, coarse, load_row, acc, tables, pot, first):
    points = green.shape[0]
    rows = coarse.shape[0]

    def settle(index):
        table = sum_lanes(acc[...])
        tables[index] = table
        for start in range(0, rows, STEP_ROWS):
            at = slice(start, start + STEP_ROWS)
            ids = local_ids(coarse[at, :], points)
            value = look_up(table, lax.bitwise_and(ids, LANES - 1))
            pot[at, :] = jnp.where(lax.shift_right_logical(ids, 7) == index, value, pot[at, :])

    def step(index, carry):
        block = green_rows(green, index * LANES, load_row)
        settle(index - 1)
        acc[...] = block
        return carry

    if first == 0:
        acc[...] = green_rows(green, 0, load_row)
    for index in range(1, points // LANES):
        step(index, 0)
    settle(points // LANES - 1)


def next_rows(ref, start, count):
    if start + count < ref.shape[0]:
        return ref[start + 1 : start + count + 1, :]
    return jnp.concatenate([ref[start + 1 :, :], jnp.zeros((1, LANES), ref.dtype)], 0)


def south_rows(first, block):
    return jnp.concatenate([first, block[:-1]], 0)


def pack_kernel(*refs, points):
    far, (to_east, to_west, to_lat), near, done = refs[:7], refs[7:10], refs[10:17], refs[17]
    copies = [pltpu.make_async_copy(far[k], near[k], done.at[k]) for k in range(7)]
    for copy in copies:
        copy.start()
    lam, east, north, depth, drag, ocean, coarse = near
    rows = lam.shape[0]
    tall = rows // LANES
    lat = lax.axis_index("lat")
    order = (
        (LAM, 0, lam, 3), (FLUX, 1, east, 3), (None, 2, north, 0), (DEPTH, 3, depth, 3),
        (DRAG, 4, drag, 3), (OCEAN, 5, ocean, 1), (POINT, 6, coarse, 2),
    )
    for field, index, ref, pieces in order:
        copies[index].wait()
        if field is None:
            continue
        block = ref[...]
        if field == POINT:
            block = local_ids(block, points)
        sides = take_sides(block.astype(f32), pieces)
        at = slice(field * tall, (field + 1) * tall)
        to_west[at, :] = fold(sides[0:1])
        to_east[at, :] = fold(sides[1:2])

    def border(row):
        return jnp.concatenate(
            [
                lam[row : row + 1, :],
                depth[row : row + 1, :],
                drag[row : row + 1, :],
                ocean[row : row + 1, :].astype(f32),
                local_ids(coarse[row : row + 1, :], points).astype(f32),
                north[row : row + 1, :],
                jnp.zeros((2, LANES), f32),
            ],
            0,
        )

    to_lat[...] = jnp.where(lat == 0, border(rows - 1), border(0))


def inner_kernel(
    lam, east, north, depth, drag, ocean, coarse,
    held, gu, cu, gv, cv, sums, left, right, held_sides, source, *, points,
):
    rows = lam.shape[0]
    inner = iota((STEP_ROWS, LANES), 1) < LANES - 1
    carry = jnp.zeros((1, LANES), f32)
    for start in range(0, rows, STEP_ROWS):
        at = slice(start, start + STEP_ROWS)
        lam_c, depth_c, drag_c = lam[at, :], depth[at, :], drag[at, :]
        ocean_c = ocean[at, :].astype(f32)
        damp = jnp.where(
            inner,
            ocean_c * roll_east(ocean_c) / (1.0 + drag_step * 0.5 * (drag_c + roll_east(drag_c))),
            0.0,
        )
        ratio = damp * (flux_ratio * 0.5) * (depth_c + roll_east(depth_c))
        adj_u = damp * east[at, :] + ratio * (roll_east(lam_c) - lam_c)
        cu[at, :] = ratio
        gu[at, :] = damp * adj_u
        ocean_n = next_rows(ocean, start, STEP_ROWS).astype(f32)
        damp = (
            ocean_c
            * ocean_n
            / (1.0 + drag_step * 0.5 * (drag_c + next_rows(drag, start, STEP_ROWS)))
        )
        ratio = damp * (flux_ratio * 0.5) * (depth_c + next_rows(depth, start, STEP_ROWS))
        adj_v = damp * north[at, :] + ratio * (next_rows(lam, start, STEP_ROWS) - lam_c)
        cv[at, :] = ratio
        gv[at, :] = damp * adj_v
        src = slope_ratio * (roll_west(adj_u) - adj_u + south_rows(carry, adj_v) - adj_v)
        carry = adj_v[STEP_ROWS - 1 :]
        source[at, :] = src
        held[at, :] = lam_c + src
    total = jnp.zeros(sums.shape, f32)
    for start in range(0, rows, SEG_ROWS):
        at = slice(start, start + SEG_ROWS)
        cells = slice(start * LANES, (start + SEG_ROWS) * LANES)
        high, low = one_hots(local_ids(coarse[at, :], points), points)
        left[:, cells] = high
        right[:, cells] = low
        total = total + segment_part(source[at, :], high, low, True)
    sums[...] = total
    sides = take_sides(held[...])
    held_sides[...] = jnp.concatenate([fold(sides[0:1]), fold(sides[1:2])], 0)


def face(low, high, flux):
    damp = low[OCEAN] * high[OCEAN] / (1.0 + drag_step * 0.5 * (low[DRAG] + high[DRAG]))
    ratio = damp * (flux_ratio * 0.5) * (low[DEPTH] + high[DEPTH])
    adj = damp * flux + ratio * (high[LAM] - low[LAM])
    return adj, ratio, damp * adj


def west_rows():
    return iota((8, LANES), 0) < 4


def rim_kernel(
    own_east, own_west, own_lat, from_west, from_east, from_lat, sums, held_sides,
    payload, faces, lat_lines, *, points,
):
    lat = lax.axis_index("lat")
    half = held_sides.shape[0] // 2

    def pair(west, east):
        return [
            jnp.concatenate(
                [west[k * half : (k + 1) * half, :], east[k * half : (k + 1) * half, :]], 0
            )
            for k in range(6)
        ]

    own, far = pair(own_west, own_east), pair(from_west, from_east)
    is_west = west_rows()
    low = [jnp.where(is_west, there, here) for here, there in zip(own, far)]
    high = [jnp.where(is_west, here, there) for here, there in zip(own, far)]
    adj, ratio, gain = face(low, high, low[FLUX])
    mine, other = own_lat[...], from_lat[...]
    lower = jnp.where(lat == 0, mine, other)
    upper = jnp.where(lat == 0, other, mine)
    lower = [lower[k : k + 1] for k in range(6)]
    upper = [upper[k : k + 1] for k in range(6)]
    adj_l, c_l, g_l = face(lower, upper, lower[FLUX])
    lat_lines[...] = jnp.concatenate(
        [
            adj_l, c_l, g_l, other[POINT : POINT + 1], mine[POINT : POINT + 1],
            jnp.zeros((3, LANES), f32),
        ],
        0,
    )
    sign = jnp.where(is_west, slope_ratio, -slope_ratio)
    sign_l = jnp.where(lat == 0, -slope_ratio, slope_ratio)
    flow = sign * adj
    sub, lane = lax.bitwise_and(iota((8, LANES), 0), half - 1), iota((8, LANES), 1)
    corner = ((lat == 0) & (sub == half - 1) & (lane == LANES - 1)) | (
        (lat == 1) & (sub == 0) & (lane == 0)
    )
    at_corner = jnp.where(
        is_west,
        jnp.broadcast_to(adj_l[:, 0:1], (8, LANES)),
        jnp.broadcast_to(adj_l[:, LANES - 1 :], (8, LANES)),
    )
    faces[ADJ] = adj
    faces[RATIO] = ratio
    faces[GAIN] = gain
    faces[BASE] = held_sides[...] + flow + jnp.where(corner, sign_l * at_corner, 0.0)
    faces[MASK] = own[OCEAN]
    faces[OWN_ID] = own[POINT]
    faces[FAR_ID] = far[POINT]
    pad = jnp.zeros((1, LANES), f32)
    values = jnp.concatenate([flow, sign_l * adj_l, pad], 0)
    ids = jnp.concatenate([own[POINT], mine[POINT : POINT + 1], pad], 0).astype(i32)
    total = sum_pieces(sums[...]) + segment_few(values, ids, points)
    counts = as_points(sums[PIECES * HIGH : (PIECES + 1) * HIGH, :], points)
    inverse = 1.0 / counts
    loads = as_points(total, points) * inverse
    part = jnp.concatenate([loads, inverse], 0)
    if part.shape[0] < 8:
        part = jnp.concatenate([part, jnp.zeros((8 - part.shape[0], LANES), f32)], 0)
    for target in range(payload.shape[0]):
        payload[target] = part


def neighbours(n_lon, n_lat):
    lon, lat = lax.axis_index("lon"), lax.axis_index("lat")
    west = lax.rem(lon + n_lon - 1, n_lon) * n_lat + lat
    east = lax.rem(lon + 1, n_lon) * n_lat + lat
    other = lon * n_lat + (1 - lat)
    return west, east, other


def second_kernel(
    first, green, coarse, ocean, held_in, gu, cu, gv, cv, left, right, faces, lat_lines,
    payload, held, adj_u_out, adj_v_out, lam_sides, lam_edge, acc, tables, pot, lam, source,
    *, points, n_lon, n_lat,
):
    rows = coarse.shape[0]
    blocks = points // LANES
    lat = lax.axis_index("lat")
    south_end = jnp.where(lat == 1, 1.0, 0.0)
    north_end = jnp.where(lat == 0, 1.0, 0.0)
    green_spread(
        green, coarse, lambda k: first[k // blocks, k % blocks : k % blocks + 1, :],
        acc, tables, pot, 0,
    )
    put = put_sides(faces[ADJ], [(slope_ratio, -slope_ratio)])
    adj_l = lat_lines[ADJ_L : ADJ_L + 1, :]
    c_l = lat_lines[C_L : C_L + 1, :]
    g_l = lat_lines[G_L : G_L + 1, :]
    row = iota((STEP_ROWS, LANES), 0)
    lam[rows : rows + 8, :] = jnp.zeros((8, LANES), f32)
    for start in range(0, rows, STEP_ROWS):
        at = slice(start, start + STEP_ROWS)
        value = held_in[at, :] + put[at, :] - attract_coef * pot[at, :]
        if start == 0:
            value = value + jnp.where(row == 0, south_end * slope_ratio * adj_l, 0.0)
        if start == rows - STEP_ROWS:
            value = value - jnp.where(row == STEP_ROWS - 1, north_end * slope_ratio * adj_l, 0.0)
        lam[at, :] = ocean[at, :].astype(f32) * value
    carry = jnp.zeros((1, LANES), f32)
    for start in range(0, rows, STEP_ROWS):
        at = slice(start, start + STEP_ROWS)
        lam_c = lam[at, :]
        adj_u = gu[at, :] + cu[at, :] * (roll_east(lam_c) - lam_c)
        adj_v = gv[at, :] + cv[at, :] * (lam[start + 1 : start + STEP_ROWS + 1, :] - lam_c)
        src = slope_ratio * (roll_west(adj_u) - adj_u + south_rows(carry, adj_v) - adj_v)
        carry = adj_v[STEP_ROWS - 1 :]
        adj_u_out[at, :] = adj_u
        adj_v_out[at, :] = adj_v
        source[at, :] = src
        held[at, :] = lam_c + src
    is_west = west_rows()
    sides = faces[MASK] * (
        faces[BASE]
        - attract_coef * spread([tables[k] for k in range(blocks)], faces[OWN_ID].astype(i32))
    )
    lam_sides[...] = sides
    pull = faces[RATIO] * sides
    flow = slope_ratio * jnp.where(is_west, pull, pull - faces[GAIN])
    edge = jnp.where(lat == 0, lam[rows - 1 : rows, :], lam[0:1, :])
    lam_edge[...] = edge
    pull = c_l * edge
    flow_l = slope_ratio * jnp.where(lat == 0, pull - g_l, pull)
    pad = jnp.zeros((1, LANES), f32)
    total = segment_part(
        jnp.concatenate([flow, flow_l, pad], 0),
        *one_hots(
            jnp.concatenate([faces[OWN_ID], lat_lines[OWN_L : OWN_L + 1, :], pad], 0).astype(i32),
            points,
        ),
    )
    def add(index, total):
        at = pl.ds(pl.multiple_of(index * SEG_ROWS, SEG_ROWS), SEG_ROWS)
        cells = pl.ds(pl.multiple_of(index * SEG_ROWS * LANES, SEG_ROWS * LANES), SEG_ROWS * LANES)
        return total + segment_part(source[at, :], left[:, cells], right[:, cells])

    total = lax.fori_loop(0, rows // SEG_ROWS, add, total)
    own = as_points(sum_pieces(total), points)
    far_id = faces[FAR_ID].astype(i32)
    half = far_id.shape[0] // 2

    def away(values, ids):
        return as_points(segment_few(-values, ids, points), points)

    west_part = away(flow[:half], far_id[:half])
    east_part = away(flow[half:], far_id[half:])
    lat_part = away(
        jnp.concatenate([flow_l, pad], 0),
        jnp.concatenate([lat_lines[ID_L : ID_L + 1, :], pad], 0).astype(i32),
    )
    west, east, other = neighbours(n_lon, n_lat)
    part = jnp.concatenate([own, east_part, west_part, lat_part], 0)
    begin = 4 * blocks
    deep = begin + half
    edge_rows = jnp.concatenate([edge, jnp.zeros((half - 1, LANES), f32)], 0)
    for target in range(n_lon * n_lat):
        shared = jnp.where(
            target == west, sides[:half], jnp.where(target == east, sides[half:], edge_rows)
        )
        payload[target * deep : (target + 1) * deep, :] = jnp.concatenate([part, shared], 0)


def edge_kernel(
    first, second, green, ocean, held, faces, lat_lines, lam_sides, lam_edge,
    edge, loads, acc, put, north_line, *, points, n_lon, n_lat,
):
    rows = held.shape[0]
    blocks = points // LANES
    half = rows // LANES
    deep = 4 * blocks + half
    lat = lax.axis_index("lat")

    def received(owner, kind):
        start = owner * deep + kind * blocks
        return second[start : start + blocks, :]

    for lon in range(n_lon):
        for band in range(n_lat):
            here = lon * n_lat + band
            west = (lon - 1) % n_lon * n_lat + band
            east = (lon + 1) % n_lon * n_lat + band
            other = lon * n_lat + 1 - band
            total = received(here, 0) + received(west, 1) + received(east, 2) + received(other, 3)
            loads[here * blocks : (here + 1) * blocks, :] = (
                total * first[here, blocks : 2 * blocks, :]
            )
    acc[...] = green_rows(green, 0, lambda k: loads[k : k + 1, :])
    potential = sum_lanes(acc[...])
    west, east, other = neighbours(n_lon, n_lat)

    def shared(owner, count):
        return second[pl.ds(owner * deep + 4 * blocks, count), :]

    far = jnp.concatenate([shared(west, half), shared(east, half)], 0)
    rise = jnp.where(west_rows(), lam_sides[...] - far, far - lam_sides[...])
    adj = faces[GAIN] + faces[RATIO] * rise
    put[...] = put_sides(adj, [(slope_ratio, -slope_ratio), (0.0, 1.0)])
    rise = shared(other, 1) - lam_edge[...]
    adj_l = lat_lines[G_L : G_L + 1, :] + lat_lines[C_L : C_L + 1, :] * jnp.where(
        lat == 0, rise, -rise
    )
    from_north = jnp.where(lat == 0, adj_l, 0.0)
    from_south = jnp.where(lat == 1, adj_l, 0.0)
    put[0:1, :LANES] = put[0:1, :LANES] + slope_ratio * from_south
    put[rows - 1 : rows, :LANES] = put[rows - 1 : rows, :LANES] - slope_ratio * from_north
    north_line[...] = from_north
    edge[...] = ocean[0:1, :].astype(f32) * (
        held[0:1, :] + put[0:1, :LANES] - attract_coef * potential[0:1, :]
    )


def last_kernel(
    loads, start_acc, put, green, coarse, ocean, held, lam_out, payload, acc, tables, pot,
    *, points, n_lon,
):
    rows = coarse.shape[0]
    acc[...] = start_acc[...]
    green_spread(green, coarse, lambda k: loads[k : k + 1, :], acc, tables, pot, 1)
    for start in range(0, rows, STEP_ROWS):
        at = slice(start, start + STEP_ROWS)
        lam_out[at, :] = ocean[at, :].astype(f32) * (
            held[at, :] + put[at, :LANES] - attract_coef * pot[at, :]
        )
    span = rows // n_lon
    for target in range(n_lon):
        start = target * (span + 1)
        payload[start : start + span, :] = lam_out[target * span : (target + 1) * span, :]
        if target < n_lon - 1:
            stop = (target + 1) * span
            payload[start + span : start + span + 1, :] = lam_out[stop : stop + 1, :]
        else:
            payload[start + span : start + span + 1, :] = jnp.zeros((1, LANES), f32)


def bands_kernel(
    parts, lam, adj_u, adj_v, put, north_line,
    lam_out, east_out, north_out, bands, east, north, planes, done, *, count,
):
    span = parts.shape[0] // count - 1
    rows = lam.shape[0]
    copies = [
        pltpu.make_async_copy(lam, lam_out, done.at[0]),
        pltpu.make_async_copy(east, east_out, done.at[1]),
        pltpu.make_async_copy(north, north_out, done.at[2]),
    ] + [
        pltpu.make_async_copy(planes.at[k], bands.at[k, 0], done.at[3 + k]) for k in range(3)
    ]
    copies[0].start()
    lane = iota((span, LANES), 1)
    for k in range(count):
        start = k * (span + 1)
        planes[0, :, k * LANES : (k + 1) * LANES] = parts[start : start + span, :]
    copies[3].start()
    for k in range(count):
        start = k * (span + 1)
        here = parts[start : start + span, :]
        planes[2, :, k * LANES : (k + 1) * LANES] = parts[start + 1 : start + 1 + span, :] - here
    copies[5].start()
    for k in range(count):
        at = slice(k * LANES, (k + 1) * LANES)
        here = planes[0, :, at]
        after = (k + 1) % count
        there = planes[0, :, after * LANES : (after + 1) * LANES]
        planes[1, :, at] = jnp.where(lane == LANES - 1, roll_east(there), roll_east(here)) - here
    copies[4].start()
    east[...] = adj_u[...] + put[:, LANES:]
    copies[1].start()
    north[...] = adj_v[...]
    north[rows - 1 : rows, :] = adj_v[rows - 1 : rows, :] + north_line[...]
    copies[2].start()
    for copy in copies:
        copy.wait()


def call(kernel, shapes, scratch, args, name, far=False, far_out=False):
    vmem = pl.BlockSpec(memory_space=pltpu.VMEM)
    shapes = [(shape, f32) if isinstance(shape[0], int) else shape for shape in shapes]
    return pl.pallas_call(
        kernel,
        out_shape=[jax.ShapeDtypeStruct(shape, kind) for shape, kind in shapes],
        in_specs=[pl.BlockSpec(memory_space=pltpu.HBM) if far else vmem] * len(args),
        out_specs=[pl.BlockSpec(memory_space=pl.ANY) if far_out else vmem] * len(shapes),
        scratch_shapes=scratch,
        compiler_params=pltpu.CompilerParams(vmem_limit_bytes=(52 << 20) if far else 16 << 20),
        cost_estimate=pl.CostEstimate(flops=4 << 30, bytes_accessed=16 << 20, transcendentals=0),
        name=name,
    )(*args)


def body(n_lon, n_lat, lam_in, flux_east, flux_north, depth, drag, ocean, coarse_of, green):
    rows, cols = lam_in.shape
    points = green.shape[0]
    blocks = points // LANES
    owners = n_lon * n_lat
    grid = (rows, cols)
    fields = (lam_in, flux_east, flux_north, depth, drag, ocean, coarse_of)
    tall = rows // LANES
    to_east, to_west, to_lat, *fields = call(
        functools.partial(pack_kernel, points=points),
        [(6 * tall, cols), (6 * tall, cols), (8, cols)]
        + [(grid, field.dtype) for field in fields],
        [pltpu.SemaphoreType.DMA((7,))], fields, "pack", far=True,
    )
    ocean, coarse_of = fields[5:]
    forward = [(k, (k + 1) % n_lon) for k in range(n_lon)]
    backward = [(target, source) for source, target in forward]
    from_west = lax.ppermute(to_east, "lon", forward)
    from_east = lax.ppermute(to_west, "lon", backward)
    from_lat = lax.ppermute(to_lat, "lat", [(0, 1), (1, 0)])
    held, gu, cu, gv, cv, sums, left, right, held_sides = call(
        functools.partial(inner_kernel, points=points),
        [grid] * 5
        + [((PIECES + 1) * HIGH, LOW), ((HIGH, rows * cols), bf16), ((LOW, rows * cols), bf16)]
        + [(2 * tall, cols)],
        [pltpu.VMEM(grid, f32)], fields, "inner",
    )
    payload, faces, lat_lines = call(
        functools.partial(rim_kernel, points=points),
        [(owners, 8, LANES), (7, 2 * tall, cols), (8, cols)], [],
        (to_east, to_west, to_lat, from_west, from_east, from_lat, sums, held_sides), "rim",
    )
    first = lax.all_to_all(payload, ("lon", "lat"), 0, 0, tiled=True)
    deep = 4 * blocks + tall
    green_scratch = [
        pltpu.VMEM((LANES, LANES), f32),
        pltpu.VMEM((blocks, 8, LANES), f32),
        pltpu.VMEM(grid, f32),
    ]
    payload, held, adj_u, adj_v, lam_sides, lam_edge = call(
        functools.partial(second_kernel, points=points, n_lon=n_lon, n_lat=n_lat),
        [(owners * deep, LANES), grid, grid, grid, (2 * tall, cols), (1, cols)],
        green_scratch + [pltpu.VMEM((rows + 8, cols), f32), pltpu.VMEM(grid, f32)],
        (first, green, coarse_of, ocean, held, gu, cu, gv, cv, left, right, faces, lat_lines),
        "second",
    )
    second = lax.all_to_all(
        payload.reshape(owners, deep, 1, LANES), ("lon", "lat"), 0, 0, tiled=True
    ).reshape(payload.shape)
    span = rows // n_lon
    edge, loads, start_acc, put, north_line = call(
        functools.partial(edge_kernel, points=points, n_lon=n_lon, n_lat=n_lat),
        [(1, cols), (owners * blocks, LANES), (LANES, LANES), (rows, 2 * cols), (1, cols)],
        [],
        (first, second, green, ocean, held, faces, lat_lines, lam_sides, lam_edge), "edge",
    )
    lam, payload = call(
        functools.partial(last_kernel, points=points, n_lon=n_lon),
        [grid, (rows + n_lon, cols)],
        green_scratch,
        (loads, start_acc, put, green, coarse_of, ocean, held), "last",
    )
    edge = lax.ppermute(edge, "lat", [(1, 0)])
    payload = lax.dynamic_update_slice(payload, edge, (rows + n_lon - 1, 0))
    parts = lax.all_to_all(
        payload.reshape(n_lon, span + 1, 1, LANES), "lon", 0, 0, tiled=True
    ).reshape(payload.shape)
    return tuple(
        call(
            functools.partial(bands_kernel, count=n_lon),
            [grid, grid, grid, (3, 1, span, n_lon * cols)],
            [
                pltpu.VMEM(grid, f32),
                pltpu.VMEM(grid, f32),
                pltpu.VMEM((3, span, n_lon * cols), f32),
                pltpu.SemaphoreType.DMA((6,)),
            ],
            (parts, lam, adj_u, adj_v, put, north_line), "bands", far_out=True,
        )
    )


def solution(mesh):
    cells = P(("groups", "lat"), "lon")
    n_lon, n_lat = mesh.shape["lon"], mesh.shape["lat"]
    return jax.shard_map(
        functools.partial(body, n_lon, n_lat),
        mesh=mesh,
        in_specs=(cells,) * 6 + (P("lat", "lon"), P(("lon", "lat"), None)),
        out_specs=(cells,) * 3 + (P(None, ("groups", "lat"), "lon", None),),
        check_vma=False,
    )
```

```python
import functools

import jax
import jax.numpy as jnp
from jax import lax
from jax.experimental import pallas as pl
from jax.experimental.pallas import tpu as pltpu
from jax.sharding import PartitionSpec as P

f32 = jnp.float32
bf16 = jnp.bfloat16
i32 = jnp.int32

LANES = 128
LOW = 32
HIGH = 16
PIECES = 2
SEG_ROWS = 256
STEP_ROWS = 128

flux_ratio = 0.25
slope_ratio = 0.25
drag_step = 1.0
attract_coef = 0.5

LAM, DEPTH, DRAG, OCEAN, POINT, FLUX = range(6)
ADJ, RATIO, GAIN, BASE, MASK, OWN_ID, FAR_ID = range(7)
ADJ_L, C_L, G_L, ID_L, OWN_L = range(5)


def iota(shape, dim):
    return lax.broadcasted_iota(i32, shape, dim)


def roll_east(x):
    return pltpu.roll(x, LANES - 1, 1)


def roll_west(x):
    return pltpu.roll(x, 1, 1)


def local_ids(ids, points):
    return lax.bitwise_and(ids, points - 1)


def bf16_pieces(values, count=PIECES):
    out = []
    for piece in range(count):
        top = values.astype(bf16).astype(f32)
        out.append(top)
        if piece < count - 1:
            values = values - top
    return out


def one_hots(ids, points):
    blocks = points // LANES
    high = lax.shift_right_logical(ids, 5)
    high = lax.bitwise_and(high, 3) * blocks + lax.shift_right_logical(high, 2)
    low = lax.bitwise_and(ids, LOW - 1)
    high_iota = iota((HIGH, LANES), 0)
    low_iota = iota((LOW, LANES), 0)
    left, right = [], []
    for row in range(ids.shape[0]):
        mask = jnp.broadcast_to(high[row : row + 1], (HIGH, LANES)) == high_iota
        left.append(jnp.where(mask, 1.0, 0.0).astype(bf16))
        mask = jnp.broadcast_to(low[row : row + 1], (LOW, LANES)) == low_iota
        right.append(jnp.where(mask, 1.0, 0.0).astype(bf16))
    return jnp.concatenate(left, 1), jnp.concatenate(right, 1)


def segment_part(values, left, right, with_counts=False):
    parts = []
    for piece in bf16_pieces(values):
        line = jnp.concatenate(
            [
                jnp.broadcast_to(piece[row : row + 1], (HIGH, LANES)).astype(bf16)
                for row in range(values.shape[0])
            ],
            1,
        )
        parts.append(left * line)
    if with_counts:
        parts.append(left)
    return lax.dot_general(
        jnp.concatenate(parts, 0), right, (((1,), (1,)), ((), ())), preferred_element_type=f32
    )


def segment_few(values, ids, points):
    return sum_pieces(segment_part(values, *one_hots(ids, points)))


def sum_pieces(parts):
    total = parts[:HIGH]
    for piece in range(1, PIECES):
        total = total + parts[piece * HIGH : (piece + 1) * HIGH]
    return total


def as_points(table, points):
    blocks = points // LANES
    return jnp.concatenate([table[q * blocks : (q + 1) * blocks] for q in range(4)], 1)


def fold(line):
    return jnp.concatenate(
        [line[:, k * LANES : (k + 1) * LANES] for k in range(line.shape[1] // LANES)], 0
    )


def unfold(block):
    return jnp.concatenate([block[k : k + 1] for k in range(block.shape[0])], 1)


def take_sides(block, count=3):
    sub, lane = iota((8, LANES), 0), iota((8, LANES), 1)
    pick = ((sub == 0) & (lane == 0)) | ((sub == 1) & (lane == LANES - 1))
    pick = pick.astype(f32).astype(bf16)
    out = None
    for piece in reversed(bf16_pieces(block, count)):
        part = lax.dot_general(
            pick, piece.astype(bf16), (((1,), (1,)), ((), ())), preferred_element_type=f32
        )
        out = part if out is None else out + part
    return out


def put_sides(pair, entries):
    half = pair.shape[0] // 2
    lines = jnp.concatenate([unfold(pair[:half]), unfold(pair[half:])], 0)
    rows = lines.shape[1]
    pieces = bf16_pieces(lines, 3)
    stack = jnp.concatenate(pieces + [jnp.zeros((2, rows), f32)], 0)
    sub, lane = iota((8, LANES), 0), iota((8, LANES), 1)
    west = (sub < 6) & (lax.bitwise_and(sub, 1) == 0) & (lane == 0)
    east = (sub < 6) & (lax.bitwise_and(sub, 1) == 1) & (lane == LANES - 1)
    picks = [jnp.where(west, first, jnp.where(east, last, 0.0)) for first, last in entries]
    return lax.dot_general(
        stack, jnp.concatenate(picks, 1), (((0,), (0,)), ((), ())), preferred_element_type=f32
    )


def sum_lanes(block):
    out = None
    for piece in reversed(bf16_pieces(block, 3)):
        part = lax.dot_general(
            jnp.ones((8, LANES), bf16), piece.astype(bf16), (((1,), (1,)), ((), ())),
            preferred_element_type=f32,
        )
        out = part if out is None else out + part
    return out


def green_rows(green_ref, start, load_row):
    acc = jnp.zeros((LANES, LANES), f32)
    for k in range(green_ref.shape[1] // LANES):
        acc = acc + green_ref[
            pl.ds(start, LANES), k * LANES : (k + 1) * LANES
        ] * jnp.broadcast_to(load_row(k), (LANES, LANES))
    return acc


def look_up(table, ids):
    rows = ids.shape[0]
    table = jnp.broadcast_to(table[None], (rows // 8, 8, LANES)).reshape(rows, LANES)
    return jnp.take_along_axis(table, ids, axis=1, mode="promise_in_bounds")


def spread(tables, ids):
    low = lax.bitwise_and(ids, LANES - 1)
    block = lax.shift_right_logical(ids, 7)
    out = None
    for k, table in enumerate(tables):
        value = look_up(table, low)
        out = value if out is None else jnp.where(block == k, value, out)
    return out


def green_spread(green, coarse, load_row, acc, tables, pot, first):
    points = green.shape[0]
    rows = coarse.shape[0]

    def settle(index):
        table = sum_lanes(acc[...])
        tables[index] = table
        for start in range(0, rows, STEP_ROWS):
            at = slice(start, start + STEP_ROWS)
            ids = local_ids(coarse[at, :], points)
            value = look_up(table, lax.bitwise_and(ids, LANES - 1))
            pot[at, :] = jnp.where(lax.shift_right_logical(ids, 7) == index, value, pot[at, :])

    def step(index, carry):
        block = green_rows(green, index * LANES, load_row)
        settle(index - 1)
        acc[...] = block
        return carry

    if first == 0:
        acc[...] = green_rows(green, 0, load_row)
    for index in range(1, points // LANES):
        step(index, 0)
    settle(points // LANES - 1)


def next_rows(ref, start, count):
    if start + count < ref.shape[0]:
        return ref[start + 1 : start + count + 1, :]
    return jnp.concatenate([ref[start + 1 :, :], jnp.zeros((1, LANES), ref.dtype)], 0)


def south_rows(first, block):
    return jnp.concatenate([first, block[:-1]], 0)


def pack_kernel(*refs, points):
    far, (to_east, to_west, to_lat), near, done = refs[:7], refs[7:10], refs[10:17], refs[17]
    copies = [pltpu.make_async_copy(far[k], near[k], done.at[k]) for k in range(7)]
    for copy in copies:
        copy.start()
    lam, east, north, depth, drag, ocean, coarse = near
    rows = lam.shape[0]
    tall = rows // LANES
    lat = lax.axis_index("lat")
    order = (
        (LAM, 0, lam, 3), (FLUX, 1, east, 3), (None, 2, north, 0), (DEPTH, 3, depth, 3),
        (DRAG, 4, drag, 3), (OCEAN, 5, ocean, 1), (POINT, 6, coarse, 2),
    )
    for field, index, ref, pieces in order:
        copies[index].wait()
        if field is None:
            continue
        block = ref[...]
        if field == POINT:
            block = local_ids(block, points)
        sides = take_sides(block.astype(f32), pieces)
        at = slice(field * tall, (field + 1) * tall)
        to_west[at, :] = fold(sides[0:1])
        to_east[at, :] = fold(sides[1:2])

    def border(row):
        return jnp.concatenate(
            [
                lam[row : row + 1, :],
                depth[row : row + 1, :],
                drag[row : row + 1, :],
                ocean[row : row + 1, :].astype(f32),
                local_ids(coarse[row : row + 1, :], points).astype(f32),
                north[row : row + 1, :],
                jnp.zeros((2, LANES), f32),
            ],
            0,
        )

    to_lat[...] = jnp.where(lat == 0, border(rows - 1), border(0))


def inner_kernel(
    lam, east, north, depth, drag, ocean, coarse,
    held, gu, cu, gv, cv, sums, left, right, held_sides, source, *, points,
):
    rows = lam.shape[0]
    inner = iota((STEP_ROWS, LANES), 1) < LANES - 1
    carry = jnp.zeros((1, LANES), f32)
    for start in range(0, rows, STEP_ROWS):
        at = slice(start, start + STEP_ROWS)
        lam_c, depth_c, drag_c = lam[at, :], depth[at, :], drag[at, :]
        ocean_c = ocean[at, :].astype(f32)
        damp = jnp.where(
            inner,
            ocean_c * roll_east(ocean_c) / (1.0 + drag_step * 0.5 * (drag_c + roll_east(drag_c))),
            0.0,
        )
        ratio = damp * (flux_ratio * 0.5) * (depth_c + roll_east(depth_c))
        adj_u = damp * east[at, :] + ratio * (roll_east(lam_c) - lam_c)
        cu[at, :] = ratio
        gu[at, :] = damp * adj_u
        ocean_n = next_rows(ocean, start, STEP_ROWS).astype(f32)
        damp = (
            ocean_c
            * ocean_n
            / (1.0 + drag_step * 0.5 * (drag_c + next_rows(drag, start, STEP_ROWS)))
        )
        ratio = damp * (flux_ratio * 0.5) * (depth_c + next_rows(depth, start, STEP_ROWS))
        adj_v = damp * north[at, :] + ratio * (next_rows(lam, start, STEP_ROWS) - lam_c)
        cv[at, :] = ratio
        gv[at, :] = damp * adj_v
        src = slope_ratio * (roll_west(adj_u) - adj_u + south_rows(carry, adj_v) - adj_v)
        carry = adj_v[STEP_ROWS - 1 :]
        source[at, :] = src
        held[at, :] = lam_c + src
    total = jnp.zeros(sums.shape, f32)
    for start in range(0, rows, SEG_ROWS):
        at = slice(start, start + SEG_ROWS)
        cells = slice(start * LANES, (start + SEG_ROWS) * LANES)
        high, low = one_hots(local_ids(coarse[at, :], points), points)
        left[:, cells] = high
        right[:, cells] = low
        total = total + segment_part(source[at, :], high, low, True)
    sums[...] = total
    sides = take_sides(held[...])
    held_sides[...] = jnp.concatenate([fold(sides[0:1]), fold(sides[1:2])], 0)


def face(low, high, flux):
    damp = low[OCEAN] * high[OCEAN] / (1.0 + drag_step * 0.5 * (low[DRAG] + high[DRAG]))
    ratio = damp * (flux_ratio * 0.5) * (low[DEPTH] + high[DEPTH])
    adj = damp * flux + ratio * (high[LAM] - low[LAM])
    return adj, ratio, damp * adj


def west_rows():
    return iota((8, LANES), 0) < 4


def rim_kernel(
    own_east, own_west, own_lat, from_west, from_east, from_lat, sums, held_sides,
    payload, faces, lat_lines, *, points,
):
    lat = lax.axis_index("lat")
    half = held_sides.shape[0] // 2

    def pair(west, east):
        return [
            jnp.concatenate(
                [west[k * half : (k + 1) * half, :], east[k * half : (k + 1) * half, :]], 0
            )
            for k in range(6)
        ]

    own, far = pair(own_west, own_east), pair(from_west, from_east)
    is_west = west_rows()
    low = [jnp.where(is_west, there, here) for here, there in zip(own, far)]
    high = [jnp.where(is_west, here, there) for here, there in zip(own, far)]
    adj, ratio, gain = face(low, high, low[FLUX])
    mine, other = own_lat[...], from_lat[1 - lat]
    lower = jnp.where(lat == 0, mine, other)
    upper = jnp.where(lat == 0, other, mine)
    lower = [lower[k : k + 1] for k in range(6)]
    upper = [upper[k : k + 1] for k in range(6)]
    adj_l, c_l, g_l = face(lower, upper, lower[FLUX])
    lat_lines[...] = jnp.concatenate(
        [
            adj_l, c_l, g_l, other[POINT : POINT + 1], mine[POINT : POINT + 1],
            jnp.zeros((3, LANES), f32),
        ],
        0,
    )
    sign = jnp.where(is_west, slope_ratio, -slope_ratio)
    sign_l = jnp.where(lat == 0, -slope_ratio, slope_ratio)
    flow = sign * adj
    sub, lane = lax.bitwise_and(iota((8, LANES), 0), half - 1), iota((8, LANES), 1)
    corner = ((lat == 0) & (sub == half - 1) & (lane == LANES - 1)) | (
        (lat == 1) & (sub == 0) & (lane == 0)
    )
    at_corner = jnp.where(
        is_west,
        jnp.broadcast_to(adj_l[:, 0:1], (8, LANES)),
        jnp.broadcast_to(adj_l[:, LANES - 1 :], (8, LANES)),
    )
    faces[ADJ] = adj
    faces[RATIO] = ratio
    faces[GAIN] = gain
    faces[BASE] = held_sides[...] + flow + jnp.where(corner, sign_l * at_corner, 0.0)
    faces[MASK] = own[OCEAN]
    faces[OWN_ID] = own[POINT]
    faces[FAR_ID] = far[POINT]
    pad = jnp.zeros((1, LANES), f32)
    values = jnp.concatenate([flow, sign_l * adj_l, pad], 0)
    ids = jnp.concatenate([own[POINT], mine[POINT : POINT + 1], pad], 0).astype(i32)
    total = sum_pieces(sums[...]) + segment_few(values, ids, points)
    counts = as_points(sums[PIECES * HIGH : (PIECES + 1) * HIGH, :], points)
    inverse = 1.0 / counts
    loads = as_points(total, points) * inverse
    part = jnp.concatenate([loads, inverse], 0)
    if part.shape[0] < 8:
        part = jnp.concatenate([part, jnp.zeros((8 - part.shape[0], LANES), f32)], 0)
    for target in range(payload.shape[0]):
        payload[target] = part


def neighbours(n_lon, n_lat):
    lon, lat = lax.axis_index("lon"), lax.axis_index("lat")
    west = lax.rem(lon + n_lon - 1, n_lon) * n_lat + lat
    east = lax.rem(lon + 1, n_lon) * n_lat + lat
    other = lon * n_lat + (1 - lat)
    return west, east, other


def second_kernel(
    first, green, coarse, ocean, held_in, gu, cu, gv, cv, left, right, faces, lat_lines,
    payload, held, adj_u_out, adj_v_out, lam_sides, lam_edge, acc, tables, pot, lam, source,
    *, points, n_lon, n_lat,
):
    rows = coarse.shape[0]
    blocks = points // LANES
    lat = lax.axis_index("lat")
    south_end = jnp.where(lat == 1, 1.0, 0.0)
    north_end = jnp.where(lat == 0, 1.0, 0.0)
    green_spread(
        green, coarse, lambda k: first[k // blocks, k % blocks : k % blocks + 1, :],
        acc, tables, pot, 0,
    )
    put = put_sides(faces[ADJ], [(slope_ratio, -slope_ratio)])
    adj_l = lat_lines[ADJ_L : ADJ_L + 1, :]
    c_l = lat_lines[C_L : C_L + 1, :]
    g_l = lat_lines[G_L : G_L + 1, :]
    row = iota((STEP_ROWS, LANES), 0)
    lam[rows : rows + 8, :] = jnp.zeros((8, LANES), f32)
    for start in range(0, rows, STEP_ROWS):
        at = slice(start, start + STEP_ROWS)
        value = held_in[at, :] + put[at, :] - attract_coef * pot[at, :]
        if start == 0:
            value = value + jnp.where(row == 0, south_end * slope_ratio * adj_l, 0.0)
        if start == rows - STEP_ROWS:
            value = value - jnp.where(row == STEP_ROWS - 1, north_end * slope_ratio * adj_l, 0.0)
        lam[at, :] = ocean[at, :].astype(f32) * value
    carry = jnp.zeros((1, LANES), f32)
    for start in range(0, rows, STEP_ROWS):
        at = slice(start, start + STEP_ROWS)
        lam_c = lam[at, :]
        adj_u = gu[at, :] + cu[at, :] * (roll_east(lam_c) - lam_c)
        adj_v = gv[at, :] + cv[at, :] * (lam[start + 1 : start + STEP_ROWS + 1, :] - lam_c)
        src = slope_ratio * (roll_west(adj_u) - adj_u + south_rows(carry, adj_v) - adj_v)
        carry = adj_v[STEP_ROWS - 1 :]
        adj_u_out[at, :] = adj_u
        adj_v_out[at, :] = adj_v
        source[at, :] = src
        held[at, :] = lam_c + src
    is_west = west_rows()
    sides = faces[MASK] * (
        faces[BASE]
        - attract_coef * spread([tables[k] for k in range(blocks)], faces[OWN_ID].astype(i32))
    )
    lam_sides[...] = sides
    pull = faces[RATIO] * sides
    flow = slope_ratio * jnp.where(is_west, pull, pull - faces[GAIN])
    edge = jnp.where(lat == 0, lam[rows - 1 : rows, :], lam[0:1, :])
    lam_edge[...] = edge
    pull = c_l * edge
    flow_l = slope_ratio * jnp.where(lat == 0, pull - g_l, pull)
    pad = jnp.zeros((1, LANES), f32)
    total = segment_part(
        jnp.concatenate([flow, flow_l, pad], 0),
        *one_hots(
            jnp.concatenate([faces[OWN_ID], lat_lines[OWN_L : OWN_L + 1, :], pad], 0).astype(i32),
            points,
        ),
    )
    def add(index, total):
        at = pl.ds(pl.multiple_of(index * SEG_ROWS, SEG_ROWS), SEG_ROWS)
        cells = pl.ds(pl.multiple_of(index * SEG_ROWS * LANES, SEG_ROWS * LANES), SEG_ROWS * LANES)
        return total + segment_part(source[at, :], left[:, cells], right[:, cells])

    total = lax.fori_loop(0, rows // SEG_ROWS, add, total)
    own = as_points(sum_pieces(total), points)
    far_id = faces[FAR_ID].astype(i32)
    half = far_id.shape[0] // 2

    def away(values, ids):
        return as_points(segment_few(-values, ids, points), points)

    west_part = away(flow[:half], far_id[:half])
    east_part = away(flow[half:], far_id[half:])
    lat_part = away(
        jnp.concatenate([flow_l, pad], 0),
        jnp.concatenate([lat_lines[ID_L : ID_L + 1, :], pad], 0).astype(i32),
    )
    west, east, other = neighbours(n_lon, n_lat)
    part = jnp.concatenate([own, east_part, west_part, lat_part], 0)
    begin = 4 * blocks
    deep = begin + half
    edge_rows = jnp.concatenate([edge, jnp.zeros((half - 1, LANES), f32)], 0)
    for target in range(n_lon * n_lat):
        shared = jnp.where(
            target == west, sides[:half], jnp.where(target == east, sides[half:], edge_rows)
        )
        payload[target * deep : (target + 1) * deep, :] = jnp.concatenate([part, shared], 0)


def edge_kernel(
    first, second, green, ocean, held, faces, lat_lines, lam_sides, lam_edge,
    edge, loads, acc, put, north_line, *, points, n_lon, n_lat,
):
    rows = held.shape[0]
    blocks = points // LANES
    half = rows // LANES
    deep = 4 * blocks + half
    lat = lax.axis_index("lat")

    def received(owner, kind):
        start = owner * deep + kind * blocks
        return second[start : start + blocks, :]

    for lon in range(n_lon):
        for band in range(n_lat):
            here = lon * n_lat + band
            west = (lon - 1) % n_lon * n_lat + band
            east = (lon + 1) % n_lon * n_lat + band
            other = lon * n_lat + 1 - band
            total = received(here, 0) + received(west, 1) + received(east, 2) + received(other, 3)
            loads[here * blocks : (here + 1) * blocks, :] = (
                total * first[here, blocks : 2 * blocks, :]
            )
    acc[...] = green_rows(green, 0, lambda k: loads[k : k + 1, :])
    potential = sum_lanes(acc[...])
    west, east, other = neighbours(n_lon, n_lat)

    def shared(owner, count):
        return second[pl.ds(owner * deep + 4 * blocks, count), :]

    far = jnp.concatenate([shared(west, half), shared(east, half)], 0)
    rise = jnp.where(west_rows(), lam_sides[...] - far, far - lam_sides[...])
    adj = faces[GAIN] + faces[RATIO] * rise
    put[...] = put_sides(adj, [(slope_ratio, -slope_ratio), (0.0, 1.0)])
    rise = shared(other, 1) - lam_edge[...]
    adj_l = lat_lines[G_L : G_L + 1, :] + lat_lines[C_L : C_L + 1, :] * jnp.where(
        lat == 0, rise, -rise
    )
    from_north = jnp.where(lat == 0, adj_l, 0.0)
    from_south = jnp.where(lat == 1, adj_l, 0.0)
    put[0:1, :LANES] = put[0:1, :LANES] + slope_ratio * from_south
    put[rows - 1 : rows, :LANES] = put[rows - 1 : rows, :LANES] - slope_ratio * from_north
    north_line[...] = from_north
    edge[...] = ocean[0:1, :].astype(f32) * (
        held[0:1, :] + put[0:1, :LANES] - attract_coef * potential[0:1, :]
    )


def last_kernel(
    loads, start_acc, put, green, coarse, ocean, held, lam_out, payload, acc, tables, pot,
    *, points, n_lon,
):
    rows = coarse.shape[0]
    acc[...] = start_acc[...]
    green_spread(green, coarse, lambda k: loads[k : k + 1, :], acc, tables, pot, 1)
    for start in range(0, rows, STEP_ROWS):
        at = slice(start, start + STEP_ROWS)
        lam_out[at, :] = ocean[at, :].astype(f32) * (
            held[at, :] + put[at, :LANES] - attract_coef * pot[at, :]
        )
    span = rows // n_lon
    for target in range(n_lon):
        start = target * (span + 1)
        payload[start : start + span, :] = lam_out[target * span : (target + 1) * span, :]
        if target < n_lon - 1:
            stop = (target + 1) * span
            payload[start + span : start + span + 1, :] = lam_out[stop : stop + 1, :]
        else:
            payload[start + span : start + span + 1, :] = jnp.zeros((1, LANES), f32)


def bands_kernel(
    parts, lam, adj_u, adj_v, put, north_line,
    lam_out, east_out, north_out, bands, east, north, planes, done, *, count,
):
    span = parts.shape[0] // count - 1
    rows = lam.shape[0]
    copies = [
        pltpu.make_async_copy(lam, lam_out, done.at[0]),
        pltpu.make_async_copy(east, east_out, done.at[1]),
        pltpu.make_async_copy(north, north_out, done.at[2]),
    ] + [
        pltpu.make_async_copy(planes.at[k], bands.at[k, 0], done.at[3 + k]) for k in range(3)
    ]
    copies[0].start()
    lane = iota((span, LANES), 1)
    top = (lax.axis_index("lat") == 1) & (lax.axis_index("lon") == count - 1)
    last = (iota((span, LANES), 0) == span - 1) & top
    for k in range(count):
        start = k * (span + 1)
        planes[0, :, k * LANES : (k + 1) * LANES] = parts[start : start + span, :]
    copies[3].start()
    for k in range(count):
        start = k * (span + 1)
        here = parts[start : start + span, :]
        north_of = jnp.where(last, 0.0, parts[start + 1 : start + 1 + span, :])
        planes[2, :, k * LANES : (k + 1) * LANES] = north_of - here
    copies[5].start()
    for k in range(count):
        at = slice(k * LANES, (k + 1) * LANES)
        here = planes[0, :, at]
        after = (k + 1) % count
        there = planes[0, :, after * LANES : (after + 1) * LANES]
        planes[1, :, at] = jnp.where(lane == LANES - 1, roll_east(there), roll_east(here)) - here
    copies[4].start()
    east[...] = adj_u[...] + put[:, LANES:]
    copies[1].start()
    north[...] = adj_v[...]
    north[rows - 1 : rows, :] = adj_v[rows - 1 : rows, :] + north_line[...]
    copies[2].start()
    for copy in copies:
        copy.wait()


def call(kernel, shapes, scratch, args, name, far=False, far_out=False):
    vmem = pl.BlockSpec(memory_space=pltpu.VMEM)
    shapes = [(shape, f32) if isinstance(shape[0], int) else shape for shape in shapes]
    return pl.pallas_call(
        kernel,
        out_shape=[jax.ShapeDtypeStruct(shape, kind) for shape, kind in shapes],
        in_specs=[pl.BlockSpec(memory_space=pltpu.HBM) if far else vmem] * len(args),
        out_specs=[pl.BlockSpec(memory_space=pl.ANY) if far_out else vmem] * len(shapes),
        scratch_shapes=scratch,
        compiler_params=pltpu.CompilerParams(vmem_limit_bytes=(52 << 20) if far else 16 << 20),
        cost_estimate=pl.CostEstimate(flops=4 << 30, bytes_accessed=16 << 20, transcendentals=0),
        name=name,
    )(*args)


def body(n_lon, n_lat, lam_in, flux_east, flux_north, depth, drag, ocean, coarse_of, green):
    rows, cols = lam_in.shape
    points = green.shape[0]
    blocks = points // LANES
    owners = n_lon * n_lat
    grid = (rows, cols)
    fields = (lam_in, flux_east, flux_north, depth, drag, ocean, coarse_of)
    tall = rows // LANES
    to_east, to_west, to_lat, *fields = call(
        functools.partial(pack_kernel, points=points),
        [(6 * tall, cols), (6 * tall, cols), (8, cols)]
        + [(grid, field.dtype) for field in fields],
        [pltpu.SemaphoreType.DMA((7,))], fields, "pack", far=True,
    )
    ocean, coarse_of = fields[5:]
    forward = [(k, (k + 1) % n_lon) for k in range(n_lon)]
    backward = [(target, source) for source, target in forward]
    from_west = lax.ppermute(to_east, "lon", forward)
    from_east = lax.ppermute(to_west, "lon", backward)
    from_lat = lax.all_gather(to_lat, "lat", axis=0)
    held, gu, cu, gv, cv, sums, left, right, held_sides = call(
        functools.partial(inner_kernel, points=points),
        [grid] * 5
        + [((PIECES + 1) * HIGH, LOW), ((HIGH, rows * cols), bf16), ((LOW, rows * cols), bf16)]
        + [(2 * tall, cols)],
        [pltpu.VMEM(grid, f32)], fields, "inner",
    )
    payload, faces, lat_lines = call(
        functools.partial(rim_kernel, points=points),
        [(owners, 8, LANES), (7, 2 * tall, cols), (8, cols)], [],
        (to_east, to_west, to_lat, from_west, from_east, from_lat, sums, held_sides), "rim",
    )
    first = lax.all_to_all(payload, ("lon", "lat"), 0, 0, tiled=True)
    deep = 4 * blocks + tall
    green_scratch = [
        pltpu.VMEM((LANES, LANES), f32),
        pltpu.VMEM((blocks, 8, LANES), f32),
        pltpu.VMEM(grid, f32),
    ]
    payload, held, adj_u, adj_v, lam_sides, lam_edge = call(
        functools.partial(second_kernel, points=points, n_lon=n_lon, n_lat=n_lat),
        [(owners * deep, LANES), grid, grid, grid, (2 * tall, cols), (1, cols)],
        green_scratch + [pltpu.VMEM((rows + 8, cols), f32), pltpu.VMEM(grid, f32)],
        (first, green, coarse_of, ocean, held, gu, cu, gv, cv, left, right, faces, lat_lines),
        "second",
    )
    second = lax.all_to_all(
        payload.reshape(owners, deep, 1, LANES), ("lon", "lat"), 0, 0, tiled=True
    ).reshape(payload.shape)
    span = rows // n_lon
    edge, loads, start_acc, put, north_line = call(
        functools.partial(edge_kernel, points=points, n_lon=n_lon, n_lat=n_lat),
        [(1, cols), (owners * blocks, LANES), (LANES, LANES), (rows, 2 * cols), (1, cols)],
        [],
        (first, second, green, ocean, held, faces, lat_lines, lam_sides, lam_edge), "edge",
    )
    lam, payload = call(
        functools.partial(last_kernel, points=points, n_lon=n_lon),
        [grid, (rows + n_lon, cols)],
        green_scratch,
        (loads, start_acc, put, green, coarse_of, ocean, held), "last",
    )
    edge = lax.all_gather(edge, "lat", axis=0)[1]
    payload = lax.dynamic_update_slice(payload, edge, (rows + n_lon - 1, 0))
    parts = lax.all_to_all(
        payload.reshape(n_lon, span + 1, 1, LANES), "lon", 0, 0, tiled=True
    ).reshape(payload.shape)
    return tuple(
        call(
            functools.partial(bands_kernel, count=n_lon),
            [grid, grid, grid, (3, 1, span, n_lon * cols)],
            [
                pltpu.VMEM(grid, f32),
                pltpu.VMEM(grid, f32),
                pltpu.VMEM((3, span, n_lon * cols), f32),
                pltpu.SemaphoreType.DMA((6,)),
            ],
            (parts, lam, adj_u, adj_v, put, north_line), "bands", far_out=True,
        )
    )


def solution(mesh):
    cells = P(("groups", "lat"), "lon")
    n_lon, n_lat = mesh.shape["lon"], mesh.shape["lat"]
    return jax.shard_map(
        functools.partial(body, n_lon, n_lat),
        mesh=mesh,
        in_specs=(cells,) * 6 + (P("lat", "lon"), P(("lon", "lat"), None)),
        out_specs=(cells,) * 3 + (P(None, ("groups", "lat"), "lon", None),),
        check_vma=False,
    )
```

```python
import functools

import jax
import jax.numpy as jnp
from jax import lax
from jax.experimental import pallas as pl
from jax.experimental.pallas import tpu as pltpu
from jax.sharding import PartitionSpec as P

f32 = jnp.float32
bf16 = jnp.bfloat16
i32 = jnp.int32

LANES = 128
LOW = 32
HIGH = 16
PIECES = 2
SEG_ROWS = 256
STEP_ROWS = 128

flux_ratio = 0.25
slope_ratio = 0.25
drag_step = 1.0
attract_coef = 0.5

LAM, DEPTH, DRAG, OCEAN, POINT, FLUX = range(6)
ADJ, RATIO, GAIN, BASE, MASK, OWN_ID, FAR_ID = range(7)
ADJ_L, C_L, G_L, ID_L, OWN_L = range(5)


def iota(shape, dim):
    return lax.broadcasted_iota(i32, shape, dim)


def roll_east(x):
    return pltpu.roll(x, LANES - 1, 1)


def roll_west(x):
    return pltpu.roll(x, 1, 1)


def local_ids(ids, points):
    return lax.bitwise_and(ids, points - 1)


def bf16_pieces(values, count=PIECES):
    out = []
    for piece in range(count):
        top = values.astype(bf16).astype(f32)
        out.append(top)
        if piece < count - 1:
            values = values - top
    return out


def one_hots(ids, points):
    blocks = points // LANES
    high = lax.shift_right_logical(ids, 5)
    high = lax.bitwise_and(high, 3) * blocks + lax.shift_right_logical(high, 2)
    low = lax.bitwise_and(ids, LOW - 1)
    high_iota = iota((HIGH, LANES), 0)
    low_iota = iota((LOW, LANES), 0)
    left, right = [], []
    for row in range(ids.shape[0]):
        mask = jnp.broadcast_to(high[row : row + 1], (HIGH, LANES)) == high_iota
        left.append(jnp.where(mask, 1.0, 0.0).astype(bf16))
        mask = jnp.broadcast_to(low[row : row + 1], (LOW, LANES)) == low_iota
        right.append(jnp.where(mask, 1.0, 0.0).astype(bf16))
    return jnp.concatenate(left, 1), jnp.concatenate(right, 1)


def segment_part(values, left, right, with_counts=False):
    parts = []
    for piece in bf16_pieces(values):
        line = jnp.concatenate(
            [
                jnp.broadcast_to(piece[row : row + 1], (HIGH, LANES)).astype(bf16)
                for row in range(values.shape[0])
            ],
            1,
        )
        parts.append(left * line)
    if with_counts:
        parts.append(left)
    return lax.dot_general(
        jnp.concatenate(parts, 0), right, (((1,), (1,)), ((), ())), preferred_element_type=f32
    )


def segment_few(values, ids, points):
    return sum_pieces(segment_part(values, *one_hots(ids, points)))


def sum_pieces(parts):
    total = parts[:HIGH]
    for piece in range(1, PIECES):
        total = total + parts[piece * HIGH : (piece + 1) * HIGH]
    return total


def as_points(table, points):
    blocks = points // LANES
    return jnp.concatenate([table[q * blocks : (q + 1) * blocks] for q in range(4)], 1)


def fold(line):
    return jnp.concatenate(
        [line[:, k * LANES : (k + 1) * LANES] for k in range(line.shape[1] // LANES)], 0
    )


def unfold(block):
    return jnp.concatenate([block[k : k + 1] for k in range(block.shape[0])], 1)


def take_sides(block, count=3):
    sub, lane = iota((8, LANES), 0), iota((8, LANES), 1)
    pick = ((sub == 0) & (lane == 0)) | ((sub == 1) & (lane == LANES - 1))
    pick = pick.astype(f32).astype(bf16)
    out = None
    for piece in reversed(bf16_pieces(block, count)):
        part = lax.dot_general(
            pick, piece.astype(bf16), (((1,), (1,)), ((), ())), preferred_element_type=f32
        )
        out = part if out is None else out + part
    return out


def put_sides(pair, entries):
    half = pair.shape[0] // 2
    lines = jnp.concatenate([unfold(pair[:half]), unfold(pair[half:])], 0)
    rows = lines.shape[1]
    pieces = bf16_pieces(lines, 3)
    stack = jnp.concatenate(pieces + [jnp.zeros((2, rows), f32)], 0)
    sub, lane = iota((8, LANES), 0), iota((8, LANES), 1)
    west = (sub < 6) & (lax.bitwise_and(sub, 1) == 0) & (lane == 0)
    east = (sub < 6) & (lax.bitwise_and(sub, 1) == 1) & (lane == LANES - 1)
    picks = [jnp.where(west, first, jnp.where(east, last, 0.0)) for first, last in entries]
    return lax.dot_general(
        stack, jnp.concatenate(picks, 1), (((0,), (0,)), ((), ())), preferred_element_type=f32
    )


def sum_lanes(block):
    out = None
    for piece in reversed(bf16_pieces(block, 3)):
        part = lax.dot_general(
            jnp.ones((8, LANES), bf16), piece.astype(bf16), (((1,), (1,)), ((), ())),
            preferred_element_type=f32,
        )
        out = part if out is None else out + part
    return out


def green_rows(green_ref, start, load_row):
    acc = jnp.zeros((LANES, LANES), f32)
    for k in range(green_ref.shape[1] // LANES):
        acc = acc + green_ref[
            pl.ds(start, LANES), k * LANES : (k + 1) * LANES
        ] * jnp.broadcast_to(load_row(k), (LANES, LANES))
    return acc


def look_up(table, ids):
    rows = ids.shape[0]
    table = jnp.broadcast_to(table[None], (rows // 8, 8, LANES)).reshape(rows, LANES)
    return jnp.take_along_axis(table, ids, axis=1, mode="promise_in_bounds")


def spread(tables, ids):
    low = lax.bitwise_and(ids, LANES - 1)
    block = lax.shift_right_logical(ids, 7)
    out = None
    for k, table in enumerate(tables):
        value = look_up(table, low)
        out = value if out is None else jnp.where(block == k, value, out)
    return out


def green_spread(green, coarse, load_row, acc, tables, pot, first):
    points = green.shape[0]
    rows = coarse.shape[0]

    def settle(index):
        table = sum_lanes(acc[...])
        tables[index] = table
        for start in range(0, rows, STEP_ROWS):
            at = slice(start, start + STEP_ROWS)
            ids = local_ids(coarse[at, :], points)
            value = look_up(table, lax.bitwise_and(ids, LANES - 1))
            pot[at, :] = jnp.where(lax.shift_right_logical(ids, 7) == index, value, pot[at, :])

    def step(index, carry):
        block = green_rows(green, index * LANES, load_row)
        settle(index - 1)
        acc[...] = block
        return carry

    if first == 0:
        acc[...] = green_rows(green, 0, load_row)
    for index in range(1, points // LANES):
        step(index, 0)
    settle(points // LANES - 1)


def next_rows(ref, start, count):
    if start + count < ref.shape[0]:
        return ref[start + 1 : start + count + 1, :]
    return jnp.concatenate([ref[start + 1 :, :], jnp.zeros((1, LANES), ref.dtype)], 0)


def south_rows(first, block):
    return jnp.concatenate([first, block[:-1]], 0)


def pack_kernel(*refs, points):
    far, (to_east, to_west, to_lat), near, done = refs[:7], refs[7:10], refs[10:17], refs[17]
    copies = [pltpu.make_async_copy(far[k], near[k], done.at[k]) for k in range(7)]
    for copy in copies:
        copy.start()
    lam, east, north, depth, drag, ocean, coarse = near
    rows = lam.shape[0]
    tall = rows // LANES
    lat = lax.axis_index("lat")
    order = (
        (LAM, 0, lam, 3), (FLUX, 1, east, 3), (None, 2, north, 0), (DEPTH, 3, depth, 3),
        (DRAG, 4, drag, 3), (OCEAN, 5, ocean, 1), (POINT, 6, coarse, 2),
    )
    for field, index, ref, pieces in order:
        copies[index].wait()
        if field is None:
            continue
        block = ref[...]
        if field == POINT:
            block = local_ids(block, points)
        sides = take_sides(block.astype(f32), pieces)
        at = slice(field * tall, (field + 1) * tall)
        to_west[at, :] = fold(sides[0:1])
        to_east[at, :] = fold(sides[1:2])

    def border(row):
        return jnp.concatenate(
            [
                lam[row : row + 1, :],
                depth[row : row + 1, :],
                drag[row : row + 1, :],
                ocean[row : row + 1, :].astype(f32),
                local_ids(coarse[row : row + 1, :], points).astype(f32),
                north[row : row + 1, :],
                jnp.zeros((2, LANES), f32),
            ],
            0,
        )

    to_lat[...] = jnp.where(lat == 0, border(rows - 1), border(0))


def inner_kernel(
    lam, east, north, depth, drag, ocean, coarse,
    held, gu, cu, gv, cv, sums, left, right, held_sides, source, *, points,
):
    rows = lam.shape[0]
    inner = iota((STEP_ROWS, LANES), 1) < LANES - 1
    carry = jnp.zeros((1, LANES), f32)
    for start in range(0, rows, STEP_ROWS):
        at = slice(start, start + STEP_ROWS)
        lam_c, depth_c, drag_c = lam[at, :], depth[at, :], drag[at, :]
        ocean_c = ocean[at, :].astype(f32)
        damp = jnp.where(
            inner,
            ocean_c * roll_east(ocean_c) / (1.0 + drag_step * 0.5 * (drag_c + roll_east(drag_c))),
            0.0,
        )
        ratio = damp * (flux_ratio * 0.5) * (depth_c + roll_east(depth_c))
        adj_u = damp * east[at, :] + ratio * (roll_east(lam_c) - lam_c)
        cu[at, :] = ratio
        gu[at, :] = damp * adj_u
        ocean_n = next_rows(ocean, start, STEP_ROWS).astype(f32)
        damp = (
            ocean_c
            * ocean_n
            / (1.0 + drag_step * 0.5 * (drag_c + next_rows(drag, start, STEP_ROWS)))
        )
        ratio = damp * (flux_ratio * 0.5) * (depth_c + next_rows(depth, start, STEP_ROWS))
        adj_v = damp * north[at, :] + ratio * (next_rows(lam, start, STEP_ROWS) - lam_c)
        cv[at, :] = ratio
        gv[at, :] = damp * adj_v
        src = slope_ratio * (roll_west(adj_u) - adj_u + south_rows(carry, adj_v) - adj_v)
        carry = adj_v[STEP_ROWS - 1 :]
        source[at, :] = src
        held[at, :] = lam_c + src
    total = jnp.zeros(sums.shape, f32)
    for start in range(0, rows, SEG_ROWS):
        at = slice(start, start + SEG_ROWS)
        cells = slice(start * LANES, (start + SEG_ROWS) * LANES)
        high, low = one_hots(local_ids(coarse[at, :], points), points)
        left[:, cells] = high
        right[:, cells] = low
        total = total + segment_part(source[at, :], high, low, True)
    sums[...] = total
    sides = take_sides(held[...])
    held_sides[...] = jnp.concatenate([fold(sides[0:1]), fold(sides[1:2])], 0)


def face(low, high, flux):
    damp = low[OCEAN] * high[OCEAN] / (1.0 + drag_step * 0.5 * (low[DRAG] + high[DRAG]))
    ratio = damp * (flux_ratio * 0.5) * (low[DEPTH] + high[DEPTH])
    adj = damp * flux + ratio * (high[LAM] - low[LAM])
    return adj, ratio, damp * adj


def west_rows():
    return iota((8, LANES), 0) < 4


def rim_kernel(
    own_east, own_west, own_lat, from_west, from_east, from_lat, sums, held_sides,
    payload, faces, lat_lines, *, points,
):
    lat = lax.axis_index("lat")
    half = held_sides.shape[0] // 2

    def pair(west, east):
        return [
            jnp.concatenate(
                [west[k * half : (k + 1) * half, :], east[k * half : (k + 1) * half, :]], 0
            )
            for k in range(6)
        ]

    own, far = pair(own_west, own_east), pair(from_west, from_east)
    is_west = west_rows()
    low = [jnp.where(is_west, there, here) for here, there in zip(own, far)]
    high = [jnp.where(is_west, here, there) for here, there in zip(own, far)]
    adj, ratio, gain = face(low, high, low[FLUX])
    mine, other = own_lat[...], from_lat[...]
    lower = jnp.where(lat == 0, mine, other)
    upper = jnp.where(lat == 0, other, mine)
    lower = [lower[k : k + 1] for k in range(6)]
    upper = [upper[k : k + 1] for k in range(6)]
    adj_l, c_l, g_l = face(lower, upper, lower[FLUX])
    lat_lines[...] = jnp.concatenate(
        [
            adj_l, c_l, g_l, other[POINT : POINT + 1], mine[POINT : POINT + 1],
            jnp.zeros((3, LANES), f32),
        ],
        0,
    )
    sign = jnp.where(is_west, slope_ratio, -slope_ratio)
    sign_l = jnp.where(lat == 0, -slope_ratio, slope_ratio)
    flow = sign * adj
    sub, lane = lax.bitwise_and(iota((8, LANES), 0), half - 1), iota((8, LANES), 1)
    corner = ((lat == 0) & (sub == half - 1) & (lane == LANES - 1)) | (
        (lat == 1) & (sub == 0) & (lane == 0)
    )
    at_corner = jnp.where(
        is_west,
        jnp.broadcast_to(adj_l[:, 0:1], (8, LANES)),
        jnp.broadcast_to(adj_l[:, LANES - 1 :], (8, LANES)),
    )
    faces[ADJ] = adj
    faces[RATIO] = ratio
    faces[GAIN] = gain
    faces[BASE] = held_sides[...] + flow + jnp.where(corner, sign_l * at_corner, 0.0)
    faces[MASK] = own[OCEAN]
    faces[OWN_ID] = own[POINT]
    faces[FAR_ID] = far[POINT]
    pad = jnp.zeros((1, LANES), f32)
    values = jnp.concatenate([flow, sign_l * adj_l, pad], 0)
    ids = jnp.concatenate([own[POINT], mine[POINT : POINT + 1], pad], 0).astype(i32)
    total = sum_pieces(sums[...]) + segment_few(values, ids, points)
    counts = as_points(sums[PIECES * HIGH : (PIECES + 1) * HIGH, :], points)
    inverse = 1.0 / counts
    loads = as_points(total, points) * inverse
    part = jnp.concatenate([loads, inverse], 0)
    if part.shape[0] < 8:
        part = jnp.concatenate([part, jnp.zeros((8 - part.shape[0], LANES), f32)], 0)
    for target in range(payload.shape[0]):
        payload[target] = part


def neighbours(n_lon, n_lat):
    lon, lat = lax.axis_index("lon"), lax.axis_index("lat")
    west = lax.rem(lon + n_lon - 1, n_lon) * n_lat + lat
    east = lax.rem(lon + 1, n_lon) * n_lat + lat
    other = lon * n_lat + (1 - lat)
    return west, east, other


def second_kernel(
    first, green, coarse, ocean, held_in, gu, cu, gv, cv, left, right, faces, lat_lines,
    payload, held, adj_u_out, adj_v_out, lam_sides, lam_edge, acc, tables, pot, lam, source,
    *, points, n_lon, n_lat,
):
    rows = coarse.shape[0]
    blocks = points // LANES
    lat = lax.axis_index("lat")
    south_end = jnp.where(lat == 1, 1.0, 0.0)
    north_end = jnp.where(lat == 0, 1.0, 0.0)
    green_spread(
        green, coarse, lambda k: first[k // blocks, k % blocks : k % blocks + 1, :],
        acc, tables, pot, 0,
    )
    put = put_sides(faces[ADJ], [(slope_ratio, -slope_ratio)])
    adj_l = lat_lines[ADJ_L : ADJ_L + 1, :]
    c_l = lat_lines[C_L : C_L + 1, :]
    g_l = lat_lines[G_L : G_L + 1, :]
    row = iota((STEP_ROWS, LANES), 0)
    lam[rows : rows + 8, :] = jnp.zeros((8, LANES), f32)
    for start in range(0, rows, STEP_ROWS):
        at = slice(start, start + STEP_ROWS)
        value = held_in[at, :] + put[at, :] - attract_coef * pot[at, :]
        if start == 0:
            value = value + jnp.where(row == 0, south_end * slope_ratio * adj_l, 0.0)
        if start == rows - STEP_ROWS:
            value = value - jnp.where(row == STEP_ROWS - 1, north_end * slope_ratio * adj_l, 0.0)
        lam[at, :] = ocean[at, :].astype(f32) * value
    carry = jnp.zeros((1, LANES), f32)
    for start in range(0, rows, STEP_ROWS):
        at = slice(start, start + STEP_ROWS)
        lam_c = lam[at, :]
        adj_u = gu[at, :] + cu[at, :] * (roll_east(lam_c) - lam_c)
        adj_v = gv[at, :] + cv[at, :] * (lam[start + 1 : start + STEP_ROWS + 1, :] - lam_c)
        src = slope_ratio * (roll_west(adj_u) - adj_u + south_rows(carry, adj_v) - adj_v)
        carry = adj_v[STEP_ROWS - 1 :]
        adj_u_out[at, :] = adj_u
        adj_v_out[at, :] = adj_v
        source[at, :] = src
        held[at, :] = lam_c + src
    is_west = west_rows()
    sides = faces[MASK] * (
        faces[BASE]
        - attract_coef * spread([tables[k] for k in range(blocks)], faces[OWN_ID].astype(i32))
    )
    lam_sides[...] = sides
    pull = faces[RATIO] * sides
    flow = slope_ratio * jnp.where(is_west, pull, pull - faces[GAIN])
    edge = jnp.where(lat == 0, lam[rows - 1 : rows, :], lam[0:1, :])
    lam_edge[...] = edge
    pull = c_l * edge
    flow_l = slope_ratio * jnp.where(lat == 0, pull - g_l, pull)
    pad = jnp.zeros((1, LANES), f32)
    total = segment_part(
        jnp.concatenate([flow, flow_l, pad], 0),
        *one_hots(
            jnp.concatenate([faces[OWN_ID], lat_lines[OWN_L : OWN_L + 1, :], pad], 0).astype(i32),
            points,
        ),
    )
    def add(index, total):
        at = pl.ds(pl.multiple_of(index * SEG_ROWS, SEG_ROWS), SEG_ROWS)
        cells = pl.ds(pl.multiple_of(index * SEG_ROWS * LANES, SEG_ROWS * LANES), SEG_ROWS * LANES)
        return total + segment_part(source[at, :], left[:, cells], right[:, cells])

    total = lax.fori_loop(0, rows // SEG_ROWS, add, total)
    own = as_points(sum_pieces(total), points)
    far_id = faces[FAR_ID].astype(i32)
    half = far_id.shape[0] // 2

    def away(values, ids):
        return as_points(segment_few(-values, ids, points), points)

    west_part = away(flow[:half], far_id[:half])
    east_part = away(flow[half:], far_id[half:])
    lat_part = away(
        jnp.concatenate([flow_l, pad], 0),
        jnp.concatenate([lat_lines[ID_L : ID_L + 1, :], pad], 0).astype(i32),
    )
    west, east, other = neighbours(n_lon, n_lat)
    part = jnp.concatenate([own, east_part, west_part, lat_part], 0)
    begin = 4 * blocks
    deep = begin + half
    edge_rows = jnp.concatenate([edge, jnp.zeros((half - 1, LANES), f32)], 0)
    for target in range(n_lon * n_lat):
        shared = jnp.where(
            target == west, sides[:half], jnp.where(target == east, sides[half:], edge_rows)
        )
        payload[target * deep : (target + 1) * deep, :] = jnp.concatenate([part, shared], 0)


def edge_kernel(
    first, second, green, ocean, held, faces, lat_lines, lam_sides, lam_edge,
    edge, loads, acc, put, north_line, *, points, n_lon, n_lat,
):
    rows = held.shape[0]
    blocks = points // LANES
    half = rows // LANES
    deep = 4 * blocks + half
    lat = lax.axis_index("lat")

    def received(owner, kind):
        start = owner * deep + kind * blocks
        return second[start : start + blocks, :]

    for lon in range(n_lon):
        for band in range(n_lat):
            here = lon * n_lat + band
            west = (lon - 1) % n_lon * n_lat + band
            east = (lon + 1) % n_lon * n_lat + band
            other = lon * n_lat + 1 - band
            total = received(here, 0) + received(west, 1) + received(east, 2) + received(other, 3)
            loads[here * blocks : (here + 1) * blocks, :] = (
                total * first[here, blocks : 2 * blocks, :]
            )
    acc[...] = green_rows(green, 0, lambda k: loads[k : k + 1, :])
    potential = sum_lanes(acc[...])
    west, east, other = neighbours(n_lon, n_lat)

    def shared(owner, count):
        return second[pl.ds(owner * deep + 4 * blocks, count), :]

    far = jnp.concatenate([shared(west, half), shared(east, half)], 0)
    rise = jnp.where(west_rows(), lam_sides[...] - far, far - lam_sides[...])
    adj = faces[GAIN] + faces[RATIO] * rise
    put[...] = put_sides(adj, [(slope_ratio, -slope_ratio), (0.0, 1.0)])
    rise = shared(other, 1) - lam_edge[...]
    adj_l = lat_lines[G_L : G_L + 1, :] + lat_lines[C_L : C_L + 1, :] * jnp.where(
        lat == 0, rise, -rise
    )
    from_north = jnp.where(lat == 0, adj_l, 0.0)
    from_south = jnp.where(lat == 1, adj_l, 0.0)
    put[0:1, :LANES] = put[0:1, :LANES] + slope_ratio * from_south
    put[rows - 1 : rows, :LANES] = put[rows - 1 : rows, :LANES] - slope_ratio * from_north
    north_line[...] = from_north
    edge[...] = ocean[0:1, :].astype(f32) * (
        held[0:1, :] + put[0:1, :LANES] - attract_coef * potential[0:1, :]
    )


def last_kernel(
    loads, start_acc, put, green, coarse, ocean, held, lam_out, payload, acc, tables, pot,
    *, points, n_lon,
):
    rows = coarse.shape[0]
    acc[...] = start_acc[...]
    green_spread(green, coarse, lambda k: loads[k : k + 1, :], acc, tables, pot, 1)
    for start in range(0, rows, STEP_ROWS):
        at = slice(start, start + STEP_ROWS)
        lam_out[at, :] = ocean[at, :].astype(f32) * (
            held[at, :] + put[at, :LANES] - attract_coef * pot[at, :]
        )
    span = rows // n_lon
    for target in range(n_lon):
        start = target * (span + 1)
        payload[start : start + span, :] = lam_out[target * span : (target + 1) * span, :]
        if target < n_lon - 1:
            stop = (target + 1) * span
            payload[start + span : start + span + 1, :] = lam_out[stop : stop + 1, :]
        else:
            payload[start + span : start + span + 1, :] = jnp.zeros((1, LANES), f32)


def bands_kernel(
    parts, lam, adj_u, adj_v, put, north_line,
    lam_out, east_out, north_out, bands, east, north, planes, done, *, count,
):
    span = parts.shape[0] // count - 1
    rows = lam.shape[0]
    copies = [
        pltpu.make_async_copy(lam, lam_out, done.at[0]),
        pltpu.make_async_copy(east, east_out, done.at[1]),
        pltpu.make_async_copy(north, north_out, done.at[2]),
    ] + [
        pltpu.make_async_copy(planes.at[k], bands.at[k, 0], done.at[3 + k]) for k in range(3)
    ]
    copies[0].start()
    lane = iota((span, LANES), 1)
    top = (lax.axis_index("lat") == 1) & (lax.axis_index("lon") == count - 1)
    last = (iota((span, LANES), 0) == span - 1) & top
    for k in range(count):
        start = k * (span + 1)
        planes[0, :, k * LANES : (k + 1) * LANES] = parts[start : start + span, :]
    copies[3].start()
    for k in range(count):
        start = k * (span + 1)
        here = parts[start : start + span, :]
        north_of = jnp.where(last, 0.0, parts[start + 1 : start + 1 + span, :])
        planes[2, :, k * LANES : (k + 1) * LANES] = north_of - here
    copies[5].start()
    for k in range(count):
        at = slice(k * LANES, (k + 1) * LANES)
        here = planes[0, :, at]
        after = (k + 1) % count
        there = planes[0, :, after * LANES : (after + 1) * LANES]
        planes[1, :, at] = jnp.where(lane == LANES - 1, roll_east(there), roll_east(here)) - here
    copies[4].start()
    east[...] = adj_u[...] + put[:, LANES:]
    copies[1].start()
    north[...] = adj_v[...]
    north[rows - 1 : rows, :] = adj_v[rows - 1 : rows, :] + north_line[...]
    copies[2].start()
    for copy in copies:
        copy.wait()


def call(kernel, shapes, scratch, args, name, far=False, far_out=False):
    vmem = pl.BlockSpec(memory_space=pltpu.VMEM)
    shapes = [(shape, f32) if isinstance(shape[0], int) else shape for shape in shapes]
    return pl.pallas_call(
        kernel,
        out_shape=[jax.ShapeDtypeStruct(shape, kind) for shape, kind in shapes],
        in_specs=[pl.BlockSpec(memory_space=pltpu.HBM) if far else vmem] * len(args),
        out_specs=[pl.BlockSpec(memory_space=pl.ANY) if far_out else vmem] * len(shapes),
        scratch_shapes=scratch,
        compiler_params=pltpu.CompilerParams(vmem_limit_bytes=(52 << 20) if far else 16 << 20),
        cost_estimate=pl.CostEstimate(flops=4 << 30, bytes_accessed=16 << 20, transcendentals=0),
        name=name,
    )(*args)


def body(n_lon, n_lat, lam_in, flux_east, flux_north, depth, drag, ocean, coarse_of, green):
    rows, cols = lam_in.shape
    points = green.shape[0]
    blocks = points // LANES
    owners = n_lon * n_lat
    grid = (rows, cols)
    fields = (lam_in, flux_east, flux_north, depth, drag, ocean, coarse_of)
    tall = rows // LANES
    to_east, to_west, to_lat, *fields = call(
        functools.partial(pack_kernel, points=points),
        [(6 * tall, cols), (6 * tall, cols), (8, cols)]
        + [(grid, field.dtype) for field in fields],
        [pltpu.SemaphoreType.DMA((7,))], fields, "pack", far=True,
    )
    ocean, coarse_of = fields[5:]
    forward = [(k, (k + 1) % n_lon) for k in range(n_lon)]
    backward = [(target, source) for source, target in forward]
    from_west = lax.ppermute(to_east, "lon", forward)
    from_east = lax.ppermute(to_west, "lon", backward)
    from_lat = lax.ppermute(to_lat, "lat", [(0, 1), (1, 0)])
    held, gu, cu, gv, cv, sums, left, right, held_sides = call(
        functools.partial(inner_kernel, points=points),
        [grid] * 5
        + [((PIECES + 1) * HIGH, LOW), ((HIGH, rows * cols), bf16), ((LOW, rows * cols), bf16)]
        + [(2 * tall, cols)],
        [pltpu.VMEM(grid, f32)], fields, "inner",
    )
    payload, faces, lat_lines = call(
        functools.partial(rim_kernel, points=points),
        [(owners, 8, LANES), (7, 2 * tall, cols), (8, cols)], [],
        (to_east, to_west, to_lat, from_west, from_east, from_lat, sums, held_sides), "rim",
    )
    first = lax.all_to_all(payload, ("lon", "lat"), 0, 0, tiled=True)
    deep = 4 * blocks + tall
    green_scratch = [
        pltpu.VMEM((LANES, LANES), f32),
        pltpu.VMEM((blocks, 8, LANES), f32),
        pltpu.VMEM(grid, f32),
    ]
    payload, held, adj_u, adj_v, lam_sides, lam_edge = call(
        functools.partial(second_kernel, points=points, n_lon=n_lon, n_lat=n_lat),
        [(owners * deep, LANES), grid, grid, grid, (2 * tall, cols), (1, cols)],
        green_scratch + [pltpu.VMEM((rows + 8, cols), f32), pltpu.VMEM(grid, f32)],
        (first, green, coarse_of, ocean, held, gu, cu, gv, cv, left, right, faces, lat_lines),
        "second",
    )
    second = lax.all_to_all(
        payload.reshape(owners, deep, 1, LANES), ("lon", "lat"), 0, 0, tiled=True
    ).reshape(payload.shape)
    span = rows // n_lon
    edge, loads, start_acc, put, north_line = call(
        functools.partial(edge_kernel, points=points, n_lon=n_lon, n_lat=n_lat),
        [(1, cols), (owners * blocks, LANES), (LANES, LANES), (rows, 2 * cols), (1, cols)],
        [],
        (first, second, green, ocean, held, faces, lat_lines, lam_sides, lam_edge), "edge",
    )
    lam, payload = call(
        functools.partial(last_kernel, points=points, n_lon=n_lon),
        [grid, (rows + n_lon, cols)],
        green_scratch,
        (loads, start_acc, put, green, coarse_of, ocean, held), "last",
    )
    edge = lax.all_gather(edge, "lat", axis=0)[1]
    payload = lax.dynamic_update_slice(payload, edge, (rows + n_lon - 1, 0))
    parts = lax.all_to_all(
        payload.reshape(n_lon, span + 1, 1, LANES), "lon", 0, 0, tiled=True
    ).reshape(payload.shape)
    return tuple(
        call(
            functools.partial(bands_kernel, count=n_lon),
            [grid, grid, grid, (3, 1, span, n_lon * cols)],
            [
                pltpu.VMEM(grid, f32),
                pltpu.VMEM(grid, f32),
                pltpu.VMEM((3, span, n_lon * cols), f32),
                pltpu.SemaphoreType.DMA((6,)),
            ],
            (parts, lam, adj_u, adj_v, put, north_line), "bands", far_out=True,
        )
    )


def solution(mesh):
    cells = P(("groups", "lat"), "lon")
    n_lon, n_lat = mesh.shape["lon"], mesh.shape["lat"]
    return jax.shard_map(
        functools.partial(body, n_lon, n_lat),
        mesh=mesh,
        in_specs=(cells,) * 6 + (P("lat", "lon"), P(("lon", "lat"), None)),
        out_specs=(cells,) * 3 + (P(None, ("groups", "lat"), "lon", None),),
        check_vma=False,
    )
```

```python
import functools

import jax
import jax.numpy as jnp
from jax import lax
from jax.experimental import pallas as pl
from jax.experimental.pallas import tpu as pltpu
from jax.sharding import PartitionSpec as P

f32 = jnp.float32
bf16 = jnp.bfloat16
i32 = jnp.int32

LANES = 128
LOW = 32
HIGH = 16
PIECES = 2
INNER_LIMIT = 36
SEG_ROWS = 256
STEP_ROWS = 128

flux_ratio = 0.25
slope_ratio = 0.25
drag_step = 1.0
attract_coef = 0.5

LAM, DEPTH, DRAG, OCEAN, POINT, FLUX = range(6)
ADJ, RATIO, GAIN, BASE, MASK, OWN_ID, FAR_ID = range(7)
ADJ_L, C_L, G_L, ID_L, OWN_L, MASK_L = range(6)


def iota(shape, dim):
    return lax.broadcasted_iota(i32, shape, dim)


def roll_east(x):
    return pltpu.roll(x, LANES - 1, 1)


def roll_west(x):
    return pltpu.roll(x, 1, 1)


def local_ids(ids, points):
    return lax.bitwise_and(ids, points - 1)


def bf16_pieces(values, count=PIECES):
    out = []
    for piece in range(count):
        top = values.astype(bf16).astype(f32)
        out.append(top)
        if piece < count - 1:
            values = values - top
    return out


def one_hots(ids, points):
    blocks = points // LANES
    high = lax.shift_right_logical(ids, 5)
    high = lax.bitwise_and(high, 3) * blocks + lax.shift_right_logical(high, 2)
    low = lax.bitwise_and(ids, LOW - 1)
    high_iota = iota((HIGH, LANES), 0)
    low_iota = iota((LOW, LANES), 0)
    left, right = [], []
    for row in range(ids.shape[0]):
        mask = jnp.broadcast_to(high[row : row + 1], (HIGH, LANES)) == high_iota
        left.append(jnp.where(mask, 1.0, 0.0).astype(bf16))
        mask = jnp.broadcast_to(low[row : row + 1], (LOW, LANES)) == low_iota
        right.append(jnp.where(mask, 1.0, 0.0).astype(bf16))
    return jnp.concatenate(left, 1), jnp.concatenate(right, 1)


def segment_part(values, left, right, with_counts=False):
    parts = []
    for piece in bf16_pieces(values):
        line = jnp.concatenate(
            [
                jnp.broadcast_to(piece[row : row + 1], (HIGH, LANES)).astype(bf16)
                for row in range(values.shape[0])
            ],
            1,
        )
        parts.append(left * line)
    if with_counts:
        parts.append(left)
    return lax.dot_general(
        jnp.concatenate(parts, 0), right, (((1,), (1,)), ((), ())), preferred_element_type=f32
    )


def segment_few(values, ids, points):
    return sum_pieces(segment_part(values, *one_hots(ids, points)))


def sum_pieces(parts):
    total = parts[:HIGH]
    for piece in range(1, PIECES):
        total = total + parts[piece * HIGH : (piece + 1) * HIGH]
    return total


def as_points(table, points):
    blocks = points // LANES
    return jnp.concatenate([table[q * blocks : (q + 1) * blocks] for q in range(4)], 1)


def fold(line):
    return jnp.concatenate(
        [line[:, k * LANES : (k + 1) * LANES] for k in range(line.shape[1] // LANES)], 0
    )


def unfold(block):
    return jnp.concatenate([block[k : k + 1] for k in range(block.shape[0])], 1)


def take_sides(block, count=3):
    sub, lane = iota((8, LANES), 0), iota((8, LANES), 1)
    pick = ((sub == 0) & (lane == 0)) | ((sub == 1) & (lane == LANES - 1))
    pick = pick.astype(f32).astype(bf16)
    out = None
    for piece in reversed(bf16_pieces(block, count)):
        part = lax.dot_general(
            pick, piece.astype(bf16), (((1,), (1,)), ((), ())), preferred_element_type=f32
        )
        out = part if out is None else out + part
    return out


def put_sides(pair, entries):
    half = pair.shape[0] // 2
    lines = jnp.concatenate([unfold(pair[:half]), unfold(pair[half:])], 0)
    rows = lines.shape[1]
    pieces = bf16_pieces(lines, 3)
    stack = jnp.concatenate(pieces + [jnp.zeros((2, rows), f32)], 0)
    sub, lane = iota((8, LANES), 0), iota((8, LANES), 1)
    west = (sub < 6) & (lax.bitwise_and(sub, 1) == 0) & (lane == 0)
    east = (sub < 6) & (lax.bitwise_and(sub, 1) == 1) & (lane == LANES - 1)
    picks = [jnp.where(west, first, jnp.where(east, last, 0.0)) for first, last in entries]
    return lax.dot_general(
        stack, jnp.concatenate(picks, 1), (((0,), (0,)), ((), ())), preferred_element_type=f32
    )


def sum_lanes(block):
    out = None
    for piece in reversed(bf16_pieces(block, 3)):
        part = lax.dot_general(
            jnp.ones((8, LANES), bf16), piece.astype(bf16), (((1,), (1,)), ((), ())),
            preferred_element_type=f32,
        )
        out = part if out is None else out + part
    return out


def green_rows(green_ref, start, load_row):
    acc = jnp.zeros((LANES, LANES), f32)
    for k in range(green_ref.shape[1] // LANES):
        acc = acc + green_ref[
            pl.ds(start, LANES), k * LANES : (k + 1) * LANES
        ] * jnp.broadcast_to(load_row(k), (LANES, LANES))
    return acc


def look_up(table, ids):
    rows = ids.shape[0]
    table = jnp.broadcast_to(table[None], (rows // 8, 8, LANES)).reshape(rows, LANES)
    return jnp.take_along_axis(table, ids, axis=1, mode="promise_in_bounds")


def spread(tables, ids):
    low = lax.bitwise_and(ids, LANES - 1)
    block = lax.shift_right_logical(ids, 7)
    out = None
    for k, table in enumerate(tables):
        value = look_up(table, low)
        out = value if out is None else jnp.where(block == k, value, out)
    return out


def green_spread(green, coarse, load_row, acc, tables, pot):
    points = green.shape[0]
    rows = coarse.shape[0]

    def settle(index):
        table = sum_lanes(acc[...])
        tables[index] = table
        for start in range(0, rows, STEP_ROWS):
            at = slice(start, start + STEP_ROWS)
            ids = local_ids(coarse[at, :], points)
            value = look_up(table, lax.bitwise_and(ids, LANES - 1))
            pot[at, :] = jnp.where(lax.shift_right_logical(ids, 7) == index, value, pot[at, :])

    def step(index, carry):
        block = green_rows(green, index * LANES, load_row)
        settle(index - 1)
        acc[...] = block
        return carry

    acc[...] = green_rows(green, 0, load_row)
    for index in range(1, points // LANES):
        step(index, 0)
    settle(points // LANES - 1)


def next_rows(ref, start, count):
    if start + count < ref.shape[0]:
        return ref[start + 1 : start + count + 1, :]
    return jnp.concatenate([ref[start + 1 :, :], jnp.zeros((1, LANES), ref.dtype)], 0)


def south_rows(first, block):
    return jnp.concatenate([first, block[:-1]], 0)


def pack_kernel(*refs, points):
    far, (to_east, to_west, to_lat), near, done = refs[:7], refs[7:10], refs[10:17], refs[17]
    copies = [pltpu.make_async_copy(far[k], near[k], done.at[k]) for k in range(7)]
    for copy in copies:
        copy.start()
    lam, east, north, depth, drag, ocean, coarse = near
    rows = lam.shape[0]
    tall = rows // LANES
    lat = lax.axis_index("lat")
    order = (
        (LAM, 0, lam, 3), (FLUX, 1, east, 3), (None, 2, north, 0), (DEPTH, 3, depth, 3),
        (DRAG, 4, drag, 3), (OCEAN, 5, ocean, 1), (POINT, 6, coarse, 2),
    )
    for field, index, ref, pieces in order:
        copies[index].wait()
        if field is None:
            continue
        block = ref[...]
        if field == POINT:
            block = local_ids(block, points)
        sides = take_sides(block.astype(f32), pieces)
        at = slice(field * tall, (field + 1) * tall)
        to_west[at, :] = fold(sides[0:1])
        to_east[at, :] = fold(sides[1:2])

    def border(row):
        return jnp.concatenate(
            [
                lam[row : row + 1, :],
                depth[row : row + 1, :],
                drag[row : row + 1, :],
                ocean[row : row + 1, :].astype(f32),
                local_ids(coarse[row : row + 1, :], points).astype(f32),
                north[row : row + 1, :],
                jnp.zeros((2, LANES), f32),
            ],
            0,
        )

    to_lat[...] = jnp.where(lat == 0, border(rows - 1), border(0))


def inner_kernel(
    lam, east, north, depth, drag, ocean, coarse, green,
    held, gu, cu, gv, cv, sums, left, right, held_sides, green_top, source, done, *, points,
):
    copy = pltpu.make_async_copy(green.at[pl.ds(0, LANES)], green_top, done)
    copy.start()
    rows = lam.shape[0]
    inner = iota((STEP_ROWS, LANES), 1) < LANES - 1
    carry = jnp.zeros((1, LANES), f32)
    for start in range(0, rows, STEP_ROWS):
        at = slice(start, start + STEP_ROWS)
        lam_c, depth_c, drag_c = lam[at, :], depth[at, :], drag[at, :]
        ocean_c = ocean[at, :].astype(f32)
        damp = jnp.where(
            inner,
            ocean_c * roll_east(ocean_c) / (1.0 + drag_step * 0.5 * (drag_c + roll_east(drag_c))),
            0.0,
        )
        ratio = damp * (flux_ratio * 0.5) * (depth_c + roll_east(depth_c))
        adj_u = damp * east[at, :] + ratio * (roll_east(lam_c) - lam_c)
        cu[at, :] = ratio
        gu[at, :] = damp * adj_u
        ocean_n = next_rows(ocean, start, STEP_ROWS).astype(f32)
        damp = (
            ocean_c
            * ocean_n
            / (1.0 + drag_step * 0.5 * (drag_c + next_rows(drag, start, STEP_ROWS)))
        )
        ratio = damp * (flux_ratio * 0.5) * (depth_c + next_rows(depth, start, STEP_ROWS))
        adj_v = damp * north[at, :] + ratio * (next_rows(lam, start, STEP_ROWS) - lam_c)
        cv[at, :] = ratio
        gv[at, :] = damp * adj_v
        src = slope_ratio * (roll_west(adj_u) - adj_u + south_rows(carry, adj_v) - adj_v)
        carry = adj_v[STEP_ROWS - 1 :]
        source[at, :] = src
        held[at, :] = lam_c + src
    total = jnp.zeros(sums.shape, f32)
    for start in range(0, rows, SEG_ROWS):
        at = slice(start, start + SEG_ROWS)
        cells = slice(start * LANES, (start + SEG_ROWS) * LANES)
        high, low = one_hots(local_ids(coarse[at, :], points), points)
        left[:, cells] = high
        right[:, cells] = low
        total = total + segment_part(source[at, :], high, low, True)
    sums[...] = total
    sides = take_sides(held[...])
    held_sides[...] = jnp.concatenate([fold(sides[0:1]), fold(sides[1:2])], 0)
    copy.wait()


def face(low, high, flux):
    damp = low[OCEAN] * high[OCEAN] / (1.0 + drag_step * 0.5 * (low[DRAG] + high[DRAG]))
    ratio = damp * (flux_ratio * 0.5) * (low[DEPTH] + high[DEPTH])
    adj = damp * flux + ratio * (high[LAM] - low[LAM])
    return adj, ratio, damp * adj


def west_rows():
    return iota((8, LANES), 0) < 4


def rim_kernel(
    own_east, own_west, own_lat, from_west, from_east, from_lat, sums, held_sides,
    payload, faces, lat_lines, *, points,
):
    lat = lax.axis_index("lat")
    half = held_sides.shape[0] // 2

    def pair(west, east):
        return [
            jnp.concatenate(
                [west[k * half : (k + 1) * half, :], east[k * half : (k + 1) * half, :]], 0
            )
            for k in range(6)
        ]

    own, far = pair(own_west, own_east), pair(from_west, from_east)
    is_west = west_rows()
    low = [jnp.where(is_west, there, here) for here, there in zip(own, far)]
    high = [jnp.where(is_west, here, there) for here, there in zip(own, far)]
    adj, ratio, gain = face(low, high, low[FLUX])
    mine, other = own_lat[...], from_lat[...]
    lower = jnp.where(lat == 0, mine, other)
    upper = jnp.where(lat == 0, other, mine)
    lower = [lower[k : k + 1] for k in range(6)]
    upper = [upper[k : k + 1] for k in range(6)]
    adj_l, c_l, g_l = face(lower, upper, lower[FLUX])
    lat_lines[...] = jnp.concatenate(
        [
            adj_l, c_l, g_l, other[POINT : POINT + 1], mine[POINT : POINT + 1],
            other[OCEAN : OCEAN + 1], jnp.zeros((2, LANES), f32),
        ],
        0,
    )
    sign = jnp.where(is_west, slope_ratio, -slope_ratio)
    sign_l = jnp.where(lat == 0, -slope_ratio, slope_ratio)
    flow = sign * adj
    sub, lane = lax.bitwise_and(iota((8, LANES), 0), half - 1), iota((8, LANES), 1)
    corner = ((lat == 0) & (sub == half - 1) & (lane == LANES - 1)) | (
        (lat == 1) & (sub == 0) & (lane == 0)
    )
    at_corner = jnp.where(
        is_west,
        jnp.broadcast_to(adj_l[:, 0:1], (8, LANES)),
        jnp.broadcast_to(adj_l[:, LANES - 1 :], (8, LANES)),
    )
    faces[ADJ] = adj
    faces[RATIO] = ratio
    faces[GAIN] = gain
    faces[BASE] = held_sides[...] + flow + jnp.where(corner, sign_l * at_corner, 0.0)
    faces[MASK] = own[OCEAN]
    faces[OWN_ID] = own[POINT]
    faces[FAR_ID] = far[POINT]
    pad = jnp.zeros((1, LANES), f32)
    values = jnp.concatenate([flow, sign_l * adj_l, pad], 0)
    ids = jnp.concatenate([own[POINT], mine[POINT : POINT + 1], pad], 0).astype(i32)
    total = sum_pieces(sums[...]) + segment_few(values, ids, points)
    counts = as_points(sums[PIECES * HIGH : (PIECES + 1) * HIGH, :], points)
    inverse = 1.0 / counts
    loads = as_points(total, points) * inverse
    part = jnp.concatenate([loads, inverse], 0)
    if part.shape[0] < 8:
        part = jnp.concatenate([part, jnp.zeros((8 - part.shape[0], LANES), f32)], 0)
    for target in range(payload.shape[0]):
        payload[target] = part


def neighbours(n_lon, n_lat):
    lon, lat = lax.axis_index("lon"), lax.axis_index("lat")
    west = lax.rem(lon + n_lon - 1, n_lon) * n_lat + lat
    east = lax.rem(lon + 1, n_lon) * n_lat + lat
    other = lon * n_lat + (1 - lat)
    return west, east, other


def second_kernel(
    first, green, coarse, ocean, held_in, gu, cu, gv, cv, left, right, faces, lat_lines,
    payload, held, adj_u_out, adj_v_out, lam_sides, lam_edge, acc, tables, pot, lam, source,
    *, points, n_lon, n_lat,
):
    rows = coarse.shape[0]
    blocks = points // LANES
    lat = lax.axis_index("lat")
    south_end = jnp.where(lat == 1, 1.0, 0.0)
    north_end = jnp.where(lat == 0, 1.0, 0.0)
    green_spread(
        green, coarse, lambda k: first[k // blocks, k % blocks : k % blocks + 1, :],
        acc, tables, pot,
    )
    put = put_sides(faces[ADJ], [(slope_ratio, -slope_ratio)])
    adj_l = lat_lines[ADJ_L : ADJ_L + 1, :]
    c_l = lat_lines[C_L : C_L + 1, :]
    g_l = lat_lines[G_L : G_L + 1, :]
    row = iota((STEP_ROWS, LANES), 0)
    lam[rows : rows + 8, :] = jnp.zeros((8, LANES), f32)
    for start in range(0, rows, STEP_ROWS):
        at = slice(start, start + STEP_ROWS)
        value = held_in[at, :] + put[at, :] - attract_coef * pot[at, :]
        if start == 0:
            value = value + jnp.where(row == 0, south_end * slope_ratio * adj_l, 0.0)
        if start == rows - STEP_ROWS:
            value = value - jnp.where(row == STEP_ROWS - 1, north_end * slope_ratio * adj_l, 0.0)
        lam[at, :] = ocean[at, :].astype(f32) * value
    carry = jnp.zeros((1, LANES), f32)
    for start in range(0, rows, STEP_ROWS):
        at = slice(start, start + STEP_ROWS)
        lam_c = lam[at, :]
        adj_u = gu[at, :] + cu[at, :] * (roll_east(lam_c) - lam_c)
        adj_v = gv[at, :] + cv[at, :] * (lam[start + 1 : start + STEP_ROWS + 1, :] - lam_c)
        src = slope_ratio * (roll_west(adj_u) - adj_u + south_rows(carry, adj_v) - adj_v)
        carry = adj_v[STEP_ROWS - 1 :]
        adj_u_out[at, :] = adj_u
        adj_v_out[at, :] = adj_v
        source[at, :] = src
        held[at, :] = lam_c + src
    is_west = west_rows()
    sides = faces[MASK] * (
        faces[BASE]
        - attract_coef * spread([tables[k] for k in range(blocks)], faces[OWN_ID].astype(i32))
    )
    lam_sides[...] = sides
    pull = faces[RATIO] * sides
    flow = slope_ratio * jnp.where(is_west, pull, pull - faces[GAIN])
    edge = jnp.where(lat == 0, lam[rows - 1 : rows, :], lam[0:1, :])
    lam_edge[...] = edge
    pull = c_l * edge
    flow_l = slope_ratio * jnp.where(lat == 0, pull - g_l, pull)
    pad = jnp.zeros((1, LANES), f32)
    total = segment_part(
        jnp.concatenate([flow, flow_l, pad], 0),
        *one_hots(
            jnp.concatenate([faces[OWN_ID], lat_lines[OWN_L : OWN_L + 1, :], pad], 0).astype(i32),
            points,
        ),
    )
    def add(index, total):
        at = pl.ds(pl.multiple_of(index * SEG_ROWS, SEG_ROWS), SEG_ROWS)
        cells = pl.ds(pl.multiple_of(index * SEG_ROWS * LANES, SEG_ROWS * LANES), SEG_ROWS * LANES)
        return total + segment_part(source[at, :], left[:, cells], right[:, cells])

    total = lax.fori_loop(0, rows // SEG_ROWS, add, total)
    own = as_points(sum_pieces(total), points)
    far_id = faces[FAR_ID].astype(i32)
    half = far_id.shape[0] // 2

    def away(values, ids):
        return as_points(segment_few(-values, ids, points), points)

    west_part = away(flow[:half], far_id[:half])
    east_part = away(flow[half:], far_id[half:])
    lat_part = away(
        jnp.concatenate([flow_l, pad], 0),
        jnp.concatenate([lat_lines[ID_L : ID_L + 1, :], pad], 0).astype(i32),
    )
    west, east, other = neighbours(n_lon, n_lat)
    part = jnp.concatenate([own, east_part, west_part, lat_part], 0)
    begin = 4 * blocks
    deep = begin + half
    first_lane = iota((1, LANES), 1) == 0

    def corners(block):
        return jnp.where(
            first_lane,
            block[0:1],
            jnp.broadcast_to(block[half : half + 1, 0:1], (1, LANES)),
        )

    edge_rows = jnp.concatenate(
        [edge, held[0:1, :], corners(faces[GAIN]), corners(faces[RATIO])]
        + [jnp.zeros((1, LANES), f32)] * (half - 4),
        0,
    )
    for target in range(n_lon * n_lat):
        shared = jnp.where(
            target == west, sides[:half], jnp.where(target == east, sides[half:], edge_rows)
        )
        payload[target * deep : (target + 1) * deep, :] = jnp.concatenate([part, shared], 0)


def last_kernel(
    first, second, green, green_north, coarse, ocean, held, faces, lat_lines, lam_sides, lam_edge,
    lam_out, payload, put, north_line, loads, top, done, acc, tables, pot,
    *, points, n_lon, n_lat,
):
    copy = pltpu.make_async_copy(green_north, top, done)
    copy.start()
    rows = held.shape[0]
    blocks = points // LANES
    half = rows // LANES
    deep = 4 * blocks + half
    lat = lax.axis_index("lat")

    def received(owner, kind):
        start = owner * deep + kind * blocks
        return second[start : start + blocks, :]

    for lon in range(n_lon):
        for band in range(n_lat):
            here = lon * n_lat + band
            west = (lon - 1) % n_lon * n_lat + band
            east = (lon + 1) % n_lon * n_lat + band
            other = lon * n_lat + 1 - band
            total = received(here, 0) + received(west, 1) + received(east, 2) + received(other, 3)
            loads[here * blocks : (here + 1) * blocks, :] = (
                total * first[here, blocks : 2 * blocks, :]
            )
    west, east, other = neighbours(n_lon, n_lat)

    def shared(owner, row, count):
        return second[pl.ds(owner * deep + 4 * blocks + row, count), :]

    far = jnp.concatenate([shared(west, 0, half), shared(east, 0, half)], 0)
    rise = jnp.where(west_rows(), lam_sides[...] - far, far - lam_sides[...])
    adj = faces[GAIN] + faces[RATIO] * rise
    put[...] = put_sides(adj, [(slope_ratio, -slope_ratio), (0.0, 1.0)])
    rise = shared(other, 0, 1) - lam_edge[...]
    adj_l = lat_lines[G_L : G_L + 1, :] + lat_lines[C_L : C_L + 1, :] * jnp.where(
        lat == 0, rise, -rise
    )
    from_north = jnp.where(lat == 0, adj_l, 0.0)
    from_south = jnp.where(lat == 1, adj_l, 0.0)
    put[0:1, :LANES] = put[0:1, :LANES] + slope_ratio * from_south
    put[rows - 1 : rows, :LANES] = put[rows - 1 : rows, :LANES] - slope_ratio * from_north
    north_line[...] = from_north
    green_spread(green, coarse, lambda k: loads[k : k + 1, :], acc, tables, pot)
    for start in range(0, rows, STEP_ROWS):
        at = slice(start, start + STEP_ROWS)
        lam_out[at, :] = ocean[at, :].astype(f32) * (
            held[at, :] + put[at, :LANES] - attract_coef * pot[at, :]
        )
    copy.wait()
    potential = sum_lanes(green_rows(top, 0, lambda k: loads[k : k + 1, :]))[0:1]
    diagonal = lambda owner: shared(owner + 1 - 2 * lat, 0, 1)
    lam_n = shared(other, 0, 1)
    lane = iota((1, LANES), 1)
    rise = jnp.where(
        lane == 0, lam_n - roll_west(diagonal(west)), roll_east(diagonal(east)) - lam_n
    )
    adj = shared(other, 2, 1) + shared(other, 3, 1) * rise
    flow = jnp.where(lane == 0, adj, jnp.where(lane == LANES - 1, -adj, 0.0)) + adj_l
    lam_north = lat_lines[MASK_L : MASK_L + 1, :] * (
        shared(other, 1, 1) + slope_ratio * flow - attract_coef * potential
    )
    span = rows // n_lon
    for target in range(n_lon):
        start = target * (span + 1)
        payload[start : start + span, :] = lam_out[target * span : (target + 1) * span, :]
        if target < n_lon - 1:
            stop = (target + 1) * span
            payload[start + span : start + span + 1, :] = lam_out[stop : stop + 1, :]
        else:
            payload[start + span : start + span + 1, :] = lam_north


def bands_kernel(
    parts, lam, adj_u, adj_v, put, north_line,
    lam_out, east_out, north_out, bands, east, north, planes, done, *, count,
):
    span = parts.shape[0] // count - 1
    rows = lam.shape[0]
    copies = [
        pltpu.make_async_copy(lam, lam_out, done.at[0]),
        pltpu.make_async_copy(east, east_out, done.at[1]),
        pltpu.make_async_copy(north, north_out, done.at[2]),
    ] + [
        pltpu.make_async_copy(planes.at[k], bands.at[k, 0], done.at[3 + k]) for k in range(3)
    ]
    copies[0].start()
    lane = iota((span, LANES), 1)
    top = (lax.axis_index("lat") == 1) & (lax.axis_index("lon") == count - 1)
    last = (iota((span, LANES), 0) == span - 1) & top
    for k in range(count):
        start = k * (span + 1)
        planes[0, :, k * LANES : (k + 1) * LANES] = parts[start : start + span, :]
    copies[3].start()
    for k in range(count):
        start = k * (span + 1)
        here = parts[start : start + span, :]
        north_of = jnp.where(last, 0.0, parts[start + 1 : start + 1 + span, :])
        planes[2, :, k * LANES : (k + 1) * LANES] = north_of - here
    copies[5].start()
    for k in range(count):
        at = slice(k * LANES, (k + 1) * LANES)
        here = planes[0, :, at]
        after = (k + 1) % count
        there = planes[0, :, after * LANES : (after + 1) * LANES]
        planes[1, :, at] = jnp.where(lane == LANES - 1, roll_east(there), roll_east(here)) - here
    copies[4].start()
    east[...] = adj_u[...] + put[:, LANES:]
    copies[1].start()
    north[...] = adj_v[...]
    north[rows - 1 : rows, :] = adj_v[rows - 1 : rows, :] + north_line[...]
    copies[2].start()
    for copy in copies:
        copy.wait()


def call(kernel, shapes, scratch, args, name, far=(), far_out=(), limit=16, weight=4):
    vmem = pl.BlockSpec(memory_space=pltpu.VMEM)
    away = pl.BlockSpec(memory_space=pl.ANY)
    shapes = [(shape, f32) if isinstance(shape[0], int) else shape for shape in shapes]
    return pl.pallas_call(
        kernel,
        out_shape=[jax.ShapeDtypeStruct(shape, kind) for shape, kind in shapes],
        in_specs=[away if k in far else vmem for k in range(len(args))],
        out_specs=[away if k in far_out else vmem for k in range(len(shapes))],
        scratch_shapes=scratch,
        compiler_params=pltpu.CompilerParams(vmem_limit_bytes=limit << 20),
        cost_estimate=pl.CostEstimate(flops=weight << 30, bytes_accessed=16 << 20, transcendentals=0),
        name=name,
    )(*args)


def body(n_lon, n_lat, lam_in, flux_east, flux_north, depth, drag, ocean, coarse_of, green):
    rows, cols = lam_in.shape
    points = green.shape[0]
    blocks = points // LANES
    owners = n_lon * n_lat
    grid = (rows, cols)
    fields = (lam_in, flux_east, flux_north, depth, drag, ocean, coarse_of)
    tall = rows // LANES
    to_east, to_west, to_lat, *fields = call(
        functools.partial(pack_kernel, points=points),
        [(6 * tall, cols), (6 * tall, cols), (8, cols)]
        + [(grid, field.dtype) for field in fields],
        [pltpu.SemaphoreType.DMA((7,))], fields, "pack", far=range(7), limit=52,
    )
    ocean, coarse_of = fields[5:]
    forward = [(k, (k + 1) % n_lon) for k in range(n_lon)]
    backward = [(target, source) for source, target in forward]
    from_west = lax.ppermute(to_east, "lon", forward)
    from_east = lax.ppermute(to_west, "lon", backward)
    from_lat = lax.ppermute(to_lat, "lat", [(0, 1), (1, 0)])
    held, gu, cu, gv, cv, sums, left, right, held_sides, green_top = call(
        functools.partial(inner_kernel, points=points),
        [grid] * 5
        + [((PIECES + 1) * HIGH, LOW), ((HIGH, rows * cols), bf16), ((LOW, rows * cols), bf16)]
        + [(2 * tall, cols), (LANES, green.shape[1])],
        [pltpu.VMEM(grid, f32), pltpu.SemaphoreType.DMA(())], (*fields, green), "inner",
        far=(7,), far_out=(9,), limit=INNER_LIMIT,
    )
    green_top, from_west, from_east, from_lat = lax.optimization_barrier(
        (green_top, from_west, from_east, from_lat)
    )
    green_north = lax.ppermute(green_top, "lat", [(0, 1), (1, 0)])
    payload, faces, lat_lines = call(
        functools.partial(rim_kernel, points=points),
        [(owners, 8, LANES), (7, 2 * tall, cols), (8, cols)], [],
        (to_east, to_west, to_lat, from_west, from_east, from_lat, sums, held_sides), "rim",
        weight=16,
    )
    first = lax.all_to_all(payload, ("lon", "lat"), 0, 0, tiled=True)
    deep = 4 * blocks + tall
    green_scratch = [
        pltpu.VMEM((LANES, LANES), f32),
        pltpu.VMEM((blocks, 8, LANES), f32),
        pltpu.VMEM(grid, f32),
    ]
    payload, held, adj_u, adj_v, lam_sides, lam_edge = call(
        functools.partial(second_kernel, points=points, n_lon=n_lon, n_lat=n_lat),
        [(owners * deep, LANES), grid, grid, grid, (2 * tall, cols), (1, cols)],
        green_scratch + [pltpu.VMEM((rows + 8, cols), f32), pltpu.VMEM(grid, f32)],
        (first, green, coarse_of, ocean, held, gu, cu, gv, cv, left, right, faces, lat_lines),
        "second",
    )
    second = lax.all_to_all(
        payload.reshape(owners, deep, 1, LANES), ("lon", "lat"), 0, 0, tiled=True
    ).reshape(payload.shape)
    span = rows // n_lon
    lam, payload, put, north_line = call(
        functools.partial(last_kernel, points=points, n_lon=n_lon, n_lat=n_lat),
        [grid, (rows + n_lon, cols), (rows, 2 * cols), (1, cols)],
        [
            pltpu.VMEM((owners * blocks, LANES), f32),
            pltpu.VMEM(green_top.shape, f32),
            pltpu.SemaphoreType.DMA(()),
        ]
        + green_scratch,
        (
            first, second, green, green_north, coarse_of, ocean, held, faces, lat_lines,
            lam_sides, lam_edge,
        ),
        "last", far=(3,),
    )
    parts = lax.all_to_all(
        payload.reshape(n_lon, span + 1, 1, LANES), "lon", 0, 0, tiled=True
    ).reshape(payload.shape)
    return tuple(
        call(
            functools.partial(bands_kernel, count=n_lon),
            [grid, grid, grid, (3, 1, span, n_lon * cols)],
            [
                pltpu.VMEM(grid, f32),
                pltpu.VMEM(grid, f32),
                pltpu.VMEM((3, span, n_lon * cols), f32),
                pltpu.SemaphoreType.DMA((6,)),
            ],
            (parts, lam, adj_u, adj_v, put, north_line), "bands", far_out=range(4),
        )
    )


def solution(mesh):
    cells = P(("groups", "lat"), "lon")
    n_lon, n_lat = mesh.shape["lon"], mesh.shape["lat"]
    return jax.shard_map(
        functools.partial(body, n_lon, n_lat),
        mesh=mesh,
        in_specs=(cells,) * 6 + (P("lat", "lon"), P(("lon", "lat"), None)),
        out_specs=(cells,) * 3 + (P(None, ("groups", "lat"), "lon", None),),
        check_vma=False,
    )
```

```python
import functools

import jax
import jax.numpy as jnp
from jax import lax
from jax.experimental import pallas as pl
from jax.experimental.pallas import tpu as pltpu
from jax.sharding import PartitionSpec as P

f32 = jnp.float32
bf16 = jnp.bfloat16
i32 = jnp.int32

LANES = 128
LOW = 32
HIGH = 16
PIECES = 2
INNER_LIMIT = 36
SEG_ROWS = 256
STEP_ROWS = 128

flux_ratio = 0.25
slope_ratio = 0.25
drag_step = 1.0
attract_coef = 0.5

LAM, DEPTH, DRAG, OCEAN, POINT, FLUX = range(6)
ADJ, RATIO, GAIN, BASE, MASK, OWN_ID, FAR_ID = range(7)
ADJ_L, C_L, G_L, ID_L, OWN_L, MASK_L = range(6)


def iota(shape, dim):
    return lax.broadcasted_iota(i32, shape, dim)


def roll_east(x):
    return pltpu.roll(x, LANES - 1, 1)


def roll_west(x):
    return pltpu.roll(x, 1, 1)


def local_ids(ids, points):
    return lax.bitwise_and(ids, points - 1)


def bf16_pieces(values, count=PIECES):
    out = []
    for piece in range(count):
        top = values.astype(bf16).astype(f32)
        out.append(top)
        if piece < count - 1:
            values = values - top
    return out


def one_hots(ids, points):
    blocks = points // LANES
    high = lax.shift_right_logical(ids, 5)
    high = lax.bitwise_and(high, 3) * blocks + lax.shift_right_logical(high, 2)
    low = lax.bitwise_and(ids, LOW - 1)
    high_iota = iota((HIGH, LANES), 0)
    low_iota = iota((LOW, LANES), 0)
    left, right = [], []
    for row in range(ids.shape[0]):
        mask = jnp.broadcast_to(high[row : row + 1], (HIGH, LANES)) == high_iota
        left.append(jnp.where(mask, 1.0, 0.0).astype(bf16))
        mask = jnp.broadcast_to(low[row : row + 1], (LOW, LANES)) == low_iota
        right.append(jnp.where(mask, 1.0, 0.0).astype(bf16))
    return jnp.concatenate(left, 1), jnp.concatenate(right, 1)


def segment_part(values, left, right, with_counts=False):
    parts = []
    for piece in bf16_pieces(values):
        line = jnp.concatenate(
            [
                jnp.broadcast_to(piece[row : row + 1], (HIGH, LANES)).astype(bf16)
                for row in range(values.shape[0])
            ],
            1,
        )
        parts.append(left * line)
    if with_counts:
        parts.append(left)
    return lax.dot_general(
        jnp.concatenate(parts, 0), right, (((1,), (1,)), ((), ())), preferred_element_type=f32
    )


def segment_few(values, ids, points):
    return sum_pieces(segment_part(values, *one_hots(ids, points)))


def sum_pieces(parts):
    total = parts[:HIGH]
    for piece in range(1, PIECES):
        total = total + parts[piece * HIGH : (piece + 1) * HIGH]
    return total


def as_points(table, points):
    blocks = points // LANES
    return jnp.concatenate([table[q * blocks : (q + 1) * blocks] for q in range(4)], 1)


def fold(line):
    return jnp.concatenate(
        [line[:, k * LANES : (k + 1) * LANES] for k in range(line.shape[1] // LANES)], 0
    )


def unfold(block):
    return jnp.concatenate([block[k : k + 1] for k in range(block.shape[0])], 1)


def take_sides(block, count=3):
    sub, lane = iota((8, LANES), 0), iota((8, LANES), 1)
    pick = ((sub == 0) & (lane == 0)) | ((sub == 1) & (lane == LANES - 1))
    pick = pick.astype(f32).astype(bf16)
    out = None
    for piece in reversed(bf16_pieces(block, count)):
        part = lax.dot_general(
            pick, piece.astype(bf16), (((1,), (1,)), ((), ())), preferred_element_type=f32
        )
        out = part if out is None else out + part
    return out


def put_sides(pair, entries):
    half = pair.shape[0] // 2
    lines = jnp.concatenate([unfold(pair[:half]), unfold(pair[half:])], 0)
    rows = lines.shape[1]
    pieces = bf16_pieces(lines, 3)
    stack = jnp.concatenate(pieces + [jnp.zeros((2, rows), f32)], 0)
    sub, lane = iota((8, LANES), 0), iota((8, LANES), 1)
    west = (sub < 6) & (lax.bitwise_and(sub, 1) == 0) & (lane == 0)
    east = (sub < 6) & (lax.bitwise_and(sub, 1) == 1) & (lane == LANES - 1)
    picks = [jnp.where(west, first, jnp.where(east, last, 0.0)) for first, last in entries]
    return lax.dot_general(
        stack, jnp.concatenate(picks, 1), (((0,), (0,)), ((), ())), preferred_element_type=f32
    )


def sum_lanes(block):
    out = None
    for piece in reversed(bf16_pieces(block, 3)):
        part = lax.dot_general(
            jnp.ones((8, LANES), bf16), piece.astype(bf16), (((1,), (1,)), ((), ())),
            preferred_element_type=f32,
        )
        out = part if out is None else out + part
    return out


def green_rows(green_ref, start, load_row):
    acc = jnp.zeros((LANES, LANES), f32)
    for k in range(green_ref.shape[1] // LANES):
        acc = acc + green_ref[
            pl.ds(start, LANES), k * LANES : (k + 1) * LANES
        ] * jnp.broadcast_to(load_row(k), (LANES, LANES))
    return acc


def look_up(table, ids):
    rows = ids.shape[0]
    table = jnp.broadcast_to(table[None], (rows // 8, 8, LANES)).reshape(rows, LANES)
    return jnp.take_along_axis(table, ids, axis=1, mode="promise_in_bounds")


def spread(tables, ids):
    low = lax.bitwise_and(ids, LANES - 1)
    block = lax.shift_right_logical(ids, 7)
    out = None
    for k, table in enumerate(tables):
        value = look_up(table, low)
        out = value if out is None else jnp.where(block == k, value, out)
    return out


def green_spread(green, coarse, load_row, acc, tables, pot):
    points = green.shape[0]
    rows = coarse.shape[0]

    def settle(index):
        table = sum_lanes(acc[...])
        tables[index] = table
        for start in range(0, rows, STEP_ROWS):
            at = slice(start, start + STEP_ROWS)
            ids = local_ids(coarse[at, :], points)
            value = look_up(table, lax.bitwise_and(ids, LANES - 1))
            pot[at, :] = jnp.where(lax.shift_right_logical(ids, 7) == index, value, pot[at, :])

    def step(index, carry):
        block = green_rows(green, index * LANES, load_row)
        settle(index - 1)
        acc[...] = block
        return carry

    acc[...] = green_rows(green, 0, load_row)
    for index in range(1, points // LANES):
        step(index, 0)
    settle(points // LANES - 1)


def next_rows(ref, start, count):
    if start + count < ref.shape[0]:
        return ref[start + 1 : start + count + 1, :]
    return jnp.concatenate([ref[start + 1 :, :], jnp.zeros((1, LANES), ref.dtype)], 0)


def south_rows(first, block):
    return jnp.concatenate([first, block[:-1]], 0)


def pack_kernel(*refs, points):
    far, (to_east, to_west, to_lat), near, done = refs[:7], refs[7:10], refs[10:17], refs[17]
    copies = [pltpu.make_async_copy(far[k], near[k], done.at[k]) for k in range(7)]
    for copy in copies:
        copy.start()
    lam, east, north, depth, drag, ocean, coarse = near
    rows = lam.shape[0]
    tall = rows // LANES
    lat = lax.axis_index("lat")
    order = (
        (LAM, 0, lam, 3), (FLUX, 1, east, 3), (None, 2, north, 0), (DEPTH, 3, depth, 3),
        (DRAG, 4, drag, 3), (OCEAN, 5, ocean, 1), (POINT, 6, coarse, 2),
    )
    for field, index, ref, pieces in order:
        copies[index].wait()
        if field is None:
            continue
        block = ref[...]
        if field == POINT:
            block = local_ids(block, points)
        sides = take_sides(block.astype(f32), pieces)
        at = slice(field * tall, (field + 1) * tall)
        to_west[at, :] = fold(sides[0:1])
        to_east[at, :] = fold(sides[1:2])

    def border(row):
        return jnp.concatenate(
            [
                lam[row : row + 1, :],
                depth[row : row + 1, :],
                drag[row : row + 1, :],
                ocean[row : row + 1, :].astype(f32),
                local_ids(coarse[row : row + 1, :], points).astype(f32),
                north[row : row + 1, :],
                jnp.zeros((2, LANES), f32),
            ],
            0,
        )

    to_lat[...] = jnp.where(lat == 0, border(rows - 1), border(0))


def inner_kernel(
    lam, east, north, depth, drag, ocean, coarse, green,
    held, gu, cu, gv, cv, sums, left, right, held_sides, green_top, source, done, *, points,
):
    copy = pltpu.make_async_copy(green.at[pl.ds(0, LANES)], green_top, done)
    copy.start()
    rows = lam.shape[0]
    inner = iota((STEP_ROWS, LANES), 1) < LANES - 1
    carry = jnp.zeros((1, LANES), f32)
    for start in range(0, rows, STEP_ROWS):
        at = slice(start, start + STEP_ROWS)
        lam_c, depth_c, drag_c = lam[at, :], depth[at, :], drag[at, :]
        ocean_c = ocean[at, :].astype(f32)
        damp = jnp.where(
            inner,
            ocean_c * roll_east(ocean_c) / (1.0 + drag_step * 0.5 * (drag_c + roll_east(drag_c))),
            0.0,
        )
        ratio = damp * (flux_ratio * 0.5) * (depth_c + roll_east(depth_c))
        adj_u = damp * east[at, :] + ratio * (roll_east(lam_c) - lam_c)
        cu[at, :] = ratio
        gu[at, :] = damp * adj_u
        ocean_n = next_rows(ocean, start, STEP_ROWS).astype(f32)
        damp = (
            ocean_c
            * ocean_n
            / (1.0 + drag_step * 0.5 * (drag_c + next_rows(drag, start, STEP_ROWS)))
        )
        ratio = damp * (flux_ratio * 0.5) * (depth_c + next_rows(depth, start, STEP_ROWS))
        adj_v = damp * north[at, :] + ratio * (next_rows(lam, start, STEP_ROWS) - lam_c)
        cv[at, :] = ratio
        gv[at, :] = damp * adj_v
        src = slope_ratio * (roll_west(adj_u) - adj_u + south_rows(carry, adj_v) - adj_v)
        carry = adj_v[STEP_ROWS - 1 :]
        source[at, :] = src
        held[at, :] = lam_c + src
    total = jnp.zeros(sums.shape, f32)
    for start in range(0, rows, SEG_ROWS):
        at = slice(start, start + SEG_ROWS)
        cells = slice(start * LANES, (start + SEG_ROWS) * LANES)
        high, low = one_hots(local_ids(coarse[at, :], points), points)
        left[:, cells] = high
        right[:, cells] = low
        total = total + segment_part(source[at, :], high, low, True)
    sums[...] = total
    sides = take_sides(held[...])
    held_sides[...] = jnp.concatenate([fold(sides[0:1]), fold(sides[1:2])], 0)
    copy.wait()


def face(low, high, flux):
    damp = low[OCEAN] * high[OCEAN] / (1.0 + drag_step * 0.5 * (low[DRAG] + high[DRAG]))
    ratio = damp * (flux_ratio * 0.5) * (low[DEPTH] + high[DEPTH])
    adj = damp * flux + ratio * (high[LAM] - low[LAM])
    return adj, ratio, damp * adj


def west_rows():
    return iota((8, LANES), 0) < 4


def rim_kernel(
    own_east, own_west, own_lat, from_west, from_east, from_lat, sums, held_sides,
    payload, faces, lat_lines, *, points,
):
    lat = lax.axis_index("lat")
    half = held_sides.shape[0] // 2

    def pair(west, east):
        return [
            jnp.concatenate(
                [west[k * half : (k + 1) * half, :], east[k * half : (k + 1) * half, :]], 0
            )
            for k in range(6)
        ]

    own, far = pair(own_west, own_east), pair(from_west, from_east)
    is_west = west_rows()
    low = [jnp.where(is_west, there, here) for here, there in zip(own, far)]
    high = [jnp.where(is_west, here, there) for here, there in zip(own, far)]
    adj, ratio, gain = face(low, high, low[FLUX])
    mine, other = own_lat[...], from_lat[...]
    lower = jnp.where(lat == 0, mine, other)
    upper = jnp.where(lat == 0, other, mine)
    lower = [lower[k : k + 1] for k in range(6)]
    upper = [upper[k : k + 1] for k in range(6)]
    adj_l, c_l, g_l = face(lower, upper, lower[FLUX])
    lat_lines[...] = jnp.concatenate(
        [
            adj_l, c_l, g_l, other[POINT : POINT + 1], mine[POINT : POINT + 1],
            other[OCEAN : OCEAN + 1], jnp.zeros((2, LANES), f32),
        ],
        0,
    )
    sign = jnp.where(is_west, slope_ratio, -slope_ratio)
    sign_l = jnp.where(lat == 0, -slope_ratio, slope_ratio)
    flow = sign * adj
    sub, lane = lax.bitwise_and(iota((8, LANES), 0), half - 1), iota((8, LANES), 1)
    corner = ((lat == 0) & (sub == half - 1) & (lane == LANES - 1)) | (
        (lat == 1) & (sub == 0) & (lane == 0)
    )
    at_corner = jnp.where(
        is_west,
        jnp.broadcast_to(adj_l[:, 0:1], (8, LANES)),
        jnp.broadcast_to(adj_l[:, LANES - 1 :], (8, LANES)),
    )
    faces[ADJ] = adj
    faces[RATIO] = ratio
    faces[GAIN] = gain
    faces[BASE] = held_sides[...] + flow + jnp.where(corner, sign_l * at_corner, 0.0)
    faces[MASK] = own[OCEAN]
    faces[OWN_ID] = own[POINT]
    faces[FAR_ID] = far[POINT]
    pad = jnp.zeros((1, LANES), f32)
    values = jnp.concatenate([flow, sign_l * adj_l, pad], 0)
    ids = jnp.concatenate([own[POINT], mine[POINT : POINT + 1], pad], 0).astype(i32)
    total = sum_pieces(sums[...]) + segment_few(values, ids, points)
    counts = as_points(sums[PIECES * HIGH : (PIECES + 1) * HIGH, :], points)
    inverse = 1.0 / counts
    loads = as_points(total, points) * inverse
    part = jnp.concatenate([loads, inverse], 0)
    if part.shape[0] < 8:
        part = jnp.concatenate([part, jnp.zeros((8 - part.shape[0], LANES), f32)], 0)
    for target in range(payload.shape[0]):
        payload[target] = part


def neighbours(n_lon, n_lat):
    lon, lat = lax.axis_index("lon"), lax.axis_index("lat")
    west = lax.rem(lon + n_lon - 1, n_lon) * n_lat + lat
    east = lax.rem(lon + 1, n_lon) * n_lat + lat
    other = lon * n_lat + (1 - lat)
    return west, east, other


def second_kernel(
    first, green, coarse, ocean, held_in, gu, cu, gv, cv, left, right, faces, lat_lines,
    payload, held, adj_u_out, adj_v_out, lam_sides, lam_edge, acc, tables, pot, lam, source,
    *, points, n_lon, n_lat,
):
    rows = coarse.shape[0]
    blocks = points // LANES
    lat = lax.axis_index("lat")
    south_end = jnp.where(lat == 1, 1.0, 0.0)
    north_end = jnp.where(lat == 0, 1.0, 0.0)
    green_spread(
        green, coarse, lambda k: first[k // blocks, k % blocks : k % blocks + 1, :],
        acc, tables, pot,
    )
    put = put_sides(faces[ADJ], [(slope_ratio, -slope_ratio)])
    adj_l = lat_lines[ADJ_L : ADJ_L + 1, :]
    c_l = lat_lines[C_L : C_L + 1, :]
    g_l = lat_lines[G_L : G_L + 1, :]
    row = iota((STEP_ROWS, LANES), 0)
    lam[rows : rows + 8, :] = jnp.zeros((8, LANES), f32)
    for start in range(0, rows, STEP_ROWS):
        at = slice(start, start + STEP_ROWS)
        value = held_in[at, :] + put[at, :] - attract_coef * pot[at, :]
        if start == 0:
            value = value + jnp.where(row == 0, south_end * slope_ratio * adj_l, 0.0)
        if start == rows - STEP_ROWS:
            value = value - jnp.where(row == STEP_ROWS - 1, north_end * slope_ratio * adj_l, 0.0)
        lam[at, :] = ocean[at, :].astype(f32) * value
    carry = jnp.zeros((1, LANES), f32)
    for start in range(0, rows, STEP_ROWS):
        at = slice(start, start + STEP_ROWS)
        lam_c = lam[at, :]
        adj_u = gu[at, :] + cu[at, :] * (roll_east(lam_c) - lam_c)
        adj_v = gv[at, :] + cv[at, :] * (lam[start + 1 : start + STEP_ROWS + 1, :] - lam_c)
        src = slope_ratio * (roll_west(adj_u) - adj_u + south_rows(carry, adj_v) - adj_v)
        carry = adj_v[STEP_ROWS - 1 :]
        adj_u_out[at, :] = adj_u
        adj_v_out[at, :] = adj_v
        source[at, :] = src
        held[at, :] = lam_c + src
    is_west = west_rows()
    sides = faces[MASK] * (
        faces[BASE]
        - attract_coef * spread([tables[k] for k in range(blocks)], faces[OWN_ID].astype(i32))
    )
    lam_sides[...] = sides
    pull = faces[RATIO] * sides
    flow = slope_ratio * jnp.where(is_west, pull, pull - faces[GAIN])
    edge = jnp.where(lat == 0, lam[rows - 1 : rows, :], lam[0:1, :])
    lam_edge[...] = edge
    pull = c_l * edge
    flow_l = slope_ratio * jnp.where(lat == 0, pull - g_l, pull)
    pad = jnp.zeros((1, LANES), f32)
    total = segment_part(
        jnp.concatenate([flow, flow_l, pad], 0),
        *one_hots(
            jnp.concatenate([faces[OWN_ID], lat_lines[OWN_L : OWN_L + 1, :], pad], 0).astype(i32),
            points,
        ),
    )
    def add(index, total):
        at = pl.ds(pl.multiple_of(index * SEG_ROWS, SEG_ROWS), SEG_ROWS)
        cells = pl.ds(pl.multiple_of(index * SEG_ROWS * LANES, SEG_ROWS * LANES), SEG_ROWS * LANES)
        return total + segment_part(source[at, :], left[:, cells], right[:, cells])

    total = lax.fori_loop(0, rows // SEG_ROWS, add, total)
    own = as_points(sum_pieces(total), points)
    far_id = faces[FAR_ID].astype(i32)
    half = far_id.shape[0] // 2

    def away(values, ids):
        return as_points(segment_few(-values, ids, points), points)

    west_part = away(flow[:half], far_id[:half])
    east_part = away(flow[half:], far_id[half:])
    lat_part = away(
        jnp.concatenate([flow_l, pad], 0),
        jnp.concatenate([lat_lines[ID_L : ID_L + 1, :], pad], 0).astype(i32),
    )
    west, east, other = neighbours(n_lon, n_lat)
    part = jnp.concatenate([own, east_part, west_part, lat_part], 0)
    begin = 4 * blocks
    deep = begin + half
    first_lane = iota((1, LANES), 1) == 0

    def corners(block):
        return jnp.where(
            first_lane,
            block[0:1],
            jnp.broadcast_to(block[half : half + 1, 0:1], (1, LANES)),
        )

    edge_rows = jnp.concatenate(
        [edge, held[0:1, :], corners(faces[GAIN]), corners(faces[RATIO])]
        + [jnp.zeros((1, LANES), f32)] * (half - 4),
        0,
    )
    for target in range(n_lon * n_lat):
        shared = jnp.where(
            target == west, sides[:half], jnp.where(target == east, sides[half:], edge_rows)
        )
        payload[target * deep : (target + 1) * deep, :] = jnp.concatenate([part, shared], 0)


def last_kernel(
    first, second, green, green_north, coarse, ocean, held, faces, lat_lines, lam_sides, lam_edge,
    lam_out, payload, put, north_line, loads, top, done, acc, tables, pot,
    *, points, n_lon, n_lat,
):
    copy = pltpu.make_async_copy(green_north, top, done)
    copy.start()
    rows = held.shape[0]
    blocks = points // LANES
    half = rows // LANES
    deep = 4 * blocks + half
    lat = lax.axis_index("lat")

    def received(owner, kind):
        start = owner * deep + kind * blocks
        return second[start : start + blocks, :]

    for lon in range(n_lon):
        for band in range(n_lat):
            here = lon * n_lat + band
            west = (lon - 1) % n_lon * n_lat + band
            east = (lon + 1) % n_lon * n_lat + band
            other = lon * n_lat + 1 - band
            total = received(here, 0) + received(west, 1) + received(east, 2) + received(other, 3)
            loads[here * blocks : (here + 1) * blocks, :] = (
                total * first[here, blocks : 2 * blocks, :]
            )
    west, east, other = neighbours(n_lon, n_lat)

    def shared(owner, row, count):
        return second[pl.ds(owner * deep + 4 * blocks + row, count), :]

    far = jnp.concatenate([shared(west, 0, half), shared(east, 0, half)], 0)
    rise = jnp.where(west_rows(), lam_sides[...] - far, far - lam_sides[...])
    adj = faces[GAIN] + faces[RATIO] * rise
    put[...] = put_sides(adj, [(slope_ratio, -slope_ratio), (0.0, 1.0)])
    rise = shared(other, 0, 1) - lam_edge[...]
    adj_l = lat_lines[G_L : G_L + 1, :] + lat_lines[C_L : C_L + 1, :] * jnp.where(
        lat == 0, rise, -rise
    )
    from_north = jnp.where(lat == 0, adj_l, 0.0)
    from_south = jnp.where(lat == 1, adj_l, 0.0)
    put[0:1, :LANES] = put[0:1, :LANES] + slope_ratio * from_south
    put[rows - 1 : rows, :LANES] = put[rows - 1 : rows, :LANES] - slope_ratio * from_north
    north_line[...] = from_north
    green_spread(green, coarse, lambda k: loads[k : k + 1, :], acc, tables, pot)
    for start in range(0, rows, STEP_ROWS):
        at = slice(start, start + STEP_ROWS)
        lam_out[at, :] = ocean[at, :].astype(f32) * (
            held[at, :] + put[at, :LANES] - attract_coef * pot[at, :]
        )
    copy.wait()
    potential = sum_lanes(green_rows(top, 0, lambda k: loads[k : k + 1, :]))[0:1]
    diagonal = lambda owner: shared(owner + 1 - 2 * lat, 0, 1)
    lam_n = shared(other, 0, 1)
    lane = iota((1, LANES), 1)
    rise = jnp.where(
        lane == 0, lam_n - roll_west(diagonal(west)), roll_east(diagonal(east)) - lam_n
    )
    adj = shared(other, 2, 1) + shared(other, 3, 1) * rise
    flow = jnp.where(lane == 0, adj, jnp.where(lane == LANES - 1, -adj, 0.0)) + adj_l
    lam_north = lat_lines[MASK_L : MASK_L + 1, :] * (
        shared(other, 1, 1) + slope_ratio * flow - attract_coef * potential
    )
    span = rows // n_lon
    for target in range(n_lon):
        start = target * (span + 1)
        payload[start : start + span, :] = lam_out[target * span : (target + 1) * span, :]
        if target < n_lon - 1:
            stop = (target + 1) * span
            payload[start + span : start + span + 1, :] = lam_out[stop : stop + 1, :]
        else:
            payload[start + span : start + span + 1, :] = lam_north


def bands_kernel(
    parts, lam, adj_u, adj_v, put, north_line,
    lam_out, east_out, north_out, bands, east, north, planes, done, *, count,
):
    span = parts.shape[0] // count - 1
    rows = lam.shape[0]
    copies = [
        pltpu.make_async_copy(lam, lam_out, done.at[0]),
        pltpu.make_async_copy(east, east_out, done.at[1]),
        pltpu.make_async_copy(north, north_out, done.at[2]),
    ] + [
        pltpu.make_async_copy(planes.at[k], bands.at[k, 0], done.at[3 + k]) for k in range(3)
    ]
    copies[0].start()
    lane = iota((span, LANES), 1)
    top = (lax.axis_index("lat") == 1) & (lax.axis_index("lon") == count - 1)
    last = (iota((span, LANES), 0) == span - 1) & top
    for k in range(count):
        start = k * (span + 1)
        planes[0, :, k * LANES : (k + 1) * LANES] = parts[start : start + span, :]
    copies[3].start()
    for k in range(count):
        start = k * (span + 1)
        here = parts[start : start + span, :]
        north_of = jnp.where(last, 0.0, parts[start + 1 : start + 1 + span, :])
        planes[2, :, k * LANES : (k + 1) * LANES] = north_of - here
    copies[5].start()
    for k in range(count):
        at = slice(k * LANES, (k + 1) * LANES)
        here = planes[0, :, at]
        after = (k + 1) % count
        there = planes[0, :, after * LANES : (after + 1) * LANES]
        planes[1, :, at] = jnp.where(lane == LANES - 1, roll_east(there), roll_east(here)) - here
    copies[4].start()
    east[...] = adj_u[...] + put[:, LANES:]
    copies[1].start()
    north[...] = adj_v[...]
    north[rows - 1 : rows, :] = adj_v[rows - 1 : rows, :] + north_line[...]
    copies[2].start()
    for copy in copies:
        copy.wait()


def call(kernel, shapes, scratch, args, name, far=(), far_out=(), limit=16, weight=4):
    vmem = pl.BlockSpec(memory_space=pltpu.VMEM)
    away = pl.BlockSpec(memory_space=pl.ANY)
    shapes = [(shape, f32) if isinstance(shape[0], int) else shape for shape in shapes]
    return pl.pallas_call(
        kernel,
        out_shape=[jax.ShapeDtypeStruct(shape, kind) for shape, kind in shapes],
        in_specs=[away if k in far else vmem for k in range(len(args))],
        out_specs=[away if k in far_out else vmem for k in range(len(shapes))],
        scratch_shapes=scratch,
        compiler_params=pltpu.CompilerParams(vmem_limit_bytes=limit << 20),
        cost_estimate=pl.CostEstimate(flops=weight << 30, bytes_accessed=16 << 20, transcendentals=0),
        name=name,
    )(*args)


def body(n_lon, n_lat, lam_in, flux_east, flux_north, depth, drag, ocean, coarse_of, green):
    rows, cols = lam_in.shape
    points = green.shape[0]
    blocks = points // LANES
    owners = n_lon * n_lat
    grid = (rows, cols)
    fields = (lam_in, flux_east, flux_north, depth, drag, ocean, coarse_of)
    tall = rows // LANES
    to_east, to_west, to_lat, *fields = call(
        functools.partial(pack_kernel, points=points),
        [(6 * tall, cols), (6 * tall, cols), (8, cols)]
        + [(grid, field.dtype) for field in fields],
        [pltpu.SemaphoreType.DMA((7,))], fields, "pack", far=range(7), limit=52,
    )
    ocean, coarse_of = fields[5:]
    forward = [(k, (k + 1) % n_lon) for k in range(n_lon)]
    backward = [(target, source) for source, target in forward]
    from_west = lax.ppermute(to_east, "lon", forward)
    from_east = lax.ppermute(to_west, "lon", backward)
    from_lat = lax.ppermute(to_lat, "lat", [(0, 1), (1, 0)])
    held, gu, cu, gv, cv, sums, left, right, held_sides, green_top = call(
        functools.partial(inner_kernel, points=points),
        [grid] * 5
        + [((PIECES + 1) * HIGH, LOW), ((HIGH, rows * cols), bf16), ((LOW, rows * cols), bf16)]
        + [(2 * tall, cols), (LANES, green.shape[1])],
        [pltpu.VMEM(grid, f32), pltpu.SemaphoreType.DMA(())], (*fields, green), "inner",
        far=(7,), limit=INNER_LIMIT,
    )
    green_top, from_west, from_east, from_lat = lax.optimization_barrier(
        (green_top, from_west, from_east, from_lat)
    )
    green_north = lax.ppermute(green_top, "lat", [(0, 1), (1, 0)])
    payload, faces, lat_lines = call(
        functools.partial(rim_kernel, points=points),
        [(owners, 8, LANES), (7, 2 * tall, cols), (8, cols)], [],
        (to_east, to_west, to_lat, from_west, from_east, from_lat, sums, held_sides), "rim",
        weight=16,
    )
    first = lax.all_to_all(payload, ("lon", "lat"), 0, 0, tiled=True)
    deep = 4 * blocks + tall
    green_scratch = [
        pltpu.VMEM((LANES, LANES), f32),
        pltpu.VMEM((blocks, 8, LANES), f32),
        pltpu.VMEM(grid, f32),
    ]
    payload, held, adj_u, adj_v, lam_sides, lam_edge = call(
        functools.partial(second_kernel, points=points, n_lon=n_lon, n_lat=n_lat),
        [(owners * deep, LANES), grid, grid, grid, (2 * tall, cols), (1, cols)],
        green_scratch + [pltpu.VMEM((rows + 8, cols), f32), pltpu.VMEM(grid, f32)],
        (first, green, coarse_of, ocean, held, gu, cu, gv, cv, left, right, faces, lat_lines),
        "second",
    )
    second = lax.all_to_all(
        payload.reshape(owners, deep, 1, LANES), ("lon", "lat"), 0, 0, tiled=True
    ).reshape(payload.shape)
    span = rows // n_lon
    lam, payload, put, north_line = call(
        functools.partial(last_kernel, points=points, n_lon=n_lon, n_lat=n_lat),
        [grid, (rows + n_lon, cols), (rows, 2 * cols), (1, cols)],
        [
            pltpu.VMEM((owners * blocks, LANES), f32),
            pltpu.VMEM(green_top.shape, f32),
            pltpu.SemaphoreType.DMA(()),
        ]
        + green_scratch,
        (
            first, second, green, green_north, coarse_of, ocean, held, faces, lat_lines,
            lam_sides, lam_edge,
        ),
        "last", far=(3,),
    )
    parts = lax.all_to_all(
        payload.reshape(n_lon, span + 1, 1, LANES), "lon", 0, 0, tiled=True
    ).reshape(payload.shape)
    return tuple(
        call(
            functools.partial(bands_kernel, count=n_lon),
            [grid, grid, grid, (3, 1, span, n_lon * cols)],
            [
                pltpu.VMEM(grid, f32),
                pltpu.VMEM(grid, f32),
                pltpu.VMEM((3, span, n_lon * cols), f32),
                pltpu.SemaphoreType.DMA((6,)),
            ],
            (parts, lam, adj_u, adj_v, put, north_line), "bands", far_out=range(4),
        )
    )


def solution(mesh):
    cells = P(("groups", "lat"), "lon")
    n_lon, n_lat = mesh.shape["lon"], mesh.shape["lat"]
    return jax.shard_map(
        functools.partial(body, n_lon, n_lat),
        mesh=mesh,
        in_specs=(cells,) * 6 + (P("lat", "lon"), P(("lon", "lat"), None)),
        out_specs=(cells,) * 3 + (P(None, ("groups", "lat"), "lon", None),),
        check_vma=False,
    )
```

```python
import functools

import jax
import jax.numpy as jnp
from jax import lax
from jax.experimental import pallas as pl
from jax.experimental.pallas import tpu as pltpu
from jax.sharding import PartitionSpec as P

f32 = jnp.float32
bf16 = jnp.bfloat16
i32 = jnp.int32

LANES = 128
LOW = 32
HIGH = 16
PIECES = 2
INNER_LIMIT = 36
SEG_ROWS = 256
STEP_ROWS = 128

flux_ratio = 0.25
slope_ratio = 0.25
drag_step = 1.0
attract_coef = 0.5

LAM, DEPTH, DRAG, OCEAN, POINT, FLUX = range(6)
ADJ, RATIO, GAIN, BASE, MASK, OWN_ID, FAR_ID = range(7)
ADJ_L, C_L, G_L, ID_L, OWN_L, MASK_L = range(6)


def iota(shape, dim):
    return lax.broadcasted_iota(i32, shape, dim)


def roll_east(x):
    return pltpu.roll(x, LANES - 1, 1)


def roll_west(x):
    return pltpu.roll(x, 1, 1)


def local_ids(ids, points):
    return lax.bitwise_and(ids, points - 1)


def bf16_pieces(values, count=PIECES):
    out = []
    for piece in range(count):
        top = values.astype(bf16).astype(f32)
        out.append(top)
        if piece < count - 1:
            values = values - top
    return out


def one_hots(ids, points):
    blocks = points // LANES
    high = lax.shift_right_logical(ids, 5)
    high = lax.bitwise_and(high, 3) * blocks + lax.shift_right_logical(high, 2)
    low = lax.bitwise_and(ids, LOW - 1)
    high_iota = iota((HIGH, LANES), 0)
    low_iota = iota((LOW, LANES), 0)
    left, right = [], []
    for row in range(ids.shape[0]):
        mask = jnp.broadcast_to(high[row : row + 1], (HIGH, LANES)) == high_iota
        left.append(jnp.where(mask, 1.0, 0.0).astype(bf16))
        mask = jnp.broadcast_to(low[row : row + 1], (LOW, LANES)) == low_iota
        right.append(jnp.where(mask, 1.0, 0.0).astype(bf16))
    return jnp.concatenate(left, 1), jnp.concatenate(right, 1)


def segment_part(values, left, right, with_counts=False):
    parts = []
    for piece in bf16_pieces(values):
        line = jnp.concatenate(
            [
                jnp.broadcast_to(piece[row : row + 1], (HIGH, LANES)).astype(bf16)
                for row in range(values.shape[0])
            ],
            1,
        )
        parts.append(left * line)
    if with_counts:
        parts.append(left)
    return lax.dot_general(
        jnp.concatenate(parts, 0), right, (((1,), (1,)), ((), ())), preferred_element_type=f32
    )


def segment_few(values, ids, points):
    return sum_pieces(segment_part(values, *one_hots(ids, points)))


def sum_pieces(parts):
    total = parts[:HIGH]
    for piece in range(1, PIECES):
        total = total + parts[piece * HIGH : (piece + 1) * HIGH]
    return total


def as_points(table, points):
    blocks = points // LANES
    return jnp.concatenate([table[q * blocks : (q + 1) * blocks] for q in range(4)], 1)


def fold(line):
    return jnp.concatenate(
        [line[:, k * LANES : (k + 1) * LANES] for k in range(line.shape[1] // LANES)], 0
    )


def unfold(block):
    return jnp.concatenate([block[k : k + 1] for k in range(block.shape[0])], 1)


def take_sides(block, count=3):
    sub, lane = iota((8, LANES), 0), iota((8, LANES), 1)
    pick = ((sub == 0) & (lane == 0)) | ((sub == 1) & (lane == LANES - 1))
    pick = pick.astype(f32).astype(bf16)
    out = None
    for piece in reversed(bf16_pieces(block, count)):
        part = lax.dot_general(
            pick, piece.astype(bf16), (((1,), (1,)), ((), ())), preferred_element_type=f32
        )
        out = part if out is None else out + part
    return out


def put_sides(pair, entries):
    half = pair.shape[0] // 2
    lines = jnp.concatenate([unfold(pair[:half]), unfold(pair[half:])], 0)
    rows = lines.shape[1]
    pieces = bf16_pieces(lines, 3)
    stack = jnp.concatenate(pieces + [jnp.zeros((2, rows), f32)], 0)
    sub, lane = iota((8, LANES), 0), iota((8, LANES), 1)
    west = (sub < 6) & (lax.bitwise_and(sub, 1) == 0) & (lane == 0)
    east = (sub < 6) & (lax.bitwise_and(sub, 1) == 1) & (lane == LANES - 1)
    picks = [jnp.where(west, first, jnp.where(east, last, 0.0)) for first, last in entries]
    return lax.dot_general(
        stack, jnp.concatenate(picks, 1), (((0,), (0,)), ((), ())), preferred_element_type=f32
    )


def sum_lanes(block):
    out = None
    for piece in reversed(bf16_pieces(block, 3)):
        part = lax.dot_general(
            jnp.ones((8, LANES), bf16), piece.astype(bf16), (((1,), (1,)), ((), ())),
            preferred_element_type=f32,
        )
        out = part if out is None else out + part
    return out


def green_rows(green_ref, start, load_row):
    acc = jnp.zeros((LANES, LANES), f32)
    for k in range(green_ref.shape[1] // LANES):
        acc = acc + green_ref[
            pl.ds(start, LANES), k * LANES : (k + 1) * LANES
        ] * jnp.broadcast_to(load_row(k), (LANES, LANES))
    return acc


def look_up(table, ids):
    rows = ids.shape[0]
    table = jnp.broadcast_to(table[None], (rows // 8, 8, LANES)).reshape(rows, LANES)
    return jnp.take_along_axis(table, ids, axis=1, mode="promise_in_bounds")


def spread(tables, ids):
    low = lax.bitwise_and(ids, LANES - 1)
    block = lax.shift_right_logical(ids, 7)
    out = None
    for k, table in enumerate(tables):
        value = look_up(table, low)
        out = value if out is None else jnp.where(block == k, value, out)
    return out


def green_spread(green, coarse, load_row, acc, tables, pot):
    points = green.shape[0]
    rows = coarse.shape[0]

    def settle(index):
        table = sum_lanes(acc[...])
        tables[index] = table
        for start in range(0, rows, STEP_ROWS):
            at = slice(start, start + STEP_ROWS)
            ids = local_ids(coarse[at, :], points)
            value = look_up(table, lax.bitwise_and(ids, LANES - 1))
            pot[at, :] = jnp.where(lax.shift_right_logical(ids, 7) == index, value, pot[at, :])

    def step(index, carry):
        block = green_rows(green, index * LANES, load_row)
        settle(index - 1)
        acc[...] = block
        return carry

    acc[...] = green_rows(green, 0, load_row)
    for index in range(1, points // LANES):
        step(index, 0)
    settle(points // LANES - 1)


def next_rows(ref, start, count):
    if start + count < ref.shape[0]:
        return ref[start + 1 : start + count + 1, :]
    return jnp.concatenate([ref[start + 1 :, :], jnp.zeros((1, LANES), ref.dtype)], 0)


def south_rows(first, block):
    return jnp.concatenate([first, block[:-1]], 0)


def pack_kernel(*refs, points):
    far, (to_east, to_west, to_lat), near, done = refs[:7], refs[7:10], refs[10:17], refs[17]
    copies = [pltpu.make_async_copy(far[k], near[k], done.at[k]) for k in range(7)]
    for copy in copies:
        copy.start()
    lam, east, north, depth, drag, ocean, coarse = near
    rows = lam.shape[0]
    tall = rows // LANES
    lat = lax.axis_index("lat")
    order = (
        (LAM, 0, lam, 3), (FLUX, 1, east, 3), (None, 2, north, 0), (DEPTH, 3, depth, 3),
        (DRAG, 4, drag, 3), (OCEAN, 5, ocean, 1), (POINT, 6, coarse, 2),
    )
    for field, index, ref, pieces in order:
        copies[index].wait()
        if field is None:
            continue
        block = ref[...]
        if field == POINT:
            block = local_ids(block, points)
        sides = take_sides(block.astype(f32), pieces)
        at = slice(field * tall, (field + 1) * tall)
        to_west[at, :] = fold(sides[0:1])
        to_east[at, :] = fold(sides[1:2])

    def border(row):
        return jnp.concatenate(
            [
                lam[row : row + 1, :],
                depth[row : row + 1, :],
                drag[row : row + 1, :],
                ocean[row : row + 1, :].astype(f32),
                local_ids(coarse[row : row + 1, :], points).astype(f32),
                north[row : row + 1, :],
                jnp.zeros((2, LANES), f32),
            ],
            0,
        )

    to_lat[...] = jnp.where(lat == 0, border(rows - 1), border(0))


def inner_kernel(
    lam, east, north, depth, drag, ocean, coarse, green,
    held, gu, cu, gv, cv, sums, left, right, held_sides, green_top, source, top, done, *, points,
):
    tall = LANES // 4
    parts = [pl.ds(k * tall, tall) for k in range(4)]
    inward = [
        pltpu.make_async_copy(green.at[part], top.at[part], done.at[k])
        for k, part in enumerate(parts)
    ]
    outward = [
        pltpu.make_async_copy(top.at[part], green_top.at[part], done.at[4 + k])
        for k, part in enumerate(parts)
    ]
    for copy in inward:
        copy.start()

    def pass_on(which):
        for k in which:
            inward[k].wait()
            outward[k].start()

    rows = lam.shape[0]
    inner = iota((STEP_ROWS, LANES), 1) < LANES - 1
    carry = jnp.zeros((1, LANES), f32)
    for start in range(0, rows, STEP_ROWS):
        at = slice(start, start + STEP_ROWS)
        lam_c, depth_c, drag_c = lam[at, :], depth[at, :], drag[at, :]
        ocean_c = ocean[at, :].astype(f32)
        damp = jnp.where(
            inner,
            ocean_c * roll_east(ocean_c) / (1.0 + drag_step * 0.5 * (drag_c + roll_east(drag_c))),
            0.0,
        )
        ratio = damp * (flux_ratio * 0.5) * (depth_c + roll_east(depth_c))
        adj_u = damp * east[at, :] + ratio * (roll_east(lam_c) - lam_c)
        cu[at, :] = ratio
        gu[at, :] = damp * adj_u
        ocean_n = next_rows(ocean, start, STEP_ROWS).astype(f32)
        damp = (
            ocean_c
            * ocean_n
            / (1.0 + drag_step * 0.5 * (drag_c + next_rows(drag, start, STEP_ROWS)))
        )
        ratio = damp * (flux_ratio * 0.5) * (depth_c + next_rows(depth, start, STEP_ROWS))
        adj_v = damp * north[at, :] + ratio * (next_rows(lam, start, STEP_ROWS) - lam_c)
        cv[at, :] = ratio
        gv[at, :] = damp * adj_v
        src = slope_ratio * (roll_west(adj_u) - adj_u + south_rows(carry, adj_v) - adj_v)
        carry = adj_v[STEP_ROWS - 1 :]
        source[at, :] = src
        held[at, :] = lam_c + src
    pass_on((0, 1))
    total = jnp.zeros(sums.shape, f32)
    for start in range(0, rows, SEG_ROWS):
        if start == SEG_ROWS:
            pass_on((2, 3))
        at = slice(start, start + SEG_ROWS)
        cells = slice(start * LANES, (start + SEG_ROWS) * LANES)
        high, low = one_hots(local_ids(coarse[at, :], points), points)
        left[:, cells] = high
        right[:, cells] = low
        total = total + segment_part(source[at, :], high, low, True)
    sums[...] = total
    sides = take_sides(held[...])
    held_sides[...] = jnp.concatenate([fold(sides[0:1]), fold(sides[1:2])], 0)
    for copy in outward:
        copy.wait()


def face(low, high, flux):
    damp = low[OCEAN] * high[OCEAN] / (1.0 + drag_step * 0.5 * (low[DRAG] + high[DRAG]))
    ratio = damp * (flux_ratio * 0.5) * (low[DEPTH] + high[DEPTH])
    adj = damp * flux + ratio * (high[LAM] - low[LAM])
    return adj, ratio, damp * adj


def west_rows():
    return iota((8, LANES), 0) < 4


def rim_kernel(
    own_east, own_west, own_lat, from_west, from_east, from_lat, sums, held_sides,
    payload, faces, lat_lines, *, points,
):
    lat = lax.axis_index("lat")
    half = held_sides.shape[0] // 2

    def pair(west, east):
        return [
            jnp.concatenate(
                [west[k * half : (k + 1) * half, :], east[k * half : (k + 1) * half, :]], 0
            )
            for k in range(6)
        ]

    own, far = pair(own_west, own_east), pair(from_west, from_east)
    is_west = west_rows()
    low = [jnp.where(is_west, there, here) for here, there in zip(own, far)]
    high = [jnp.where(is_west, here, there) for here, there in zip(own, far)]
    adj, ratio, gain = face(low, high, low[FLUX])
    mine, other = own_lat[...], from_lat[...]
    lower = jnp.where(lat == 0, mine, other)
    upper = jnp.where(lat == 0, other, mine)
    lower = [lower[k : k + 1] for k in range(6)]
    upper = [upper[k : k + 1] for k in range(6)]
    adj_l, c_l, g_l = face(lower, upper, lower[FLUX])
    lat_lines[...] = jnp.concatenate(
        [
            adj_l, c_l, g_l, other[POINT : POINT + 1], mine[POINT : POINT + 1],
            other[OCEAN : OCEAN + 1], jnp.zeros((2, LANES), f32),
        ],
        0,
    )
    sign = jnp.where(is_west, slope_ratio, -slope_ratio)
    sign_l = jnp.where(lat == 0, -slope_ratio, slope_ratio)
    flow = sign * adj
    sub, lane = lax.bitwise_and(iota((8, LANES), 0), half - 1), iota((8, LANES), 1)
    corner = ((lat == 0) & (sub == half - 1) & (lane == LANES - 1)) | (
        (lat == 1) & (sub == 0) & (lane == 0)
    )
    at_corner = jnp.where(
        is_west,
        jnp.broadcast_to(adj_l[:, 0:1], (8, LANES)),
        jnp.broadcast_to(adj_l[:, LANES - 1 :], (8, LANES)),
    )
    faces[ADJ] = adj
    faces[RATIO] = ratio
    faces[GAIN] = gain
    faces[BASE] = held_sides[...] + flow + jnp.where(corner, sign_l * at_corner, 0.0)
    faces[MASK] = own[OCEAN]
    faces[OWN_ID] = own[POINT]
    faces[FAR_ID] = far[POINT]
    pad = jnp.zeros((1, LANES), f32)
    values = jnp.concatenate([flow, sign_l * adj_l, pad], 0)
    ids = jnp.concatenate([own[POINT], mine[POINT : POINT + 1], pad], 0).astype(i32)
    total = sum_pieces(sums[...]) + segment_few(values, ids, points)
    counts = as_points(sums[PIECES * HIGH : (PIECES + 1) * HIGH, :], points)
    inverse = 1.0 / counts
    loads = as_points(total, points) * inverse
    part = jnp.concatenate([loads, inverse], 0)
    if part.shape[0] < 8:
        part = jnp.concatenate([part, jnp.zeros((8 - part.shape[0], LANES), f32)], 0)
    for target in range(payload.shape[0]):
        payload[target] = part


def neighbours(n_lon, n_lat):
    lon, lat = lax.axis_index("lon"), lax.axis_index("lat")
    west = lax.rem(lon + n_lon - 1, n_lon) * n_lat + lat
    east = lax.rem(lon + 1, n_lon) * n_lat + lat
    other = lon * n_lat + (1 - lat)
    return west, east, other


def second_kernel(
    first, green, coarse, ocean, held_in, gu, cu, gv, cv, left, right, faces, lat_lines,
    payload, held, adj_u_out, adj_v_out, lam_sides, lam_edge, acc, tables, pot, lam, source,
    *, points, n_lon, n_lat,
):
    rows = coarse.shape[0]
    blocks = points // LANES
    lat = lax.axis_index("lat")
    south_end = jnp.where(lat == 1, 1.0, 0.0)
    north_end = jnp.where(lat == 0, 1.0, 0.0)
    green_spread(
        green, coarse, lambda k: first[k // blocks, k % blocks : k % blocks + 1, :],
        acc, tables, pot,
    )
    put = put_sides(faces[ADJ], [(slope_ratio, -slope_ratio)])
    adj_l = lat_lines[ADJ_L : ADJ_L + 1, :]
    c_l = lat_lines[C_L : C_L + 1, :]
    g_l = lat_lines[G_L : G_L + 1, :]
    row = iota((STEP_ROWS, LANES), 0)
    lam[rows : rows + 8, :] = jnp.zeros((8, LANES), f32)
    for start in range(0, rows, STEP_ROWS):
        at = slice(start, start + STEP_ROWS)
        value = held_in[at, :] + put[at, :] - attract_coef * pot[at, :]
        if start == 0:
            value = value + jnp.where(row == 0, south_end * slope_ratio * adj_l, 0.0)
        if start == rows - STEP_ROWS:
            value = value - jnp.where(row == STEP_ROWS - 1, north_end * slope_ratio * adj_l, 0.0)
        lam[at, :] = ocean[at, :].astype(f32) * value
    carry = jnp.zeros((1, LANES), f32)
    for start in range(0, rows, STEP_ROWS):
        at = slice(start, start + STEP_ROWS)
        lam_c = lam[at, :]
        adj_u = gu[at, :] + cu[at, :] * (roll_east(lam_c) - lam_c)
        adj_v = gv[at, :] + cv[at, :] * (lam[start + 1 : start + STEP_ROWS + 1, :] - lam_c)
        src = slope_ratio * (roll_west(adj_u) - adj_u + south_rows(carry, adj_v) - adj_v)
        carry = adj_v[STEP_ROWS - 1 :]
        adj_u_out[at, :] = adj_u
        adj_v_out[at, :] = adj_v
        source[at, :] = src
        held[at, :] = lam_c + src
    is_west = west_rows()
    sides = faces[MASK] * (
        faces[BASE]
        - attract_coef * spread([tables[k] for k in range(blocks)], faces[OWN_ID].astype(i32))
    )
    lam_sides[...] = sides
    pull = faces[RATIO] * sides
    flow = slope_ratio * jnp.where(is_west, pull, pull - faces[GAIN])
    edge = jnp.where(lat == 0, lam[rows - 1 : rows, :], lam[0:1, :])
    lam_edge[...] = edge
    pull = c_l * edge
    flow_l = slope_ratio * jnp.where(lat == 0, pull - g_l, pull)
    pad = jnp.zeros((1, LANES), f32)
    total = segment_part(
        jnp.concatenate([flow, flow_l, pad], 0),
        *one_hots(
            jnp.concatenate([faces[OWN_ID], lat_lines[OWN_L : OWN_L + 1, :], pad], 0).astype(i32),
            points,
        ),
    )
    def add(index, total):
        at = pl.ds(pl.multiple_of(index * SEG_ROWS, SEG_ROWS), SEG_ROWS)
        cells = pl.ds(pl.multiple_of(index * SEG_ROWS * LANES, SEG_ROWS * LANES), SEG_ROWS * LANES)
        return total + segment_part(source[at, :], left[:, cells], right[:, cells])

    total = lax.fori_loop(0, rows // SEG_ROWS, add, total)
    own = as_points(sum_pieces(total), points)
    far_id = faces[FAR_ID].astype(i32)
    half = far_id.shape[0] // 2

    def away(values, ids):
        return as_points(segment_few(-values, ids, points), points)

    west_part = away(flow[:half], far_id[:half])
    east_part = away(flow[half:], far_id[half:])
    lat_part = away(
        jnp.concatenate([flow_l, pad], 0),
        jnp.concatenate([lat_lines[ID_L : ID_L + 1, :], pad], 0).astype(i32),
    )
    west, east, other = neighbours(n_lon, n_lat)
    part = jnp.concatenate([own, east_part, west_part, lat_part], 0)
    begin = 4 * blocks
    deep = begin + half
    first_lane = iota((1, LANES), 1) == 0

    def corners(block):
        return jnp.where(
            first_lane,
            block[0:1],
            jnp.broadcast_to(block[half : half + 1, 0:1], (1, LANES)),
        )

    edge_rows = jnp.concatenate(
        [edge, held[0:1, :], corners(faces[GAIN]), corners(faces[RATIO])]
        + [jnp.zeros((1, LANES), f32)] * (half - 4),
        0,
    )
    for target in range(n_lon * n_lat):
        shared = jnp.where(
            target == west, sides[:half], jnp.where(target == east, sides[half:], edge_rows)
        )
        payload[target * deep : (target + 1) * deep, :] = jnp.concatenate([part, shared], 0)


def last_kernel(
    first, second, green, green_north, coarse, ocean, held, faces, lat_lines, lam_sides, lam_edge,
    lam_out, payload, put, north_line, loads, top, done, acc, tables, pot,
    *, points, n_lon, n_lat,
):
    copy = pltpu.make_async_copy(green_north, top, done)
    copy.start()
    rows = held.shape[0]
    blocks = points // LANES
    half = rows // LANES
    deep = 4 * blocks + half
    lat = lax.axis_index("lat")

    def received(owner, kind):
        start = owner * deep + kind * blocks
        return second[start : start + blocks, :]

    for lon in range(n_lon):
        for band in range(n_lat):
            here = lon * n_lat + band
            west = (lon - 1) % n_lon * n_lat + band
            east = (lon + 1) % n_lon * n_lat + band
            other = lon * n_lat + 1 - band
            total = received(here, 0) + received(west, 1) + received(east, 2) + received(other, 3)
            loads[here * blocks : (here + 1) * blocks, :] = (
                total * first[here, blocks : 2 * blocks, :]
            )
    west, east, other = neighbours(n_lon, n_lat)

    def shared(owner, row, count):
        return second[pl.ds(owner * deep + 4 * blocks + row, count), :]

    far = jnp.concatenate([shared(west, 0, half), shared(east, 0, half)], 0)
    rise = jnp.where(west_rows(), lam_sides[...] - far, far - lam_sides[...])
    adj = faces[GAIN] + faces[RATIO] * rise
    put[...] = put_sides(adj, [(slope_ratio, -slope_ratio), (0.0, 1.0)])
    rise = shared(other, 0, 1) - lam_edge[...]
    adj_l = lat_lines[G_L : G_L + 1, :] + lat_lines[C_L : C_L + 1, :] * jnp.where(
        lat == 0, rise, -rise
    )
    from_north = jnp.where(lat == 0, adj_l, 0.0)
    from_south = jnp.where(lat == 1, adj_l, 0.0)
    put[0:1, :LANES] = put[0:1, :LANES] + slope_ratio * from_south
    put[rows - 1 : rows, :LANES] = put[rows - 1 : rows, :LANES] - slope_ratio * from_north
    north_line[...] = from_north
    green_spread(green, coarse, lambda k: loads[k : k + 1, :], acc, tables, pot)
    for start in range(0, rows, STEP_ROWS):
        at = slice(start, start + STEP_ROWS)
        lam_out[at, :] = ocean[at, :].astype(f32) * (
            held[at, :] + put[at, :LANES] - attract_coef * pot[at, :]
        )
    copy.wait()
    potential = sum_lanes(green_rows(top, 0, lambda k: loads[k : k + 1, :]))[0:1]
    diagonal = lambda owner: shared(owner + 1 - 2 * lat, 0, 1)
    lam_n = shared(other, 0, 1)
    lane = iota((1, LANES), 1)
    rise = jnp.where(
        lane == 0, lam_n - roll_west(diagonal(west)), roll_east(diagonal(east)) - lam_n
    )
    adj = shared(other, 2, 1) + shared(other, 3, 1) * rise
    flow = jnp.where(lane == 0, adj, jnp.where(lane == LANES - 1, -adj, 0.0)) + adj_l
    lam_north = lat_lines[MASK_L : MASK_L + 1, :] * (
        shared(other, 1, 1) + slope_ratio * flow - attract_coef * potential
    )
    span = rows // n_lon
    for target in range(n_lon):
        start = target * (span + 1)
        payload[start : start + span, :] = lam_out[target * span : (target + 1) * span, :]
        if target < n_lon - 1:
            stop = (target + 1) * span
            payload[start + span : start + span + 1, :] = lam_out[stop : stop + 1, :]
        else:
            payload[start + span : start + span + 1, :] = lam_north


def bands_kernel(
    parts, lam, adj_u, adj_v, put, north_line,
    lam_out, east_out, north_out, bands, east, north, planes, done, *, count,
):
    span = parts.shape[0] // count - 1
    rows = lam.shape[0]
    copies = [
        pltpu.make_async_copy(lam, lam_out, done.at[0]),
        pltpu.make_async_copy(east, east_out, done.at[1]),
        pltpu.make_async_copy(north, north_out, done.at[2]),
    ] + [
        pltpu.make_async_copy(planes.at[k], bands.at[k, 0], done.at[3 + k]) for k in range(3)
    ]
    copies[0].start()
    lane = iota((span, LANES), 1)
    top = (lax.axis_index("lat") == 1) & (lax.axis_index("lon") == count - 1)
    last = (iota((span, LANES), 0) == span - 1) & top
    for k in range(count):
        start = k * (span + 1)
        planes[0, :, k * LANES : (k + 1) * LANES] = parts[start : start + span, :]
    copies[3].start()
    for k in range(count):
        start = k * (span + 1)
        here = parts[start : start + span, :]
        north_of = jnp.where(last, 0.0, parts[start + 1 : start + 1 + span, :])
        planes[2, :, k * LANES : (k + 1) * LANES] = north_of - here
    copies[5].start()
    for k in range(count):
        at = slice(k * LANES, (k + 1) * LANES)
        here = planes[0, :, at]
        after = (k + 1) % count
        there = planes[0, :, after * LANES : (after + 1) * LANES]
        planes[1, :, at] = jnp.where(lane == LANES - 1, roll_east(there), roll_east(here)) - here
    copies[4].start()
    east[...] = adj_u[...] + put[:, LANES:]
    copies[1].start()
    north[...] = adj_v[...]
    north[rows - 1 : rows, :] = adj_v[rows - 1 : rows, :] + north_line[...]
    copies[2].start()
    for copy in copies:
        copy.wait()


def call(kernel, shapes, scratch, args, name, far=(), far_out=(), limit=16, weight=4):
    vmem = pl.BlockSpec(memory_space=pltpu.VMEM)
    away = pl.BlockSpec(memory_space=pl.ANY)
    shapes = [(shape, f32) if isinstance(shape[0], int) else shape for shape in shapes]
    return pl.pallas_call(
        kernel,
        out_shape=[jax.ShapeDtypeStruct(shape, kind) for shape, kind in shapes],
        in_specs=[away if k in far else vmem for k in range(len(args))],
        out_specs=[away if k in far_out else vmem for k in range(len(shapes))],
        scratch_shapes=scratch,
        compiler_params=pltpu.CompilerParams(vmem_limit_bytes=limit << 20),
        cost_estimate=pl.CostEstimate(flops=weight << 30, bytes_accessed=16 << 20, transcendentals=0),
        name=name,
    )(*args)


def body(n_lon, n_lat, lam_in, flux_east, flux_north, depth, drag, ocean, coarse_of, green):
    rows, cols = lam_in.shape
    points = green.shape[0]
    blocks = points // LANES
    owners = n_lon * n_lat
    grid = (rows, cols)
    fields = (lam_in, flux_east, flux_north, depth, drag, ocean, coarse_of)
    tall = rows // LANES
    to_east, to_west, to_lat, *fields = call(
        functools.partial(pack_kernel, points=points),
        [(6 * tall, cols), (6 * tall, cols), (8, cols)]
        + [(grid, field.dtype) for field in fields],
        [pltpu.SemaphoreType.DMA((7,))], fields, "pack", far=range(7), limit=52,
    )
    ocean, coarse_of = fields[5:]
    forward = [(k, (k + 1) % n_lon) for k in range(n_lon)]
    backward = [(target, source) for source, target in forward]
    from_west = lax.ppermute(to_east, "lon", forward)
    from_east = lax.ppermute(to_west, "lon", backward)
    from_lat = lax.ppermute(to_lat, "lat", [(0, 1), (1, 0)])
    held, gu, cu, gv, cv, sums, left, right, held_sides, green_top = call(
        functools.partial(inner_kernel, points=points),
        [grid] * 5
        + [((PIECES + 1) * HIGH, LOW), ((HIGH, rows * cols), bf16), ((LOW, rows * cols), bf16)]
        + [(2 * tall, cols), (LANES, green.shape[1])],
        [
            pltpu.VMEM(grid, f32),
            pltpu.VMEM((LANES, green.shape[1]), f32),
            pltpu.SemaphoreType.DMA((8,)),
        ],
        (*fields, green), "inner", far=(7,), far_out=(9,), limit=INNER_LIMIT,
    )
    green_top, from_west, from_east, from_lat = lax.optimization_barrier(
        (green_top, from_west, from_east, from_lat)
    )
    green_north = lax.ppermute(green_top, "lat", [(0, 1), (1, 0)])
    payload, faces, lat_lines = call(
        functools.partial(rim_kernel, points=points),
        [(owners, 8, LANES), (7, 2 * tall, cols), (8, cols)], [],
        (to_east, to_west, to_lat, from_west, from_east, from_lat, sums, held_sides), "rim",
        weight=16,
    )
    first = lax.all_to_all(payload, ("lon", "lat"), 0, 0, tiled=True)
    deep = 4 * blocks + tall
    green_scratch = [
        pltpu.VMEM((LANES, LANES), f32),
        pltpu.VMEM((blocks, 8, LANES), f32),
        pltpu.VMEM(grid, f32),
    ]
    payload, held, adj_u, adj_v, lam_sides, lam_edge = call(
        functools.partial(second_kernel, points=points, n_lon=n_lon, n_lat=n_lat),
        [(owners * deep, LANES), grid, grid, grid, (2 * tall, cols), (1, cols)],
        green_scratch + [pltpu.VMEM((rows + 8, cols), f32), pltpu.VMEM(grid, f32)],
        (first, green, coarse_of, ocean, held, gu, cu, gv, cv, left, right, faces, lat_lines),
        "second",
    )
    second = lax.all_to_all(
        payload.reshape(owners, deep, 1, LANES), ("lon", "lat"), 0, 0, tiled=True
    ).reshape(payload.shape)
    span = rows // n_lon
    lam, payload, put, north_line = call(
        functools.partial(last_kernel, points=points, n_lon=n_lon, n_lat=n_lat),
        [grid, (rows + n_lon, cols), (rows, 2 * cols), (1, cols)],
        [
            pltpu.VMEM((owners * blocks, LANES), f32),
            pltpu.VMEM(green_top.shape, f32),
            pltpu.SemaphoreType.DMA(()),
        ]
        + green_scratch,
        (
            first, second, green, green_north, coarse_of, ocean, held, faces, lat_lines,
            lam_sides, lam_edge,
        ),
        "last", far=(3,),
    )
    parts = lax.all_to_all(
        payload.reshape(n_lon, span + 1, 1, LANES), "lon", 0, 0, tiled=True
    ).reshape(payload.shape)
    return tuple(
        call(
            functools.partial(bands_kernel, count=n_lon),
            [grid, grid, grid, (3, 1, span, n_lon * cols)],
            [
                pltpu.VMEM(grid, f32),
                pltpu.VMEM(grid, f32),
                pltpu.VMEM((3, span, n_lon * cols), f32),
                pltpu.SemaphoreType.DMA((6,)),
            ],
            (parts, lam, adj_u, adj_v, put, north_line), "bands", far_out=range(4),
        )
    )


def solution(mesh):
    cells = P(("groups", "lat"), "lon")
    n_lon, n_lat = mesh.shape["lon"], mesh.shape["lat"]
    return jax.shard_map(
        functools.partial(body, n_lon, n_lat),
        mesh=mesh,
        in_specs=(cells,) * 6 + (P("lat", "lon"), P(("lon", "lat"), None)),
        out_specs=(cells,) * 3 + (P(None, ("groups", "lat"), "lon", None),),
        check_vma=False,
    )
```

```python
import functools

import jax
import jax.numpy as jnp
from jax import lax
from jax.experimental import pallas as pl
from jax.experimental.pallas import tpu as pltpu
from jax.sharding import PartitionSpec as P

f32 = jnp.float32
bf16 = jnp.bfloat16
i32 = jnp.int32

LANES = 128
LOW = 32
HIGH = 16
PIECES = 2
INNER_LIMIT = 36
SEG_ROWS = 256
STEP_ROWS = 128

flux_ratio = 0.25
slope_ratio = 0.25
drag_step = 1.0
attract_coef = 0.5

LAM, DEPTH, DRAG, OCEAN, POINT, FLUX = range(6)
ADJ, RATIO, GAIN, BASE, MASK, OWN_ID, FAR_ID = range(7)
ADJ_L, C_L, G_L, ID_L, OWN_L, MASK_L = range(6)


def iota(shape, dim):
    return lax.broadcasted_iota(i32, shape, dim)


def roll_east(x):
    return pltpu.roll(x, LANES - 1, 1)


def roll_west(x):
    return pltpu.roll(x, 1, 1)


def local_ids(ids, points):
    return lax.bitwise_and(ids, points - 1)


def bf16_pieces(values, count=PIECES):
    out = []
    for piece in range(count):
        top = values.astype(bf16).astype(f32)
        out.append(top)
        if piece < count - 1:
            values = values - top
    return out


def one_hots(ids, points):
    blocks = points // LANES
    high = lax.shift_right_logical(ids, 5)
    high = lax.bitwise_and(high, 3) * blocks + lax.shift_right_logical(high, 2)
    low = lax.bitwise_and(ids, LOW - 1)
    high_iota = iota((HIGH, LANES), 0)
    low_iota = iota((LOW, LANES), 0)
    left, right = [], []
    for row in range(ids.shape[0]):
        mask = jnp.broadcast_to(high[row : row + 1], (HIGH, LANES)) == high_iota
        left.append(jnp.where(mask, 1.0, 0.0).astype(bf16))
        mask = jnp.broadcast_to(low[row : row + 1], (LOW, LANES)) == low_iota
        right.append(jnp.where(mask, 1.0, 0.0).astype(bf16))
    return jnp.concatenate(left, 1), jnp.concatenate(right, 1)


def segment_part(values, left, right, with_counts=False):
    parts = []
    for piece in bf16_pieces(values):
        line = jnp.concatenate(
            [
                jnp.broadcast_to(piece[row : row + 1], (HIGH, LANES)).astype(bf16)
                for row in range(values.shape[0])
            ],
            1,
        )
        parts.append(left * line)
    if with_counts:
        parts.append(left)
    return lax.dot_general(
        jnp.concatenate(parts, 0), right, (((1,), (1,)), ((), ())), preferred_element_type=f32
    )


def segment_few(values, ids, points):
    return sum_pieces(segment_part(values, *one_hots(ids, points)))


def sum_pieces(parts):
    total = parts[:HIGH]
    for piece in range(1, PIECES):
        total = total + parts[piece * HIGH : (piece + 1) * HIGH]
    return total


def as_points(table, points):
    blocks = points // LANES
    return jnp.concatenate([table[q * blocks : (q + 1) * blocks] for q in range(4)], 1)


def fold(line):
    return jnp.concatenate(
        [line[:, k * LANES : (k + 1) * LANES] for k in range(line.shape[1] // LANES)], 0
    )


def unfold(block):
    return jnp.concatenate([block[k : k + 1] for k in range(block.shape[0])], 1)


def take_sides(block, count=3):
    sub, lane = iota((8, LANES), 0), iota((8, LANES), 1)
    pick = ((sub == 0) & (lane == 0)) | ((sub == 1) & (lane == LANES - 1))
    pick = pick.astype(f32).astype(bf16)
    out = None
    for piece in reversed(bf16_pieces(block, count)):
        part = lax.dot_general(
            pick, piece.astype(bf16), (((1,), (1,)), ((), ())), preferred_element_type=f32
        )
        out = part if out is None else out + part
    return out


def put_sides(pair, entries):
    half = pair.shape[0] // 2
    lines = jnp.concatenate([unfold(pair[:half]), unfold(pair[half:])], 0)
    rows = lines.shape[1]
    pieces = bf16_pieces(lines, 3)
    stack = jnp.concatenate(pieces + [jnp.zeros((2, rows), f32)], 0)
    sub, lane = iota((8, LANES), 0), iota((8, LANES), 1)
    west = (sub < 6) & (lax.bitwise_and(sub, 1) == 0) & (lane == 0)
    east = (sub < 6) & (lax.bitwise_and(sub, 1) == 1) & (lane == LANES - 1)
    picks = [jnp.where(west, first, jnp.where(east, last, 0.0)) for first, last in entries]
    return lax.dot_general(
        stack, jnp.concatenate(picks, 1), (((0,), (0,)), ((), ())), preferred_element_type=f32
    )


def sum_lanes(block):
    out = None
    for piece in reversed(bf16_pieces(block, 3)):
        part = lax.dot_general(
            jnp.ones((8, LANES), bf16), piece.astype(bf16), (((1,), (1,)), ((), ())),
            preferred_element_type=f32,
        )
        out = part if out is None else out + part
    return out


def green_rows(green_ref, start, load_row):
    acc = jnp.zeros((LANES, LANES), f32)
    for k in range(green_ref.shape[1] // LANES):
        acc = acc + green_ref[
            pl.ds(start, LANES), k * LANES : (k + 1) * LANES
        ] * jnp.broadcast_to(load_row(k), (LANES, LANES))
    return acc


def look_up(table, ids):
    rows = ids.shape[0]
    table = jnp.broadcast_to(table[None], (rows // 8, 8, LANES)).reshape(rows, LANES)
    return jnp.take_along_axis(table, ids, axis=1, mode="promise_in_bounds")


def spread(tables, ids):
    low = lax.bitwise_and(ids, LANES - 1)
    block = lax.shift_right_logical(ids, 7)
    out = None
    for k, table in enumerate(tables):
        value = look_up(table, low)
        out = value if out is None else jnp.where(block == k, value, out)
    return out


def green_spread(green, coarse, load_row, acc, tables, pot, more=None):
    points = green.shape[0]
    rows = coarse.shape[0]

    def settle(index):
        table = sum_lanes(acc[...])
        tables[index] = table
        for start in range(0, rows, STEP_ROWS):
            at = slice(start, start + STEP_ROWS)
            ids = local_ids(coarse[at, :], points)
            value = look_up(table, lax.bitwise_and(ids, LANES - 1))
            pot[at, :] = jnp.where(lax.shift_right_logical(ids, 7) == index, value, pot[at, :])

    def step(index, carry):
        block = green_rows(green, index * LANES, load_row)
        settle(index - 1)
        acc[...] = block
        return carry

    acc[...] = green_rows(green, 0, load_row)
    for index in range(1, points // LANES):
        step(index, 0)
    beside = more() if more else None
    settle(points // LANES - 1)
    return beside


def next_rows(ref, start, count):
    if start + count < ref.shape[0]:
        return ref[start + 1 : start + count + 1, :]
    return jnp.concatenate([ref[start + 1 :, :], jnp.zeros((1, LANES), ref.dtype)], 0)


def south_rows(first, block):
    return jnp.concatenate([first, block[:-1]], 0)


def pack_kernel(*refs, points):
    far, (to_east, to_west, to_lat), near, done = refs[:7], refs[7:10], refs[10:17], refs[17]
    copies = [pltpu.make_async_copy(far[k], near[k], done.at[k]) for k in range(7)]
    for copy in copies:
        copy.start()
    lam, east, north, depth, drag, ocean, coarse = near
    rows = lam.shape[0]
    tall = rows // LANES
    lat = lax.axis_index("lat")
    order = (
        (LAM, 0, lam, 3), (FLUX, 1, east, 3), (None, 2, north, 0), (DEPTH, 3, depth, 3),
        (DRAG, 4, drag, 3), (OCEAN, 5, ocean, 1), (POINT, 6, coarse, 2),
    )
    for field, index, ref, pieces in order:
        copies[index].wait()
        if field is None:
            continue
        block = ref[...]
        if field == POINT:
            block = local_ids(block, points)
        sides = take_sides(block.astype(f32), pieces)
        at = slice(field * tall, (field + 1) * tall)
        to_west[at, :] = fold(sides[0:1])
        to_east[at, :] = fold(sides[1:2])

    def border(row):
        return jnp.concatenate(
            [
                lam[row : row + 1, :],
                depth[row : row + 1, :],
                drag[row : row + 1, :],
                ocean[row : row + 1, :].astype(f32),
                local_ids(coarse[row : row + 1, :], points).astype(f32),
                north[row : row + 1, :],
                jnp.zeros((2, LANES), f32),
            ],
            0,
        )

    to_lat[...] = jnp.where(lat == 0, border(rows - 1), border(0))


def inner_kernel(
    lam, east, north, depth, drag, ocean, coarse, green,
    held, gu, cu, gv, cv, sums, left, right, held_sides, green_top, source, done, *, points,
):
    copy = pltpu.make_async_copy(green.at[pl.ds(0, LANES)], green_top, done)
    copy.start()
    rows = lam.shape[0]
    inner = iota((STEP_ROWS, LANES), 1) < LANES - 1
    carry = jnp.zeros((1, LANES), f32)
    for start in range(0, rows, STEP_ROWS):
        at = slice(start, start + STEP_ROWS)
        lam_c, depth_c, drag_c = lam[at, :], depth[at, :], drag[at, :]
        ocean_c = ocean[at, :].astype(f32)
        damp = jnp.where(
            inner,
            ocean_c * roll_east(ocean_c) / (1.0 + drag_step * 0.5 * (drag_c + roll_east(drag_c))),
            0.0,
        )
        ratio = damp * (flux_ratio * 0.5) * (depth_c + roll_east(depth_c))
        adj_u = damp * east[at, :] + ratio * (roll_east(lam_c) - lam_c)
        cu[at, :] = ratio
        gu[at, :] = damp * adj_u
        ocean_n = next_rows(ocean, start, STEP_ROWS).astype(f32)
        damp = (
            ocean_c
            * ocean_n
            / (1.0 + drag_step * 0.5 * (drag_c + next_rows(drag, start, STEP_ROWS)))
        )
        ratio = damp * (flux_ratio * 0.5) * (depth_c + next_rows(depth, start, STEP_ROWS))
        adj_v = damp * north[at, :] + ratio * (next_rows(lam, start, STEP_ROWS) - lam_c)
        cv[at, :] = ratio
        gv[at, :] = damp * adj_v
        src = slope_ratio * (roll_west(adj_u) - adj_u + south_rows(carry, adj_v) - adj_v)
        carry = adj_v[STEP_ROWS - 1 :]
        source[at, :] = src
        held[at, :] = lam_c + src
    total = jnp.zeros(sums.shape, f32)
    for start in range(0, rows, SEG_ROWS):
        at = slice(start, start + SEG_ROWS)
        cells = slice(start * LANES, (start + SEG_ROWS) * LANES)
        high, low = one_hots(local_ids(coarse[at, :], points), points)
        left[:, cells] = high
        right[:, cells] = low
        total = total + segment_part(source[at, :], high, low, True)
    sums[...] = total
    sides = take_sides(held[...])
    held_sides[...] = jnp.concatenate([fold(sides[0:1]), fold(sides[1:2])], 0)
    copy.wait()


def face(low, high, flux):
    damp = low[OCEAN] * high[OCEAN] / (1.0 + drag_step * 0.5 * (low[DRAG] + high[DRAG]))
    ratio = damp * (flux_ratio * 0.5) * (low[DEPTH] + high[DEPTH])
    adj = damp * flux + ratio * (high[LAM] - low[LAM])
    return adj, ratio, damp * adj


def west_rows():
    return iota((8, LANES), 0) < 4


def rim_kernel(
    own_east, own_west, own_lat, from_west, from_east, from_lat, sums, held_sides, green_in,
    payload, faces, lat_lines, green_out, *, points,
):
    lat = lax.axis_index("lat")
    half = held_sides.shape[0] // 2

    def pair(west, east):
        return [
            jnp.concatenate(
                [west[k * half : (k + 1) * half, :], east[k * half : (k + 1) * half, :]], 0
            )
            for k in range(6)
        ]

    own, far = pair(own_west, own_east), pair(from_west, from_east)
    is_west = west_rows()
    low = [jnp.where(is_west, there, here) for here, there in zip(own, far)]
    high = [jnp.where(is_west, here, there) for here, there in zip(own, far)]
    adj, ratio, gain = face(low, high, low[FLUX])
    mine, other = own_lat[...], from_lat[...]
    lower = jnp.where(lat == 0, mine, other)
    upper = jnp.where(lat == 0, other, mine)
    lower = [lower[k : k + 1] for k in range(6)]
    upper = [upper[k : k + 1] for k in range(6)]
    adj_l, c_l, g_l = face(lower, upper, lower[FLUX])
    lat_lines[...] = jnp.concatenate(
        [
            adj_l, c_l, g_l, other[POINT : POINT + 1], mine[POINT : POINT + 1],
            other[OCEAN : OCEAN + 1], jnp.zeros((2, LANES), f32),
        ],
        0,
    )
    sign = jnp.where(is_west, slope_ratio, -slope_ratio)
    sign_l = jnp.where(lat == 0, -slope_ratio, slope_ratio)
    flow = sign * adj
    sub, lane = lax.bitwise_and(iota((8, LANES), 0), half - 1), iota((8, LANES), 1)
    corner = ((lat == 0) & (sub == half - 1) & (lane == LANES - 1)) | (
        (lat == 1) & (sub == 0) & (lane == 0)
    )
    at_corner = jnp.where(
        is_west,
        jnp.broadcast_to(adj_l[:, 0:1], (8, LANES)),
        jnp.broadcast_to(adj_l[:, LANES - 1 :], (8, LANES)),
    )
    faces[ADJ] = adj
    faces[RATIO] = ratio
    faces[GAIN] = gain
    faces[BASE] = held_sides[...] + flow + jnp.where(corner, sign_l * at_corner, 0.0)
    faces[MASK] = own[OCEAN]
    faces[OWN_ID] = own[POINT]
    faces[FAR_ID] = far[POINT]
    pad = jnp.zeros((1, LANES), f32)
    values = jnp.concatenate([flow, sign_l * adj_l, pad], 0)
    ids = jnp.concatenate([own[POINT], mine[POINT : POINT + 1], pad], 0).astype(i32)
    total = sum_pieces(sums[...]) + segment_few(values, ids, points)
    counts = as_points(sums[PIECES * HIGH : (PIECES + 1) * HIGH, :], points)
    inverse = 1.0 / counts
    loads = as_points(total, points) * inverse
    part = jnp.concatenate([loads, inverse], 0)
    if part.shape[0] < 8:
        part = jnp.concatenate([part, jnp.zeros((8 - part.shape[0], LANES), f32)], 0)
    for target in range(payload.shape[0]):
        payload[target] = part


def neighbours(n_lon, n_lat):
    lon, lat = lax.axis_index("lon"), lax.axis_index("lat")
    west = lax.rem(lon + n_lon - 1, n_lon) * n_lat + lat
    east = lax.rem(lon + 1, n_lon) * n_lat + lat
    other = lon * n_lat + (1 - lat)
    return west, east, other


def second_kernel(
    first, green, coarse, ocean, held_in, gu, cu, gv, cv, left, right, faces, lat_lines,
    payload, held, adj_u_out, adj_v_out, lam_sides, lam_edge, acc, tables, pot, lam, source,
    *, points, n_lon, n_lat,
):
    rows = coarse.shape[0]
    blocks = points // LANES
    lat = lax.axis_index("lat")
    south_end = jnp.where(lat == 1, 1.0, 0.0)
    north_end = jnp.where(lat == 0, 1.0, 0.0)
    green_spread(
        green, coarse, lambda k: first[k // blocks, k % blocks : k % blocks + 1, :],
        acc, tables, pot,
    )
    put = put_sides(faces[ADJ], [(slope_ratio, -slope_ratio)])
    adj_l = lat_lines[ADJ_L : ADJ_L + 1, :]
    c_l = lat_lines[C_L : C_L + 1, :]
    g_l = lat_lines[G_L : G_L + 1, :]
    row = iota((STEP_ROWS, LANES), 0)
    lam[rows : rows + 8, :] = jnp.zeros((8, LANES), f32)
    for start in range(0, rows, STEP_ROWS):
        at = slice(start, start + STEP_ROWS)
        value = held_in[at, :] + put[at, :] - attract_coef * pot[at, :]
        if start == 0:
            value = value + jnp.where(row == 0, south_end * slope_ratio * adj_l, 0.0)
        if start == rows - STEP_ROWS:
            value = value - jnp.where(row == STEP_ROWS - 1, north_end * slope_ratio * adj_l, 0.0)
        lam[at, :] = ocean[at, :].astype(f32) * value
    carry = jnp.zeros((1, LANES), f32)
    for start in range(0, rows, STEP_ROWS):
        at = slice(start, start + STEP_ROWS)
        lam_c = lam[at, :]
        adj_u = gu[at, :] + cu[at, :] * (roll_east(lam_c) - lam_c)
        adj_v = gv[at, :] + cv[at, :] * (lam[start + 1 : start + STEP_ROWS + 1, :] - lam_c)
        src = slope_ratio * (roll_west(adj_u) - adj_u + south_rows(carry, adj_v) - adj_v)
        carry = adj_v[STEP_ROWS - 1 :]
        adj_u_out[at, :] = adj_u
        adj_v_out[at, :] = adj_v
        source[at, :] = src
        held[at, :] = lam_c + src
    is_west = west_rows()
    sides = faces[MASK] * (
        faces[BASE]
        - attract_coef * spread([tables[k] for k in range(blocks)], faces[OWN_ID].astype(i32))
    )
    lam_sides[...] = sides
    pull = faces[RATIO] * sides
    flow = slope_ratio * jnp.where(is_west, pull, pull - faces[GAIN])
    edge = jnp.where(lat == 0, lam[rows - 1 : rows, :], lam[0:1, :])
    lam_edge[...] = edge
    pull = c_l * edge
    flow_l = slope_ratio * jnp.where(lat == 0, pull - g_l, pull)
    pad = jnp.zeros((1, LANES), f32)
    total = segment_part(
        jnp.concatenate([flow, flow_l, pad], 0),
        *one_hots(
            jnp.concatenate([faces[OWN_ID], lat_lines[OWN_L : OWN_L + 1, :], pad], 0).astype(i32),
            points,
        ),
    )
    def add(index, total):
        at = pl.ds(pl.multiple_of(index * SEG_ROWS, SEG_ROWS), SEG_ROWS)
        cells = pl.ds(pl.multiple_of(index * SEG_ROWS * LANES, SEG_ROWS * LANES), SEG_ROWS * LANES)
        return total + segment_part(source[at, :], left[:, cells], right[:, cells])

    total = lax.fori_loop(0, rows // SEG_ROWS, add, total)
    own = as_points(sum_pieces(total), points)
    far_id = faces[FAR_ID].astype(i32)
    half = far_id.shape[0] // 2

    def away(values, ids):
        return as_points(segment_few(-values, ids, points), points)

    west_part = away(flow[:half], far_id[:half])
    east_part = away(flow[half:], far_id[half:])
    lat_part = away(
        jnp.concatenate([flow_l, pad], 0),
        jnp.concatenate([lat_lines[ID_L : ID_L + 1, :], pad], 0).astype(i32),
    )
    west, east, other = neighbours(n_lon, n_lat)
    part = jnp.concatenate([own, east_part, west_part, lat_part], 0)
    begin = 4 * blocks
    deep = begin + half
    first_lane = iota((1, LANES), 1) == 0

    def corners(block):
        return jnp.where(
            first_lane,
            block[0:1],
            jnp.broadcast_to(block[half : half + 1, 0:1], (1, LANES)),
        )

    edge_rows = jnp.concatenate(
        [edge, held[0:1, :], corners(faces[GAIN]), corners(faces[RATIO])]
        + [jnp.zeros((1, LANES), f32)] * (half - 4),
        0,
    )
    for target in range(n_lon * n_lat):
        shared = jnp.where(
            target == west, sides[:half], jnp.where(target == east, sides[half:], edge_rows)
        )
        payload[target * deep : (target + 1) * deep, :] = jnp.concatenate([part, shared], 0)


def last_kernel(
    first, second, green, green_north, coarse, ocean, held, faces, lat_lines, lam_sides, lam_edge,
    lam_out, payload, put, north_line, loads, acc, tables, pot,
    *, points, n_lon, n_lat,
):
    rows = held.shape[0]
    blocks = points // LANES
    half = rows // LANES
    deep = 4 * blocks + half
    lat = lax.axis_index("lat")

    def received(owner, kind):
        start = owner * deep + kind * blocks
        return second[start : start + blocks, :]

    for lon in range(n_lon):
        for band in range(n_lat):
            here = lon * n_lat + band
            west = (lon - 1) % n_lon * n_lat + band
            east = (lon + 1) % n_lon * n_lat + band
            other = lon * n_lat + 1 - band
            total = received(here, 0) + received(west, 1) + received(east, 2) + received(other, 3)
            loads[here * blocks : (here + 1) * blocks, :] = (
                total * first[here, blocks : 2 * blocks, :]
            )
    west, east, other = neighbours(n_lon, n_lat)

    def shared(owner, row, count):
        return second[pl.ds(owner * deep + 4 * blocks + row, count), :]

    far = jnp.concatenate([shared(west, 0, half), shared(east, 0, half)], 0)
    rise = jnp.where(west_rows(), lam_sides[...] - far, far - lam_sides[...])
    adj = faces[GAIN] + faces[RATIO] * rise
    put[...] = put_sides(adj, [(slope_ratio, -slope_ratio), (0.0, 1.0)])
    rise = shared(other, 0, 1) - lam_edge[...]
    adj_l = lat_lines[G_L : G_L + 1, :] + lat_lines[C_L : C_L + 1, :] * jnp.where(
        lat == 0, rise, -rise
    )
    from_north = jnp.where(lat == 0, adj_l, 0.0)
    from_south = jnp.where(lat == 1, adj_l, 0.0)
    put[0:1, :LANES] = put[0:1, :LANES] + slope_ratio * from_south
    put[rows - 1 : rows, :LANES] = put[rows - 1 : rows, :LANES] - slope_ratio * from_north
    north_line[...] = from_north
    load_row = lambda k: loads[k : k + 1, :]
    north_sums = green_spread(
        green, coarse, load_row, acc, tables, pot, lambda: green_rows(green_north, 0, load_row)
    )
    for start in range(0, rows, STEP_ROWS):
        at = slice(start, start + STEP_ROWS)
        lam_out[at, :] = ocean[at, :].astype(f32) * (
            held[at, :] + put[at, :LANES] - attract_coef * pot[at, :]
        )
    potential = sum_lanes(north_sums)[0:1]
    diagonal = lambda owner: shared(owner + 1 - 2 * lat, 0, 1)
    lam_n = shared(other, 0, 1)
    lane = iota((1, LANES), 1)
    rise = jnp.where(
        lane == 0, lam_n - roll_west(diagonal(west)), roll_east(diagonal(east)) - lam_n
    )
    adj = shared(other, 2, 1) + shared(other, 3, 1) * rise
    flow = jnp.where(lane == 0, adj, jnp.where(lane == LANES - 1, -adj, 0.0)) + adj_l
    lam_north = lat_lines[MASK_L : MASK_L + 1, :] * (
        shared(other, 1, 1) + slope_ratio * flow - attract_coef * potential
    )
    span = rows // n_lon
    for target in range(n_lon):
        start = target * (span + 1)
        payload[start : start + span, :] = lam_out[target * span : (target + 1) * span, :]
        if target < n_lon - 1:
            stop = (target + 1) * span
            payload[start + span : start + span + 1, :] = lam_out[stop : stop + 1, :]
        else:
            payload[start + span : start + span + 1, :] = lam_north


def bands_kernel(
    parts, lam, adj_u, adj_v, put, north_line,
    lam_out, east_out, north_out, bands, east, north, planes, done, *, count,
):
    span = parts.shape[0] // count - 1
    rows = lam.shape[0]
    copies = [
        pltpu.make_async_copy(lam, lam_out, done.at[0]),
        pltpu.make_async_copy(east, east_out, done.at[1]),
        pltpu.make_async_copy(north, north_out, done.at[2]),
    ] + [
        pltpu.make_async_copy(planes.at[k], bands.at[k, 0], done.at[3 + k]) for k in range(3)
    ]
    copies[0].start()
    lane = iota((span, LANES), 1)
    top = (lax.axis_index("lat") == 1) & (lax.axis_index("lon") == count - 1)
    last = (iota((span, LANES), 0) == span - 1) & top
    for k in range(count):
        start = k * (span + 1)
        planes[0, :, k * LANES : (k + 1) * LANES] = parts[start : start + span, :]
    copies[3].start()
    for k in range(count):
        start = k * (span + 1)
        here = parts[start : start + span, :]
        north_of = jnp.where(last, 0.0, parts[start + 1 : start + 1 + span, :])
        planes[2, :, k * LANES : (k + 1) * LANES] = north_of - here
    copies[5].start()
    for k in range(count):
        at = slice(k * LANES, (k + 1) * LANES)
        here = planes[0, :, at]
        after = (k + 1) % count
        there = planes[0, :, after * LANES : (after + 1) * LANES]
        planes[1, :, at] = jnp.where(lane == LANES - 1, roll_east(there), roll_east(here)) - here
    copies[4].start()
    east[...] = adj_u[...] + put[:, LANES:]
    copies[1].start()
    north[...] = adj_v[...]
    north[rows - 1 : rows, :] = adj_v[rows - 1 : rows, :] + north_line[...]
    copies[2].start()
    for copy in copies:
        copy.wait()


def call(kernel, shapes, scratch, args, name, far=(), far_out=(), limit=16, weight=4, aliases=None):
    vmem = pl.BlockSpec(memory_space=pltpu.VMEM)
    away = pl.BlockSpec(memory_space=pl.ANY)
    shapes = [(shape, f32) if isinstance(shape[0], int) else shape for shape in shapes]
    return pl.pallas_call(
        kernel,
        out_shape=[jax.ShapeDtypeStruct(shape, kind) for shape, kind in shapes],
        in_specs=[away if k in far else vmem for k in range(len(args))],
        out_specs=[away if k in far_out else vmem for k in range(len(shapes))],
        scratch_shapes=scratch,
        compiler_params=pltpu.CompilerParams(vmem_limit_bytes=limit << 20),
        cost_estimate=pl.CostEstimate(flops=weight << 30, bytes_accessed=16 << 20, transcendentals=0),
        input_output_aliases=aliases or {},
        name=name,
    )(*args)


def body(n_lon, n_lat, lam_in, flux_east, flux_north, depth, drag, ocean, coarse_of, green):
    rows, cols = lam_in.shape
    points = green.shape[0]
    blocks = points // LANES
    owners = n_lon * n_lat
    grid = (rows, cols)
    fields = (lam_in, flux_east, flux_north, depth, drag, ocean, coarse_of)
    tall = rows // LANES
    to_east, to_west, to_lat, *fields = call(
        functools.partial(pack_kernel, points=points),
        [(6 * tall, cols), (6 * tall, cols), (8, cols)]
        + [(grid, field.dtype) for field in fields],
        [pltpu.SemaphoreType.DMA((7,))], fields, "pack", far=range(7), limit=52,
    )
    ocean, coarse_of = fields[5:]
    forward = [(k, (k + 1) % n_lon) for k in range(n_lon)]
    backward = [(target, source) for source, target in forward]
    from_west = lax.ppermute(to_east, "lon", forward)
    from_east = lax.ppermute(to_west, "lon", backward)
    from_lat = lax.ppermute(to_lat, "lat", [(0, 1), (1, 0)])
    held, gu, cu, gv, cv, sums, left, right, held_sides, green_top = call(
        functools.partial(inner_kernel, points=points),
        [grid] * 5
        + [((PIECES + 1) * HIGH, LOW), ((HIGH, rows * cols), bf16), ((LOW, rows * cols), bf16)]
        + [(2 * tall, cols), (LANES, green.shape[1])],
        [pltpu.VMEM(grid, f32), pltpu.SemaphoreType.DMA(())], (*fields, green), "inner",
        far=(7,), limit=INNER_LIMIT,
    )
    payload, faces, lat_lines, green_top = call(
        functools.partial(rim_kernel, points=points),
        [(owners, 8, LANES), (7, 2 * tall, cols), (8, cols), green_top.shape], [],
        (
            to_east, to_west, to_lat, from_west, from_east, from_lat, sums, held_sides, green_top,
        ),
        "rim", far=(8,), far_out=(3,), weight=16, aliases={8: 3},
    )
    green_north = lax.ppermute(green_top, "lat", [(0, 1), (1, 0)])
    first = lax.all_to_all(payload, ("lon", "lat"), 0, 0, tiled=True)
    deep = 4 * blocks + tall
    green_scratch = [
        pltpu.VMEM((LANES, LANES), f32),
        pltpu.VMEM((blocks, 8, LANES), f32),
        pltpu.VMEM(grid, f32),
    ]
    payload, held, adj_u, adj_v, lam_sides, lam_edge = call(
        functools.partial(second_kernel, points=points, n_lon=n_lon, n_lat=n_lat),
        [(owners * deep, LANES), grid, grid, grid, (2 * tall, cols), (1, cols)],
        green_scratch + [pltpu.VMEM((rows + 8, cols), f32), pltpu.VMEM(grid, f32)],
        (first, green, coarse_of, ocean, held, gu, cu, gv, cv, left, right, faces, lat_lines),
        "second",
    )
    second = lax.all_to_all(
        payload.reshape(owners, deep, 1, LANES), ("lon", "lat"), 0, 0, tiled=True
    ).reshape(payload.shape)
    span = rows // n_lon
    lam, payload, put, north_line = call(
        functools.partial(last_kernel, points=points, n_lon=n_lon, n_lat=n_lat),
        [grid, (rows + n_lon, cols), (rows, 2 * cols), (1, cols)],
        [
            pltpu.VMEM((owners * blocks, LANES), f32),
        ]
        + green_scratch,
        (
            first, second, green, green_north, coarse_of, ocean, held, faces, lat_lines,
            lam_sides, lam_edge,
        ),
        "last",
    )
    parts = lax.all_to_all(
        payload.reshape(n_lon, span + 1, 1, LANES), "lon", 0, 0, tiled=True
    ).reshape(payload.shape)
    return tuple(
        call(
            functools.partial(bands_kernel, count=n_lon),
            [grid, grid, grid, (3, 1, span, n_lon * cols)],
            [
                pltpu.VMEM(grid, f32),
                pltpu.VMEM(grid, f32),
                pltpu.VMEM((3, span, n_lon * cols), f32),
                pltpu.SemaphoreType.DMA((6,)),
            ],
            (parts, lam, adj_u, adj_v, put, north_line), "bands", far_out=range(4),
        )
    )


def solution(mesh):
    cells = P(("groups", "lat"), "lon")
    n_lon, n_lat = mesh.shape["lon"], mesh.shape["lat"]
    return jax.shard_map(
        functools.partial(body, n_lon, n_lat),
        mesh=mesh,
        in_specs=(cells,) * 6 + (P("lat", "lon"), P(("lon", "lat"), None)),
        out_specs=(cells,) * 3 + (P(None, ("groups", "lat"), "lon", None),),
        check_vma=False,
    )
```

```python
import functools

import jax
import jax.numpy as jnp
from jax import lax
from jax.experimental import pallas as pl
from jax.experimental.pallas import tpu as pltpu
from jax.sharding import PartitionSpec as P

f32 = jnp.float32
bf16 = jnp.bfloat16
i32 = jnp.int32

LANES = 128
LOW = 32
HIGH = 16
PIECES = 2
INNER_LIMIT = 36
SEG_ROWS = 256
STEP_ROWS = 128

flux_ratio = 0.25
slope_ratio = 0.25
drag_step = 1.0
attract_coef = 0.5

LAM, DEPTH, DRAG, OCEAN, POINT, FLUX = range(6)
ADJ, RATIO, GAIN, BASE, MASK, OWN_ID, FAR_ID = range(7)
ADJ_L, C_L, G_L, ID_L, OWN_L, MASK_L = range(6)


def iota(shape, dim):
    return lax.broadcasted_iota(i32, shape, dim)


def roll_east(x):
    return pltpu.roll(x, LANES - 1, 1)


def roll_west(x):
    return pltpu.roll(x, 1, 1)


def local_ids(ids, points):
    return lax.bitwise_and(ids, points - 1)


def bf16_pieces(values, count=PIECES):
    out = []
    for piece in range(count):
        top = values.astype(bf16).astype(f32)
        out.append(top)
        if piece < count - 1:
            values = values - top
    return out


def one_hots(ids, points):
    blocks = points // LANES
    high = lax.shift_right_logical(ids, 5)
    high = lax.bitwise_and(high, 3) * blocks + lax.shift_right_logical(high, 2)
    low = lax.bitwise_and(ids, LOW - 1)
    high_iota = iota((HIGH, LANES), 0)
    low_iota = iota((LOW, LANES), 0)
    left, right = [], []
    for row in range(ids.shape[0]):
        mask = jnp.broadcast_to(high[row : row + 1], (HIGH, LANES)) == high_iota
        left.append(jnp.where(mask, 1.0, 0.0).astype(bf16))
        mask = jnp.broadcast_to(low[row : row + 1], (LOW, LANES)) == low_iota
        right.append(jnp.where(mask, 1.0, 0.0).astype(bf16))
    return jnp.concatenate(left, 1), jnp.concatenate(right, 1)


def segment_part(values, left, right, with_counts=False):
    parts = []
    for piece in bf16_pieces(values):
        line = jnp.concatenate(
            [
                jnp.broadcast_to(piece[row : row + 1], (HIGH, LANES)).astype(bf16)
                for row in range(values.shape[0])
            ],
            1,
        )
        parts.append(left * line)
    if with_counts:
        parts.append(left)
    return lax.dot_general(
        jnp.concatenate(parts, 0), right, (((1,), (1,)), ((), ())), preferred_element_type=f32
    )


def segment_few(values, ids, points):
    return sum_pieces(segment_part(values, *one_hots(ids, points)))


def sum_pieces(parts):
    total = parts[:HIGH]
    for piece in range(1, PIECES):
        total = total + parts[piece * HIGH : (piece + 1) * HIGH]
    return total


def as_points(table, points):
    blocks = points // LANES
    return jnp.concatenate([table[q * blocks : (q + 1) * blocks] for q in range(4)], 1)


def fold(line):
    return jnp.concatenate(
        [line[:, k * LANES : (k + 1) * LANES] for k in range(line.shape[1] // LANES)], 0
    )


def unfold(block):
    return jnp.concatenate([block[k : k + 1] for k in range(block.shape[0])], 1)


def take_sides(block, count=3):
    sub, lane = iota((8, LANES), 0), iota((8, LANES), 1)
    pick = ((sub == 0) & (lane == 0)) | ((sub == 1) & (lane == LANES - 1))
    pick = pick.astype(f32).astype(bf16)
    out = None
    for piece in reversed(bf16_pieces(block, count)):
        part = lax.dot_general(
            pick, piece.astype(bf16), (((1,), (1,)), ((), ())), preferred_element_type=f32
        )
        out = part if out is None else out + part
    return out


def put_sides(pair, entries):
    half = pair.shape[0] // 2
    lines = jnp.concatenate([unfold(pair[:half]), unfold(pair[half:])], 0)
    rows = lines.shape[1]
    pieces = bf16_pieces(lines, 3)
    stack = jnp.concatenate(pieces + [jnp.zeros((2, rows), f32)], 0)
    sub, lane = iota((8, LANES), 0), iota((8, LANES), 1)
    west = (sub < 6) & (lax.bitwise_and(sub, 1) == 0) & (lane == 0)
    east = (sub < 6) & (lax.bitwise_and(sub, 1) == 1) & (lane == LANES - 1)
    picks = [jnp.where(west, first, jnp.where(east, last, 0.0)) for first, last in entries]
    return lax.dot_general(
        stack, jnp.concatenate(picks, 1), (((0,), (0,)), ((), ())), preferred_element_type=f32
    )


def sum_lanes(block):
    out = None
    for piece in reversed(bf16_pieces(block, 3)):
        part = lax.dot_general(
            jnp.ones((8, LANES), bf16), piece.astype(bf16), (((1,), (1,)), ((), ())),
            preferred_element_type=f32,
        )
        out = part if out is None else out + part
    return out


def green_rows(green_ref, start, load_row):
    acc = jnp.zeros((LANES, LANES), f32)
    for k in range(green_ref.shape[1] // LANES):
        acc = acc + green_ref[
            pl.ds(start, LANES), k * LANES : (k + 1) * LANES
        ] * jnp.broadcast_to(load_row(k), (LANES, LANES))
    return acc


def look_up(table, ids):
    rows = ids.shape[0]
    table = jnp.broadcast_to(table[None], (rows // 8, 8, LANES)).reshape(rows, LANES)
    return jnp.take_along_axis(table, ids, axis=1, mode="promise_in_bounds")


def spread(tables, ids):
    low = lax.bitwise_and(ids, LANES - 1)
    block = lax.shift_right_logical(ids, 7)
    out = None
    for k, table in enumerate(tables):
        value = look_up(table, low)
        out = value if out is None else jnp.where(block == k, value, out)
    return out


def green_spread(green, coarse, load_row, acc, tables, pot, more=None):
    points = green.shape[0]
    rows = coarse.shape[0]

    def settle(index):
        table = sum_lanes(acc[...])
        tables[index] = table
        for start in range(0, rows, STEP_ROWS):
            at = slice(start, start + STEP_ROWS)
            ids = local_ids(coarse[at, :], points)
            value = look_up(table, lax.bitwise_and(ids, LANES - 1))
            pot[at, :] = jnp.where(lax.shift_right_logical(ids, 7) == index, value, pot[at, :])

    def step(index, carry):
        block = green_rows(green, index * LANES, load_row)
        settle(index - 1)
        acc[...] = block
        return carry

    acc[...] = green_rows(green, 0, load_row)
    for index in range(1, points // LANES):
        step(index, 0)
    beside = more() if more else None
    settle(points // LANES - 1)
    return beside


def next_rows(ref, start, count):
    if start + count < ref.shape[0]:
        return ref[start + 1 : start + count + 1, :]
    return jnp.concatenate([ref[start + 1 :, :], jnp.zeros((1, LANES), ref.dtype)], 0)


def south_rows(first, block):
    return jnp.concatenate([first, block[:-1]], 0)


def pack_kernel(*refs, points):
    far, (to_east, to_west, to_lat), near, done = refs[:7], refs[7:10], refs[10:17], refs[17]
    copies = [pltpu.make_async_copy(far[k], near[k], done.at[k]) for k in range(7)]
    for copy in copies:
        copy.start()
    lam, east, north, depth, drag, ocean, coarse = near
    rows = lam.shape[0]
    tall = rows // LANES
    lat = lax.axis_index("lat")
    order = (
        (LAM, 0, lam, 2), (FLUX, 1, east, 2), (None, 2, north, 0), (DEPTH, 3, depth, 2),
        (DRAG, 4, drag, 2), (OCEAN, 5, ocean, 1), (POINT, 6, coarse, 2),
    )
    for field, index, ref, pieces in order:
        copies[index].wait()
        if field is None:
            continue
        block = ref[...]
        if field == POINT:
            block = local_ids(block, points)
        sides = take_sides(block.astype(f32), pieces)
        at = slice(field * tall, (field + 1) * tall)
        to_west[at, :] = fold(sides[0:1])
        to_east[at, :] = fold(sides[1:2])

    def border(row):
        return jnp.concatenate(
            [
                lam[row : row + 1, :],
                depth[row : row + 1, :],
                drag[row : row + 1, :],
                ocean[row : row + 1, :].astype(f32),
                local_ids(coarse[row : row + 1, :], points).astype(f32),
                north[row : row + 1, :],
                jnp.zeros((2, LANES), f32),
            ],
            0,
        )

    to_lat[...] = jnp.where(lat == 0, border(rows - 1), border(0))


def inner_kernel(
    lam, east, north, depth, drag, ocean, coarse, green,
    held, gu, cu, gv, cv, sums, left, right, held_sides, green_top, source, done, *, points,
):
    copy = pltpu.make_async_copy(green.at[pl.ds(0, LANES)], green_top, done)
    copy.start()
    rows = lam.shape[0]
    inner = iota((STEP_ROWS, LANES), 1) < LANES - 1
    carry = jnp.zeros((1, LANES), f32)
    for start in range(0, rows, STEP_ROWS):
        at = slice(start, start + STEP_ROWS)
        lam_c, depth_c, drag_c = lam[at, :], depth[at, :], drag[at, :]
        ocean_c = ocean[at, :].astype(f32)
        damp = jnp.where(
            inner,
            ocean_c * roll_east(ocean_c) / (1.0 + drag_step * 0.5 * (drag_c + roll_east(drag_c))),
            0.0,
        )
        ratio = damp * (flux_ratio * 0.5) * (depth_c + roll_east(depth_c))
        adj_u = damp * east[at, :] + ratio * (roll_east(lam_c) - lam_c)
        cu[at, :] = ratio
        gu[at, :] = damp * adj_u
        ocean_n = next_rows(ocean, start, STEP_ROWS).astype(f32)
        damp = (
            ocean_c
            * ocean_n
            / (1.0 + drag_step * 0.5 * (drag_c + next_rows(drag, start, STEP_ROWS)))
        )
        ratio = damp * (flux_ratio * 0.5) * (depth_c + next_rows(depth, start, STEP_ROWS))
        adj_v = damp * north[at, :] + ratio * (next_rows(lam, start, STEP_ROWS) - lam_c)
        cv[at, :] = ratio
        gv[at, :] = damp * adj_v
        src = slope_ratio * (roll_west(adj_u) - adj_u + south_rows(carry, adj_v) - adj_v)
        carry = adj_v[STEP_ROWS - 1 :]
        source[at, :] = src
        held[at, :] = lam_c + src
    total = jnp.zeros(sums.shape, f32)
    for start in range(0, rows, SEG_ROWS):
        at = slice(start, start + SEG_ROWS)
        cells = slice(start * LANES, (start + SEG_ROWS) * LANES)
        high, low = one_hots(local_ids(coarse[at, :], points), points)
        left[:, cells] = high
        right[:, cells] = low
        total = total + segment_part(source[at, :], high, low, True)
    sums[...] = total
    sides = take_sides(held[...])
    held_sides[...] = jnp.concatenate([fold(sides[0:1]), fold(sides[1:2])], 0)
    copy.wait()


def face(low, high, flux):
    damp = low[OCEAN] * high[OCEAN] / (1.0 + drag_step * 0.5 * (low[DRAG] + high[DRAG]))
    ratio = damp * (flux_ratio * 0.5) * (low[DEPTH] + high[DEPTH])
    adj = damp * flux + ratio * (high[LAM] - low[LAM])
    return adj, ratio, damp * adj


def west_rows():
    return iota((8, LANES), 0) < 4


def rim_kernel(
    own_east, own_west, own_lat, from_west, from_east, from_lat, sums, held_sides, green_in,
    payload, faces, lat_lines, green_out, *, points,
):
    lat = lax.axis_index("lat")
    half = held_sides.shape[0] // 2

    def pair(west, east):
        return [
            jnp.concatenate(
                [west[k * half : (k + 1) * half, :], east[k * half : (k + 1) * half, :]], 0
            )
            for k in range(6)
        ]

    own, far = pair(own_west, own_east), pair(from_west, from_east)
    is_west = west_rows()
    low = [jnp.where(is_west, there, here) for here, there in zip(own, far)]
    high = [jnp.where(is_west, here, there) for here, there in zip(own, far)]
    adj, ratio, gain = face(low, high, low[FLUX])
    mine, other = own_lat[...], from_lat[...]
    lower = jnp.where(lat == 0, mine, other)
    upper = jnp.where(lat == 0, other, mine)
    lower = [lower[k : k + 1] for k in range(6)]
    upper = [upper[k : k + 1] for k in range(6)]
    adj_l, c_l, g_l = face(lower, upper, lower[FLUX])
    lat_lines[...] = jnp.concatenate(
        [
            adj_l, c_l, g_l, other[POINT : POINT + 1], mine[POINT : POINT + 1],
            other[OCEAN : OCEAN + 1], jnp.zeros((2, LANES), f32),
        ],
        0,
    )
    sign = jnp.where(is_west, slope_ratio, -slope_ratio)
    sign_l = jnp.where(lat == 0, -slope_ratio, slope_ratio)
    flow = sign * adj
    sub, lane = lax.bitwise_and(iota((8, LANES), 0), half - 1), iota((8, LANES), 1)
    corner = ((lat == 0) & (sub == half - 1) & (lane == LANES - 1)) | (
        (lat == 1) & (sub == 0) & (lane == 0)
    )
    at_corner = jnp.where(
        is_west,
        jnp.broadcast_to(adj_l[:, 0:1], (8, LANES)),
        jnp.broadcast_to(adj_l[:, LANES - 1 :], (8, LANES)),
    )
    faces[ADJ] = adj
    faces[RATIO] = ratio
    faces[GAIN] = gain
    faces[BASE] = held_sides[...] + flow + jnp.where(corner, sign_l * at_corner, 0.0)
    faces[MASK] = own[OCEAN]
    faces[OWN_ID] = own[POINT]
    faces[FAR_ID] = far[POINT]
    pad = jnp.zeros((1, LANES), f32)
    values = jnp.concatenate([flow, sign_l * adj_l, pad], 0)
    ids = jnp.concatenate([own[POINT], mine[POINT : POINT + 1], pad], 0).astype(i32)
    total = sum_pieces(sums[...]) + segment_few(values, ids, points)
    counts = as_points(sums[PIECES * HIGH : (PIECES + 1) * HIGH, :], points)
    inverse = 1.0 / counts
    loads = as_points(total, points) * inverse
    part = jnp.concatenate([loads, inverse], 0)
    if part.shape[0] < 8:
        part = jnp.concatenate([part, jnp.zeros((8 - part.shape[0], LANES), f32)], 0)
    for target in range(payload.shape[0]):
        payload[target] = part


def neighbours(n_lon, n_lat):
    lon, lat = lax.axis_index("lon"), lax.axis_index("lat")
    west = lax.rem(lon + n_lon - 1, n_lon) * n_lat + lat
    east = lax.rem(lon + 1, n_lon) * n_lat + lat
    other = lon * n_lat + (1 - lat)
    return west, east, other


def second_kernel(
    first, green, coarse, ocean, held_in, gu, cu, gv, cv, left, right, faces, lat_lines,
    payload, held, adj_u_out, adj_v_out, lam_sides, lam_edge, acc, tables, pot, lam, source,
    *, points, n_lon, n_lat,
):
    rows = coarse.shape[0]
    blocks = points // LANES
    lat = lax.axis_index("lat")
    south_end = jnp.where(lat == 1, 1.0, 0.0)
    north_end = jnp.where(lat == 0, 1.0, 0.0)
    green_spread(
        green, coarse, lambda k: first[k // blocks, k % blocks : k % blocks + 1, :],
        acc, tables, pot,
    )
    put = put_sides(faces[ADJ], [(slope_ratio, -slope_ratio)])
    adj_l = lat_lines[ADJ_L : ADJ_L + 1, :]
    c_l = lat_lines[C_L : C_L + 1, :]
    g_l = lat_lines[G_L : G_L + 1, :]
    row = iota((STEP_ROWS, LANES), 0)
    lam[rows : rows + 8, :] = jnp.zeros((8, LANES), f32)
    for start in range(0, rows, STEP_ROWS):
        at = slice(start, start + STEP_ROWS)
        value = held_in[at, :] + put[at, :] - attract_coef * pot[at, :]
        if start == 0:
            value = value + jnp.where(row == 0, south_end * slope_ratio * adj_l, 0.0)
        if start == rows - STEP_ROWS:
            value = value - jnp.where(row == STEP_ROWS - 1, north_end * slope_ratio * adj_l, 0.0)
        lam[at, :] = ocean[at, :].astype(f32) * value
    carry = jnp.zeros((1, LANES), f32)
    for start in range(0, rows, STEP_ROWS):
        at = slice(start, start + STEP_ROWS)
        lam_c = lam[at, :]
        adj_u = gu[at, :] + cu[at, :] * (roll_east(lam_c) - lam_c)
        adj_v = gv[at, :] + cv[at, :] * (lam[start + 1 : start + STEP_ROWS + 1, :] - lam_c)
        src = slope_ratio * (roll_west(adj_u) - adj_u + south_rows(carry, adj_v) - adj_v)
        carry = adj_v[STEP_ROWS - 1 :]
        adj_u_out[at, :] = adj_u
        adj_v_out[at, :] = adj_v
        source[at, :] = src
        held[at, :] = lam_c + src
    is_west = west_rows()
    sides = faces[MASK] * (
        faces[BASE]
        - attract_coef * spread([tables[k] for k in range(blocks)], faces[OWN_ID].astype(i32))
    )
    lam_sides[...] = sides
    pull = faces[RATIO] * sides
    flow = slope_ratio * jnp.where(is_west, pull, pull - faces[GAIN])
    edge = jnp.where(lat == 0, lam[rows - 1 : rows, :], lam[0:1, :])
    lam_edge[...] = edge
    pull = c_l * edge
    flow_l = slope_ratio * jnp.where(lat == 0, pull - g_l, pull)
    pad = jnp.zeros((1, LANES), f32)
    total = segment_part(
        jnp.concatenate([flow, flow_l, pad], 0),
        *one_hots(
            jnp.concatenate([faces[OWN_ID], lat_lines[OWN_L : OWN_L + 1, :], pad], 0).astype(i32),
            points,
        ),
    )
    def add(index, total):
        at = pl.ds(pl.multiple_of(index * SEG_ROWS, SEG_ROWS), SEG_ROWS)
        cells = pl.ds(pl.multiple_of(index * SEG_ROWS * LANES, SEG_ROWS * LANES), SEG_ROWS * LANES)
        return total + segment_part(source[at, :], left[:, cells], right[:, cells])

    total = lax.fori_loop(0, rows // SEG_ROWS, add, total)
    own = as_points(sum_pieces(total), points)
    far_id = faces[FAR_ID].astype(i32)
    half = far_id.shape[0] // 2

    def away(values, ids):
        return as_points(segment_few(-values, ids, points), points)

    west_part = away(flow[:half], far_id[:half])
    east_part = away(flow[half:], far_id[half:])
    lat_part = away(
        jnp.concatenate([flow_l, pad], 0),
        jnp.concatenate([lat_lines[ID_L : ID_L + 1, :], pad], 0).astype(i32),
    )
    west, east, other = neighbours(n_lon, n_lat)
    part = jnp.concatenate([own, east_part, west_part, lat_part], 0)
    begin = 4 * blocks
    deep = begin + half
    first_lane = iota((1, LANES), 1) == 0

    def corners(block):
        return jnp.where(
            first_lane,
            block[0:1],
            jnp.broadcast_to(block[half : half + 1, 0:1], (1, LANES)),
        )

    edge_rows = jnp.concatenate(
        [edge, held[0:1, :], corners(faces[GAIN]), corners(faces[RATIO])]
        + [jnp.zeros((1, LANES), f32)] * (half - 4),
        0,
    )
    for target in range(n_lon * n_lat):
        shared = jnp.where(
            target == west, sides[:half], jnp.where(target == east, sides[half:], edge_rows)
        )
        payload[target * deep : (target + 1) * deep, :] = jnp.concatenate([part, shared], 0)


def last_kernel(
    first, second, green, green_north, coarse, ocean, held, adj_u, adj_v, faces, lat_lines,
    lam_sides, lam_edge, lam_out, payload, east_out, north_out,
    put, east_buf, north_buf, done, loads, acc, tables, pot,
    *, points, n_lon, n_lat,
):
    copies = [
        pltpu.make_async_copy(east_buf, east_out, done.at[0]),
        pltpu.make_async_copy(north_buf, north_out, done.at[1]),
    ]
    rows = held.shape[0]
    blocks = points // LANES
    half = rows // LANES
    deep = 4 * blocks + half
    lat = lax.axis_index("lat")

    def received(owner, kind):
        start = owner * deep + kind * blocks
        return second[start : start + blocks, :]

    for lon in range(n_lon):
        for band in range(n_lat):
            here = lon * n_lat + band
            west = (lon - 1) % n_lon * n_lat + band
            east = (lon + 1) % n_lon * n_lat + band
            other = lon * n_lat + 1 - band
            total = received(here, 0) + received(west, 1) + received(east, 2) + received(other, 3)
            loads[here * blocks : (here + 1) * blocks, :] = (
                total * first[here, blocks : 2 * blocks, :]
            )
    west, east, other = neighbours(n_lon, n_lat)

    def shared(owner, row, count):
        return second[pl.ds(owner * deep + 4 * blocks + row, count), :]

    far = jnp.concatenate([shared(west, 0, half), shared(east, 0, half)], 0)
    rise = jnp.where(west_rows(), lam_sides[...] - far, far - lam_sides[...])
    adj = faces[GAIN] + faces[RATIO] * rise
    put[...] = put_sides(adj, [(slope_ratio, -slope_ratio), (0.0, 1.0)])
    rise = shared(other, 0, 1) - lam_edge[...]
    adj_l = lat_lines[G_L : G_L + 1, :] + lat_lines[C_L : C_L + 1, :] * jnp.where(
        lat == 0, rise, -rise
    )
    from_north = jnp.where(lat == 0, adj_l, 0.0)
    from_south = jnp.where(lat == 1, adj_l, 0.0)
    put[0:1, :LANES] = put[0:1, :LANES] + slope_ratio * from_south
    put[rows - 1 : rows, :LANES] = put[rows - 1 : rows, :LANES] - slope_ratio * from_north
    east_buf[...] = adj_u[...] + put[:, LANES:]
    north_buf[...] = adj_v[...]
    north_buf[rows - 1 : rows, :] = adj_v[rows - 1 : rows, :] + from_north
    for copy in copies:
        copy.start()
    load_row = lambda k: loads[k : k + 1, :]
    north_sums = green_spread(
        green, coarse, load_row, acc, tables, pot, lambda: green_rows(green_north, 0, load_row)
    )
    for start in range(0, rows, STEP_ROWS):
        at = slice(start, start + STEP_ROWS)
        lam_out[at, :] = ocean[at, :].astype(f32) * (
            held[at, :] + put[at, :LANES] - attract_coef * pot[at, :]
        )
    potential = sum_lanes(north_sums)[0:1]
    diagonal = lambda owner: shared(owner + 1 - 2 * lat, 0, 1)
    lam_n = shared(other, 0, 1)
    lane = iota((1, LANES), 1)
    rise = jnp.where(
        lane == 0, lam_n - roll_west(diagonal(west)), roll_east(diagonal(east)) - lam_n
    )
    adj = shared(other, 2, 1) + shared(other, 3, 1) * rise
    flow = jnp.where(lane == 0, adj, jnp.where(lane == LANES - 1, -adj, 0.0)) + adj_l
    lam_north = lat_lines[MASK_L : MASK_L + 1, :] * (
        shared(other, 1, 1) + slope_ratio * flow - attract_coef * potential
    )
    span = rows // n_lon
    for target in range(n_lon):
        start = target * (span + 1)
        payload[start : start + span, :] = lam_out[target * span : (target + 1) * span, :]
        if target < n_lon - 1:
            stop = (target + 1) * span
            payload[start + span : start + span + 1, :] = lam_out[stop : stop + 1, :]
        else:
            payload[start + span : start + span + 1, :] = lam_north
    for copy in copies:
        copy.wait()


def bands_kernel(parts, lam, lam_out, bands, planes, done, *, count):
    span = parts.shape[0] // count - 1
    copies = [pltpu.make_async_copy(lam, lam_out, done.at[3])] + [
        pltpu.make_async_copy(planes.at[k], bands.at[k, 0], done.at[k]) for k in range(3)
    ]
    copies[0].start()
    lane = iota((span, LANES), 1)
    top = (lax.axis_index("lat") == 1) & (lax.axis_index("lon") == count - 1)
    last = (iota((span, LANES), 0) == span - 1) & top
    for k in range(count):
        start = k * (span + 1)
        planes[0, :, k * LANES : (k + 1) * LANES] = parts[start : start + span, :]
    copies[1].start()
    for k in range(count):
        start = k * (span + 1)
        here = parts[start : start + span, :]
        north_of = jnp.where(last, 0.0, parts[start + 1 : start + 1 + span, :])
        planes[2, :, k * LANES : (k + 1) * LANES] = north_of - here
    copies[3].start()
    for k in range(count):
        at = slice(k * LANES, (k + 1) * LANES)
        here = planes[0, :, at]
        after = (k + 1) % count
        there = planes[0, :, after * LANES : (after + 1) * LANES]
        planes[1, :, at] = jnp.where(lane == LANES - 1, roll_east(there), roll_east(here)) - here
    copies[2].start()
    for copy in copies:
        copy.wait()


def call(kernel, shapes, scratch, args, name, far=(), far_out=(), limit=16, weight=4, aliases=None):
    vmem = pl.BlockSpec(memory_space=pltpu.VMEM)
    away = pl.BlockSpec(memory_space=pl.ANY)
    shapes = [(shape, f32) if isinstance(shape[0], int) else shape for shape in shapes]
    return pl.pallas_call(
        kernel,
        out_shape=[jax.ShapeDtypeStruct(shape, kind) for shape, kind in shapes],
        in_specs=[away if k in far else vmem for k in range(len(args))],
        out_specs=[away if k in far_out else vmem for k in range(len(shapes))],
        scratch_shapes=scratch,
        compiler_params=pltpu.CompilerParams(vmem_limit_bytes=limit << 20),
        cost_estimate=pl.CostEstimate(flops=weight << 30, bytes_accessed=16 << 20, transcendentals=0),
        input_output_aliases=aliases or {},
        name=name,
    )(*args)


def body(n_lon, n_lat, lam_in, flux_east, flux_north, depth, drag, ocean, coarse_of, green):
    rows, cols = lam_in.shape
    points = green.shape[0]
    blocks = points // LANES
    owners = n_lon * n_lat
    grid = (rows, cols)
    fields = (lam_in, flux_east, flux_north, depth, drag, ocean, coarse_of)
    tall = rows // LANES
    to_east, to_west, to_lat, *fields = call(
        functools.partial(pack_kernel, points=points),
        [(6 * tall, cols), (6 * tall, cols), (8, cols)]
        + [(grid, field.dtype) for field in fields],
        [pltpu.SemaphoreType.DMA((7,))], fields, "pack", far=range(7), limit=52,
    )
    ocean, coarse_of = fields[5:]
    forward = [(k, (k + 1) % n_lon) for k in range(n_lon)]
    backward = [(target, source) for source, target in forward]
    from_west = lax.ppermute(to_east, "lon", forward)
    from_east = lax.ppermute(to_west, "lon", backward)
    from_lat = lax.ppermute(to_lat, "lat", [(0, 1), (1, 0)])
    held, gu, cu, gv, cv, sums, left, right, held_sides, green_top = call(
        functools.partial(inner_kernel, points=points),
        [grid] * 5
        + [((PIECES + 1) * HIGH, LOW), ((HIGH, rows * cols), bf16), ((LOW, rows * cols), bf16)]
        + [(2 * tall, cols), (LANES, green.shape[1])],
        [pltpu.VMEM(grid, f32), pltpu.SemaphoreType.DMA(())], (*fields, green), "inner",
        far=(7,), limit=INNER_LIMIT,
    )
    payload, faces, lat_lines, green_top = call(
        functools.partial(rim_kernel, points=points),
        [(owners, 8, LANES), (7, 2 * tall, cols), (8, cols), green_top.shape], [],
        (
            to_east, to_west, to_lat, from_west, from_east, from_lat, sums, held_sides, green_top,
        ),
        "rim", far=(8,), far_out=(3,), weight=16, aliases={8: 3},
    )
    green_north = lax.ppermute(green_top, "lat", [(0, 1), (1, 0)])
    first = lax.all_to_all(payload, ("lon", "lat"), 0, 0, tiled=True)
    deep = 4 * blocks + tall
    green_scratch = [
        pltpu.VMEM((LANES, LANES), f32),
        pltpu.VMEM((blocks, 8, LANES), f32),
        pltpu.VMEM(grid, f32),
    ]
    payload, held, adj_u, adj_v, lam_sides, lam_edge = call(
        functools.partial(second_kernel, points=points, n_lon=n_lon, n_lat=n_lat),
        [(owners * deep, LANES), grid, grid, grid, (2 * tall, cols), (1, cols)],
        green_scratch + [pltpu.VMEM((rows + 8, cols), f32), pltpu.VMEM(grid, f32)],
        (first, green, coarse_of, ocean, held, gu, cu, gv, cv, left, right, faces, lat_lines),
        "second",
    )
    second = lax.all_to_all(
        payload.reshape(owners, deep, 1, LANES), ("lon", "lat"), 0, 0, tiled=True
    ).reshape(payload.shape)
    span = rows // n_lon
    lam, payload, east, north = call(
        functools.partial(last_kernel, points=points, n_lon=n_lon, n_lat=n_lat),
        [grid, (rows + n_lon, cols), grid, grid],
        [
            pltpu.VMEM((rows, 2 * cols), f32),
            pltpu.VMEM(grid, f32),
            pltpu.VMEM(grid, f32),
            pltpu.SemaphoreType.DMA((2,)),
            pltpu.VMEM((owners * blocks, LANES), f32),
        ]
        + green_scratch,
        (
            first, second, green, green_north, coarse_of, ocean, held, adj_u, adj_v, faces,
            lat_lines, lam_sides, lam_edge,
        ),
        "last", far_out=(2, 3),
    )
    parts = lax.all_to_all(
        payload.reshape(n_lon, span + 1, 1, LANES), "lon", 0, 0, tiled=True
    ).reshape(payload.shape)
    lam, bands = call(
        functools.partial(bands_kernel, count=n_lon),
        [grid, (3, 1, span, n_lon * cols)],
        [pltpu.VMEM((3, span, n_lon * cols), f32), pltpu.SemaphoreType.DMA((4,))],
        (parts, lam), "bands", far_out=(0, 1),
    )
    return lam, east, north, bands


def solution(mesh):
    cells = P(("groups", "lat"), "lon")
    n_lon, n_lat = mesh.shape["lon"], mesh.shape["lat"]
    return jax.shard_map(
        functools.partial(body, n_lon, n_lat),
        mesh=mesh,
        in_specs=(cells,) * 6 + (P("lat", "lon"), P(("lon", "lat"), None)),
        out_specs=(cells,) * 3 + (P(None, ("groups", "lat"), "lon", None),),
        check_vma=False,
    )
```

```python
import functools

import jax
import jax.numpy as jnp
from jax import lax
from jax.experimental import pallas as pl
from jax.experimental.pallas import tpu as pltpu
from jax.sharding import PartitionSpec as P

f32 = jnp.float32
bf16 = jnp.bfloat16
i32 = jnp.int32

LANES = 128
LOW = 32
HIGH = 16
PIECES = 2
INNER_LIMIT = 36
SEG_ROWS = 256
STEP_ROWS = 128

flux_ratio = 0.25
slope_ratio = 0.25
drag_step = 1.0
attract_coef = 0.5

LAM, DEPTH, DRAG, OCEAN, POINT, FLUX = range(6)
ADJ, RATIO, GAIN, BASE, MASK, OWN_ID, FAR_ID = range(7)
ADJ_L, C_L, G_L, ID_L, OWN_L, MASK_L = range(6)


def iota(shape, dim):
    return lax.broadcasted_iota(i32, shape, dim)


def roll_east(x):
    return pltpu.roll(x, LANES - 1, 1)


def roll_west(x):
    return pltpu.roll(x, 1, 1)


def local_ids(ids, points):
    return lax.bitwise_and(ids, points - 1)


def bf16_pieces(values, count=PIECES):
    out = []
    for piece in range(count):
        top = values.astype(bf16).astype(f32)
        out.append(top)
        if piece < count - 1:
            values = values - top
    return out


def one_hots(ids, points):
    blocks = points // LANES
    high = lax.shift_right_logical(ids, 5)
    high = lax.bitwise_and(high, 3) * blocks + lax.shift_right_logical(high, 2)
    low = lax.bitwise_and(ids, LOW - 1)
    high_iota = iota((HIGH, LANES), 0)
    low_iota = iota((LOW, LANES), 0)
    left, right = [], []
    for row in range(ids.shape[0]):
        mask = jnp.broadcast_to(high[row : row + 1], (HIGH, LANES)) == high_iota
        left.append(jnp.where(mask, 1.0, 0.0).astype(bf16))
        mask = jnp.broadcast_to(low[row : row + 1], (LOW, LANES)) == low_iota
        right.append(jnp.where(mask, 1.0, 0.0).astype(bf16))
    return jnp.concatenate(left, 1), jnp.concatenate(right, 1)


def segment_part(values, left, right, with_counts=False):
    parts = []
    for piece in bf16_pieces(values):
        line = jnp.concatenate(
            [
                jnp.broadcast_to(piece[row : row + 1], (HIGH, LANES)).astype(bf16)
                for row in range(values.shape[0])
            ],
            1,
        )
        parts.append(left * line)
    if with_counts:
        parts.append(left)
    return lax.dot_general(
        jnp.concatenate(parts, 0), right, (((1,), (1,)), ((), ())), preferred_element_type=f32
    )


def segment_few(values, ids, points):
    return sum_pieces(segment_part(values, *one_hots(ids, points)))


def sum_pieces(parts):
    total = parts[:HIGH]
    for piece in range(1, PIECES):
        total = total + parts[piece * HIGH : (piece + 1) * HIGH]
    return total


def as_points(table, points):
    blocks = points // LANES
    return jnp.concatenate([table[q * blocks : (q + 1) * blocks] for q in range(4)], 1)


def fold(line):
    return jnp.concatenate(
        [line[:, k * LANES : (k + 1) * LANES] for k in range(line.shape[1] // LANES)], 0
    )


def unfold(block):
    return jnp.concatenate([block[k : k + 1] for k in range(block.shape[0])], 1)


def take_sides(block, count=3):
    sub, lane = iota((8, LANES), 0), iota((8, LANES), 1)
    pick = ((sub == 0) & (lane == 0)) | ((sub == 1) & (lane == LANES - 1))
    pick = pick.astype(f32).astype(bf16)
    out = None
    for piece in reversed(bf16_pieces(block, count)):
        part = lax.dot_general(
            pick, piece.astype(bf16), (((1,), (1,)), ((), ())), preferred_element_type=f32
        )
        out = part if out is None else out + part
    return out


def put_sides(pair, entries):
    half = pair.shape[0] // 2
    lines = jnp.concatenate([unfold(pair[:half]), unfold(pair[half:])], 0)
    rows = lines.shape[1]
    pieces = bf16_pieces(lines, 3)
    stack = jnp.concatenate(pieces + [jnp.zeros((2, rows), f32)], 0)
    sub, lane = iota((8, LANES), 0), iota((8, LANES), 1)
    west = (sub < 6) & (lax.bitwise_and(sub, 1) == 0) & (lane == 0)
    east = (sub < 6) & (lax.bitwise_and(sub, 1) == 1) & (lane == LANES - 1)
    picks = [jnp.where(west, first, jnp.where(east, last, 0.0)) for first, last in entries]
    return lax.dot_general(
        stack, jnp.concatenate(picks, 1), (((0,), (0,)), ((), ())), preferred_element_type=f32
    )


def sum_lanes(block):
    out = None
    for piece in reversed(bf16_pieces(block, 3)):
        part = lax.dot_general(
            jnp.ones((8, LANES), bf16), piece.astype(bf16), (((1,), (1,)), ((), ())),
            preferred_element_type=f32,
        )
        out = part if out is None else out + part
    return out


def green_rows(green_ref, start, load_row):
    acc = jnp.zeros((LANES, LANES), f32)
    for k in range(green_ref.shape[1] // LANES):
        acc = acc + green_ref[
            pl.ds(start, LANES), k * LANES : (k + 1) * LANES
        ] * jnp.broadcast_to(load_row(k), (LANES, LANES))
    return acc


def look_up(table, ids):
    rows = ids.shape[0]
    table = jnp.broadcast_to(table[None], (rows // 8, 8, LANES)).reshape(rows, LANES)
    return jnp.take_along_axis(table, ids, axis=1, mode="promise_in_bounds")


def spread(tables, ids):
    low = lax.bitwise_and(ids, LANES - 1)
    block = lax.shift_right_logical(ids, 7)
    out = None
    for k, table in enumerate(tables):
        value = look_up(table, low)
        out = value if out is None else jnp.where(block == k, value, out)
    return out


def green_spread(green, coarse, load_row, acc, tables, pot, more=None):
    points = green.shape[0]
    rows = coarse.shape[0]

    def settle(index):
        table = sum_lanes(acc[...])
        tables[index] = table
        for start in range(0, rows, STEP_ROWS):
            at = slice(start, start + STEP_ROWS)
            ids = local_ids(coarse[at, :], points)
            value = look_up(table, lax.bitwise_and(ids, LANES - 1))
            pot[at, :] = jnp.where(lax.shift_right_logical(ids, 7) == index, value, pot[at, :])

    def step(index, carry):
        block = green_rows(green, index * LANES, load_row)
        settle(index - 1)
        acc[...] = block
        return carry

    acc[...] = green_rows(green, 0, load_row)
    for index in range(1, points // LANES):
        step(index, 0)
    beside = more() if more else None
    settle(points // LANES - 1)
    return beside


def next_rows(ref, start, count):
    if start + count < ref.shape[0]:
        return ref[start + 1 : start + count + 1, :]
    return jnp.concatenate([ref[start + 1 :, :], jnp.zeros((1, LANES), ref.dtype)], 0)


def south_rows(first, block):
    return jnp.concatenate([first, block[:-1]], 0)


def pack_kernel(*refs, points):
    far, (to_east, to_west, to_lat), near, done = refs[:7], refs[7:10], refs[10:17], refs[17]
    copies = [pltpu.make_async_copy(far[k], near[k], done.at[k]) for k in range(7)]
    for copy in copies:
        copy.start()
    lam, east, north, depth, drag, ocean, coarse = near
    rows = lam.shape[0]
    tall = rows // LANES
    lat = lax.axis_index("lat")
    order = (
        (LAM, 0, lam, 2), (FLUX, 1, east, 2), (None, 2, north, 0), (DEPTH, 3, depth, 2),
        (DRAG, 4, drag, 2), (OCEAN, 5, ocean, 1), (POINT, 6, coarse, 2),
    )
    for field, index, ref, pieces in order:
        copies[index].wait()
        if field is None:
            continue
        block = ref[...]
        if field == POINT:
            block = local_ids(block, points)
        sides = take_sides(block.astype(f32), pieces)
        at = slice(field * tall, (field + 1) * tall)
        to_west[at, :] = fold(sides[0:1])
        to_east[at, :] = fold(sides[1:2])

    def border(row):
        return jnp.concatenate(
            [
                lam[row : row + 1, :],
                depth[row : row + 1, :],
                drag[row : row + 1, :],
                ocean[row : row + 1, :].astype(f32),
                local_ids(coarse[row : row + 1, :], points).astype(f32),
                north[row : row + 1, :],
                jnp.zeros((2, LANES), f32),
            ],
            0,
        )

    to_lat[...] = jnp.where(lat == 0, border(rows - 1), border(0))


def inner_kernel(
    lam, east, north, depth, drag, ocean, coarse, green,
    held, gu, cu, gv, cv, sums, left, right, held_sides, green_top, source, done, *, points,
):
    copy = pltpu.make_async_copy(green.at[pl.ds(0, LANES)], green_top, done)
    copy.start()
    rows = lam.shape[0]
    inner = iota((STEP_ROWS, LANES), 1) < LANES - 1
    carry = jnp.zeros((1, LANES), f32)
    for start in range(0, rows, STEP_ROWS):
        at = slice(start, start + STEP_ROWS)
        lam_c, depth_c, drag_c = lam[at, :], depth[at, :], drag[at, :]
        ocean_c = ocean[at, :].astype(f32)
        damp = jnp.where(
            inner,
            ocean_c * roll_east(ocean_c) / (1.0 + drag_step * 0.5 * (drag_c + roll_east(drag_c))),
            0.0,
        )
        ratio = damp * (flux_ratio * 0.5) * (depth_c + roll_east(depth_c))
        adj_u = damp * east[at, :] + ratio * (roll_east(lam_c) - lam_c)
        cu[at, :] = ratio
        gu[at, :] = damp * adj_u
        ocean_n = next_rows(ocean, start, STEP_ROWS).astype(f32)
        damp = (
            ocean_c
            * ocean_n
            / (1.0 + drag_step * 0.5 * (drag_c + next_rows(drag, start, STEP_ROWS)))
        )
        ratio = damp * (flux_ratio * 0.5) * (depth_c + next_rows(depth, start, STEP_ROWS))
        adj_v = damp * north[at, :] + ratio * (next_rows(lam, start, STEP_ROWS) - lam_c)
        cv[at, :] = ratio
        gv[at, :] = damp * adj_v
        src = slope_ratio * (roll_west(adj_u) - adj_u + south_rows(carry, adj_v) - adj_v)
        carry = adj_v[STEP_ROWS - 1 :]
        source[at, :] = src
        held[at, :] = lam_c + src
    total = jnp.zeros(sums.shape, f32)
    for start in range(0, rows, SEG_ROWS):
        at = slice(start, start + SEG_ROWS)
        cells = slice(start * LANES, (start + SEG_ROWS) * LANES)
        high, low = one_hots(local_ids(coarse[at, :], points), points)
        left[:, cells] = high
        right[:, cells] = low
        total = total + segment_part(source[at, :], high, low, True)
    sums[...] = total
    sides = take_sides(held[...])
    held_sides[...] = jnp.concatenate([fold(sides[0:1]), fold(sides[1:2])], 0)
    copy.wait()


def face(low, high, flux):
    damp = low[OCEAN] * high[OCEAN] / (1.0 + drag_step * 0.5 * (low[DRAG] + high[DRAG]))
    ratio = damp * (flux_ratio * 0.5) * (low[DEPTH] + high[DEPTH])
    adj = damp * flux + ratio * (high[LAM] - low[LAM])
    return adj, ratio, damp * adj


def west_rows():
    return iota((8, LANES), 0) < 4


def rim_kernel(
    own_east, own_west, own_lat, from_west, from_east, from_lat, sums, held_sides, green_in,
    payload, faces, lat_lines, green_out, *, points,
):
    lat = lax.axis_index("lat")
    half = held_sides.shape[0] // 2

    def pair(west, east):
        return [
            jnp.concatenate(
                [west[k * half : (k + 1) * half, :], east[k * half : (k + 1) * half, :]], 0
            )
            for k in range(6)
        ]

    own, far = pair(own_west, own_east), pair(from_west, from_east)
    is_west = west_rows()
    low = [jnp.where(is_west, there, here) for here, there in zip(own, far)]
    high = [jnp.where(is_west, here, there) for here, there in zip(own, far)]
    adj, ratio, gain = face(low, high, low[FLUX])
    mine, other = own_lat[...], from_lat[...]
    lower = jnp.where(lat == 0, mine, other)
    upper = jnp.where(lat == 0, other, mine)
    lower = [lower[k : k + 1] for k in range(6)]
    upper = [upper[k : k + 1] for k in range(6)]
    adj_l, c_l, g_l = face(lower, upper, lower[FLUX])
    lat_lines[...] = jnp.concatenate(
        [
            adj_l, c_l, g_l, other[POINT : POINT + 1], mine[POINT : POINT + 1],
            other[OCEAN : OCEAN + 1], jnp.zeros((2, LANES), f32),
        ],
        0,
    )
    sign = jnp.where(is_west, slope_ratio, -slope_ratio)
    sign_l = jnp.where(lat == 0, -slope_ratio, slope_ratio)
    flow = sign * adj
    sub, lane = lax.bitwise_and(iota((8, LANES), 0), half - 1), iota((8, LANES), 1)
    corner = ((lat == 0) & (sub == half - 1) & (lane == LANES - 1)) | (
        (lat == 1) & (sub == 0) & (lane == 0)
    )
    at_corner = jnp.where(
        is_west,
        jnp.broadcast_to(adj_l[:, 0:1], (8, LANES)),
        jnp.broadcast_to(adj_l[:, LANES - 1 :], (8, LANES)),
    )
    faces[ADJ] = adj
    faces[RATIO] = ratio
    faces[GAIN] = gain
    faces[BASE] = held_sides[...] + flow + jnp.where(corner, sign_l * at_corner, 0.0)
    faces[MASK] = own[OCEAN]
    faces[OWN_ID] = own[POINT]
    faces[FAR_ID] = far[POINT]
    pad = jnp.zeros((1, LANES), f32)
    values = jnp.concatenate([flow, sign_l * adj_l, pad], 0)
    ids = jnp.concatenate([own[POINT], mine[POINT : POINT + 1], pad], 0).astype(i32)
    total = sum_pieces(sums[...]) + segment_few(values, ids, points)
    counts = as_points(sums[PIECES * HIGH : (PIECES + 1) * HIGH, :], points)
    inverse = 1.0 / counts
    loads = as_points(total, points) * inverse
    part = jnp.concatenate([loads, inverse], 0)
    if part.shape[0] < 8:
        part = jnp.concatenate([part, jnp.zeros((8 - part.shape[0], LANES), f32)], 0)
    for target in range(payload.shape[0]):
        payload[target] = part


def neighbours(n_lon, n_lat):
    lon, lat = lax.axis_index("lon"), lax.axis_index("lat")
    west = lax.rem(lon + n_lon - 1, n_lon) * n_lat + lat
    east = lax.rem(lon + 1, n_lon) * n_lat + lat
    other = lon * n_lat + (1 - lat)
    return west, east, other


def second_kernel(
    first, green, coarse, ocean, held_in, gu, cu, gv, cv, left, right, faces, lat_lines,
    payload, held, adj_u_out, adj_v_out, lam_sides, lam_edge, acc, tables, pot, lam, source,
    *, points, n_lon, n_lat,
):
    rows = coarse.shape[0]
    blocks = points // LANES
    lat = lax.axis_index("lat")
    south_end = jnp.where(lat == 1, 1.0, 0.0)
    north_end = jnp.where(lat == 0, 1.0, 0.0)
    green_spread(
        green, coarse, lambda k: first[k // blocks, k % blocks : k % blocks + 1, :],
        acc, tables, pot,
    )
    put = put_sides(faces[ADJ], [(slope_ratio, -slope_ratio)])
    adj_l = lat_lines[ADJ_L : ADJ_L + 1, :]
    c_l = lat_lines[C_L : C_L + 1, :]
    g_l = lat_lines[G_L : G_L + 1, :]
    row = iota((STEP_ROWS, LANES), 0)
    lam[rows : rows + 8, :] = jnp.zeros((8, LANES), f32)
    for start in range(0, rows, STEP_ROWS):
        at = slice(start, start + STEP_ROWS)
        value = held_in[at, :] + put[at, :] - attract_coef * pot[at, :]
        if start == 0:
            value = value + jnp.where(row == 0, south_end * slope_ratio * adj_l, 0.0)
        if start == rows - STEP_ROWS:
            value = value - jnp.where(row == STEP_ROWS - 1, north_end * slope_ratio * adj_l, 0.0)
        lam[at, :] = ocean[at, :].astype(f32) * value
    carry = jnp.zeros((1, LANES), f32)
    for start in range(0, rows, STEP_ROWS):
        at = slice(start, start + STEP_ROWS)
        lam_c = lam[at, :]
        adj_u = gu[at, :] + cu[at, :] * (roll_east(lam_c) - lam_c)
        adj_v = gv[at, :] + cv[at, :] * (lam[start + 1 : start + STEP_ROWS + 1, :] - lam_c)
        src = slope_ratio * (roll_west(adj_u) - adj_u + south_rows(carry, adj_v) - adj_v)
        carry = adj_v[STEP_ROWS - 1 :]
        adj_u_out[at, :] = adj_u
        adj_v_out[at, :] = adj_v
        source[at, :] = src
        held[at, :] = lam_c + src
    is_west = west_rows()
    sides = faces[MASK] * (
        faces[BASE]
        - attract_coef * spread([tables[k] for k in range(blocks)], faces[OWN_ID].astype(i32))
    )
    lam_sides[...] = sides
    pull = faces[RATIO] * sides
    flow = slope_ratio * jnp.where(is_west, pull, pull - faces[GAIN])
    edge = jnp.where(lat == 0, lam[rows - 1 : rows, :], lam[0:1, :])
    lam_edge[...] = edge
    pull = c_l * edge
    flow_l = slope_ratio * jnp.where(lat == 0, pull - g_l, pull)
    pad = jnp.zeros((1, LANES), f32)
    total = segment_part(
        jnp.concatenate([flow, flow_l, pad], 0),
        *one_hots(
            jnp.concatenate([faces[OWN_ID], lat_lines[OWN_L : OWN_L + 1, :], pad], 0).astype(i32),
            points,
        ),
    )
    def add(index, total):
        at = pl.ds(pl.multiple_of(index * SEG_ROWS, SEG_ROWS), SEG_ROWS)
        cells = pl.ds(pl.multiple_of(index * SEG_ROWS * LANES, SEG_ROWS * LANES), SEG_ROWS * LANES)
        return total + segment_part(source[at, :], left[:, cells], right[:, cells])

    total = lax.fori_loop(0, rows // SEG_ROWS, add, total)
    own = as_points(sum_pieces(total), points)
    far_id = faces[FAR_ID].astype(i32)
    half = far_id.shape[0] // 2

    def away(values, ids):
        return as_points(segment_few(-values, ids, points), points)

    west_part = away(flow[:half], far_id[:half])
    east_part = away(flow[half:], far_id[half:])
    lat_part = away(
        jnp.concatenate([flow_l, pad], 0),
        jnp.concatenate([lat_lines[ID_L : ID_L + 1, :], pad], 0).astype(i32),
    )
    west, east, other = neighbours(n_lon, n_lat)
    part = jnp.concatenate([own, east_part, west_part, lat_part], 0)
    begin = 4 * blocks
    deep = begin + half
    first_lane = iota((1, LANES), 1) == 0

    def corners(block):
        return jnp.where(
            first_lane,
            block[0:1],
            jnp.broadcast_to(block[half : half + 1, 0:1], (1, LANES)),
        )

    edge_rows = jnp.concatenate(
        [edge, held[0:1, :], corners(faces[GAIN]), corners(faces[RATIO])]
        + [jnp.zeros((1, LANES), f32)] * (half - 4),
        0,
    )
    for target in range(n_lon * n_lat):
        shared = jnp.where(
            target == west, sides[:half], jnp.where(target == east, sides[half:], edge_rows)
        )
        payload[target * deep : (target + 1) * deep, :] = jnp.concatenate([part, shared], 0)


def last_kernel(
    first, second, green, green_north, coarse, ocean, held, faces, lat_lines, lam_sides, lam_edge,
    lam_out, payload, put, north_line, loads, acc, tables, pot,
    *, points, n_lon, n_lat,
):
    rows = held.shape[0]
    blocks = points // LANES
    half = rows // LANES
    deep = 4 * blocks + half
    lat = lax.axis_index("lat")

    def received(owner, kind):
        start = owner * deep + kind * blocks
        return second[start : start + blocks, :]

    for lon in range(n_lon):
        for band in range(n_lat):
            here = lon * n_lat + band
            west = (lon - 1) % n_lon * n_lat + band
            east = (lon + 1) % n_lon * n_lat + band
            other = lon * n_lat + 1 - band
            total = received(here, 0) + received(west, 1) + received(east, 2) + received(other, 3)
            loads[here * blocks : (here + 1) * blocks, :] = (
                total * first[here, blocks : 2 * blocks, :]
            )
    west, east, other = neighbours(n_lon, n_lat)

    def shared(owner, row, count):
        return second[pl.ds(owner * deep + 4 * blocks + row, count), :]

    far = jnp.concatenate([shared(west, 0, half), shared(east, 0, half)], 0)
    rise = jnp.where(west_rows(), lam_sides[...] - far, far - lam_sides[...])
    adj = faces[GAIN] + faces[RATIO] * rise
    put[...] = put_sides(adj, [(slope_ratio, -slope_ratio), (0.0, 1.0)])
    rise = shared(other, 0, 1) - lam_edge[...]
    adj_l = lat_lines[G_L : G_L + 1, :] + lat_lines[C_L : C_L + 1, :] * jnp.where(
        lat == 0, rise, -rise
    )
    from_north = jnp.where(lat == 0, adj_l, 0.0)
    from_south = jnp.where(lat == 1, adj_l, 0.0)
    put[0:1, :LANES] = put[0:1, :LANES] + slope_ratio * from_south
    put[rows - 1 : rows, :LANES] = put[rows - 1 : rows, :LANES] - slope_ratio * from_north
    north_line[...] = from_north
    load_row = lambda k: loads[k : k + 1, :]
    north_sums = green_spread(
        green, coarse, load_row, acc, tables, pot, lambda: green_rows(green_north, 0, load_row)
    )
    for start in range(0, rows, STEP_ROWS):
        at = slice(start, start + STEP_ROWS)
        lam_out[at, :] = ocean[at, :].astype(f32) * (
            held[at, :] + put[at, :LANES] - attract_coef * pot[at, :]
        )
    potential = sum_lanes(north_sums)[0:1]
    diagonal = lambda owner: shared(owner + 1 - 2 * lat, 0, 1)
    lam_n = shared(other, 0, 1)
    lane = iota((1, LANES), 1)
    rise = jnp.where(
        lane == 0, lam_n - roll_west(diagonal(west)), roll_east(diagonal(east)) - lam_n
    )
    adj = shared(other, 2, 1) + shared(other, 3, 1) * rise
    flow = jnp.where(lane == 0, adj, jnp.where(lane == LANES - 1, -adj, 0.0)) + adj_l
    lam_north = lat_lines[MASK_L : MASK_L + 1, :] * (
        shared(other, 1, 1) + slope_ratio * flow - attract_coef * potential
    )
    span = rows // n_lon
    for target in range(n_lon):
        start = target * (span + 1)
        payload[start : start + span, :] = lam_out[target * span : (target + 1) * span, :]
        if target < n_lon - 1:
            stop = (target + 1) * span
            payload[start + span : start + span + 1, :] = lam_out[stop : stop + 1, :]
        else:
            payload[start + span : start + span + 1, :] = lam_north


def bands_kernel(
    parts, lam, adj_u, adj_v, put, north_line,
    lam_out, east_out, north_out, bands, east, north, planes, done, *, count,
):
    span = parts.shape[0] // count - 1
    rows = lam.shape[0]
    copies = [
        pltpu.make_async_copy(lam, lam_out, done.at[0]),
        pltpu.make_async_copy(east, east_out, done.at[1]),
        pltpu.make_async_copy(north, north_out, done.at[2]),
    ] + [
        pltpu.make_async_copy(planes.at[k], bands.at[k, 0], done.at[3 + k]) for k in range(3)
    ]
    copies[0].start()
    lane = iota((span, LANES), 1)
    top = (lax.axis_index("lat") == 1) & (lax.axis_index("lon") == count - 1)
    last = (iota((span, LANES), 0) == span - 1) & top
    for k in range(count):
        start = k * (span + 1)
        planes[0, :, k * LANES : (k + 1) * LANES] = parts[start : start + span, :]
    copies[3].start()
    for k in range(count):
        start = k * (span + 1)
        here = parts[start : start + span, :]
        north_of = jnp.where(last, 0.0, parts[start + 1 : start + 1 + span, :])
        planes[2, :, k * LANES : (k + 1) * LANES] = north_of - here
    copies[5].start()
    for k in range(count):
        at = slice(k * LANES, (k + 1) * LANES)
        here = planes[0, :, at]
        after = (k + 1) % count
        there = planes[0, :, after * LANES : (after + 1) * LANES]
        planes[1, :, at] = jnp.where(lane == LANES - 1, roll_east(there), roll_east(here)) - here
    copies[4].start()
    east[...] = adj_u[...] + put[:, LANES:]
    copies[1].start()
    north[...] = adj_v[...]
    north[rows - 1 : rows, :] = adj_v[rows - 1 : rows, :] + north_line[...]
    copies[2].start()
    for copy in copies:
        copy.wait()


def call(kernel, shapes, scratch, args, name, far=(), far_out=(), limit=16, weight=4, aliases=None):
    vmem = pl.BlockSpec(memory_space=pltpu.VMEM)
    away = pl.BlockSpec(memory_space=pl.ANY)
    shapes = [(shape, f32) if isinstance(shape[0], int) else shape for shape in shapes]
    return pl.pallas_call(
        kernel,
        out_shape=[jax.ShapeDtypeStruct(shape, kind) for shape, kind in shapes],
        in_specs=[away if k in far else vmem for k in range(len(args))],
        out_specs=[away if k in far_out else vmem for k in range(len(shapes))],
        scratch_shapes=scratch,
        compiler_params=pltpu.CompilerParams(vmem_limit_bytes=limit << 20),
        cost_estimate=pl.CostEstimate(flops=weight << 30, bytes_accessed=16 << 20, transcendentals=0),
        input_output_aliases=aliases or {},
        name=name,
    )(*args)


def body(n_lon, n_lat, lam_in, flux_east, flux_north, depth, drag, ocean, coarse_of, green):
    rows, cols = lam_in.shape
    points = green.shape[0]
    blocks = points // LANES
    owners = n_lon * n_lat
    grid = (rows, cols)
    fields = (lam_in, flux_east, flux_north, depth, drag, ocean, coarse_of)
    tall = rows // LANES
    to_east, to_west, to_lat, *fields = call(
        functools.partial(pack_kernel, points=points),
        [(6 * tall, cols), (6 * tall, cols), (8, cols)]
        + [(grid, field.dtype) for field in fields],
        [pltpu.SemaphoreType.DMA((7,))], fields, "pack", far=range(7), limit=52,
    )
    ocean, coarse_of = fields[5:]
    forward = [(k, (k + 1) % n_lon) for k in range(n_lon)]
    backward = [(target, source) for source, target in forward]
    from_east = lax.ppermute(to_west, "lon", backward)
    from_west = lax.ppermute(to_east, "lon", forward)
    from_lat = lax.ppermute(to_lat, "lat", [(0, 1), (1, 0)])
    held, gu, cu, gv, cv, sums, left, right, held_sides, green_top = call(
        functools.partial(inner_kernel, points=points),
        [grid] * 5
        + [((PIECES + 1) * HIGH, LOW), ((HIGH, rows * cols), bf16), ((LOW, rows * cols), bf16)]
        + [(2 * tall, cols), (LANES, green.shape[1])],
        [pltpu.VMEM(grid, f32), pltpu.SemaphoreType.DMA(())], (*fields, green), "inner",
        far=(7,), limit=INNER_LIMIT,
    )
    payload, faces, lat_lines, green_top = call(
        functools.partial(rim_kernel, points=points),
        [(owners, 8, LANES), (7, 2 * tall, cols), (8, cols), green_top.shape], [],
        (
            to_east, to_west, to_lat, from_west, from_east, from_lat, sums, held_sides, green_top,
        ),
        "rim", far=(8,), far_out=(3,), weight=16, aliases={8: 3},
    )
    green_north = lax.ppermute(green_top, "lat", [(0, 1), (1, 0)])
    first = lax.all_to_all(payload, ("lon", "lat"), 0, 0, tiled=True)
    deep = 4 * blocks + tall
    green_scratch = [
        pltpu.VMEM((LANES, LANES), f32),
        pltpu.VMEM((blocks, 8, LANES), f32),
        pltpu.VMEM(grid, f32),
    ]
    payload, held, adj_u, adj_v, lam_sides, lam_edge = call(
        functools.partial(second_kernel, points=points, n_lon=n_lon, n_lat=n_lat),
        [(owners * deep, LANES), grid, grid, grid, (2 * tall, cols), (1, cols)],
        green_scratch + [pltpu.VMEM((rows + 8, cols), f32), pltpu.VMEM(grid, f32)],
        (first, green, coarse_of, ocean, held, gu, cu, gv, cv, left, right, faces, lat_lines),
        "second",
    )
    second = lax.all_to_all(
        payload.reshape(owners, deep, 1, LANES), ("lon", "lat"), 0, 0, tiled=True
    ).reshape(payload.shape)
    span = rows // n_lon
    lam, payload, put, north_line = call(
        functools.partial(last_kernel, points=points, n_lon=n_lon, n_lat=n_lat),
        [grid, (rows + n_lon, cols), (rows, 2 * cols), (1, cols)],
        [
            pltpu.VMEM((owners * blocks, LANES), f32),
        ]
        + green_scratch,
        (
            first, second, green, green_north, coarse_of, ocean, held, faces, lat_lines,
            lam_sides, lam_edge,
        ),
        "last",
    )
    parts = lax.all_to_all(
        payload.reshape(n_lon, span + 1, 1, LANES), "lon", 0, 0, tiled=True
    ).reshape(payload.shape)
    return tuple(
        call(
            functools.partial(bands_kernel, count=n_lon),
            [grid, grid, grid, (3, 1, span, n_lon * cols)],
            [
                pltpu.VMEM(grid, f32),
                pltpu.VMEM(grid, f32),
                pltpu.VMEM((3, span, n_lon * cols), f32),
                pltpu.SemaphoreType.DMA((6,)),
            ],
            (parts, lam, adj_u, adj_v, put, north_line), "bands", far_out=range(4),
        )
    )


def solution(mesh):
    cells = P(("groups", "lat"), "lon")
    n_lon, n_lat = mesh.shape["lon"], mesh.shape["lat"]
    return jax.shard_map(
        functools.partial(body, n_lon, n_lat),
        mesh=mesh,
        in_specs=(cells,) * 6 + (P("lat", "lon"), P(("lon", "lat"), None)),
        out_specs=(cells,) * 3 + (P(None, ("groups", "lat"), "lon", None),),
        check_vma=False,
    )
```

```python
import functools

import jax
import jax.numpy as jnp
from jax import lax
from jax.experimental import pallas as pl
from jax.experimental.pallas import tpu as pltpu
from jax.sharding import PartitionSpec as P

f32 = jnp.float32
bf16 = jnp.bfloat16
i32 = jnp.int32

LANES = 128
LOW = 32
HIGH = 16
PIECES = 2
INNER_LIMIT = 36
SEG_ROWS = 256
STEP_ROWS = 128

flux_ratio = 0.25
slope_ratio = 0.25
drag_step = 1.0
attract_coef = 0.5

LAM, DEPTH, DRAG, OCEAN, POINT, FLUX = range(6)
ADJ, RATIO, GAIN, BASE, MASK, OWN_ID, FAR_ID = range(7)
ADJ_L, C_L, G_L, ID_L, OWN_L, MASK_L = range(6)


def iota(shape, dim):
    return lax.broadcasted_iota(i32, shape, dim)


def roll_east(x):
    return pltpu.roll(x, LANES - 1, 1)


def roll_west(x):
    return pltpu.roll(x, 1, 1)


def local_ids(ids, points):
    return lax.bitwise_and(ids, points - 1)


def bf16_pieces(values, count=PIECES):
    out = []
    for piece in range(count):
        top = values.astype(bf16).astype(f32)
        out.append(top)
        if piece < count - 1:
            values = values - top
    return out


def one_hots(ids, points):
    blocks = points // LANES
    high = lax.shift_right_logical(ids, 5)
    high = lax.bitwise_and(high, 3) * blocks + lax.shift_right_logical(high, 2)
    low = lax.bitwise_and(ids, LOW - 1)
    high_iota = iota((HIGH, LANES), 0)
    low_iota = iota((LOW, LANES), 0)
    left, right = [], []
    for row in range(ids.shape[0]):
        mask = jnp.broadcast_to(high[row : row + 1], (HIGH, LANES)) == high_iota
        left.append(jnp.where(mask, 1.0, 0.0).astype(bf16))
        mask = jnp.broadcast_to(low[row : row + 1], (LOW, LANES)) == low_iota
        right.append(jnp.where(mask, 1.0, 0.0).astype(bf16))
    return jnp.concatenate(left, 1), jnp.concatenate(right, 1)


def segment_part(values, left, right, with_counts=False):
    parts = []
    for piece in bf16_pieces(values):
        line = jnp.concatenate(
            [
                jnp.broadcast_to(piece[row : row + 1], (HIGH, LANES)).astype(bf16)
                for row in range(values.shape[0])
            ],
            1,
        )
        parts.append(left * line)
    if with_counts:
        parts.append(left)
    return lax.dot_general(
        jnp.concatenate(parts, 0), right, (((1,), (1,)), ((), ())), preferred_element_type=f32
    )


def segment_few(values, ids, points):
    return sum_pieces(segment_part(values, *one_hots(ids, points)))


def sum_pieces(parts):
    total = parts[:HIGH]
    for piece in range(1, PIECES):
        total = total + parts[piece * HIGH : (piece + 1) * HIGH]
    return total


def as_points(table, points):
    blocks = points // LANES
    return jnp.concatenate([table[q * blocks : (q + 1) * blocks] for q in range(4)], 1)


def fold(line):
    return jnp.concatenate(
        [line[:, k * LANES : (k + 1) * LANES] for k in range(line.shape[1] // LANES)], 0
    )


def unfold(block):
    return jnp.concatenate([block[k : k + 1] for k in range(block.shape[0])], 1)


def take_sides(block, count=3):
    sub, lane = iota((8, LANES), 0), iota((8, LANES), 1)
    pick = ((sub == 0) & (lane == 0)) | ((sub == 1) & (lane == LANES - 1))
    pick = pick.astype(f32).astype(bf16)
    out = None
    for piece in reversed(bf16_pieces(block, count)):
        part = lax.dot_general(
            pick, piece.astype(bf16), (((1,), (1,)), ((), ())), preferred_element_type=f32
        )
        out = part if out is None else out + part
    return out


def put_sides(pair, entries):
    half = pair.shape[0] // 2
    lines = jnp.concatenate([unfold(pair[:half]), unfold(pair[half:])], 0)
    rows = lines.shape[1]
    pieces = bf16_pieces(lines, 3)
    stack = jnp.concatenate(pieces + [jnp.zeros((2, rows), f32)], 0)
    sub, lane = iota((8, LANES), 0), iota((8, LANES), 1)
    west = (sub < 6) & (lax.bitwise_and(sub, 1) == 0) & (lane == 0)
    east = (sub < 6) & (lax.bitwise_and(sub, 1) == 1) & (lane == LANES - 1)
    picks = [jnp.where(west, first, jnp.where(east, last, 0.0)) for first, last in entries]
    return lax.dot_general(
        stack, jnp.concatenate(picks, 1), (((0,), (0,)), ((), ())), preferred_element_type=f32
    )


def sum_lanes(block):
    out = None
    for piece in reversed(bf16_pieces(block, 3)):
        part = lax.dot_general(
            jnp.ones((8, LANES), bf16), piece.astype(bf16), (((1,), (1,)), ((), ())),
            preferred_element_type=f32,
        )
        out = part if out is None else out + part
    return out


def green_rows(green_ref, start, load_row):
    acc = jnp.zeros((LANES, LANES), f32)
    for k in range(green_ref.shape[1] // LANES):
        acc = acc + green_ref[
            pl.ds(start, LANES), k * LANES : (k + 1) * LANES
        ] * jnp.broadcast_to(load_row(k), (LANES, LANES))
    return acc


def look_up(table, ids):
    rows = ids.shape[0]
    table = jnp.broadcast_to(table[None], (rows // 8, 8, LANES)).reshape(rows, LANES)
    return jnp.take_along_axis(table, ids, axis=1, mode="promise_in_bounds")


def spread(tables, ids):
    low = lax.bitwise_and(ids, LANES - 1)
    block = lax.shift_right_logical(ids, 7)
    out = None
    for k, table in enumerate(tables):
        value = look_up(table, low)
        out = value if out is None else jnp.where(block == k, value, out)
    return out


def green_spread(green, coarse, load_row, acc, tables, pot, more=None):
    points = green.shape[0]
    rows = coarse.shape[0]

    def settle(index):
        table = sum_lanes(acc[...])
        tables[index] = table
        for start in range(0, rows, STEP_ROWS):
            at = slice(start, start + STEP_ROWS)
            ids = local_ids(coarse[at, :], points)
            value = look_up(table, lax.bitwise_and(ids, LANES - 1))
            pot[at, :] = jnp.where(lax.shift_right_logical(ids, 7) == index, value, pot[at, :])

    def step(index, carry):
        block = green_rows(green, index * LANES, load_row)
        settle(index - 1)
        acc[...] = block
        return carry

    acc[...] = green_rows(green, 0, load_row)
    for index in range(1, points // LANES):
        step(index, 0)
    beside = more() if more else None
    settle(points // LANES - 1)
    return beside


def next_rows(ref, start, count):
    if start + count < ref.shape[0]:
        return ref[start + 1 : start + count + 1, :]
    return jnp.concatenate([ref[start + 1 :, :], jnp.zeros((1, LANES), ref.dtype)], 0)


def south_rows(first, block):
    return jnp.concatenate([first, block[:-1]], 0)


def pack_kernel(*refs, points):
    far, (to_east, to_west, to_lat), near, done = refs[:7], refs[7:10], refs[10:17], refs[17]
    copies = [pltpu.make_async_copy(far[k], near[k], done.at[k]) for k in range(7)]
    for copy in copies:
        copy.start()
    lam, east, north, depth, drag, ocean, coarse = near
    rows = lam.shape[0]
    tall = rows // LANES
    lat = lax.axis_index("lat")
    order = (
        (LAM, 0, lam, 2), (FLUX, 1, east, 2), (None, 2, north, 0), (DEPTH, 3, depth, 2),
        (DRAG, 4, drag, 2), (OCEAN, 5, ocean, 1), (POINT, 6, coarse, 2),
    )
    for field, index, ref, pieces in order:
        copies[index].wait()
        if field is None:
            continue
        block = ref[...]
        if field == POINT:
            block = local_ids(block, points)
        sides = take_sides(block.astype(f32), pieces)
        at = slice(field * tall, (field + 1) * tall)
        to_west[at, :] = fold(sides[0:1])
        to_east[at, :] = fold(sides[1:2])

    def border(row):
        return jnp.concatenate(
            [
                lam[row : row + 1, :],
                depth[row : row + 1, :],
                drag[row : row + 1, :],
                ocean[row : row + 1, :].astype(f32),
                local_ids(coarse[row : row + 1, :], points).astype(f32),
                north[row : row + 1, :],
                jnp.zeros((2, LANES), f32),
            ],
            0,
        )

    to_lat[...] = jnp.where(lat == 0, border(rows - 1), border(0))


def inner_kernel(
    lam, east, north, depth, drag, ocean, coarse, green,
    held, gu, cu, gv, cv, sums, left, right, held_sides, green_top, source, done, *, points,
):
    copy = pltpu.make_async_copy(green.at[pl.ds(0, LANES)], green_top, done)
    copy.start()
    rows = lam.shape[0]
    inner = iota((STEP_ROWS, LANES), 1) < LANES - 1
    carry = jnp.zeros((1, LANES), f32)
    for start in range(0, rows, STEP_ROWS):
        at = slice(start, start + STEP_ROWS)
        lam_c, depth_c, drag_c = lam[at, :], depth[at, :], drag[at, :]
        ocean_c = ocean[at, :].astype(f32)
        damp = jnp.where(
            inner,
            ocean_c * roll_east(ocean_c) / (1.0 + drag_step * 0.5 * (drag_c + roll_east(drag_c))),
            0.0,
        )
        ratio = damp * (flux_ratio * 0.5) * (depth_c + roll_east(depth_c))
        adj_u = damp * east[at, :] + ratio * (roll_east(lam_c) - lam_c)
        cu[at, :] = ratio
        gu[at, :] = damp * adj_u
        ocean_n = next_rows(ocean, start, STEP_ROWS).astype(f32)
        damp = (
            ocean_c
            * ocean_n
            / (1.0 + drag_step * 0.5 * (drag_c + next_rows(drag, start, STEP_ROWS)))
        )
        ratio = damp * (flux_ratio * 0.5) * (depth_c + next_rows(depth, start, STEP_ROWS))
        adj_v = damp * north[at, :] + ratio * (next_rows(lam, start, STEP_ROWS) - lam_c)
        cv[at, :] = ratio
        gv[at, :] = damp * adj_v
        src = slope_ratio * (roll_west(adj_u) - adj_u + south_rows(carry, adj_v) - adj_v)
        carry = adj_v[STEP_ROWS - 1 :]
        source[at, :] = src
        held[at, :] = lam_c + src
    total = jnp.zeros(sums.shape, f32)
    for start in range(0, rows, SEG_ROWS):
        at = slice(start, start + SEG_ROWS)
        cells = slice(start * LANES, (start + SEG_ROWS) * LANES)
        high, low = one_hots(local_ids(coarse[at, :], points), points)
        left[:, cells] = high
        right[:, cells] = low
        total = total + segment_part(source[at, :], high, low, True)
    sums[...] = total
    sides = take_sides(held[...])
    held_sides[...] = jnp.concatenate([fold(sides[0:1]), fold(sides[1:2])], 0)
    copy.wait()


def face(low, high, flux):
    damp = low[OCEAN] * high[OCEAN] / (1.0 + drag_step * 0.5 * (low[DRAG] + high[DRAG]))
    ratio = damp * (flux_ratio * 0.5) * (low[DEPTH] + high[DEPTH])
    adj = damp * flux + ratio * (high[LAM] - low[LAM])
    return adj, ratio, damp * adj


def west_rows():
    return iota((8, LANES), 0) < 4


def rim_kernel(
    own_east, own_west, own_lat, from_west, from_east, from_lat, sums, held_sides, green_in,
    payload, faces, lat_lines, green_out, *, points,
):
    lat = lax.axis_index("lat")
    half = held_sides.shape[0] // 2

    def pair(west, east):
        return [
            jnp.concatenate(
                [west[k * half : (k + 1) * half, :], east[k * half : (k + 1) * half, :]], 0
            )
            for k in range(6)
        ]

    own, far = pair(own_west, own_east), pair(from_west, from_east)
    is_west = west_rows()
    low = [jnp.where(is_west, there, here) for here, there in zip(own, far)]
    high = [jnp.where(is_west, here, there) for here, there in zip(own, far)]
    adj, ratio, gain = face(low, high, low[FLUX])
    mine, other = own_lat[...], from_lat[...]
    lower = jnp.where(lat == 0, mine, other)
    upper = jnp.where(lat == 0, other, mine)
    lower = [lower[k : k + 1] for k in range(6)]
    upper = [upper[k : k + 1] for k in range(6)]
    adj_l, c_l, g_l = face(lower, upper, lower[FLUX])
    lat_lines[...] = jnp.concatenate(
        [
            adj_l, c_l, g_l, other[POINT : POINT + 1], mine[POINT : POINT + 1],
            other[OCEAN : OCEAN + 1], jnp.zeros((2, LANES), f32),
        ],
        0,
    )
    sign = jnp.where(is_west, slope_ratio, -slope_ratio)
    sign_l = jnp.where(lat == 0, -slope_ratio, slope_ratio)
    flow = sign * adj
    sub, lane = lax.bitwise_and(iota((8, LANES), 0), half - 1), iota((8, LANES), 1)
    corner = ((lat == 0) & (sub == half - 1) & (lane == LANES - 1)) | (
        (lat == 1) & (sub == 0) & (lane == 0)
    )
    at_corner = jnp.where(
        is_west,
        jnp.broadcast_to(adj_l[:, 0:1], (8, LANES)),
        jnp.broadcast_to(adj_l[:, LANES - 1 :], (8, LANES)),
    )
    faces[ADJ] = adj
    faces[RATIO] = ratio
    faces[GAIN] = gain
    faces[BASE] = held_sides[...] + flow + jnp.where(corner, sign_l * at_corner, 0.0)
    faces[MASK] = own[OCEAN]
    faces[OWN_ID] = own[POINT]
    faces[FAR_ID] = far[POINT]
    pad = jnp.zeros((1, LANES), f32)
    values = jnp.concatenate([flow, sign_l * adj_l, pad], 0)
    ids = jnp.concatenate([own[POINT], mine[POINT : POINT + 1], pad], 0).astype(i32)
    total = sum_pieces(sums[...]) + segment_few(values, ids, points)
    counts = as_points(sums[PIECES * HIGH : (PIECES + 1) * HIGH, :], points)
    inverse = 1.0 / counts
    loads = as_points(total, points) * inverse
    part = jnp.concatenate([loads, inverse], 0)
    if part.shape[0] < 8:
        part = jnp.concatenate([part, jnp.zeros((8 - part.shape[0], LANES), f32)], 0)
    for target in range(payload.shape[0]):
        payload[target] = part


def neighbours(n_lon, n_lat):
    lon, lat = lax.axis_index("lon"), lax.axis_index("lat")
    west = lax.rem(lon + n_lon - 1, n_lon) * n_lat + lat
    east = lax.rem(lon + 1, n_lon) * n_lat + lat
    other = lon * n_lat + (1 - lat)
    return west, east, other


def second_kernel(
    first, green, coarse, ocean, held_in, gu, cu, gv, cv, left, right, faces, lat_lines,
    payload, held, adj_u_out, adj_v_out, lam_sides, lam_edge, acc, tables, pot, lam, source,
    *, points, n_lon, n_lat,
):
    rows = coarse.shape[0]
    blocks = points // LANES
    lat = lax.axis_index("lat")
    south_end = jnp.where(lat == 1, 1.0, 0.0)
    north_end = jnp.where(lat == 0, 1.0, 0.0)
    green_spread(
        green, coarse, lambda k: first[k // blocks, k % blocks : k % blocks + 1, :],
        acc, tables, pot,
    )
    put = put_sides(faces[ADJ], [(slope_ratio, -slope_ratio)])
    adj_l = lat_lines[ADJ_L : ADJ_L + 1, :]
    c_l = lat_lines[C_L : C_L + 1, :]
    g_l = lat_lines[G_L : G_L + 1, :]
    row = iota((STEP_ROWS, LANES), 0)
    lam[rows : rows + 8, :] = jnp.zeros((8, LANES), f32)
    for start in range(0, rows, STEP_ROWS):
        at = slice(start, start + STEP_ROWS)
        value = held_in[at, :] + put[at, :] - attract_coef * pot[at, :]
        if start == 0:
            value = value + jnp.where(row == 0, south_end * slope_ratio * adj_l, 0.0)
        if start == rows - STEP_ROWS:
            value = value - jnp.where(row == STEP_ROWS - 1, north_end * slope_ratio * adj_l, 0.0)
        lam[at, :] = ocean[at, :].astype(f32) * value
    carry = jnp.zeros((1, LANES), f32)
    for start in range(0, rows, STEP_ROWS):
        at = slice(start, start + STEP_ROWS)
        lam_c = lam[at, :]
        adj_u = gu[at, :] + cu[at, :] * (roll_east(lam_c) - lam_c)
        adj_v = gv[at, :] + cv[at, :] * (lam[start + 1 : start + STEP_ROWS + 1, :] - lam_c)
        src = slope_ratio * (roll_west(adj_u) - adj_u + south_rows(carry, adj_v) - adj_v)
        carry = adj_v[STEP_ROWS - 1 :]
        adj_u_out[at, :] = adj_u
        adj_v_out[at, :] = adj_v
        source[at, :] = src
        held[at, :] = lam_c + src
    is_west = west_rows()
    sides = faces[MASK] * (
        faces[BASE]
        - attract_coef * spread([tables[k] for k in range(blocks)], faces[OWN_ID].astype(i32))
    )
    lam_sides[...] = sides
    pull = faces[RATIO] * sides
    flow = slope_ratio * jnp.where(is_west, pull, pull - faces[GAIN])
    edge = jnp.where(lat == 0, lam[rows - 1 : rows, :], lam[0:1, :])
    lam_edge[...] = edge
    pull = c_l * edge
    flow_l = slope_ratio * jnp.where(lat == 0, pull - g_l, pull)
    pad = jnp.zeros((1, LANES), f32)
    total = segment_part(
        jnp.concatenate([flow, flow_l, pad], 0),
        *one_hots(
            jnp.concatenate([faces[OWN_ID], lat_lines[OWN_L : OWN_L + 1, :], pad], 0).astype(i32),
            points,
        ),
    )
    def add(index, total):
        at = pl.ds(pl.multiple_of(index * SEG_ROWS, SEG_ROWS), SEG_ROWS)
        cells = pl.ds(pl.multiple_of(index * SEG_ROWS * LANES, SEG_ROWS * LANES), SEG_ROWS * LANES)
        return total + segment_part(source[at, :], left[:, cells], right[:, cells])

    total = lax.fori_loop(0, rows // SEG_ROWS, add, total)
    own = as_points(sum_pieces(total), points)
    far_id = faces[FAR_ID].astype(i32)
    half = far_id.shape[0] // 2

    def away(values, ids):
        return as_points(segment_few(-values, ids, points), points)

    west_part = away(flow[:half], far_id[:half])
    east_part = away(flow[half:], far_id[half:])
    lat_part = away(
        jnp.concatenate([flow_l, pad], 0),
        jnp.concatenate([lat_lines[ID_L : ID_L + 1, :], pad], 0).astype(i32),
    )
    west, east, other = neighbours(n_lon, n_lat)
    part = jnp.concatenate([own, east_part, west_part, lat_part], 0)
    begin = 4 * blocks
    deep = begin + half
    first_lane = iota((1, LANES), 1) == 0

    def corners(block):
        return jnp.where(
            first_lane,
            block[0:1],
            jnp.broadcast_to(block[half : half + 1, 0:1], (1, LANES)),
        )

    edge_rows = jnp.concatenate(
        [edge, held[0:1, :], corners(faces[GAIN]), corners(faces[RATIO])]
        + [jnp.zeros((1, LANES), f32)] * (half - 4),
        0,
    )
    for target in range(n_lon * n_lat):
        shared = jnp.where(
            target == west, sides[:half], jnp.where(target == east, sides[half:], edge_rows)
        )
        payload[target * deep : (target + 1) * deep, :] = jnp.concatenate([part, shared], 0)


def last_kernel(
    first, second, green, green_north, coarse, ocean, held, faces, lat_lines, lam_sides, lam_edge,
    lam_out, payload, put, north_line, loads, acc, tables, pot,
    *, points, n_lon, n_lat,
):
    rows = held.shape[0]
    blocks = points // LANES
    half = rows // LANES
    deep = 4 * blocks + half
    lat = lax.axis_index("lat")

    def received(owner, kind):
        start = owner * deep + kind * blocks
        return second[start : start + blocks, :]

    for lon in range(n_lon):
        for band in range(n_lat):
            here = lon * n_lat + band
            west = (lon - 1) % n_lon * n_lat + band
            east = (lon + 1) % n_lon * n_lat + band
            other = lon * n_lat + 1 - band
            total = received(here, 0) + received(west, 1) + received(east, 2) + received(other, 3)
            loads[here * blocks : (here + 1) * blocks, :] = (
                total * first[here, blocks : 2 * blocks, :]
            )
    west, east, other = neighbours(n_lon, n_lat)

    def shared(owner, row, count):
        return second[pl.ds(owner * deep + 4 * blocks + row, count), :]

    far = jnp.concatenate([shared(west, 0, half), shared(east, 0, half)], 0)
    rise = jnp.where(west_rows(), lam_sides[...] - far, far - lam_sides[...])
    adj = faces[GAIN] + faces[RATIO] * rise
    put[...] = put_sides(adj, [(slope_ratio, -slope_ratio), (0.0, 1.0)])
    rise = shared(other, 0, 1) - lam_edge[...]
    adj_l = lat_lines[G_L : G_L + 1, :] + lat_lines[C_L : C_L + 1, :] * jnp.where(
        lat == 0, rise, -rise
    )
    from_north = jnp.where(lat == 0, adj_l, 0.0)
    from_south = jnp.where(lat == 1, adj_l, 0.0)
    put[0:1, :LANES] = put[0:1, :LANES] + slope_ratio * from_south
    put[rows - 1 : rows, :LANES] = put[rows - 1 : rows, :LANES] - slope_ratio * from_north
    north_line[...] = from_north
    load_row = lambda k: loads[k : k + 1, :]
    north_sums = green_spread(
        green, coarse, load_row, acc, tables, pot, lambda: green_rows(green_north, 0, load_row)
    )
    for start in range(0, rows, STEP_ROWS):
        at = slice(start, start + STEP_ROWS)
        lam_out[at, :] = ocean[at, :].astype(f32) * (
            held[at, :] + put[at, :LANES] - attract_coef * pot[at, :]
        )
    potential = sum_lanes(north_sums)[0:1]
    diagonal = lambda owner: shared(owner + 1 - 2 * lat, 0, 1)
    lam_n = shared(other, 0, 1)
    lane = iota((1, LANES), 1)
    rise = jnp.where(
        lane == 0, lam_n - roll_west(diagonal(west)), roll_east(diagonal(east)) - lam_n
    )
    adj = shared(other, 2, 1) + shared(other, 3, 1) * rise
    flow = jnp.where(lane == 0, adj, jnp.where(lane == LANES - 1, -adj, 0.0)) + adj_l
    lam_north = lat_lines[MASK_L : MASK_L + 1, :] * (
        shared(other, 1, 1) + slope_ratio * flow - attract_coef * potential
    )
    span = rows // n_lon
    for target in range(n_lon):
        start = target * (span + 1)
        payload[start : start + span, :] = lam_out[target * span : (target + 1) * span, :]
        if target < n_lon - 1:
            stop = (target + 1) * span
            payload[start + span : start + span + 1, :] = lam_out[stop : stop + 1, :]
        else:
            payload[start + span : start + span + 1, :] = lam_north


def bands_kernel(
    parts, lam, adj_u, adj_v, put, north_line,
    lam_out, east_out, north_out, bands, east, north, planes, done, *, count,
):
    span = parts.shape[0] // count - 1
    rows = lam.shape[0]
    copies = [
        pltpu.make_async_copy(lam, lam_out, done.at[0]),
        pltpu.make_async_copy(east, east_out, done.at[1]),
        pltpu.make_async_copy(north, north_out, done.at[2]),
    ] + [
        pltpu.make_async_copy(planes.at[k], bands.at[k, 0], done.at[3 + k]) for k in range(3)
    ]
    copies[0].start()
    lane = iota((span, LANES), 1)
    top = (lax.axis_index("lat") == 1) & (lax.axis_index("lon") == count - 1)
    last = (iota((span, LANES), 0) == span - 1) & top
    for k in range(count):
        start = k * (span + 1)
        planes[0, :, k * LANES : (k + 1) * LANES] = parts[start : start + span, :]
    copies[3].start()
    for k in range(count):
        start = k * (span + 1)
        here = parts[start : start + span, :]
        north_of = jnp.where(last, 0.0, parts[start + 1 : start + 1 + span, :])
        planes[2, :, k * LANES : (k + 1) * LANES] = north_of - here
    copies[5].start()
    for k in range(count):
        at = slice(k * LANES, (k + 1) * LANES)
        here = planes[0, :, at]
        after = (k + 1) % count
        there = planes[0, :, after * LANES : (after + 1) * LANES]
        planes[1, :, at] = jnp.where(lane == LANES - 1, roll_east(there), roll_east(here)) - here
    copies[4].start()
    east[...] = adj_u[...] + put[:, LANES:]
    copies[1].start()
    north[...] = adj_v[...]
    north[rows - 1 : rows, :] = adj_v[rows - 1 : rows, :] + north_line[...]
    copies[2].start()
    for copy in copies:
        copy.wait()


def call(kernel, shapes, scratch, args, name, far=(), far_out=(), limit=16, weight=4, aliases=None):
    vmem = pl.BlockSpec(memory_space=pltpu.VMEM)
    away = pl.BlockSpec(memory_space=pl.ANY)
    shapes = [(shape, f32) if isinstance(shape[0], int) else shape for shape in shapes]
    return pl.pallas_call(
        kernel,
        out_shape=[jax.ShapeDtypeStruct(shape, kind) for shape, kind in shapes],
        in_specs=[away if k in far else vmem for k in range(len(args))],
        out_specs=[away if k in far_out else vmem for k in range(len(shapes))],
        scratch_shapes=scratch,
        compiler_params=pltpu.CompilerParams(vmem_limit_bytes=limit << 20),
        cost_estimate=pl.CostEstimate(flops=weight << 30, bytes_accessed=16 << 20, transcendentals=0),
        input_output_aliases=aliases or {},
        name=name,
    )(*args)


def body(n_lon, n_lat, lam_in, flux_east, flux_north, depth, drag, ocean, coarse_of, green):
    rows, cols = lam_in.shape
    points = green.shape[0]
    blocks = points // LANES
    owners = n_lon * n_lat
    grid = (rows, cols)
    fields = (lam_in, flux_east, flux_north, depth, drag, ocean, coarse_of)
    tall = rows // LANES
    to_east, to_west, to_lat, *fields = call(
        functools.partial(pack_kernel, points=points),
        [(6 * tall, cols), (6 * tall, cols), (8, cols)]
        + [(grid, field.dtype) for field in fields],
        [pltpu.SemaphoreType.DMA((7,))], fields, "pack", far=range(7), limit=52,
    )
    ocean, coarse_of = fields[5:]
    forward = [(k, (k + 1) % n_lon) for k in range(n_lon)]
    backward = [(target, source) for source, target in forward]
    from_lat = lax.ppermute(to_lat, "lat", [(0, 1), (1, 0)])
    from_east = lax.ppermute(to_west, "lon", backward)
    to_east, from_lat = lax.optimization_barrier((to_east, from_lat))
    from_west = lax.ppermute(to_east, "lon", forward)
    held, gu, cu, gv, cv, sums, left, right, held_sides, green_top = call(
        functools.partial(inner_kernel, points=points),
        [grid] * 5
        + [((PIECES + 1) * HIGH, LOW), ((HIGH, rows * cols), bf16), ((LOW, rows * cols), bf16)]
        + [(2 * tall, cols), (LANES, green.shape[1])],
        [pltpu.VMEM(grid, f32), pltpu.SemaphoreType.DMA(())], (*fields, green), "inner",
        far=(7,), limit=INNER_LIMIT,
    )
    payload, faces, lat_lines, green_top = call(
        functools.partial(rim_kernel, points=points),
        [(owners, 8, LANES), (7, 2 * tall, cols), (8, cols), green_top.shape], [],
        (
            to_east, to_west, to_lat, from_west, from_east, from_lat, sums, held_sides, green_top,
        ),
        "rim", far=(8,), far_out=(3,), weight=16, aliases={8: 3},
    )
    green_north = lax.ppermute(green_top, "lat", [(0, 1), (1, 0)])
    first = lax.all_to_all(payload, ("lon", "lat"), 0, 0, tiled=True)
    deep = 4 * blocks + tall
    green_scratch = [
        pltpu.VMEM((LANES, LANES), f32),
        pltpu.VMEM((blocks, 8, LANES), f32),
        pltpu.VMEM(grid, f32),
    ]
    payload, held, adj_u, adj_v, lam_sides, lam_edge = call(
        functools.partial(second_kernel, points=points, n_lon=n_lon, n_lat=n_lat),
        [(owners * deep, LANES), grid, grid, grid, (2 * tall, cols), (1, cols)],
        green_scratch + [pltpu.VMEM((rows + 8, cols), f32), pltpu.VMEM(grid, f32)],
        (first, green, coarse_of, ocean, held, gu, cu, gv, cv, left, right, faces, lat_lines),
        "second",
    )
    second = lax.all_to_all(
        payload.reshape(owners, deep, 1, LANES), ("lon", "lat"), 0, 0, tiled=True
    ).reshape(payload.shape)
    span = rows // n_lon
    lam, payload, put, north_line = call(
        functools.partial(last_kernel, points=points, n_lon=n_lon, n_lat=n_lat),
        [grid, (rows + n_lon, cols), (rows, 2 * cols), (1, cols)],
        [
            pltpu.VMEM((owners * blocks, LANES), f32),
        ]
        + green_scratch,
        (
            first, second, green, green_north, coarse_of, ocean, held, faces, lat_lines,
            lam_sides, lam_edge,
        ),
        "last",
    )
    parts = lax.all_to_all(
        payload.reshape(n_lon, span + 1, 1, LANES), "lon", 0, 0, tiled=True
    ).reshape(payload.shape)
    return tuple(
        call(
            functools.partial(bands_kernel, count=n_lon),
            [grid, grid, grid, (3, 1, span, n_lon * cols)],
            [
                pltpu.VMEM(grid, f32),
                pltpu.VMEM(grid, f32),
                pltpu.VMEM((3, span, n_lon * cols), f32),
                pltpu.SemaphoreType.DMA((6,)),
            ],
            (parts, lam, adj_u, adj_v, put, north_line), "bands", far_out=range(4),
        )
    )


def solution(mesh):
    cells = P(("groups", "lat"), "lon")
    n_lon, n_lat = mesh.shape["lon"], mesh.shape["lat"]
    return jax.shard_map(
        functools.partial(body, n_lon, n_lat),
        mesh=mesh,
        in_specs=(cells,) * 6 + (P("lat", "lon"), P(("lon", "lat"), None)),
        out_specs=(cells,) * 3 + (P(None, ("groups", "lat"), "lon", None),),
        check_vma=False,
    )
```

```python
import functools

import jax
import jax.numpy as jnp
from jax import lax
from jax.experimental import pallas as pl
from jax.experimental.pallas import tpu as pltpu
from jax.sharding import PartitionSpec as P

f32 = jnp.float32
bf16 = jnp.bfloat16
i32 = jnp.int32

LANES = 128
LOW = 32
HIGH = 16
PIECES = 2
INNER_LIMIT = 36
SEG_ROWS = 256
STEP_ROWS = 128

flux_ratio = 0.25
slope_ratio = 0.25
drag_step = 1.0
attract_coef = 0.5

LAM, DEPTH, DRAG, OCEAN, POINT, FLUX = range(6)
ADJ, RATIO, GAIN, BASE, MASK, OWN_ID, FAR_ID = range(7)
ADJ_L, C_L, G_L, ID_L, OWN_L, MASK_L = range(6)


def iota(shape, dim):
    return lax.broadcasted_iota(i32, shape, dim)


def roll_east(x):
    return pltpu.roll(x, LANES - 1, 1)


def roll_west(x):
    return pltpu.roll(x, 1, 1)


def local_ids(ids, points):
    return lax.bitwise_and(ids, points - 1)


def bf16_pieces(values, count=PIECES):
    out = []
    for piece in range(count):
        top = values.astype(bf16).astype(f32)
        out.append(top)
        if piece < count - 1:
            values = values - top
    return out


def one_hots(ids, points):
    blocks = points // LANES
    high = lax.shift_right_logical(ids, 5)
    high = lax.bitwise_and(high, 3) * blocks + lax.shift_right_logical(high, 2)
    low = lax.bitwise_and(ids, LOW - 1)
    high_iota = iota((HIGH, LANES), 0)
    low_iota = iota((LOW, LANES), 0)
    left, right = [], []
    for row in range(ids.shape[0]):
        mask = jnp.broadcast_to(high[row : row + 1], (HIGH, LANES)) == high_iota
        left.append(jnp.where(mask, 1.0, 0.0).astype(bf16))
        mask = jnp.broadcast_to(low[row : row + 1], (LOW, LANES)) == low_iota
        right.append(jnp.where(mask, 1.0, 0.0).astype(bf16))
    return jnp.concatenate(left, 1), jnp.concatenate(right, 1)


def segment_part(values, left, right, with_counts=False):
    parts = []
    for piece in bf16_pieces(values):
        line = jnp.concatenate(
            [
                jnp.broadcast_to(piece[row : row + 1], (HIGH, LANES)).astype(bf16)
                for row in range(values.shape[0])
            ],
            1,
        )
        parts.append(left * line)
    if with_counts:
        parts.append(left)
    return lax.dot_general(
        jnp.concatenate(parts, 0), right, (((1,), (1,)), ((), ())), preferred_element_type=f32
    )


def segment_few(values, ids, points):
    return sum_pieces(segment_part(values, *one_hots(ids, points)))


def sum_pieces(parts):
    total = parts[:HIGH]
    for piece in range(1, PIECES):
        total = total + parts[piece * HIGH : (piece + 1) * HIGH]
    return total


def as_points(table, points):
    blocks = points // LANES
    return jnp.concatenate([table[q * blocks : (q + 1) * blocks] for q in range(4)], 1)


def fold(line):
    return jnp.concatenate(
        [line[:, k * LANES : (k + 1) * LANES] for k in range(line.shape[1] // LANES)], 0
    )


def unfold(block):
    return jnp.concatenate([block[k : k + 1] for k in range(block.shape[0])], 1)


def take_sides(block, count=3):
    sub, lane = iota((8, LANES), 0), iota((8, LANES), 1)
    pick = ((sub == 0) & (lane == 0)) | ((sub == 1) & (lane == LANES - 1))
    pick = pick.astype(f32).astype(bf16)
    out = None
    for piece in reversed(bf16_pieces(block, count)):
        part = lax.dot_general(
            pick, piece.astype(bf16), (((1,), (1,)), ((), ())), preferred_element_type=f32
        )
        out = part if out is None else out + part
    return out


def put_sides(pair, entries):
    half = pair.shape[0] // 2
    lines = jnp.concatenate([unfold(pair[:half]), unfold(pair[half:])], 0)
    rows = lines.shape[1]
    pieces = bf16_pieces(lines, 3)
    stack = jnp.concatenate(pieces + [jnp.zeros((2, rows), f32)], 0)
    sub, lane = iota((8, LANES), 0), iota((8, LANES), 1)
    west = (sub < 6) & (lax.bitwise_and(sub, 1) == 0) & (lane == 0)
    east = (sub < 6) & (lax.bitwise_and(sub, 1) == 1) & (lane == LANES - 1)
    picks = [jnp.where(west, first, jnp.where(east, last, 0.0)) for first, last in entries]
    return lax.dot_general(
        stack, jnp.concatenate(picks, 1), (((0,), (0,)), ((), ())), preferred_element_type=f32
    )


def sum_lanes(block):
    out = None
    for piece in reversed(bf16_pieces(block, 3)):
        part = lax.dot_general(
            jnp.ones((8, LANES), bf16), piece.astype(bf16), (((1,), (1,)), ((), ())),
            preferred_element_type=f32,
        )
        out = part if out is None else out + part
    return out


def green_rows(green_ref, start, load_row):
    acc = jnp.zeros((LANES, LANES), f32)
    for k in range(green_ref.shape[1] // LANES):
        acc = acc + green_ref[
            pl.ds(start, LANES), k * LANES : (k + 1) * LANES
        ] * jnp.broadcast_to(load_row(k), (LANES, LANES))
    return acc


def look_up(table, ids):
    rows = ids.shape[0]
    table = jnp.broadcast_to(table[None], (rows // 8, 8, LANES)).reshape(rows, LANES)
    return jnp.take_along_axis(table, ids, axis=1, mode="promise_in_bounds")


def spread(tables, ids):
    low = lax.bitwise_and(ids, LANES - 1)
    block = lax.shift_right_logical(ids, 7)
    out = None
    for k, table in enumerate(tables):
        value = look_up(table, low)
        out = value if out is None else jnp.where(block == k, value, out)
    return out


def green_spread(green, coarse, load_row, acc, tables, pot, more=None):
    points = green.shape[0]
    rows = coarse.shape[0]

    def settle(index):
        table = sum_lanes(acc[...])
        tables[index] = table
        for start in range(0, rows, STEP_ROWS):
            at = slice(start, start + STEP_ROWS)
            ids = local_ids(coarse[at, :], points)
            value = look_up(table, lax.bitwise_and(ids, LANES - 1))
            if index > 0:
                value = jnp.where(lax.shift_right_logical(ids, 7) == index, value, pot[at, :])
            pot[at, :] = value

    def step(index, carry):
        block = green_rows(green, index * LANES, load_row)
        settle(index - 1)
        acc[...] = block
        return carry

    acc[...] = green_rows(green, 0, load_row)
    for index in range(1, points // LANES):
        step(index, 0)
    beside = more() if more else None
    settle(points // LANES - 1)
    return beside


def next_rows(ref, start, count):
    if start + count < ref.shape[0]:
        return ref[start + 1 : start + count + 1, :]
    return jnp.concatenate([ref[start + 1 :, :], jnp.zeros((1, LANES), ref.dtype)], 0)


def south_rows(first, block):
    return jnp.concatenate([first, block[:-1]], 0)


def pack_kernel(*refs, points):
    far, (to_east, to_west, to_lat), near, done = refs[:7], refs[7:10], refs[10:17], refs[17]
    copies = [pltpu.make_async_copy(far[k], near[k], done.at[k]) for k in range(7)]
    for copy in copies:
        copy.start()
    lam, east, north, depth, drag, ocean, coarse = near
    rows = lam.shape[0]
    tall = rows // LANES
    lat = lax.axis_index("lat")
    order = (
        (LAM, 0, lam, 2), (FLUX, 1, east, 2), (None, 2, north, 0), (DEPTH, 3, depth, 2),
        (DRAG, 4, drag, 2), (OCEAN, 5, ocean, 1), (POINT, 6, coarse, 2),
    )
    for field, index, ref, pieces in order:
        copies[index].wait()
        if field is None:
            continue
        block = ref[...]
        if field == POINT:
            block = local_ids(block, points)
        sides = take_sides(block.astype(f32), pieces)
        at = slice(field * tall, (field + 1) * tall)
        to_west[at, :] = fold(sides[0:1])
        to_east[at, :] = fold(sides[1:2])

    def border(row):
        return jnp.concatenate(
            [
                lam[row : row + 1, :],
                depth[row : row + 1, :],
                drag[row : row + 1, :],
                ocean[row : row + 1, :].astype(f32),
                local_ids(coarse[row : row + 1, :], points).astype(f32),
                north[row : row + 1, :],
                jnp.zeros((2, LANES), f32),
            ],
            0,
        )

    to_lat[...] = jnp.where(lat == 0, border(rows - 1), border(0))


def inner_kernel(
    lam, east, north, depth, drag, ocean, coarse, green,
    held, gu, cu, gv, cv, sums, left, right, held_sides, green_top, source, done, *, points,
):
    copy = pltpu.make_async_copy(green.at[pl.ds(0, LANES)], green_top, done)
    copy.start()
    rows = lam.shape[0]
    inner = iota((STEP_ROWS, LANES), 1) < LANES - 1
    carry = jnp.zeros((1, LANES), f32)
    for start in range(0, rows, STEP_ROWS):
        at = slice(start, start + STEP_ROWS)
        lam_c, depth_c, drag_c = lam[at, :], depth[at, :], drag[at, :]
        ocean_c = ocean[at, :].astype(f32)
        damp = jnp.where(
            inner,
            ocean_c * roll_east(ocean_c) / (1.0 + drag_step * 0.5 * (drag_c + roll_east(drag_c))),
            0.0,
        )
        ratio = damp * (flux_ratio * 0.5) * (depth_c + roll_east(depth_c))
        adj_u = damp * east[at, :] + ratio * (roll_east(lam_c) - lam_c)
        cu[at, :] = ratio
        gu[at, :] = damp * adj_u
        ocean_n = next_rows(ocean, start, STEP_ROWS).astype(f32)
        damp = (
            ocean_c
            * ocean_n
            / (1.0 + drag_step * 0.5 * (drag_c + next_rows(drag, start, STEP_ROWS)))
        )
        ratio = damp * (flux_ratio * 0.5) * (depth_c + next_rows(depth, start, STEP_ROWS))
        adj_v = damp * north[at, :] + ratio * (next_rows(lam, start, STEP_ROWS) - lam_c)
        cv[at, :] = ratio
        gv[at, :] = damp * adj_v
        src = slope_ratio * (roll_west(adj_u) - adj_u + south_rows(carry, adj_v) - adj_v)
        carry = adj_v[STEP_ROWS - 1 :]
        source[at, :] = src
        held[at, :] = lam_c + src
    total = jnp.zeros(sums.shape, f32)
    for start in range(0, rows, SEG_ROWS):
        at = slice(start, start + SEG_ROWS)
        cells = slice(start * LANES, (start + SEG_ROWS) * LANES)
        high, low = one_hots(local_ids(coarse[at, :], points), points)
        left[:, cells] = high
        right[:, cells] = low
        total = total + segment_part(source[at, :], high, low, True)
    sums[...] = total
    sides = take_sides(held[...])
    held_sides[...] = jnp.concatenate([fold(sides[0:1]), fold(sides[1:2])], 0)
    copy.wait()


def face(low, high, flux):
    damp = low[OCEAN] * high[OCEAN] / (1.0 + drag_step * 0.5 * (low[DRAG] + high[DRAG]))
    ratio = damp * (flux_ratio * 0.5) * (low[DEPTH] + high[DEPTH])
    adj = damp * flux + ratio * (high[LAM] - low[LAM])
    return adj, ratio, damp * adj


def west_rows():
    return iota((8, LANES), 0) < 4


def rim_kernel(
    own_east, own_west, own_lat, from_west, from_east, from_lat, sums, held_sides, green_in,
    payload, faces, lat_lines, green_out, *, points,
):
    lat = lax.axis_index("lat")
    half = held_sides.shape[0] // 2

    def pair(west, east):
        return [
            jnp.concatenate(
                [west[k * half : (k + 1) * half, :], east[k * half : (k + 1) * half, :]], 0
            )
            for k in range(6)
        ]

    own, far = pair(own_west, own_east), pair(from_west, from_east)
    is_west = west_rows()
    low = [jnp.where(is_west, there, here) for here, there in zip(own, far)]
    high = [jnp.where(is_west, here, there) for here, there in zip(own, far)]
    adj, ratio, gain = face(low, high, low[FLUX])
    mine, other = own_lat[...], from_lat[...]
    lower = jnp.where(lat == 0, mine, other)
    upper = jnp.where(lat == 0, other, mine)
    lower = [lower[k : k + 1] for k in range(6)]
    upper = [upper[k : k + 1] for k in range(6)]
    adj_l, c_l, g_l = face(lower, upper, lower[FLUX])
    lat_lines[...] = jnp.concatenate(
        [
            adj_l, c_l, g_l, other[POINT : POINT + 1], mine[POINT : POINT + 1],
            other[OCEAN : OCEAN + 1], jnp.zeros((2, LANES), f32),
        ],
        0,
    )
    sign = jnp.where(is_west, slope_ratio, -slope_ratio)
    sign_l = jnp.where(lat == 0, -slope_ratio, slope_ratio)
    flow = sign * adj
    sub, lane = lax.bitwise_and(iota((8, LANES), 0), half - 1), iota((8, LANES), 1)
    corner = ((lat == 0) & (sub == half - 1) & (lane == LANES - 1)) | (
        (lat == 1) & (sub == 0) & (lane == 0)
    )
    at_corner = jnp.where(
        is_west,
        jnp.broadcast_to(adj_l[:, 0:1], (8, LANES)),
        jnp.broadcast_to(adj_l[:, LANES - 1 :], (8, LANES)),
    )
    faces[ADJ] = adj
    faces[RATIO] = ratio
    faces[GAIN] = gain
    faces[BASE] = held_sides[...] + flow + jnp.where(corner, sign_l * at_corner, 0.0)
    faces[MASK] = own[OCEAN]
    faces[OWN_ID] = own[POINT]
    faces[FAR_ID] = far[POINT]
    pad = jnp.zeros((1, LANES), f32)
    values = jnp.concatenate([flow, sign_l * adj_l, pad], 0)
    ids = jnp.concatenate([own[POINT], mine[POINT : POINT + 1], pad], 0).astype(i32)
    total = sum_pieces(sums[...]) + segment_few(values, ids, points)
    counts = as_points(sums[PIECES * HIGH : (PIECES + 1) * HIGH, :], points)
    inverse = 1.0 / counts
    loads = as_points(total, points) * inverse
    part = jnp.concatenate([loads, inverse], 0)
    if part.shape[0] < 8:
        part = jnp.concatenate([part, jnp.zeros((8 - part.shape[0], LANES), f32)], 0)
    for target in range(payload.shape[0]):
        payload[target] = part


def neighbours(n_lon, n_lat):
    lon, lat = lax.axis_index("lon"), lax.axis_index("lat")
    west = lax.rem(lon + n_lon - 1, n_lon) * n_lat + lat
    east = lax.rem(lon + 1, n_lon) * n_lat + lat
    other = lon * n_lat + (1 - lat)
    return west, east, other


def second_kernel(
    first, green, coarse, ocean, held_in, gu, cu, gv, cv, left, right, faces, lat_lines,
    payload, held, adj_u_out, adj_v_out, lam_sides, lam_edge, acc, tables, pot, lam, source,
    *, points, n_lon, n_lat,
):
    rows = coarse.shape[0]
    blocks = points // LANES
    lat = lax.axis_index("lat")
    south_end = jnp.where(lat == 1, 1.0, 0.0)
    north_end = jnp.where(lat == 0, 1.0, 0.0)
    green_spread(
        green, coarse, lambda k: first[k // blocks, k % blocks : k % blocks + 1, :],
        acc, tables, pot,
    )
    put = put_sides(faces[ADJ], [(slope_ratio, -slope_ratio)])
    adj_l = lat_lines[ADJ_L : ADJ_L + 1, :]
    c_l = lat_lines[C_L : C_L + 1, :]
    g_l = lat_lines[G_L : G_L + 1, :]
    row = iota((STEP_ROWS, LANES), 0)
    lam[rows : rows + 8, :] = jnp.zeros((8, LANES), f32)
    for start in range(0, rows, STEP_ROWS):
        at = slice(start, start + STEP_ROWS)
        value = held_in[at, :] + put[at, :] - attract_coef * pot[at, :]
        if start == 0:
            value = value + jnp.where(row == 0, south_end * slope_ratio * adj_l, 0.0)
        if start == rows - STEP_ROWS:
            value = value - jnp.where(row == STEP_ROWS - 1, north_end * slope_ratio * adj_l, 0.0)
        lam[at, :] = ocean[at, :].astype(f32) * value
    carry = jnp.zeros((1, LANES), f32)
    for start in range(0, rows, STEP_ROWS):
        at = slice(start, start + STEP_ROWS)
        lam_c = lam[at, :]
        adj_u = gu[at, :] + cu[at, :] * (roll_east(lam_c) - lam_c)
        adj_v = gv[at, :] + cv[at, :] * (lam[start + 1 : start + STEP_ROWS + 1, :] - lam_c)
        src = slope_ratio * (roll_west(adj_u) - adj_u + south_rows(carry, adj_v) - adj_v)
        carry = adj_v[STEP_ROWS - 1 :]
        adj_u_out[at, :] = adj_u
        adj_v_out[at, :] = adj_v
        source[at, :] = src
        held[at, :] = lam_c + src
    is_west = west_rows()
    sides = faces[MASK] * (
        faces[BASE]
        - attract_coef * spread([tables[k] for k in range(blocks)], faces[OWN_ID].astype(i32))
    )
    lam_sides[...] = sides
    pull = faces[RATIO] * sides
    flow = slope_ratio * jnp.where(is_west, pull, pull - faces[GAIN])
    edge = jnp.where(lat == 0, lam[rows - 1 : rows, :], lam[0:1, :])
    lam_edge[...] = edge
    pull = c_l * edge
    flow_l = slope_ratio * jnp.where(lat == 0, pull - g_l, pull)
    pad = jnp.zeros((1, LANES), f32)
    total = segment_part(
        jnp.concatenate([flow, flow_l, pad], 0),
        *one_hots(
            jnp.concatenate([faces[OWN_ID], lat_lines[OWN_L : OWN_L + 1, :], pad], 0).astype(i32),
            points,
        ),
    )
    def add(index, total):
        at = pl.ds(pl.multiple_of(index * SEG_ROWS, SEG_ROWS), SEG_ROWS)
        cells = pl.ds(pl.multiple_of(index * SEG_ROWS * LANES, SEG_ROWS * LANES), SEG_ROWS * LANES)
        return total + segment_part(source[at, :], left[:, cells], right[:, cells])

    total = lax.fori_loop(0, rows // SEG_ROWS, add, total)
    own = as_points(sum_pieces(total), points)
    far_id = faces[FAR_ID].astype(i32)
    half = far_id.shape[0] // 2

    def away(values, ids):
        return as_points(segment_few(-values, ids, points), points)

    west_part = away(flow[:half], far_id[:half])
    east_part = away(flow[half:], far_id[half:])
    lat_part = away(
        jnp.concatenate([flow_l, pad], 0),
        jnp.concatenate([lat_lines[ID_L : ID_L + 1, :], pad], 0).astype(i32),
    )
    west, east, other = neighbours(n_lon, n_lat)
    part = jnp.concatenate([own, east_part, west_part, lat_part], 0)
    begin = 4 * blocks
    deep = begin + half
    first_lane = iota((1, LANES), 1) == 0

    def corners(block):
        return jnp.where(
            first_lane,
            block[0:1],
            jnp.broadcast_to(block[half : half + 1, 0:1], (1, LANES)),
        )

    edge_rows = jnp.concatenate(
        [edge, held[0:1, :], corners(faces[GAIN]), corners(faces[RATIO])]
        + [jnp.zeros((1, LANES), f32)] * (half - 4),
        0,
    )
    for target in range(n_lon * n_lat):
        shared = jnp.where(
            target == west, sides[:half], jnp.where(target == east, sides[half:], edge_rows)
        )
        payload[target * deep : (target + 1) * deep, :] = jnp.concatenate([part, shared], 0)


def last_kernel(
    first, second, green, green_north, coarse, ocean, held, faces, lat_lines, lam_sides, lam_edge,
    lam_out, payload, put, north_line, loads, acc, tables, pot,
    *, points, n_lon, n_lat,
):
    rows = held.shape[0]
    blocks = points // LANES
    half = rows // LANES
    deep = 4 * blocks + half
    lat = lax.axis_index("lat")

    def received(owner, kind):
        start = owner * deep + kind * blocks
        return second[start : start + blocks, :]

    for lon in range(n_lon):
        for band in range(n_lat):
            here = lon * n_lat + band
            west = (lon - 1) % n_lon * n_lat + band
            east = (lon + 1) % n_lon * n_lat + band
            other = lon * n_lat + 1 - band
            total = received(here, 0) + received(west, 1) + received(east, 2) + received(other, 3)
            loads[here * blocks : (here + 1) * blocks, :] = (
                total * first[here, blocks : 2 * blocks, :]
            )
    west, east, other = neighbours(n_lon, n_lat)

    def shared(owner, row, count):
        return second[pl.ds(owner * deep + 4 * blocks + row, count), :]

    far = jnp.concatenate([shared(west, 0, half), shared(east, 0, half)], 0)
    rise = jnp.where(west_rows(), lam_sides[...] - far, far - lam_sides[...])
    adj = faces[GAIN] + faces[RATIO] * rise
    put[...] = put_sides(adj, [(slope_ratio, -slope_ratio), (0.0, 1.0)])
    rise = shared(other, 0, 1) - lam_edge[...]
    adj_l = lat_lines[G_L : G_L + 1, :] + lat_lines[C_L : C_L + 1, :] * jnp.where(
        lat == 0, rise, -rise
    )
    from_north = jnp.where(lat == 0, adj_l, 0.0)
    from_south = jnp.where(lat == 1, adj_l, 0.0)
    put[0:1, :LANES] = put[0:1, :LANES] + slope_ratio * from_south
    put[rows - 1 : rows, :LANES] = put[rows - 1 : rows, :LANES] - slope_ratio * from_north
    north_line[...] = from_north
    load_row = lambda k: loads[k : k + 1, :]
    north_sums = green_spread(
        green, coarse, load_row, acc, tables, pot, lambda: green_rows(green_north, 0, load_row)
    )
    for start in range(0, rows, STEP_ROWS):
        at = slice(start, start + STEP_ROWS)
        lam_out[at, :] = ocean[at, :].astype(f32) * (
            held[at, :] + put[at, :LANES] - attract_coef * pot[at, :]
        )
    potential = sum_lanes(north_sums)[0:1]
    diagonal = lambda owner: shared(owner + 1 - 2 * lat, 0, 1)
    lam_n = shared(other, 0, 1)
    lane = iota((1, LANES), 1)
    rise = jnp.where(
        lane == 0, lam_n - roll_west(diagonal(west)), roll_east(diagonal(east)) - lam_n
    )
    adj = shared(other, 2, 1) + shared(other, 3, 1) * rise
    flow = jnp.where(lane == 0, adj, jnp.where(lane == LANES - 1, -adj, 0.0)) + adj_l
    lam_north = lat_lines[MASK_L : MASK_L + 1, :] * (
        shared(other, 1, 1) + slope_ratio * flow - attract_coef * potential
    )
    span = rows // n_lon
    for target in range(n_lon):
        start = target * (span + 1)
        payload[start : start + span, :] = lam_out[target * span : (target + 1) * span, :]
        if target < n_lon - 1:
            stop = (target + 1) * span
            payload[start + span : start + span + 1, :] = lam_out[stop : stop + 1, :]
        else:
            payload[start + span : start + span + 1, :] = lam_north


def bands_kernel(
    parts, lam, adj_u, adj_v, put, north_line,
    lam_out, east_out, north_out, bands, east, north, planes, done, *, count,
):
    span = parts.shape[0] // count - 1
    rows = lam.shape[0]
    copies = [
        pltpu.make_async_copy(lam, lam_out, done.at[0]),
        pltpu.make_async_copy(east, east_out, done.at[1]),
        pltpu.make_async_copy(north, north_out, done.at[2]),
    ] + [
        pltpu.make_async_copy(planes.at[k], bands.at[k, 0], done.at[3 + k]) for k in range(3)
    ]
    copies[0].start()
    lane = iota((span, LANES), 1)
    top = (lax.axis_index("lat") == 1) & (lax.axis_index("lon") == count - 1)
    last = (iota((span, LANES), 0) == span - 1) & top
    for k in range(count):
        start = k * (span + 1)
        planes[0, :, k * LANES : (k + 1) * LANES] = parts[start : start + span, :]
    copies[3].start()
    for k in range(count):
        start = k * (span + 1)
        here = parts[start : start + span, :]
        north_of = jnp.where(last, 0.0, parts[start + 1 : start + 1 + span, :])
        planes[2, :, k * LANES : (k + 1) * LANES] = north_of - here
    copies[5].start()
    for k in range(count):
        at = slice(k * LANES, (k + 1) * LANES)
        here = planes[0, :, at]
        after = (k + 1) % count
        there = planes[0, :, after * LANES : (after + 1) * LANES]
        planes[1, :, at] = jnp.where(lane == LANES - 1, roll_east(there), roll_east(here)) - here
    copies[4].start()
    east[...] = adj_u[...] + put[:, LANES:]
    copies[1].start()
    north[...] = adj_v[...]
    north[rows - 1 : rows, :] = adj_v[rows - 1 : rows, :] + north_line[...]
    copies[2].start()
    for copy in copies:
        copy.wait()


def call(kernel, shapes, scratch, args, name, far=(), far_out=(), limit=16, weight=4, aliases=None):
    vmem = pl.BlockSpec(memory_space=pltpu.VMEM)
    away = pl.BlockSpec(memory_space=pl.ANY)
    shapes = [(shape, f32) if isinstance(shape[0], int) else shape for shape in shapes]
    return pl.pallas_call(
        kernel,
        out_shape=[jax.ShapeDtypeStruct(shape, kind) for shape, kind in shapes],
        in_specs=[away if k in far else vmem for k in range(len(args))],
        out_specs=[away if k in far_out else vmem for k in range(len(shapes))],
        scratch_shapes=scratch,
        compiler_params=pltpu.CompilerParams(vmem_limit_bytes=limit << 20),
        cost_estimate=pl.CostEstimate(flops=weight << 30, bytes_accessed=16 << 20, transcendentals=0),
        input_output_aliases=aliases or {},
        name=name,
    )(*args)


def body(n_lon, n_lat, lam_in, flux_east, flux_north, depth, drag, ocean, coarse_of, green):
    rows, cols = lam_in.shape
    points = green.shape[0]
    blocks = points // LANES
    owners = n_lon * n_lat
    grid = (rows, cols)
    fields = (lam_in, flux_east, flux_north, depth, drag, ocean, coarse_of)
    tall = rows // LANES
    to_east, to_west, to_lat, *fields = call(
        functools.partial(pack_kernel, points=points),
        [(6 * tall, cols), (6 * tall, cols), (8, cols)]
        + [(grid, field.dtype) for field in fields],
        [pltpu.SemaphoreType.DMA((7,))], fields, "pack", far=range(7), limit=52,
    )
    ocean, coarse_of = fields[5:]
    forward = [(k, (k + 1) % n_lon) for k in range(n_lon)]
    backward = [(target, source) for source, target in forward]
    from_east = lax.ppermute(to_west, "lon", backward)
    from_west = lax.ppermute(to_east, "lon", forward)
    from_lat = lax.ppermute(to_lat, "lat", [(0, 1), (1, 0)])
    held, gu, cu, gv, cv, sums, left, right, held_sides, green_top = call(
        functools.partial(inner_kernel, points=points),
        [grid] * 5
        + [((PIECES + 1) * HIGH, LOW), ((HIGH, rows * cols), bf16), ((LOW, rows * cols), bf16)]
        + [(2 * tall, cols), (LANES, green.shape[1])],
        [pltpu.VMEM(grid, f32), pltpu.SemaphoreType.DMA(())], (*fields, green), "inner",
        far=(7,), limit=INNER_LIMIT,
    )
    payload, faces, lat_lines, green_top = call(
        functools.partial(rim_kernel, points=points),
        [(owners, 8, LANES), (7, 2 * tall, cols), (8, cols), green_top.shape], [],
        (
            to_east, to_west, to_lat, from_west, from_east, from_lat, sums, held_sides, green_top,
        ),
        "rim", far=(8,), far_out=(3,), weight=16, aliases={8: 3},
    )
    green_north = lax.ppermute(green_top, "lat", [(0, 1), (1, 0)])
    first = lax.all_to_all(payload, ("lon", "lat"), 0, 0, tiled=True)
    deep = 4 * blocks + tall
    green_scratch = [
        pltpu.VMEM((LANES, LANES), f32),
        pltpu.VMEM((blocks, 8, LANES), f32),
        pltpu.VMEM(grid, f32),
    ]
    payload, held, adj_u, adj_v, lam_sides, lam_edge = call(
        functools.partial(second_kernel, points=points, n_lon=n_lon, n_lat=n_lat),
        [(owners * deep, LANES), grid, grid, grid, (2 * tall, cols), (1, cols)],
        green_scratch + [pltpu.VMEM((rows + 8, cols), f32), pltpu.VMEM(grid, f32)],
        (first, green, coarse_of, ocean, held, gu, cu, gv, cv, left, right, faces, lat_lines),
        "second",
    )
    second = lax.all_to_all(
        payload.reshape(owners, deep, 1, LANES), ("lon", "lat"), 0, 0, tiled=True
    ).reshape(payload.shape)
    span = rows // n_lon
    lam, payload, put, north_line = call(
        functools.partial(last_kernel, points=points, n_lon=n_lon, n_lat=n_lat),
        [grid, (rows + n_lon, cols), (rows, 2 * cols), (1, cols)],
        [
            pltpu.VMEM((owners * blocks, LANES), f32),
        ]
        + green_scratch,
        (
            first, second, green, green_north, coarse_of, ocean, held, faces, lat_lines,
            lam_sides, lam_edge,
        ),
        "last",
    )
    parts = lax.all_to_all(
        payload.reshape(n_lon, span + 1, 1, LANES), "lon", 0, 0, tiled=True
    ).reshape(payload.shape)
    return tuple(
        call(
            functools.partial(bands_kernel, count=n_lon),
            [grid, grid, grid, (3, 1, span, n_lon * cols)],
            [
                pltpu.VMEM(grid, f32),
                pltpu.VMEM(grid, f32),
                pltpu.VMEM((3, span, n_lon * cols), f32),
                pltpu.SemaphoreType.DMA((6,)),
            ],
            (parts, lam, adj_u, adj_v, put, north_line), "bands", far_out=range(4),
        )
    )


def solution(mesh):
    cells = P(("groups", "lat"), "lon")
    n_lon, n_lat = mesh.shape["lon"], mesh.shape["lat"]
    return jax.shard_map(
        functools.partial(body, n_lon, n_lat),
        mesh=mesh,
        in_specs=(cells,) * 6 + (P("lat", "lon"), P(("lon", "lat"), None)),
        out_specs=(cells,) * 3 + (P(None, ("groups", "lat"), "lon", None),),
        check_vma=False,
    )
```
